32 devices in a mesh: expert: 4 (over z), tensor: 8 (over y, x, core).
Axes of the slice: x: 2, y: 2, z: 4, core: 2. Of those that a mesh axis runs over, the one named last changes fastest.
Arguments:
- tokens: bfloat16 [4096, 2048], P('expert'), may hold values from -6 to 6
- positions: int32 [4096], P('expert'), may hold values from 0 to 4095, as said below
- routes: int32 [4096, 8], P('expert'), may hold values from 0 to 15, as said below
- slot_ids: int32 [4096, 8], P('expert'), may hold values from 0 to 959, as said below
- attn_gain: float32 [2048], replicated, may hold values from 0.25 to 1.75
- w_query: bfloat16 [2048, 2048], P(None, 'tensor'), may hold values from -0.125 to 0.125
- w_key: bfloat16 [2048, 2048], P(None, 'tensor'), may hold values from -0.125 to 0.125
- w_value: bfloat16 [2048, 2048], P(None, 'tensor'), may hold values from -0.125 to 0.125
- query_gain: float32 [2048], P('tensor'), may hold values from 0.25 to 1.75
- key_gain: float32 [2048], P('tensor'), may hold values from 0.25 to 1.75
- w_out: bfloat16 [2048, 2048], P('tensor'), may hold values from -0.75 to 0.75
- ffn_gain: float32 [2048], replicated, may hold values from 0.25 to 1.75
- router: bfloat16 [2048, 16], replicated, may hold values from -0.0625 to 0.0625
- w_gate: bfloat16 [32, 2048, 512], P(('expert', 'tensor')), may hold values from -0.125 to 0.125
- w_up: bfloat16 [32, 2048, 512], P(('expert', 'tensor')), may hold values from -0.125 to 0.125
- w_down: bfloat16 [32, 512, 2048], P(('expert', 'tensor')), may hold values from -1 to 1
- grad_out: bfloat16 [4096, 2048], P('expert'), may hold values from -6 to 6
Outputs:
- output: bfloat16 [4096, 2048], P('expert')
- grad_tokens: bfloat16 [4096, 2048], P('expert')
- grad_attn_gain: float32 [2048], replicated
- grad_w_query: float32 [2048, 2048], P(None, 'tensor')
- grad_w_key: float32 [2048, 2048], P(None, 'tensor')
- grad_w_value: float32 [2048, 2048], P(None, 'tensor')
- grad_query_gain: float32 [2048], P('tensor')
- grad_key_gain: float32 [2048], P('tensor')
- grad_w_out: float32 [2048, 2048], P('tensor')
- grad_ffn_gain: float32 [2048], replicated
- grad_router: float32 [2048, 16], replicated
- grad_w_gate: float32 [32, 2048, 512], P(('expert', 'tensor'))
- grad_w_up: float32 [32, 2048, 512], P(('expert', 'tensor'))
- grad_w_down: float32 [32, 512, 2048], P(('expert', 'tensor'))
The draws below stay inside these ranges and needn't reach their ends.
Inputs may be any that keep to these rules, and one draw needn't show every extreme that they name: `routes`: each token names 8 different experts. Among the 1024 tokens of one index of expert, one expert, the same for every index of expert, is named exactly 768 + 768 // 4 times, every other expert at most 768 times, and every expert at least once. `slot_ids`: for each index of expert and each expert, the choices that name it hold different slots; only the expert named 768 + 768 // 4 times has slots of 768 or more, and it fills all 768 slots below that. Along the 1024 tokens of one index of expert the positions rise by 1, 2 or 3 from each token to the next; some index of expert starts at 0 and some other ends at 4095.
All inputs are finite; a program needn't handle non-finite values.
Results may differ from the reference program's by a relative error of at most 0.024.
Values may be sent and summed in bfloat16 or wider, within the bound.
No kernel may reach another device: no remote copies, remote signals or barrier semaphores. Data moves between devices by JAX's collectives and lax.ppermute only.
A program may use at most 384 MiB of HBM per device.

```python
import jax
import jax.numpy as jnp
from jax import lax

D = 2048
HEADS = 16
HEAD_DIM = 128
FFE = 1024
TOP = 8
TOK_DEV = 1024
EXPERTS = 16
CAP = 768
QD = 2048
TOKENS = 4096
N_EXPERT = 4
N_TENSOR = 8


def route_tables(base_key):
    group_count = TOKENS // TOK_DEV
    full_key, rest_key = jax.random.split(base_key)
    full_expert = jax.random.randint(full_key, (), 0, EXPERTS)
    assignments = TOK_DEV * TOP
    full_load = CAP + CAP // 4
    slot_span = CAP + CAP // 4
    expert_iota = jnp.arange(EXPERTS, dtype=jnp.int32)

    def one_group(group_key):
        load_key, token_key, order_key, slot_key = jax.random.split(group_key, 4)
        weights = jax.random.randint(load_key, (EXPERTS,), 4, 7)
        weights = jnp.where(expert_iota == full_expert, 0, weights)
        running = jnp.cumsum(weights)
        end_points = (assignments - full_load) * running // running[-1]
        load_list = jnp.diff(jnp.concatenate([jnp.zeros((1,), jnp.int32), end_points]))
        load_list = jnp.where(expert_iota == full_expert, full_load, load_list)
        bound_list = jnp.cumsum(load_list)
        sorted_ids = jnp.searchsorted(bound_list, jnp.arange(assignments, dtype=jnp.int32), side='right').astype(jnp.int32)
        route_table = sorted_ids.reshape(TOP, TOK_DEV).T
        route_table = route_table[jax.random.permutation(token_key, TOK_DEV)]
        order_scores = jax.random.randint(order_key, (TOK_DEV, TOP), 0, 1 << 16) * TOP + jnp.arange(TOP, dtype=jnp.int32)[None, :]
        route_table = jnp.take_along_axis(route_table, jnp.argsort(order_scores, axis=1), axis=1)
        flat_ids = route_table.reshape(-1)
        hit_table = (flat_ids[:, None] == expert_iota[None, :]).astype(jnp.int32)
        rank_of = jnp.sum(hit_table * (jnp.cumsum(hit_table, axis=0) - 1), axis=1)
        limits = jnp.where(expert_iota == full_expert, slot_span, CAP)
        slot_iota = jnp.arange(slot_span, dtype=jnp.int32)
        raw_scores = jax.random.randint(slot_key, (EXPERTS, slot_span), 0, 1 << 16)
        raw_scores = jnp.where(slot_iota[None, :] < limits[:, None], raw_scores, 1 << 16)
        slot_order = jnp.argsort(raw_scores * slot_span + slot_iota[None, :], axis=1).astype(jnp.int32)
        slot_table = slot_order[flat_ids, rank_of].reshape(TOK_DEV, TOP)
        return (route_table.astype(jnp.int32), slot_table.astype(jnp.int32))
    routes_all, slots_all = jax.vmap(one_group)(jax.random.split(rest_key, group_count))
    return (routes_all.reshape(TOKENS, TOP), slots_all.reshape(TOKENS, TOP))


def draw_routes(key, part):
    routes_all, slots_all = route_tables(key)
    return routes_all


def draw_slot_ids(key, part):
    routes_all, slots_all = route_tables(key)
    return slots_all


def draw_positions(key, part):
    key = jax.random.fold_in(key, 7)
    step_key, offset_key, pick_key = jax.random.split(key, 3)
    group_count = TOKENS // TOK_DEV
    steps = jax.random.randint(step_key, (group_count, TOK_DEV), 1, 4)
    steps = steps.at[:, 0].set(0)
    rising = jnp.cumsum(steps, axis=1).astype(jnp.int32)
    spans = rising[:, -1]
    rooms = 4 * TOK_DEV - 1 - spans
    offsets = jax.random.randint(offset_key, (group_count,), 0, 1 << 20) % (rooms + 1)
    picked = jax.random.permutation(pick_key, group_count)
    offsets = offsets.at[picked[0]].set(0)
    offsets = offsets.at[picked[1]].set(rooms[picked[1]])
    return (offsets[:, None] + rising).reshape(TOKENS).astype(jnp.int32)


def block_scale(own_key, dims, pieces, low, largest):
    level, own = 1.0, jax.random.fold_in(own_key, 6)
    for axis_at, parts in pieces:
        steps = jnp.exp(jax.random.uniform(jax.random.fold_in(own, axis_at), (parts,), jnp.float32, low / len(pieces), largest / len(pieces)))
        level = level * jnp.repeat(steps, dims[axis_at] // parts).reshape([-1 if axis == axis_at else 1 for axis in range(len(dims))])
    return level


def gaussian(key, extent, deviation, limit, cuts=(), kind=jnp.bfloat16):
    values = jax.random.normal(key, extent, jnp.float32) * deviation
    if len(cuts) > 0:
        values = block_scale(key, extent, cuts, -0.22, 0.18) * values
    return jnp.clip(values, min=-limit, max=limit).astype(kind)


def setup_inputs(seed: int = 0) -> dict:
    key_of = jax.random.split(jax.random.key(seed), 18)
    tokens = gaussian(key_of[0], (TOKENS, D), 1.0, 6.0, ((0, 4),))
    positions = draw_positions(jax.random.fold_in(key_of[17], 71), 0)
    routes = draw_routes(jax.random.fold_in(key_of[17], 71), 0)
    slot_ids = draw_slot_ids(jax.random.fold_in(key_of[17], 71), 0)
    attn_gain = jnp.clip(1.0 + 0.15 * jax.random.normal(key_of[4], (D,), jnp.float32), 0.25, 1.75)
    w_query = gaussian(key_of[5], (D, QD), D ** -0.5, 0.125, ((1, 8),))
    w_key = gaussian(key_of[6], (D, QD), D ** -0.5, 0.125, ((1, 8),))
    w_value = gaussian(key_of[7], (D, QD), D ** -0.5, 0.125, ((1, 8),))
    query_gain = jnp.clip(1.0 + 0.15 * jax.random.normal(key_of[8], (QD,), jnp.float32), 0.25, 1.75)
    key_gain = jnp.clip(1.0 + 0.15 * jax.random.normal(key_of[9], (QD,), jnp.float32), 0.25, 1.75)
    w_out = gaussian(key_of[10], (QD, D), (QD // 32) ** -0.5, 0.75, ((0, 8),))
    ffn_gain = jnp.clip(1.0 + 0.15 * jax.random.normal(key_of[11], (D,), jnp.float32), 0.25, 1.75)
    router = gaussian(key_of[12], (D, EXPERTS), (4 * D) ** -0.5, 0.0625)
    w_gate = gaussian(key_of[13], (EXPERTS * 2, D, FFE // 2), D ** -0.5, 0.125, ((0, 32),))
    w_up = gaussian(key_of[14], (EXPERTS * 2, D, FFE // 2), D ** -0.5, 0.125, ((0, 32),))
    w_down = gaussian(key_of[15], (EXPERTS * 2, FFE // 2, D), (max(1, TOP * FFE // EXPERTS ** 2)) ** -0.5, 1.0, ((0, 32),))
    grad_out = gaussian(key_of[16], (TOKENS, D), 1.0, 6.0, ((0, 4),))
    return {"tokens": tokens, "positions": positions, "routes": routes, "slot_ids": slot_ids, "attn_gain": attn_gain, "w_query": w_query, "w_key": w_key, "w_value": w_value, "query_gain": query_gain, "key_gain": key_gain, "w_out": w_out, "ffn_gain": ffn_gain, "router": router, "w_gate": w_gate, "w_up": w_up, "w_down": w_down, "grad_out": grad_out}


@jax.custom_vjp
def low(v):
    return lax.optimization_barrier(v.astype(jnp.bfloat16)).astype(jnp.float32)

@jax.custom_vjp
def low_back(v):
    return v

def low_keep(v):
    return (low(v), None)

def low_pass(kept, grad):
    return (grad,)

def back_keep(v):
    return (v, None)

def back_low(kept, grad):
    return (low(grad),)
low.defvjp(low_keep, low_pass)
low_back.defvjp(back_keep, back_low)
EPS = 1e-05
THETA = 10000.0
HIGHEST = lax.Precision.HIGHEST

def matmul(left_side, right_side):
    return jnp.dot(left_side, right_side, precision=HIGHEST, preferred_element_type=jnp.float32)

def rms_norm(values, gain_row):
    inverse = lax.rsqrt(lax.optimization_barrier(jnp.mean(values * values, axis=-1, keepdims=True)) + EPS)
    return values * inverse * gain_row

def head_norm(values, gain_row):
    normed = rms_norm(values, gain_row)
    return normed.reshape(values.shape[0], HEADS, HEAD_DIM)

def rotary(values, cosine_table, sine_table):
    first_half = values[..., :HEAD_DIM // 2]
    second_half = values[..., HEAD_DIM // 2:]
    return jnp.concatenate([first_half * cosine_table - second_half * sine_table, second_half * cosine_table + first_half * sine_table], axis=-1)

def attend(query_rows, key_rows, value_rows):
    scores = low_back(jnp.einsum('qhd,khd->hqk', query_rows, key_rows, precision=HIGHEST))
    causal = jnp.arange(TOK_DEV)[:, None] >= jnp.arange(TOK_DEV)[None, :]
    scores = jnp.where(causal[None], scores, -1e+30)
    weights = low(jax.nn.softmax(scores, axis=-1))
    return jnp.einsum('hqk,khd->qhd', weights, value_rows, precision=HIGHEST)

def expert_half(rows_in, gate_half, up_half, down_half, router_w, expert):
    rows_low = low_back(rows_in)
    logits = low_back(matmul(rows_low, router_w))
    chosen = (jnp.arange(EXPERTS) == expert).astype(jnp.float32)
    gate_value = lax.optimization_barrier(jnp.sum(jax.nn.softmax(logits, axis=-1) * chosen, axis=-1, keepdims=True))
    pre_gate = low_back(matmul(rows_low, gate_half))
    pre_up = low_back(matmul(rows_low, up_half))
    active = low(jax.nn.silu(pre_gate) * pre_up)
    value_rows = low_back(matmul(active, down_half))
    return low(gate_value * value_rows)

def mixture(ffn_in, router_w, gate_w, up_w, down_w, slot_table):
    padded = jnp.concatenate([ffn_in, jnp.zeros((1, D), jnp.float32)], axis=0)
    local_count = N_TENSOR // 2
    gate_all = gate_w.reshape(N_EXPERT, local_count, 2, D, FFE // 2)
    up_all = up_w.reshape(N_EXPERT, local_count, 2, D, FFE // 2)
    down_all = down_w.reshape(N_EXPERT, local_count, 2, FFE // 2, D)
    expert_ids = jnp.arange(EXPERTS, dtype=jnp.int32).reshape(N_EXPERT, local_count)

    def one_expert(accumulated, operands):
        rows_index, gate_pair, up_pair, down_pair, expert = operands
        rows_in = padded[rows_index]
        for half_index in range(2):
            contribution = expert_half(rows_in, gate_pair[half_index], up_pair[half_index], down_pair[half_index], router_w, expert)
            accumulated = accumulated.at[rows_index].add(contribution)
        return (accumulated, None)

    def one_group(accumulated, operands):
        return lax.scan(jax.checkpoint(one_expert), accumulated, operands)
    accumulated, _ = lax.scan(jax.checkpoint(one_group), jnp.zeros((TOKENS + 1, D), jnp.float32), (slot_table, gate_all, up_all, down_all, expert_ids))
    return accumulated[:TOKENS]

def reference(tokens, positions, routes, slot_ids, attn_gain, w_query, w_key, w_value, query_gain, key_gain, w_out, ffn_gain, router, w_gate, w_up, w_down, grad_out):
    table_size = EXPERTS * N_EXPERT * CAP
    sources = jnp.arange(TOKENS, dtype=jnp.int32) // TOK_DEV
    place_index = (routes * N_EXPERT + sources[:, None]) * CAP + slot_ids
    place_index = jnp.where(slot_ids < CAP, place_index, table_size).reshape(-1).astype(jnp.int32)
    owners = jnp.repeat(jnp.arange(TOKENS, dtype=jnp.int32), TOP)
    slot_table = jnp.full((table_size + 1,), TOKENS, jnp.int32).at[place_index].set(owners)[:table_size]
    slot_table = slot_table.reshape(N_EXPERT, N_TENSOR // 2, N_EXPERT * CAP)
    half_dim = HEAD_DIM // 2
    frequency = THETA ** (-2.0 * jnp.arange(half_dim, dtype=jnp.float32) / HEAD_DIM)
    angles = positions.astype(jnp.float32)[:, None] * frequency[None, :]
    cosine_table = jnp.cos(angles)[:, None, :]
    sine_table = jnp.sin(angles)[:, None, :]
    grouped_shape = (N_EXPERT, TOK_DEV, HEADS, HEAD_DIM)

    def forward(token_rows, attn_scale, query_w, key_w, value_w, query_scale, key_scale, out_w, ffn_scale, router_w, gate_w, up_w, down_w):
        attn_in = low(rms_norm(token_rows, attn_scale))
        query_raw = low_back(matmul(attn_in, query_w))
        key_raw = low_back(matmul(attn_in, key_w))
        value_rows = low_back(low(matmul(attn_in, value_w)))
        query_rows = low(rotary(head_norm(query_raw, query_scale), cosine_table, sine_table) * HEAD_DIM ** (-0.5))
        key_rows = low(rotary(head_norm(key_raw, key_scale), cosine_table, sine_table))
        mixed_heads = lax.map(jax.checkpoint(lambda operands: attend(*operands)), (query_rows.reshape(grouped_shape), key_rows.reshape(grouped_shape), value_rows.reshape(grouped_shape)))
        mixed_heads = low_back(low(mixed_heads.reshape(TOKENS, HEADS * HEAD_DIM)))
        hidden = token_rows + low_back(matmul(mixed_heads, out_w))
        ffn_in = low(rms_norm(hidden, ffn_scale))
        return hidden + mixture(ffn_in, router_w, gate_w, up_w, down_w, slot_table)
    output, pullback = jax.vjp(forward, tokens.astype(jnp.float32), attn_gain.astype(jnp.float32), w_query.astype(jnp.float32), w_key.astype(jnp.float32), w_value.astype(jnp.float32), query_gain.astype(jnp.float32), key_gain.astype(jnp.float32), w_out.astype(jnp.float32), ffn_gain.astype(jnp.float32), router.astype(jnp.float32), w_gate.astype(jnp.float32), w_up.astype(jnp.float32), w_down.astype(jnp.float32))
    gradients = pullback(grad_out.astype(jnp.float32))
    return (output.astype(jnp.bfloat16), gradients[0].astype(jnp.bfloat16), gradients[1], gradients[2], gradients[3], gradients[4], gradients[5], gradients[6], gradients[7], gradients[8], gradients[9], gradients[10], gradients[11], gradients[12])
```

```python
import jax
import jax.numpy as jnp
from jax import lax
from jax.sharding import PartitionSpec as P

HEAD_DIM = 128
TOP = 8


EPS = 1e-05
THETA = 10000.0


def rms_forward(values):
    inverse = lax.rsqrt(jnp.mean(values * values, axis=-1, keepdims=True) + EPS)
    return (values * inverse, inverse)


def rms_backward(grad_normed, normal_rows, inverse, gain_row):
    gain_grad = jnp.sum(grad_normed * normal_rows, axis=0)
    scaled = grad_normed * gain_row
    grad_rows = inverse * (
        scaled - normal_rows * jnp.mean(scaled * normal_rows, axis=-1, keepdims=True)
    )
    return (grad_rows, gain_grad)


def rotary(values, cosine_table, sine_table):
    half_dim = values.shape[-1] // 2
    first_half = values[..., :half_dim]
    second_half = values[..., half_dim:]
    return jnp.concatenate(
        [
            first_half * cosine_table - second_half * sine_table,
            second_half * cosine_table + first_half * sine_table,
        ],
        axis=-1,
    )


def causal_mask(start_row, end_row):
    return (jnp.arange(start_row, end_row)[:, None] >= jnp.arange(end_row)[None, :])[None]


def attention_forward(query_rows, key_rows, value_rows):
    length = query_rows.shape[0]
    block_rows = min(512, length)
    outputs = []
    totals = []
    for block_start in range(0, length, block_rows):
        block_end = block_start + block_rows
        scores = jnp.einsum(
            "qhd,khd->hqk",
            query_rows[block_start:block_end],
            key_rows[:block_end],
            preferred_element_type=jnp.float32,
        )
        scores = jnp.where(causal_mask(block_start, block_end), scores, -1e30)
        row_peak = jnp.max(scores, axis=-1, keepdims=True)
        exponent = jnp.exp(scores - row_peak)
        row_total = jnp.sum(exponent, axis=-1, keepdims=True)
        weights = (exponent / row_total).astype(jnp.bfloat16)
        outputs.append(
            jnp.einsum(
                "hqk,khd->qhd", weights, value_rows[:block_end], preferred_element_type=jnp.float32
            )
        )
        totals.append(row_peak + jnp.log(row_total))
    return (jnp.concatenate(outputs, axis=0), totals)


def attention_backward(query_rows, key_rows, value_rows, grad_mixed, totals):
    length = query_rows.shape[0]
    block_rows = min(512, length)
    grad_keys = jnp.zeros(key_rows.shape, jnp.float32)
    grad_values = jnp.zeros(value_rows.shape, jnp.float32)
    grad_queries = []
    for block_number, block_start in enumerate(range(0, length, block_rows)):
        block_end = block_start + block_rows
        query_block = query_rows[block_start:block_end]
        grad_block = grad_mixed[block_start:block_end]
        scores = jnp.einsum(
            "qhd,khd->hqk", query_block, key_rows[:block_end], preferred_element_type=jnp.float32
        )
        scores = jnp.where(causal_mask(block_start, block_end), scores, -1e30)
        probs_again = jnp.exp(scores - totals[block_number])
        weights = probs_again.astype(jnp.bfloat16)
        grad_probs = jnp.einsum(
            "qhd,khd->hqk", grad_block, value_rows[:block_end], preferred_element_type=jnp.float32
        )
        grad_scores = (
            probs_again * (grad_probs - jnp.sum(probs_again * grad_probs, axis=-1, keepdims=True))
        ).astype(jnp.bfloat16)
        grad_queries.append(
            jnp.einsum(
                "hqk,khd->qhd",
                grad_scores,
                key_rows[:block_end],
                preferred_element_type=jnp.float32,
            )
        )
        grad_keys = grad_keys.at[:block_end].add(
            jnp.einsum("hqk,qhd->khd", grad_scores, query_block, preferred_element_type=jnp.float32)
        )
        grad_values = grad_values.at[:block_end].add(
            jnp.einsum("hqk,qhd->khd", weights, grad_block, preferred_element_type=jnp.float32)
        )
    return (jnp.concatenate(grad_queries, axis=0), grad_keys, grad_values)


def on_device(
    tokens,
    positions,
    routes,
    slot_ids,
    attn_gain,
    w_query,
    w_key,
    w_value,
    query_gain,
    key_gain,
    w_out,
    ffn_gain,
    router,
    w_gate,
    w_up,
    w_down,
    grad_out,
):
    tensor_size = lax.axis_size("tensor")
    expert_size = lax.axis_size("expert")
    local_count = tensor_size // 2
    tensor_index = lax.axis_index("tensor")
    expert_index = lax.axis_index("expert")
    own_local = tensor_index // 2
    own_expert = expert_index * local_count + own_local
    length, model_width = tokens.shape
    heads_here = w_query.shape[1] // HEAD_DIM
    full_cols = w_query.shape[1] * tensor_size
    expert_count = router.shape[1]
    capacity = 3 * length * TOP // (2 * expert_count)
    slot_rows = expert_size * capacity
    score_scale = HEAD_DIM ** (-0.5)
    half_dim = HEAD_DIM // 2
    frequency = THETA ** (-2.0 * jnp.arange(half_dim, dtype=jnp.float32) / HEAD_DIM)
    angles = positions.astype(jnp.float32)[:, None] * frequency[None, :]
    cosine_table = jnp.cos(angles)[:, None, :]
    sine_table = jnp.sin(angles)[:, None, :]
    token_float = tokens.astype(jnp.float32)
    attn_normal, attn_inverse = rms_forward(token_float)
    attn_in = (attn_normal * attn_gain).astype(jnp.bfloat16)
    head_shape = (length, heads_here, HEAD_DIM)
    query_raw = jnp.dot(attn_in, w_query, preferred_element_type=jnp.float32).reshape(head_shape)
    key_raw = jnp.dot(attn_in, w_key, preferred_element_type=jnp.float32).reshape(head_shape)
    value_rows = (
        jnp.dot(attn_in, w_value, preferred_element_type=jnp.float32)
        .astype(jnp.bfloat16)
        .reshape(head_shape)
    )
    query_scale = query_gain.reshape(heads_here, HEAD_DIM)
    key_scale = key_gain.reshape(heads_here, HEAD_DIM)
    square_sums = lax.psum(
        (jnp.sum(query_raw * query_raw, axis=(1, 2)), jnp.sum(key_raw * key_raw, axis=(1, 2))),
        "tensor",
    )
    query_inverse = lax.rsqrt(square_sums[0] / full_cols + EPS)[:, None, None]
    key_inverse = lax.rsqrt(square_sums[1] / full_cols + EPS)[:, None, None]
    query_normal = query_raw * query_inverse
    key_normal = key_raw * key_inverse
    query_rows = (
        rotary(query_normal * query_scale, cosine_table, sine_table) * score_scale
    ).astype(jnp.bfloat16)
    key_rows = rotary(key_normal * key_scale, cosine_table, sine_table).astype(jnp.bfloat16)
    mixed_heads, totals = attention_forward(query_rows, key_rows, value_rows)
    mixed_low = mixed_heads.reshape(length, heads_here * HEAD_DIM).astype(jnp.bfloat16)
    attn_part = jnp.dot(mixed_low, w_out, preferred_element_type=jnp.float32)
    own_rows = length // tensor_size
    own_start = tensor_index * own_rows
    both = ("expert", "tensor")

    def own_slice(rows):
        return lax.dynamic_slice_in_dim(rows, own_start, own_rows, 0)

    grad_own = own_slice(grad_out)
    grad_all = lax.all_gather(grad_own, both, axis=0, tiled=True)
    expert_iota = jnp.arange(expert_count, dtype=jnp.int32)
    kept_table = jnp.sum(
        (
            (routes[None, :, :] == expert_iota[:, None, None]) & (slot_ids < capacity)[None, :, :]
        ).astype(jnp.float32),
        axis=-1,
    ).astype(jnp.bfloat16)
    kept_all = lax.all_gather(kept_table, "expert", axis=0)
    kept_own = lax.dynamic_slice_in_dim(kept_all, own_expert, 1, 1)
    kept_rows = kept_own.reshape(-1, 1).astype(jnp.float32)

    attn_own = lax.psum_scatter(
        attn_part.astype(jnp.bfloat16), "tensor", scatter_dimension=0, tiled=True
    )
    hidden = own_slice(token_float) + attn_own.astype(jnp.float32)
    ffn_normal, ffn_inverse = rms_forward(hidden)
    ffn_in = (ffn_normal * ffn_gain).astype(jnp.bfloat16)
    expert_rows = lax.all_gather(ffn_in, both, axis=0, tiled=True)

    chosen = (expert_iota == own_expert).astype(jnp.float32)
    logits = jnp.dot(expert_rows, router, preferred_element_type=jnp.float32)
    router_probs = jax.nn.softmax(logits, axis=-1)
    gate_value = jnp.sum(router_probs * chosen, axis=-1, keepdims=True) * kept_rows
    pre_gate = jnp.dot(expert_rows, w_gate[0], preferred_element_type=jnp.float32)
    pre_up = jnp.dot(expert_rows, w_up[0], preferred_element_type=jnp.float32)
    sigmoid_gate = jax.nn.sigmoid(pre_gate)
    silu_gate = pre_gate * sigmoid_gate
    active = (silu_gate * pre_up).astype(jnp.bfloat16)
    value_out = jnp.dot(active, w_down[0], preferred_element_type=jnp.float32)
    weighted = (gate_value * value_out).astype(jnp.bfloat16)
    moe_own = lax.psum_scatter(weighted, both, scatter_dimension=0, tiled=True)
    output_own = (hidden + moe_own.astype(jnp.float32)).astype(jnp.bfloat16)
    output = lax.all_gather(output_own, "tensor", axis=0, tiled=True)

    grad_value = (gate_value * grad_all.astype(jnp.float32)).astype(jnp.bfloat16)
    grad_down = jnp.einsum("rh,rd->hd", active, grad_value, preferred_element_type=jnp.float32)
    grad_inner = jnp.einsum("rd,hd->rh", grad_all, w_down[0], preferred_element_type=jnp.float32)
    grad_active = gate_value * grad_inner
    grad_gate_value = jnp.sum(grad_inner * active.astype(jnp.float32), axis=-1, keepdims=True)
    grad_pre_gate = (
        grad_active * pre_up * sigmoid_gate * (1.0 + pre_gate * (1.0 - sigmoid_gate))
    ).astype(jnp.bfloat16)
    grad_pre_up = (grad_active * silu_gate).astype(jnp.bfloat16)
    grad_gate_w = jnp.einsum(
        "rd,rh->dh", expert_rows, grad_pre_gate, preferred_element_type=jnp.float32
    )
    grad_up_w = jnp.einsum(
        "rd,rh->dh", expert_rows, grad_pre_up, preferred_element_type=jnp.float32
    )
    grad_logits = (grad_gate_value * gate_value * (chosen - router_probs)).astype(jnp.bfloat16)
    grad_router_part = jnp.einsum(
        "rd,re->de", expert_rows, grad_logits, preferred_element_type=jnp.float32
    )
    grad_expert_in = (
        jnp.einsum("rh,dh->rd", grad_pre_gate, w_gate[0], preferred_element_type=jnp.float32)
        + jnp.einsum("rh,dh->rd", grad_pre_up, w_up[0], preferred_element_type=jnp.float32)
        + jnp.einsum("re,de->rd", grad_logits, router, preferred_element_type=jnp.float32)
    )
    grad_ffn = lax.psum_scatter(
        grad_expert_in.astype(jnp.bfloat16), both, scatter_dimension=0, tiled=True
    ).astype(jnp.float32)
    grad_hidden_part, grad_ffn_gain = rms_backward(grad_ffn, ffn_normal, ffn_inverse, ffn_gain)
    grad_hidden = grad_own.astype(jnp.float32) + grad_hidden_part
    grad_hidden_low = lax.all_gather(
        grad_hidden.astype(jnp.bfloat16), "tensor", axis=0, tiled=True
    )
    grad_w_out = jnp.einsum(
        "tq,td->qd", mixed_low, grad_hidden_low, preferred_element_type=jnp.float32
    )
    grad_mixed = (
        jnp.einsum("td,qd->tq", grad_hidden_low, w_out, preferred_element_type=jnp.float32)
        .astype(jnp.bfloat16)
        .reshape(head_shape)
    )
    grad_query, grad_key, grad_value_attn = attention_backward(
        query_rows, key_rows, value_rows, grad_mixed, totals
    )
    grad_query_normed = rotary(grad_query * score_scale, cosine_table, -sine_table)
    grad_key_normed = rotary(grad_key, cosine_table, -sine_table)
    grad_query_scale = jnp.sum(grad_query_normed * query_normal, axis=0)
    grad_key_scale = jnp.sum(grad_key_normed * key_normal, axis=0)
    query_scaled = grad_query_normed * query_scale
    key_scaled = grad_key_normed * key_scale
    inner_sums = lax.psum(
        (
            jnp.sum(query_scaled * query_normal, axis=(1, 2)),
            jnp.sum(key_scaled * key_normal, axis=(1, 2)),
        ),
        "tensor",
    )
    grad_query_raw = query_inverse * (
        query_scaled - query_normal * (inner_sums[0] / full_cols)[:, None, None]
    )
    grad_key_raw = key_inverse * (
        key_scaled - key_normal * (inner_sums[1] / full_cols)[:, None, None]
    )
    query_low = grad_query_raw.reshape(length, heads_here * HEAD_DIM).astype(jnp.bfloat16)
    key_low = grad_key_raw.reshape(length, heads_here * HEAD_DIM).astype(jnp.bfloat16)
    value_low = grad_value_attn.reshape(length, heads_here * HEAD_DIM).astype(jnp.bfloat16)
    grad_w_query = jnp.einsum("td,tq->dq", attn_in, query_low, preferred_element_type=jnp.float32)
    grad_w_key = jnp.einsum("td,tq->dq", attn_in, key_low, preferred_element_type=jnp.float32)
    grad_w_value = jnp.einsum("td,tq->dq", attn_in, value_low, preferred_element_type=jnp.float32)
    grad_attn_in = jnp.einsum("tq,dq->td", query_low, w_query, preferred_element_type=jnp.float32)
    grad_attn_in = grad_attn_in + jnp.einsum(
        "tq,dq->td", key_low, w_key, preferred_element_type=jnp.float32
    )
    grad_attn_in = grad_attn_in + jnp.einsum(
        "tq,dq->td", value_low, w_value, preferred_element_type=jnp.float32
    )
    grad_attn_own = lax.psum_scatter(
        grad_attn_in.astype(jnp.bfloat16), "tensor", scatter_dimension=0, tiled=True
    ).astype(jnp.float32)
    grad_token_part, grad_attn_gain = rms_backward(
        grad_attn_own, own_slice(attn_normal), own_slice(attn_inverse), attn_gain
    )
    grad_tokens = lax.all_gather(
        (grad_hidden + grad_token_part).astype(jnp.bfloat16), "tensor", axis=0, tiled=True
    )
    head_sums = (
        lax.psum(grad_w_query.astype(jnp.bfloat16), "expert").astype(jnp.float32),
        lax.psum(grad_w_key.astype(jnp.bfloat16), "expert").astype(jnp.float32),
        lax.psum(grad_w_value.astype(jnp.bfloat16), "expert").astype(jnp.float32),
        lax.psum(grad_w_out.astype(jnp.bfloat16), "expert").astype(jnp.float32),
        lax.psum(grad_query_scale.reshape(-1).astype(jnp.bfloat16), "expert").astype(jnp.float32),
        lax.psum(grad_key_scale.reshape(-1).astype(jnp.bfloat16), "expert").astype(jnp.float32),
    )
    shared_sums = lax.psum((grad_router_part, grad_attn_gain, grad_ffn_gain), ("expert", "tensor"))
    return (
        output,
        grad_tokens,
        shared_sums[1],
        head_sums[0],
        head_sums[1],
        head_sums[2],
        head_sums[4],
        head_sums[5],
        head_sums[3],
        shared_sums[2],
        shared_sums[0],
        grad_gate_w[None],
        grad_up_w[None],
        grad_down[None],
    )


def solution(mesh):
    placed = (
        P("expert", None),
        P("expert"),
        P("expert", None),
        P("expert", None),
        P(),
        P(None, "tensor"),
        P(None, "tensor"),
        P(None, "tensor"),
        P("tensor"),
        P("tensor"),
        P("tensor", None),
        P(),
        P(),
        P(("expert", "tensor"), None, None),
        P(("expert", "tensor"), None, None),
        P(("expert", "tensor"), None, None),
        P("expert", None),
    )
    return jax.shard_map(
        on_device,
        mesh=mesh,
        in_specs=placed,
        out_specs=(
            P("expert", None),
            P("expert", None),
            P(),
            P(None, "tensor"),
            P(None, "tensor"),
            P(None, "tensor"),
            P("tensor"),
            P("tensor"),
            P("tensor", None),
            P(),
            P(),
            P(("expert", "tensor"), None, None),
            P(("expert", "tensor"), None, None),
            P(("expert", "tensor"), None, None),
        ),
        check_vma=False,
    )
```

```python
import jax
import jax.numpy as jnp
from jax import lax
from jax.experimental import pallas as pl
from jax.experimental.pallas import tpu as pltpu
from jax.sharding import PartitionSpec as P

HEAD_DIM = 128
TOP = 8


EPS = 1e-05
THETA = 10000.0


def rms_forward(values):
    inverse = lax.rsqrt(jnp.mean(values * values, axis=-1, keepdims=True) + EPS)
    return (values * inverse, inverse)


def rms_backward(grad_normed, normal_rows, inverse, gain_row):
    gain_grad = jnp.sum(grad_normed * normal_rows, axis=0)
    scaled = grad_normed * gain_row
    grad_rows = inverse * (
        scaled - normal_rows * jnp.mean(scaled * normal_rows, axis=-1, keepdims=True)
    )
    return (grad_rows, gain_grad)


def rotary(values, cosine_table, sine_table):
    half_dim = values.shape[-1] // 2
    first_half = values[..., :half_dim]
    second_half = values[..., half_dim:]
    return jnp.concatenate(
        [
            first_half * cosine_table - second_half * sine_table,
            second_half * cosine_table + first_half * sine_table,
        ],
        axis=-1,
    )


def causal_mask(start_row, end_row):
    return (jnp.arange(start_row, end_row)[:, None] >= jnp.arange(end_row)[None, :])[None]


def attention_forward(query_rows, key_rows, value_rows):
    length = query_rows.shape[0]
    block_rows = min(512, length)
    outputs = []
    totals = []
    for block_start in range(0, length, block_rows):
        block_end = block_start + block_rows
        scores = jnp.einsum(
            "qhd,khd->hqk",
            query_rows[block_start:block_end],
            key_rows[:block_end],
            preferred_element_type=jnp.float32,
        )
        scores = jnp.where(causal_mask(block_start, block_end), scores, -1e30)
        row_peak = jnp.max(scores, axis=-1, keepdims=True)
        exponent = jnp.exp(scores - row_peak)
        row_total = jnp.sum(exponent, axis=-1, keepdims=True)
        weights = (exponent / row_total).astype(jnp.bfloat16)
        outputs.append(
            jnp.einsum(
                "hqk,khd->qhd", weights, value_rows[:block_end], preferred_element_type=jnp.float32
            )
        )
        totals.append(row_peak + jnp.log(row_total))
    return (jnp.concatenate(outputs, axis=0), totals)


def attention_backward(query_rows, key_rows, value_rows, grad_mixed, totals):
    length = query_rows.shape[0]
    block_rows = min(512, length)
    grad_keys = jnp.zeros(key_rows.shape, jnp.float32)
    grad_values = jnp.zeros(value_rows.shape, jnp.float32)
    grad_queries = []
    for block_number, block_start in enumerate(range(0, length, block_rows)):
        block_end = block_start + block_rows
        query_block = query_rows[block_start:block_end]
        grad_block = grad_mixed[block_start:block_end]
        scores = jnp.einsum(
            "qhd,khd->hqk", query_block, key_rows[:block_end], preferred_element_type=jnp.float32
        )
        scores = jnp.where(causal_mask(block_start, block_end), scores, -1e30)
        probs_again = jnp.exp(scores - totals[block_number])
        weights = probs_again.astype(jnp.bfloat16)
        grad_probs = jnp.einsum(
            "qhd,khd->hqk", grad_block, value_rows[:block_end], preferred_element_type=jnp.float32
        )
        grad_scores = (
            probs_again * (grad_probs - jnp.sum(probs_again * grad_probs, axis=-1, keepdims=True))
        ).astype(jnp.bfloat16)
        grad_queries.append(
            jnp.einsum(
                "hqk,khd->qhd",
                grad_scores,
                key_rows[:block_end],
                preferred_element_type=jnp.float32,
            )
        )
        grad_keys = grad_keys.at[:block_end].add(
            jnp.einsum("hqk,qhd->khd", grad_scores, query_block, preferred_element_type=jnp.float32)
        )
        grad_values = grad_values.at[:block_end].add(
            jnp.einsum("hqk,qhd->khd", weights, grad_block, preferred_element_type=jnp.float32)
        )
    return (jnp.concatenate(grad_queries, axis=0), grad_keys, grad_values)


def swap(values, axis, bit):
    return lax.ppermute(values, axis, [(i, i ^ bit) for i in range(lax.axis_size(axis))])


def axis_bits(axis):
    size = lax.axis_size(axis)
    return [size >> (k + 1) for k in range(size.bit_length() - 1)]


def spread_sum(values, axis):
    for bit in axis_bits(axis)[::-1]:
        values = values + swap(values, axis, bit)
    return values


def plane_order(turn):
    bits = axis_bits("tensor")[:-1]
    if turn % 2:
        bits = bits[::-1]
    order = [0]
    for bit in bits:
        order = order + [bit ^ i for i in order]
    return bits, order


def plane_gather(piece, turn):
    bits, _ = plane_order(turn)
    pieces = [piece]
    for bit in bits:
        pieces = pieces + [swap(p, "tensor", bit) for p in pieces]
    near = jnp.concatenate(pieces, axis=0)
    return near, swap(near, "tensor", 1)


def plane_scatter(near, far, turn):
    bits, _ = plane_order(turn)
    total = near.astype(jnp.float32) + swap(far, "tensor", 1).astype(jnp.float32)
    for bit in bits[::-1]:
        half = total.shape[0] // 2
        sent = total[half:].astype(jnp.bfloat16)
        total = total[:half].astype(jnp.bfloat16).astype(jnp.float32) + swap(
            sent, "tensor", bit
        ).astype(jnp.float32)
    return total


def plane_rows(values, turn, own_rows):
    _, order = plane_order(turn)
    index = lax.axis_index("tensor")

    def block(i):
        return lax.dynamic_slice_in_dim(values, (index ^ i) * own_rows, own_rows, 0)

    near = jnp.concatenate([block(i) for i in order], axis=0)
    far = jnp.concatenate([block(i ^ 1) for i in order], axis=0)
    return near, far


def natural_rows(near, far, turn, own_rows):
    _, order = plane_order(turn)
    index = lax.axis_index("tensor")
    both = jnp.concatenate([near, far], axis=0)
    place = {}
    for at, i in enumerate(order):
        place[i] = at
        place[i ^ 1] = at + len(order)
    table = jnp.array([place[i] for i in range(2 * len(order))], jnp.int32)
    return jnp.concatenate(
        [
            lax.dynamic_slice_in_dim(both, table[index ^ i] * own_rows, own_rows, 0)
            for i in range(2 * len(order))
        ],
        axis=0,
    )


def contract(left, right, left_dim, right_dim):
    return lax.dot_general(
        left, right, (((left_dim,), (right_dim,)), ((), ())), preferred_element_type=jnp.float32
    )


def expert_body(half_blocks, *refs):
    (x_near, x_far, y_near, y_far, kept, chosen, router, w_gate, w_up, w_down) = refs[:10]
    (d_near, d_far, s_near, s_far, x_all, dy_all, act_all, dg_all, du_all, dl_all) = refs[-10:]
    is_near = pl.program_id(0) < half_blocks
    rows = jnp.where(is_near, x_near[...], x_far[...])
    grads = jnp.where(is_near, y_near[...], y_far[...])
    logits = contract(rows, router[...], 1, 0)
    exponent = jnp.exp(logits - jnp.max(logits, axis=-1, keepdims=True))
    probs = exponent / jnp.sum(exponent, axis=-1, keepdims=True)
    gate = jnp.sum(probs * chosen[...], axis=-1, keepdims=True) * kept[...]
    pre_gate = contract(rows, w_gate[...], 1, 0)
    pre_up = contract(rows, w_up[...], 1, 0)
    inner = contract(grads, w_down[...], 1, 1)
    sigmoid_gate = jax.nn.sigmoid(pre_gate)
    silu_gate = pre_gate * sigmoid_gate
    active = (silu_gate * pre_up).astype(jnp.bfloat16)
    grad_gate = jnp.sum(inner * active.astype(jnp.float32), axis=-1, keepdims=True)
    grad_active = gate * inner
    grad_pre_gate = (
        grad_active * pre_up * sigmoid_gate * (1.0 + pre_gate * (1.0 - sigmoid_gate))
    ).astype(jnp.bfloat16)
    grad_pre_up = (grad_active * silu_gate).astype(jnp.bfloat16)
    grad_logits = (grad_gate * gate * (chosen[...] - probs)).astype(jnp.bfloat16)
    grad_rows = (
        contract(grad_pre_gate, w_gate[...], 1, 1)
        + contract(grad_pre_up, w_up[...], 1, 1)
        + contract(grad_logits, router[...], 1, 1)
    ).astype(jnp.bfloat16)
    sent = (gate * contract(active, w_down[...], 1, 0)).astype(jnp.bfloat16)
    x_all[...] = rows
    dy_all[...] = (gate * grads.astype(jnp.float32)).astype(jnp.bfloat16)
    act_all[...] = active
    dg_all[...] = grad_pre_gate
    du_all[...] = grad_pre_up
    dl_all[...] = grad_logits

    @pl.when(is_near)
    def _():
        d_near[...] = grad_rows
        s_near[...] = sent

    @pl.when(jnp.logical_not(is_near))
    def _():
        d_far[...] = grad_rows
        s_far[...] = sent


def expert_chunk(chunk, chunks, x_pair, y_pair, kept, chosen, router, w_gate, w_up, w_down, kept_arrays):
    half_rows, width = x_pair[0].shape
    hidden_units = w_gate.shape[1]
    experts = router.shape[1]
    block_rows = min(256, half_rows)
    half_blocks = half_rows // block_rows
    total_rows = 2 * half_rows * chunks

    def near_map(i):
        return (jnp.minimum(i, half_blocks - 1), 0)

    def far_map(i):
        return (jnp.maximum(i - half_blocks, 0), 0)

    def all_map(i):
        return (i + chunk * 2 * half_blocks, 0)

    def whole(shape):
        return pl.BlockSpec(shape, lambda i: (0, 0), pipeline_mode=pl.Buffered(1))

    near = pl.BlockSpec((block_rows, width), near_map)
    far = pl.BlockSpec((block_rows, width), far_map)
    half_shape = jax.ShapeDtypeStruct((half_rows, width), jnp.bfloat16)
    wide_shape = jax.ShapeDtypeStruct((total_rows, width), jnp.bfloat16)
    unit_shape = jax.ShapeDtypeStruct((total_rows, hidden_units), jnp.bfloat16)
    logit_shape = jax.ShapeDtypeStruct((total_rows, experts), jnp.bfloat16)
    wide = pl.BlockSpec((block_rows, width), all_map)
    unit = pl.BlockSpec((block_rows, hidden_units), all_map)
    logit = pl.BlockSpec((block_rows, experts), all_map)
    extra = () if kept_arrays is None else tuple(kept_arrays)
    results = pl.pallas_call(
        lambda *refs: expert_body(half_blocks, *refs),
        grid=(2 * half_blocks,),
        in_specs=[
            near,
            far,
            near,
            far,
            pl.BlockSpec((block_rows, 1), lambda i: (i, 0)),
            whole((1, experts)),
            whole((width, experts)),
            whole((width, hidden_units)),
            whole((width, hidden_units)),
            whole((hidden_units, width)),
        ]
        + [pl.BlockSpec(memory_space=pl.ANY)] * len(extra),
        out_specs=[near, far, near, far, wide, wide, unit, unit, unit, logit],
        out_shape=[half_shape] * 4 + [wide_shape] * 2 + [unit_shape] * 3 + [logit_shape],
        input_output_aliases={10 + i: 4 + i for i in range(len(extra))},
        compiler_params=pltpu.CompilerParams(vmem_limit_bytes=56 * 1024 * 1024),
        cost_estimate=pl.CostEstimate(
            flops=2 * 2 * half_rows * width * (6 * hidden_units + 512),
            bytes_accessed=16 * half_rows * width + 6 * width * hidden_units,
            transcendentals=2 * half_rows * hidden_units,
        ),
        name="experts",
    )(x_pair[0], x_pair[1], y_pair[0], y_pair[1], kept, chosen, router, w_gate, w_up, w_down, *extra)
    return results[0:2], results[2:4], results[4:]


def on_device(
    tokens,
    positions,
    routes,
    slot_ids,
    attn_gain,
    w_query,
    w_key,
    w_value,
    query_gain,
    key_gain,
    w_out,
    ffn_gain,
    router,
    w_gate,
    w_up,
    w_down,
    grad_out,
):
    tensor_size = lax.axis_size("tensor")
    expert_size = lax.axis_size("expert")
    local_count = tensor_size // 2
    tensor_index = lax.axis_index("tensor")
    expert_index = lax.axis_index("expert")
    own_local = tensor_index // 2
    own_expert = expert_index * local_count + own_local
    length, model_width = tokens.shape
    heads_here = w_query.shape[1] // HEAD_DIM
    full_cols = w_query.shape[1] * tensor_size
    expert_count = router.shape[1]
    capacity = 3 * length * TOP // (2 * expert_count)
    own_rows = length // tensor_size

    def own_slice(rows):
        return lax.dynamic_slice_in_dim(rows, tensor_index * own_rows, own_rows, 0)

    grad_own = own_slice(grad_out)
    grad_pairs = [plane_rows(grad_out, 0, own_rows)]
    for chunk in range(1, expert_size):
        grad_pairs.append(plane_gather(swap(grad_own, "expert", chunk), chunk))
    expert_iota = jnp.arange(expert_count, dtype=jnp.int32)
    kept_table = jnp.sum(
        (
            (routes[None, :, :] == expert_iota[:, None, None]) & (slot_ids < capacity)[None, :, :]
        ).astype(jnp.float32),
        axis=-1,
    )
    kept_columns = []
    for chunk in range(expert_size):
        target = (expert_index ^ chunk) * local_count + own_local
        kept_row = lax.dynamic_slice_in_dim(kept_table, target, 1, 0).reshape(tensor_size, own_rows)
        if chunk:
            kept_row = swap(kept_row, "expert", chunk)
        kept_columns.append(
            jnp.concatenate(plane_rows(kept_row, chunk, 1), axis=0).reshape(length, 1)
        )

    score_scale = HEAD_DIM ** (-0.5)
    half_dim = HEAD_DIM // 2
    frequency = THETA ** (-2.0 * jnp.arange(half_dim, dtype=jnp.float32) / HEAD_DIM)
    angles = positions.astype(jnp.float32)[:, None] * frequency[None, :]
    cosine_table = jnp.cos(angles)[:, None, :]
    sine_table = jnp.sin(angles)[:, None, :]
    token_float = tokens.astype(jnp.float32)
    attn_normal, attn_inverse = rms_forward(token_float)
    attn_in = (attn_normal * attn_gain).astype(jnp.bfloat16)
    head_shape = (length, heads_here, HEAD_DIM)
    query_raw = jnp.dot(attn_in, w_query, preferred_element_type=jnp.float32).reshape(head_shape)
    key_raw = jnp.dot(attn_in, w_key, preferred_element_type=jnp.float32).reshape(head_shape)
    value_rows = (
        jnp.dot(attn_in, w_value, preferred_element_type=jnp.float32)
        .astype(jnp.bfloat16)
        .reshape(head_shape)
    )
    query_scale = query_gain.reshape(heads_here, HEAD_DIM)
    key_scale = key_gain.reshape(heads_here, HEAD_DIM)
    square_sums = spread_sum(
        jnp.stack(
            [jnp.sum(query_raw * query_raw, axis=(1, 2)), jnp.sum(key_raw * key_raw, axis=(1, 2))]
        ),
        "tensor",
    )
    query_inverse = lax.rsqrt(square_sums[0] / full_cols + EPS)[:, None, None]
    key_inverse = lax.rsqrt(square_sums[1] / full_cols + EPS)[:, None, None]
    query_normal = query_raw * query_inverse
    key_normal = key_raw * key_inverse
    query_rows = (
        rotary(query_normal * query_scale, cosine_table, sine_table) * score_scale
    ).astype(jnp.bfloat16)
    key_rows = rotary(key_normal * key_scale, cosine_table, sine_table).astype(jnp.bfloat16)
    mixed_heads, totals = attention_forward(query_rows, key_rows, value_rows)
    mixed_low = mixed_heads.reshape(length, heads_here * HEAD_DIM).astype(jnp.bfloat16)
    mixed_pair = plane_rows(mixed_low, 0, own_rows)
    attn_own = plane_scatter(
        *[
            jnp.dot(part, w_out, preferred_element_type=jnp.float32).astype(jnp.bfloat16)
            for part in mixed_pair
        ],
        0,
    )
    hidden = own_slice(token_float) + attn_own
    ffn_normal, ffn_inverse = rms_forward(hidden)
    ffn_in = (ffn_normal * ffn_gain).astype(jnp.bfloat16)
    chosen = (expert_iota == own_expert).astype(jnp.float32)[None, :]
    moe_sum = hidden
    grad_ffn = jnp.zeros(hidden.shape, jnp.float32)
    kept_arrays = None
    for chunk in range(expert_size):
        x_pair = plane_gather(ffn_in if chunk == 0 else swap(ffn_in, "expert", chunk), chunk)
        grad_pair, sent_pair, kept_arrays = expert_chunk(
            chunk,
            expert_size,
            x_pair,
            grad_pairs[chunk],
            kept_columns[chunk],
            chosen,
            router,
            w_gate[0],
            w_up[0],
            w_down[0],
            kept_arrays,
        )
        grad_piece = plane_scatter(*grad_pair, chunk)
        sent_piece = plane_scatter(*sent_pair, chunk)
        if chunk:
            grad_piece = swap(grad_piece.astype(jnp.bfloat16), "expert", chunk).astype(jnp.float32)
            sent_piece = swap(sent_piece.astype(jnp.bfloat16), "expert", chunk).astype(jnp.float32)
        grad_ffn = grad_ffn + grad_piece
        moe_sum = moe_sum + sent_piece
    output = lax.all_gather(moe_sum.astype(jnp.bfloat16), "tensor", axis=0, tiled=True)
    expert_rows, grad_value, active, grad_pre_gate, grad_pre_up, grad_logits = kept_arrays
    grad_down = jnp.einsum("rh,rd->hd", active, grad_value, preferred_element_type=jnp.float32)
    grad_gate_w = jnp.einsum(
        "rd,rh->dh", expert_rows, grad_pre_gate, preferred_element_type=jnp.float32
    )
    grad_up_w = jnp.einsum(
        "rd,rh->dh", expert_rows, grad_pre_up, preferred_element_type=jnp.float32
    )
    grad_router_part = jnp.einsum(
        "rd,re->ed", expert_rows, grad_logits, preferred_element_type=jnp.float32
    )
    grad_hidden_part, grad_ffn_gain = rms_backward(grad_ffn, ffn_normal, ffn_inverse, ffn_gain)
    grad_hidden = grad_own.astype(jnp.float32) + grad_hidden_part
    hidden_pair = plane_gather(grad_hidden.astype(jnp.bfloat16), 0)
    grad_w_out = contract(mixed_pair[0], hidden_pair[0], 0, 0) + contract(
        mixed_pair[1], hidden_pair[1], 0, 0
    )
    grad_mixed = natural_rows(
        *[contract(part, w_out, 1, 1).astype(jnp.bfloat16) for part in hidden_pair], 0, own_rows
    ).reshape(head_shape)
    grad_query, grad_key, grad_value_attn = attention_backward(
        query_rows, key_rows, value_rows, grad_mixed, totals
    )
    grad_query_normed = rotary(grad_query * score_scale, cosine_table, -sine_table)
    grad_key_normed = rotary(grad_key, cosine_table, -sine_table)
    grad_query_scale = jnp.sum(grad_query_normed * query_normal, axis=0)
    grad_key_scale = jnp.sum(grad_key_normed * key_normal, axis=0)
    query_scaled = grad_query_normed * query_scale
    key_scaled = grad_key_normed * key_scale
    inner_sums = spread_sum(
        jnp.stack(
            [
                jnp.sum(query_scaled * query_normal, axis=(1, 2)),
                jnp.sum(key_scaled * key_normal, axis=(1, 2)),
            ]
        ),
        "tensor",
    )
    grad_query_raw = query_inverse * (
        query_scaled - query_normal * (inner_sums[0] / full_cols)[:, None, None]
    )
    grad_key_raw = key_inverse * (
        key_scaled - key_normal * (inner_sums[1] / full_cols)[:, None, None]
    )
    query_low = grad_query_raw.reshape(length, heads_here * HEAD_DIM).astype(jnp.bfloat16)
    key_low = grad_key_raw.reshape(length, heads_here * HEAD_DIM).astype(jnp.bfloat16)
    value_low = grad_value_attn.reshape(length, heads_here * HEAD_DIM).astype(jnp.bfloat16)
    grad_w_query = jnp.einsum("td,tq->dq", attn_in, query_low, preferred_element_type=jnp.float32)
    grad_w_key = jnp.einsum("td,tq->dq", attn_in, key_low, preferred_element_type=jnp.float32)
    grad_w_value = jnp.einsum("td,tq->dq", attn_in, value_low, preferred_element_type=jnp.float32)
    low_pairs = [plane_rows(low, 1, own_rows) for low in (query_low, key_low, value_low)]
    grad_attn_own = plane_scatter(
        *[
            (
                contract(low_pairs[0][side], w_query, 1, 1)
                + contract(low_pairs[1][side], w_key, 1, 1)
                + contract(low_pairs[2][side], w_value, 1, 1)
            ).astype(jnp.bfloat16)
            for side in range(2)
        ],
        1,
    )
    grad_token_part, grad_attn_gain = rms_backward(
        grad_attn_own, own_slice(attn_normal), own_slice(attn_inverse), attn_gain
    )
    grad_tokens = natural_rows(
        *plane_gather((grad_hidden + grad_token_part).astype(jnp.bfloat16), 0), 0, own_rows
    )
    head_sums = [
        lax.psum(part.astype(jnp.bfloat16), "expert").astype(jnp.float32)
        for part in (grad_w_query, grad_w_key, grad_w_value, grad_w_out)
    ]
    scale_sums = spread_sum(
        jnp.stack([grad_query_scale.reshape(-1), grad_key_scale.reshape(-1)]), "expert"
    )
    early_sums = spread_sum(
        spread_sum(jnp.concatenate([grad_router_part, grad_ffn_gain[None, :]], axis=0), "tensor"),
        "expert",
    )
    late_sums = spread_sum(
        spread_sum(grad_attn_gain.reshape(8, model_width // 8), "tensor"), "expert"
    ).reshape(model_width)
    return (
        output,
        grad_tokens,
        late_sums,
        head_sums[0],
        head_sums[1],
        head_sums[2],
        scale_sums[0],
        scale_sums[1],
        head_sums[3],
        early_sums[expert_count],
        early_sums[:expert_count].T,
        grad_gate_w[None],
        grad_up_w[None],
        grad_down[None],
    )


def solution(mesh):
    placed = (
        P("expert", None),
        P("expert"),
        P("expert", None),
        P("expert", None),
        P(),
        P(None, "tensor"),
        P(None, "tensor"),
        P(None, "tensor"),
        P("tensor"),
        P("tensor"),
        P("tensor", None),
        P(),
        P(),
        P(("expert", "tensor"), None, None),
        P(("expert", "tensor"), None, None),
        P(("expert", "tensor"), None, None),
        P("expert", None),
    )
    return jax.shard_map(
        on_device,
        mesh=mesh,
        in_specs=placed,
        out_specs=(
            P("expert", None),
            P("expert", None),
            P(),
            P(None, "tensor"),
            P(None, "tensor"),
            P(None, "tensor"),
            P("tensor"),
            P("tensor"),
            P("tensor", None),
            P(),
            P(),
            P(("expert", "tensor"), None, None),
            P(("expert", "tensor"), None, None),
            P(("expert", "tensor"), None, None),
        ),
        check_vma=False,
    )
```

```python
import jax
import jax.numpy as jnp
from jax import lax
from jax.experimental import pallas as pl
from jax.experimental.pallas import tpu as pltpu
from jax.sharding import PartitionSpec as P

HEAD_DIM = 128
TOP = 8


EPS = 1e-05
THETA = 10000.0


def rms_forward(values):
    inverse = lax.rsqrt(jnp.mean(values * values, axis=-1, keepdims=True) + EPS)
    return (values * inverse, inverse)


def rms_backward(grad_normed, normal_rows, inverse, gain_row):
    gain_grad = jnp.sum(grad_normed * normal_rows, axis=0)
    scaled = grad_normed * gain_row
    grad_rows = inverse * (
        scaled - normal_rows * jnp.mean(scaled * normal_rows, axis=-1, keepdims=True)
    )
    return (grad_rows, gain_grad)


def rotary(values, cosine_table, sine_table):
    half_dim = values.shape[-1] // 2
    first_half = values[..., :half_dim]
    second_half = values[..., half_dim:]
    return jnp.concatenate(
        [
            first_half * cosine_table - second_half * sine_table,
            second_half * cosine_table + first_half * sine_table,
        ],
        axis=-1,
    )


def causal_mask(start_row, end_row):
    return (jnp.arange(start_row, end_row)[:, None] >= jnp.arange(end_row)[None, :])[None]


def attention_forward(query_rows, key_rows, value_rows):
    length = query_rows.shape[0]
    block_rows = min(512, length)
    outputs = []
    totals = []
    for block_start in range(0, length, block_rows):
        block_end = block_start + block_rows
        scores = jnp.einsum(
            "qhd,khd->hqk",
            query_rows[block_start:block_end],
            key_rows[:block_end],
            preferred_element_type=jnp.float32,
        )
        scores = jnp.where(causal_mask(block_start, block_end), scores, -1e30)
        row_peak = jnp.max(scores, axis=-1, keepdims=True)
        exponent = jnp.exp(scores - row_peak)
        row_total = jnp.sum(exponent, axis=-1, keepdims=True)
        weights = (exponent / row_total).astype(jnp.bfloat16)
        outputs.append(
            jnp.einsum(
                "hqk,khd->qhd", weights, value_rows[:block_end], preferred_element_type=jnp.float32
            )
        )
        totals.append(row_peak + jnp.log(row_total))
    return (jnp.concatenate(outputs, axis=0), totals)


def attention_backward(query_rows, key_rows, value_rows, grad_mixed, totals):
    length = query_rows.shape[0]
    block_rows = min(512, length)
    grad_keys = jnp.zeros(key_rows.shape, jnp.float32)
    grad_values = jnp.zeros(value_rows.shape, jnp.float32)
    grad_queries = []
    for block_number, block_start in enumerate(range(0, length, block_rows)):
        block_end = block_start + block_rows
        query_block = query_rows[block_start:block_end]
        grad_block = grad_mixed[block_start:block_end]
        scores = jnp.einsum(
            "qhd,khd->hqk", query_block, key_rows[:block_end], preferred_element_type=jnp.float32
        )
        scores = jnp.where(causal_mask(block_start, block_end), scores, -1e30)
        probs_again = jnp.exp(scores - totals[block_number])
        weights = probs_again.astype(jnp.bfloat16)
        grad_probs = jnp.einsum(
            "qhd,khd->hqk", grad_block, value_rows[:block_end], preferred_element_type=jnp.float32
        )
        grad_scores = (
            probs_again * (grad_probs - jnp.sum(probs_again * grad_probs, axis=-1, keepdims=True))
        ).astype(jnp.bfloat16)
        grad_queries.append(
            jnp.einsum(
                "hqk,khd->qhd",
                grad_scores,
                key_rows[:block_end],
                preferred_element_type=jnp.float32,
            )
        )
        grad_keys = grad_keys.at[:block_end].add(
            jnp.einsum("hqk,qhd->khd", grad_scores, query_block, preferred_element_type=jnp.float32)
        )
        grad_values = grad_values.at[:block_end].add(
            jnp.einsum("hqk,qhd->khd", weights, grad_block, preferred_element_type=jnp.float32)
        )
    return (jnp.concatenate(grad_queries, axis=0), grad_keys, grad_values)


def swap(values, axis, bit):
    return lax.ppermute(values, axis, [(i, i ^ bit) for i in range(lax.axis_size(axis))])


def axis_bits(axis):
    size = lax.axis_size(axis)
    return [size >> (k + 1) for k in range(size.bit_length() - 1)]


def spread_sum(values, axis):
    for bit in axis_bits(axis)[::-1]:
        values = values + swap(values, axis, bit)
    return values


def plane_order(turn):
    bits = axis_bits("tensor")[:-1]
    if turn % 2:
        bits = bits[::-1]
    order = [0]
    for bit in bits:
        order = order + [bit ^ i for i in order]
    return bits, order


def plane_gather(piece, turn):
    bits, _ = plane_order(turn)
    pieces = [piece]
    for bit in bits:
        pieces = pieces + [swap(p, "tensor", bit) for p in pieces]
    near = jnp.concatenate(pieces, axis=0)
    return near, swap(near, "tensor", 1)


def plane_scatter(near, far, turn):
    bits, _ = plane_order(turn)
    total = near.astype(jnp.float32) + swap(far, "tensor", 1).astype(jnp.float32)
    for bit in bits[::-1]:
        half = total.shape[0] // 2
        sent = total[half:].astype(jnp.bfloat16)
        total = total[:half].astype(jnp.bfloat16).astype(jnp.float32) + swap(
            sent, "tensor", bit
        ).astype(jnp.float32)
    return total


def plane_rows(values, turn, own_rows):
    _, order = plane_order(turn)
    index = lax.axis_index("tensor")

    def block(i):
        return lax.dynamic_slice_in_dim(values, (index ^ i) * own_rows, own_rows, 0)

    near = jnp.concatenate([block(i) for i in order], axis=0)
    far = jnp.concatenate([block(i ^ 1) for i in order], axis=0)
    return near, far


def natural_rows(near, far, turn, own_rows):
    _, order = plane_order(turn)
    index = lax.axis_index("tensor")
    both = jnp.concatenate([near, far], axis=0)
    place = {}
    for at, i in enumerate(order):
        place[i] = at
        place[i ^ 1] = at + len(order)
    table = jnp.array([place[i] for i in range(2 * len(order))], jnp.int32)
    return jnp.concatenate(
        [
            lax.dynamic_slice_in_dim(both, table[index ^ i] * own_rows, own_rows, 0)
            for i in range(2 * len(order))
        ],
        axis=0,
    )


def contract(left, right, left_dim, right_dim):
    return lax.dot_general(
        left, right, (((left_dim,), (right_dim,)), ((), ())), preferred_element_type=jnp.float32
    )


def tie(values, *after):
    return lax.optimization_barrier((values, *after))[0]


def stages(turn, bits):
    if turn % 2:
        bits = bits[::-1]
    found = [[] for _ in bits]
    order = [(0, ())]
    for bit in bits:
        order = order + [(bit ^ i, used + (bit,)) for i, used in order]
    for i, used in order[1:]:
        found[len(used) - 1].append((i, i ^ used[-1], used[-1]))
    return found


def gather_stage(pieces, turn, stage, bits, after=()):
    pieces = dict(pieces)
    for i, source, bit in stages(turn, bits)[stage]:
        sent = pieces[source]
        if after:
            sent = tie(sent, *after)
        pieces[i] = swap(sent, "tensor", bit)
    return pieces


def gather_all(piece, turn, bits):
    pieces = {0: piece}
    for stage in range(len(bits)):
        pieces = gather_stage(pieces, turn, stage, bits)
    return pieces


def scatter_stage(sums, turn, stage, bits, after=()):
    sums = dict(sums)
    for i, target, bit in stages(turn, bits)[len(bits) - 1 - stage]:
        sent = sums.pop(i).astype(jnp.bfloat16)
        if after:
            sent = tie(sent, *after)
        sums[target] = sums[target].astype(jnp.float32) + swap(sent, "tensor", bit).astype(
            jnp.float32
        )
    return sums


MEGABYTE = 1024 * 1024


def kernel_params(megabytes):
    return pltpu.CompilerParams(vmem_limit_bytes=megabytes * MEGABYTE)


def cost(flops, moved):
    return pl.CostEstimate(flops=flops, bytes_accessed=moved, transcendentals=0)


def column_of(row):
    n = row.shape[1]
    down = lax.broadcasted_iota(jnp.int32, (n, n), 0)
    across = lax.broadcasted_iota(jnp.int32, (n, n), 1)
    return jnp.sum(jnp.where(down == across, row, 0.0), axis=1, keepdims=True)


def pick(step, steps, own_ref, other_ref):
    return jnp.where(step < steps, own_ref[...], other_ref[...])


def forward_body(indices, halves, scalars, *refs):
    count = len(indices)
    pieces = refs[:count]
    kept, chosen, router, gate_own, gate_other, up_own, up_other = refs[count : count + 7]
    x_all, act_all, pre_gate_out, pre_up_out, gate_out, probs_out = refs[-6:]
    step = pl.program_id(0)

    @pl.when(step == 0)
    def _():
        rows = jnp.concatenate([piece[...] for piece in pieces], axis=0)
        x_all[...] = rows
        logits = contract(rows, router[...], 1, 0)
        exponent = jnp.exp(logits - jnp.max(logits, axis=-1, keepdims=True))
        probs = exponent / jnp.sum(exponent, axis=-1, keepdims=True)
        kept_column = jnp.concatenate(
            [column_of(kept[pl.ds(scalars[0] ^ i, 1), :]) for i in indices], axis=0
        )
        probs_out[...] = probs
        gate_out[...] = jnp.sum(probs * chosen[...], axis=-1, keepdims=True) * kept_column

    rows = x_all[...]
    pre_gate = contract(rows, pick(step, halves, gate_own, gate_other), 1, 0)
    pre_up = contract(rows, pick(step, halves, up_own, up_other), 1, 0)
    pre_gate_out[...] = pre_gate
    pre_up_out[...] = pre_up
    act_all[...] = (pre_gate * jax.nn.sigmoid(pre_gate) * pre_up).astype(jnp.bfloat16)


def hidden_blocks(units):
    block = min(256, units)
    return block, units // block


def unit_columns(width, block, steps):
    own = pl.BlockSpec((width, block), lambda j, *_: (0, jnp.minimum(j, steps - 1)))
    other = pl.BlockSpec((width, block), lambda j, *_: (0, jnp.maximum(j - steps, 0)))
    return [own, other]


def unit_rows(width, block, steps):
    own = pl.BlockSpec((block, width), lambda j, *_: (jnp.minimum(j, steps - 1), 0))
    other = pl.BlockSpec((block, width), lambda j, *_: (jnp.maximum(j - steps, 0), 0))
    return [own, other]


def fixed(shape, single=True):
    if single:
        return pl.BlockSpec(
            shape, lambda *_: (0,) * len(shape), pipeline_mode=pl.Buffered(1)
        )
    return pl.BlockSpec(shape, lambda *_: (0,) * len(shape))


def expert_forward(place, places, pieces, here, kept, chosen, router, gates, ups, chain):
    indices = sorted(pieces)
    own_rows, width = pieces[0].shape
    rows = own_rows * len(indices)
    units = gates[0].shape[1]
    experts = router.shape[1]
    block, steps = hidden_blocks(units)
    extra = () if chain is None else tuple(chain)
    count = len(indices)
    row_block = pl.BlockSpec((rows, width), lambda j, *_: (place, 0))
    act_block = pl.BlockSpec((rows, block), lambda j, *_: (place, j))
    unit_block = pl.BlockSpec((rows, block), lambda j, *_: (0, j))
    results = pl.pallas_call(
        lambda *refs: forward_body(indices, steps, *refs),
        grid_spec=pltpu.PrefetchScalarGridSpec(
            num_scalar_prefetch=1,
            grid=(2 * steps,),
            in_specs=[fixed((own_rows, width))] * count
            + [fixed(kept.shape), fixed((1, experts)), fixed((width, experts))]
            + unit_columns(width, block, steps) * 2
            + [pl.BlockSpec(memory_space=pl.ANY)] * len(extra),
            out_specs=[
                row_block,
                act_block,
                unit_block,
                unit_block,
                fixed((rows, 1), False),
                fixed((rows, experts), False),
            ],
        ),
        out_shape=[
            jax.ShapeDtypeStruct((rows * places, width), jnp.bfloat16),
            jax.ShapeDtypeStruct((rows * places, 2 * units), jnp.bfloat16),
            jax.ShapeDtypeStruct((rows, 2 * units), jnp.float32),
            jax.ShapeDtypeStruct((rows, 2 * units), jnp.float32),
            jax.ShapeDtypeStruct((rows, 1), jnp.float32),
            jax.ShapeDtypeStruct((rows, experts), jnp.float32),
        ],
        input_output_aliases={count + 8 + i: i for i in range(len(extra))},
        compiler_params=kernel_params(40),
        cost_estimate=cost(8 * rows * width * units, 4 * rows * width + 8 * width * units),
        name="expert_forward",
    )(here, *[pieces[i] for i in indices], kept, chosen, router, *gates, *ups, *extra)
    return results[:2], results[2:]


def backward_body(indices, halves, scalars, *refs):
    count = len(indices)
    grads = refs[:count]
    pre_gate, pre_up, act, gate, probs, chosen, router = refs[count : count + 7]
    down_own, down_other, gate_own, gate_other, up_own, up_other = refs[count + 7 : count + 13]
    outs = refs[-(count + 5) - 2 :]
    pieces = outs[:count]
    dy_all, gated_all, dg_all, du_all, dl_all = outs[count : count + 5]
    total, dots = outs[-2:]
    step = pl.program_id(0)
    own_rows = pieces[0].shape[0]

    @pl.when(step == 0)
    def _():
        dy_all[...] = jnp.concatenate([part[0] for part in grads], axis=0)
        dots[...] = jnp.zeros_like(dots)

    down = pick(step, halves, down_own, down_other)
    inner = contract(dy_all[...], down, 1, 1)
    pre_gate_now = pre_gate[...]
    active = act[...].astype(jnp.float32)
    sigmoid_gate = jax.nn.sigmoid(pre_gate_now)
    dots[...] += jnp.sum(inner * active, axis=-1, keepdims=True)
    grad_active = gate[...] * inner
    grad_pre_gate = (
        grad_active * pre_up[...] * sigmoid_gate * (1.0 + pre_gate_now * (1.0 - sigmoid_gate))
    ).astype(jnp.bfloat16)
    grad_pre_up = (grad_active * (pre_gate_now * sigmoid_gate)).astype(jnp.bfloat16)
    gated_all[...] = (gate[...] * active).astype(jnp.bfloat16)
    dg_all[...] = grad_pre_gate
    du_all[...] = grad_pre_up
    part = contract(grad_pre_gate, pick(step, halves, gate_own, gate_other), 1, 1) + contract(
        grad_pre_up, pick(step, halves, up_own, up_other), 1, 1
    )

    @pl.when(step == 0)
    def _():
        total[...] = part

    @pl.when(step > 0)
    def _():
        total[...] += part

    @pl.when(step == 2 * halves - 1)
    def _():
        grad_logits = (dots[...] * gate[...] * (chosen[...] - probs[...])).astype(jnp.bfloat16)
        dl_all[...] = grad_logits
        done = (total[...] + contract(grad_logits, router[...], 1, 1)).astype(jnp.bfloat16)
        for at, piece in enumerate(pieces):
            piece[...] = done[at * own_rows : (at + 1) * own_rows]


def expert_backward(
    place, places, indices, here, grad_all, saved, act_all, chosen, router, downs, gates, ups, chain
):
    pre_gate, pre_up, gate, probs = saved
    own_rows, width = grad_all.shape[1:]
    rows = own_rows * len(indices)
    units = gates[0].shape[1]
    experts = router.shape[1]
    block, steps = hidden_blocks(units)
    extra = () if chain is None else tuple(chain)
    count = len(indices)

    def grad_block(i):
        return pl.BlockSpec(
            (1, own_rows, width),
            lambda j, at: (at[1] + (at[0] ^ i), 0, 0),
            pipeline_mode=pl.Buffered(1),
        )

    unit_block = pl.BlockSpec((rows, block), lambda j, *_: (0, j))
    place_unit = pl.BlockSpec((rows, block), lambda j, *_: (place, j))
    results = pl.pallas_call(
        lambda *refs: backward_body(indices, steps, *refs),
        grid_spec=pltpu.PrefetchScalarGridSpec(
            num_scalar_prefetch=1,
            grid=(2 * steps,),
            in_specs=[grad_block(i) for i in indices]
            + [
                unit_block,
                unit_block,
                place_unit,
                fixed((rows, 1)),
                fixed((rows, experts)),
                fixed((1, experts)),
                fixed((width, experts)),
            ]
            + unit_rows(width, block, steps)
            + unit_columns(width, block, steps) * 2
            + [pl.BlockSpec(memory_space=pl.ANY)] * len(extra),
            out_specs=[fixed((own_rows, width), False)] * count
            + [
                pl.BlockSpec((rows, width), lambda j, *_: (place, 0)),
                place_unit,
                place_unit,
                place_unit,
                pl.BlockSpec((rows, experts), lambda j, *_: (place, 0)),
            ],
            scratch_shapes=[
                pltpu.VMEM((rows, width), jnp.float32),
                pltpu.VMEM((rows, 1), jnp.float32),
            ],
        ),
        out_shape=[jax.ShapeDtypeStruct((own_rows, width), jnp.bfloat16)] * count
        + [jax.ShapeDtypeStruct((rows * places, width), jnp.bfloat16)]
        + [jax.ShapeDtypeStruct((rows * places, 2 * units), jnp.bfloat16)] * 3
        + [jax.ShapeDtypeStruct((rows * places, experts), jnp.bfloat16)],
        input_output_aliases={count + 14 + i: count + i for i in range(len(extra))},
        compiler_params=kernel_params(48),
        cost_estimate=cost(12 * rows * width * units, 8 * rows * width + 12 * width * units),
        name="expert_backward",
    )(
        here,
        *[grad_all] * count,
        pre_gate,
        pre_up,
        act_all,
        gate,
        probs,
        chosen,
        router,
        *downs,
        *gates,
        *ups,
        *extra,
    )
    return dict(zip(indices, results[:count])), results[count:]


def send_body(act, gate, down_own, down_other, *pieces):
    units = down_own.shape[0]
    value = contract(act[:, :units], down_own[...], 1, 0) + contract(
        act[:, units:], down_other[...], 1, 0
    )
    sent = (gate[...] * value).astype(jnp.bfloat16)
    own_rows = pieces[0].shape[0]
    for at, piece in enumerate(pieces):
        piece[...] = sent[at * own_rows : (at + 1) * own_rows]


def expert_send(place, indices, act_all, gate, downs):
    rows = gate.shape[0]
    count = len(indices)
    units, width = downs[0].shape
    block = min(512, width)
    results = pl.pallas_call(
        send_body,
        grid=(width // block,),
        in_specs=[
            pl.BlockSpec((rows, 2 * units), lambda j: (place, 0)),
            fixed((rows, 1)),
            pl.BlockSpec((units, block), lambda j: (0, j)),
            pl.BlockSpec((units, block), lambda j: (0, j)),
        ],
        out_specs=[pl.BlockSpec((rows // count, block), lambda j: (0, j))] * count,
        out_shape=[jax.ShapeDtypeStruct((rows // count, width), jnp.bfloat16)] * count,
        compiler_params=kernel_params(32),
        cost_estimate=cost(4 * rows * width * units, 4 * rows * width + 4 * width * units),
        name="expert_send",
    )(act_all, gate, *downs)
    return dict(zip(indices, results))


def project_body(indices, halves, scalars, mixed, tokens, gain, *refs):
    weights = refs[: len(indices) * halves]
    hidden_out, low_out = refs[-2:]
    total = tokens[...].astype(jnp.float32)
    depth = weights[0].shape[0]
    attn = None
    for at, i in enumerate(indices):
        piece = mixed[scalars[0] ^ i]
        for half in range(halves):
            part = contract(
                piece[:, half * depth : (half + 1) * depth], weights[at * halves + half][...], 1, 0
            )
            attn = part if attn is None else attn + part
    hidden = total + attn
    normal, _ = rms_forward(hidden)
    hidden_out[...] = hidden
    low_out[...] = (normal * gain[...]).astype(jnp.bfloat16)


def project_out(here, indices, mixed, tokens, gain, weights, halves):
    rows, width = tokens.shape
    return pl.pallas_call(
        lambda *refs: project_body(indices, halves, *refs),
        grid_spec=pltpu.PrefetchScalarGridSpec(
            num_scalar_prefetch=1,
            grid=(1,),
            in_specs=[fixed(mixed.shape), fixed(tokens.shape), fixed((1, width))]
            + [fixed(weights[0].shape)] * len(weights),
            out_specs=[fixed((rows, width), False), fixed((rows, width), False)],
        ),
        out_shape=[
            jax.ShapeDtypeStruct((rows, width), jnp.float32),
            jax.ShapeDtypeStruct((rows, width), jnp.bfloat16),
        ],
        compiler_params=kernel_params(40),
        cost_estimate=cost(2 * rows * width * width, 2 * width * width),
        name="project_out",
    )(here, mixed, tokens, gain, *weights)


def turn_body(indices, halves, count, scalars, hidden, grad_out, gain, *refs):
    grads = refs[:count]
    weights = refs[count : count + len(indices) * halves]
    grad_hidden_out, low_out, mixed_out, gain_out = refs[-4:]
    grad_ffn = grads[0][...].astype(jnp.float32)
    for part in grads[1:]:
        grad_ffn = grad_ffn + part[...].astype(jnp.float32)
    normal, inverse = rms_forward(hidden[...])
    gain_out[...] = jnp.sum(grad_ffn * normal, axis=0, keepdims=True)
    scaled = grad_ffn * gain[...]
    grad_hidden = grad_out[...].astype(jnp.float32) + inverse * (
        scaled - normal * jnp.mean(scaled * normal, axis=-1, keepdims=True)
    )
    low = grad_hidden.astype(jnp.bfloat16)
    grad_hidden_out[...] = grad_hidden
    low_out[...] = low
    depth = weights[0].shape[0]
    for at, i in enumerate(indices):
        for half in range(halves):
            mixed_out[scalars[0] ^ i, :, half * depth : (half + 1) * depth] = contract(
                low, weights[at * halves + half][...], 1, 1
            ).astype(jnp.bfloat16)


def turn_back(here, indices, hidden, grad_out, gain, grads, weights, halves):
    rows, width = hidden.shape
    depth = weights[0].shape[0] * halves
    return pl.pallas_call(
        lambda *refs: turn_body(indices, halves, len(grads), *refs),
        grid_spec=pltpu.PrefetchScalarGridSpec(
            num_scalar_prefetch=1,
            grid=(1,),
            in_specs=[fixed((rows, width)), fixed((rows, width)), fixed((1, width))]
            + [fixed((rows, width))] * len(grads)
            + [fixed(weights[0].shape)] * len(weights),
            out_specs=[
                fixed((rows, width), False),
                fixed((rows, width), False),
                fixed((len(indices), rows, depth), False),
                fixed((1, width), False),
            ],
        ),
        out_shape=[
            jax.ShapeDtypeStruct((rows, width), jnp.float32),
            jax.ShapeDtypeStruct((rows, width), jnp.bfloat16),
            jax.ShapeDtypeStruct((len(indices), rows, depth), jnp.bfloat16),
            jax.ShapeDtypeStruct((1, width), jnp.float32),
        ],
        compiler_params=kernel_params(40),
        cost_estimate=cost(2 * rows * width * width, 2 * width * width),
        name="turn_back",
    )(here, hidden, grad_out, gain, *grads, *weights)


def on_device(
    tokens,
    positions,
    routes,
    slot_ids,
    attn_gain,
    w_query,
    w_key,
    w_value,
    query_gain,
    key_gain,
    w_out,
    ffn_gain,
    router,
    w_gate,
    w_up,
    w_down,
    grad_out,
):
    tensor_size = lax.axis_size("tensor")
    expert_size = lax.axis_size("expert")
    local_count = tensor_size // 2
    tensor_index = lax.axis_index("tensor")
    expert_index = lax.axis_index("expert")
    own_local = tensor_index // 2
    own_expert = expert_index * local_count + own_local
    length, model_width = tokens.shape
    heads_here = w_query.shape[1] // HEAD_DIM
    full_cols = w_query.shape[1] * tensor_size
    expert_count = router.shape[1]
    capacity = 3 * length * TOP // (2 * expert_count)
    own_rows = length // tensor_size
    both_axes = ("expert", "tensor")
    chunks = [0] + list(range(2, expert_size)) + [1]
    bits = axis_bits("tensor")
    near_bits = bits[:-1]
    last = len(near_bits)

    def own_slice(rows):
        return lax.dynamic_slice_in_dim(rows, tensor_index * own_rows, own_rows, 0)

    def with_sibling(weights):
        return [weights, swap(weights, "tensor", 1)]

    grad_own = own_slice(grad_out)
    grad_all = lax.all_gather(grad_own, both_axes, axis=0)
    w_halves = [w_out[: w_out.shape[0] // 2], w_out[w_out.shape[0] // 2 :]]
    out_pieces = [gather_all(half, turn, bits) for turn, half in enumerate(w_halves)]
    all_indices = sorted(out_pieces[0])
    out_weights = [out_pieces[half][i] for i in all_indices for half in range(2)]
    gates, ups, downs = with_sibling(w_gate[0]), with_sibling(w_up[0]), with_sibling(w_down[0])
    expert_iota = jnp.arange(expert_count, dtype=jnp.int32)
    kept_table = jnp.sum(
        (
            (routes.T[:, None, :] == expert_iota[None, :, None]) & (slot_ids.T < capacity)[:, None, :]
        ).astype(jnp.float32),
        axis=0,
    )
    kept_chunks = []
    for chunk in range(expert_size):
        target = (expert_index ^ chunk) * local_count + own_local
        kept_row = lax.dynamic_slice_in_dim(kept_table, target, 1, 0).reshape(tensor_size, own_rows)
        kept_chunks.append(swap(kept_row, "expert", chunk) if chunk else kept_row)

    def here(chunk):
        return jnp.stack([tensor_index, (expert_index ^ chunk) * tensor_size]).astype(jnp.int32)

    score_scale = HEAD_DIM ** (-0.5)
    half_dim = HEAD_DIM // 2
    frequency = THETA ** (-2.0 * jnp.arange(half_dim, dtype=jnp.float32) / HEAD_DIM)
    angles = positions.astype(jnp.float32)[:, None] * frequency[None, :]
    cosine_table = jnp.cos(angles)[:, None, :]
    sine_table = jnp.sin(angles)[:, None, :]
    token_float = tokens.astype(jnp.float32)
    attn_normal, attn_inverse = rms_forward(token_float)
    attn_in = (attn_normal * attn_gain).astype(jnp.bfloat16)
    head_shape = (length, heads_here, HEAD_DIM)
    query_raw = jnp.dot(attn_in, w_query, preferred_element_type=jnp.float32).reshape(head_shape)
    key_raw = jnp.dot(attn_in, w_key, preferred_element_type=jnp.float32).reshape(head_shape)
    value_rows = (
        jnp.dot(attn_in, w_value, preferred_element_type=jnp.float32)
        .astype(jnp.bfloat16)
        .reshape(head_shape)
    )
    query_scale = query_gain.reshape(heads_here, HEAD_DIM)
    key_scale = key_gain.reshape(heads_here, HEAD_DIM)
    square_sums = spread_sum(
        jnp.stack(
            [jnp.sum(query_raw * query_raw, axis=(1, 2)), jnp.sum(key_raw * key_raw, axis=(1, 2))]
        ),
        "tensor",
    )
    query_inverse = lax.rsqrt(square_sums[0] / full_cols + EPS)[:, None, None]
    key_inverse = lax.rsqrt(square_sums[1] / full_cols + EPS)[:, None, None]
    query_normal = query_raw * query_inverse
    key_normal = key_raw * key_inverse
    query_rows = (
        rotary(query_normal * query_scale, cosine_table, sine_table) * score_scale
    ).astype(jnp.bfloat16)
    key_rows = rotary(key_normal * key_scale, cosine_table, sine_table).astype(jnp.bfloat16)
    mixed_heads, totals = attention_forward(query_rows, key_rows, value_rows)
    mixed_low = mixed_heads.reshape(length, heads_here * HEAD_DIM).astype(jnp.bfloat16)
    mixed_own = lax.all_to_all(
        mixed_low.reshape(tensor_size, own_rows, -1), "tensor", split_axis=0, concat_axis=0, tiled=True
    )
    hidden, ffn_in = project_out(
        here(0), all_indices, mixed_own, own_slice(tokens), ffn_gain[None, :], out_weights, 2
    )
    chosen = (expert_iota == own_expert).astype(jnp.float32)[None, :]
    gathered = [
        {0: ffn_in if chunk == 0 else swap(ffn_in, "expert", chunk)} for chunk in chunks
    ]
    chain = None
    saved = []
    for at, chunk in enumerate(chunks):
        after = (saved[at - 2][2],) if at >= 2 else ()
        for stage in range(last):
            gathered[at] = gather_stage(gathered[at], at, stage, near_bits, after)
        chain, kept = expert_forward(
            at,
            expert_size,
            gathered[at],
            here(chunk),
            kept_chunks[chunk],
            chosen,
            router,
            gates,
            ups,
            chain,
        )
        saved.append(kept)
    x_all, act_all = chain
    indices = sorted(gathered[0])
    chain = None
    sums = []
    for at, chunk in enumerate(chunks):
        scalars = here(chunk)
        for stage in range(last):
            if at >= stage + 2:
                scalars = tie(scalars, sums[at - stage - 2][0])
        pieces, chain = expert_backward(
            at,
            expert_size,
            indices,
            scalars,
            grad_all,
            saved[at],
            act_all,
            chosen,
            router,
            downs,
            gates,
            ups,
            chain,
        )
        for stage in range(1, last):
            if at >= stage:
                sums[at - stage] = scatter_stage(
                    sums[at - stage], at - stage, stage, near_bits, (pieces[0],)
                )
        sums.append(scatter_stage(pieces, at, 0, near_bits))
    for stage in range(1, last):
        for at in range(expert_size - stage, expert_size):
            sums[at] = scatter_stage(sums[at], at, stage, near_bits)
    grad_parts = [
        sums[at][0] if chunk == 0 else swap(sums[at][0].astype(jnp.bfloat16), "expert", chunk)
        for at, chunk in enumerate(chunks)
    ]
    dy_all, gated_all, dg_all, du_all, dl_all = chain
    sent_pieces = [
        expert_send(at, indices, act_all, tie(saved[at][2], dl_all), downs)
        for at in range(expert_size)
    ]

    grad_hidden, hidden_low, grad_mixed_own, grad_ffn_gain = turn_back(
        here(0), all_indices, hidden, grad_own, ffn_gain[None, :], grad_parts, out_weights, 2
    )
    grad_mixed = lax.all_to_all(
        grad_mixed_own, "tensor", split_axis=0, concat_axis=0, tiled=True
    ).reshape(head_shape)

    moe_sum = hidden
    for at, chunk in enumerate(chunks):
        pieces = sent_pieces[at]
        for stage in range(last):
            pieces = scatter_stage(pieces, at, stage, near_bits, (hidden_low,))
        piece = pieces[0]
        if chunk:
            piece = swap(piece.astype(jnp.bfloat16), "expert", chunk).astype(jnp.float32)
        moe_sum = moe_sum + piece
    output = lax.all_gather(moe_sum.astype(jnp.bfloat16), "tensor", axis=0, tiled=True)

    units = dg_all.shape[1] // 2

    def both_cores(left, right, left_units):
        if left_units:
            own = contract(left[:, :units], right, 0, 0)
            other = contract(left[:, units:], right, 0, 0)
        else:
            own = contract(left, right[:, :units], 0, 0)
            other = contract(left, right[:, units:], 0, 0)
        return own + swap(other.astype(jnp.bfloat16), "tensor", 1).astype(jnp.float32)

    grad_gate_w = both_cores(x_all, dg_all, False)
    grad_up_w = both_cores(x_all, du_all, False)
    grad_down = both_cores(gated_all, dy_all, True)
    grad_router_part = contract(dl_all, x_all, 0, 0)

    hidden_low_all = lax.all_gather(hidden_low, "tensor", axis=0, tiled=True)
    grad_w_out = contract(mixed_low, hidden_low_all, 0, 0)
    grad_query, grad_key, grad_value_attn = attention_backward(
        query_rows, key_rows, value_rows, grad_mixed, totals
    )
    grad_query_normed = rotary(grad_query * score_scale, cosine_table, -sine_table)
    grad_key_normed = rotary(grad_key, cosine_table, -sine_table)
    grad_query_scale = jnp.sum(grad_query_normed * query_normal, axis=0)
    grad_key_scale = jnp.sum(grad_key_normed * key_normal, axis=0)
    query_scaled = grad_query_normed * query_scale
    key_scaled = grad_key_normed * key_scale
    inner_sums = spread_sum(
        jnp.stack(
            [
                jnp.sum(query_scaled * query_normal, axis=(1, 2)),
                jnp.sum(key_scaled * key_normal, axis=(1, 2)),
            ]
        ),
        "tensor",
    )
    grad_query_raw = query_inverse * (
        query_scaled - query_normal * (inner_sums[0] / full_cols)[:, None, None]
    )
    grad_key_raw = key_inverse * (
        key_scaled - key_normal * (inner_sums[1] / full_cols)[:, None, None]
    )
    query_low = grad_query_raw.reshape(length, heads_here * HEAD_DIM).astype(jnp.bfloat16)
    key_low = grad_key_raw.reshape(length, heads_here * HEAD_DIM).astype(jnp.bfloat16)
    value_low = grad_value_attn.reshape(length, heads_here * HEAD_DIM).astype(jnp.bfloat16)
    grad_w_query = jnp.einsum("td,tq->dq", attn_in, query_low, preferred_element_type=jnp.float32)
    grad_w_key = jnp.einsum("td,tq->dq", attn_in, key_low, preferred_element_type=jnp.float32)
    grad_w_value = jnp.einsum("td,tq->dq", attn_in, value_low, preferred_element_type=jnp.float32)
    low_pairs = [plane_rows(low, 1, own_rows) for low in (query_low, key_low, value_low)]
    grad_attn_own = plane_scatter(
        *[
            (
                contract(low_pairs[0][side], w_query, 1, 1)
                + contract(low_pairs[1][side], w_key, 1, 1)
                + contract(low_pairs[2][side], w_value, 1, 1)
            ).astype(jnp.bfloat16)
            for side in range(2)
        ],
        1,
    )
    grad_token_part, grad_attn_gain = rms_backward(
        grad_attn_own, own_slice(attn_normal), own_slice(attn_inverse), attn_gain
    )
    grad_tokens = natural_rows(
        *plane_gather((grad_hidden + grad_token_part).astype(jnp.bfloat16), 0), 0, own_rows
    )
    def plane_sum(parts, after=()):
        parts = [part.astype(jnp.bfloat16) for part in parts]
        if after:
            parts = [tie(part, *after) for part in parts]
        return lax.psum(parts, "expert")

    (sum_out,) = plane_sum([grad_w_out])
    (sum_value,) = plane_sum([grad_w_value], (sum_out,))
    sum_query, sum_key = plane_sum([grad_w_query, grad_w_key], (sum_value,))
    head_sums = [part.astype(jnp.float32) for part in (sum_query, sum_key, sum_value, sum_out)]
    scale_sums = spread_sum(
        jnp.stack([grad_query_scale.reshape(-1), grad_key_scale.reshape(-1)]), "expert"
    )
    early_sums = spread_sum(
        spread_sum(jnp.concatenate([grad_router_part, grad_ffn_gain], axis=0), "tensor"), "expert"
    )
    late_sums = spread_sum(
        spread_sum(grad_attn_gain.reshape(8, model_width // 8), "tensor"), "expert"
    ).reshape(model_width)
    return (
        output,
        grad_tokens,
        late_sums,
        head_sums[0],
        head_sums[1],
        head_sums[2],
        scale_sums[0],
        scale_sums[1],
        head_sums[3],
        early_sums[expert_count],
        early_sums[:expert_count].T,
        grad_gate_w[None],
        grad_up_w[None],
        grad_down[None],
    )


def solution(mesh):
    placed = (
        P("expert", None),
        P("expert"),
        P("expert", None),
        P("expert", None),
        P(),
        P(None, "tensor"),
        P(None, "tensor"),
        P(None, "tensor"),
        P("tensor"),
        P("tensor"),
        P("tensor", None),
        P(),
        P(),
        P(("expert", "tensor"), None, None),
        P(("expert", "tensor"), None, None),
        P(("expert", "tensor"), None, None),
        P("expert", None),
    )
    return jax.shard_map(
        on_device,
        mesh=mesh,
        in_specs=placed,
        out_specs=(
            P("expert", None),
            P("expert", None),
            P(),
            P(None, "tensor"),
            P(None, "tensor"),
            P(None, "tensor"),
            P("tensor"),
            P("tensor"),
            P("tensor", None),
            P(),
            P(),
            P(("expert", "tensor"), None, None),
            P(("expert", "tensor"), None, None),
            P(("expert", "tensor"), None, None),
        ),
        check_vma=False,
    )
```

```python
import jax
import jax.numpy as jnp
from jax import lax
from jax.experimental import pallas as pl
from jax.experimental.pallas import tpu as pltpu
from jax.sharding import PartitionSpec as P

HEAD_DIM = 128
TOP = 8


EPS = 1e-05
THETA = 10000.0


def rms_forward(values):
    inverse = lax.rsqrt(jnp.mean(values * values, axis=-1, keepdims=True) + EPS)
    return (values * inverse, inverse)


def rms_backward(grad_normed, normal_rows, inverse, gain_row):
    gain_grad = jnp.sum(grad_normed * normal_rows, axis=0)
    scaled = grad_normed * gain_row
    grad_rows = inverse * (
        scaled - normal_rows * jnp.mean(scaled * normal_rows, axis=-1, keepdims=True)
    )
    return (grad_rows, gain_grad)


def rotary(values, cosine_table, sine_table):
    half_dim = values.shape[-1] // 2
    first_half = values[..., :half_dim]
    second_half = values[..., half_dim:]
    return jnp.concatenate(
        [
            first_half * cosine_table - second_half * sine_table,
            second_half * cosine_table + first_half * sine_table,
        ],
        axis=-1,
    )


def causal_mask(start_row, end_row):
    return (jnp.arange(start_row, end_row)[:, None] >= jnp.arange(end_row)[None, :])[None]


def attention_forward(query_rows, key_rows, value_rows):
    length = query_rows.shape[0]
    block_rows = min(512, length)
    outputs = []
    totals = []
    for block_start in range(0, length, block_rows):
        block_end = block_start + block_rows
        scores = jnp.einsum(
            "qhd,khd->hqk",
            query_rows[block_start:block_end],
            key_rows[:block_end],
            preferred_element_type=jnp.float32,
        )
        scores = jnp.where(causal_mask(block_start, block_end), scores, -1e30)
        row_peak = jnp.max(scores, axis=-1, keepdims=True)
        exponent = jnp.exp(scores - row_peak)
        row_total = jnp.sum(exponent, axis=-1, keepdims=True)
        weights = (exponent / row_total).astype(jnp.bfloat16)
        outputs.append(
            jnp.einsum(
                "hqk,khd->qhd", weights, value_rows[:block_end], preferred_element_type=jnp.float32
            )
        )
        totals.append(row_peak + jnp.log(row_total))
    return (jnp.concatenate(outputs, axis=0), totals)


def attention_backward(query_rows, key_rows, value_rows, grad_mixed, totals):
    length = query_rows.shape[0]
    block_rows = min(512, length)
    grad_keys = jnp.zeros(key_rows.shape, jnp.float32)
    grad_values = jnp.zeros(value_rows.shape, jnp.float32)
    grad_queries = []
    for block_number, block_start in enumerate(range(0, length, block_rows)):
        block_end = block_start + block_rows
        query_block = query_rows[block_start:block_end]
        grad_block = grad_mixed[block_start:block_end]
        scores = jnp.einsum(
            "qhd,khd->hqk", query_block, key_rows[:block_end], preferred_element_type=jnp.float32
        )
        scores = jnp.where(causal_mask(block_start, block_end), scores, -1e30)
        probs_again = jnp.exp(scores - totals[block_number])
        weights = probs_again.astype(jnp.bfloat16)
        grad_probs = jnp.einsum(
            "qhd,khd->hqk", grad_block, value_rows[:block_end], preferred_element_type=jnp.float32
        )
        grad_scores = (
            probs_again * (grad_probs - jnp.sum(probs_again * grad_probs, axis=-1, keepdims=True))
        ).astype(jnp.bfloat16)
        grad_queries.append(
            jnp.einsum(
                "hqk,khd->qhd",
                grad_scores,
                key_rows[:block_end],
                preferred_element_type=jnp.float32,
            )
        )
        grad_keys = grad_keys.at[:block_end].add(
            jnp.einsum("hqk,qhd->khd", grad_scores, query_block, preferred_element_type=jnp.float32)
        )
        grad_values = grad_values.at[:block_end].add(
            jnp.einsum("hqk,qhd->khd", weights, grad_block, preferred_element_type=jnp.float32)
        )
    return (jnp.concatenate(grad_queries, axis=0), grad_keys, grad_values)


def swap(values, axis, bit):
    return lax.ppermute(values, axis, [(i, i ^ bit) for i in range(lax.axis_size(axis))])


def axis_bits(axis):
    size = lax.axis_size(axis)
    return [size >> (k + 1) for k in range(size.bit_length() - 1)]


def spread_sum(values, axis):
    for bit in axis_bits(axis)[::-1]:
        values = values + swap(values, axis, bit)
    return values


def plane_order(turn):
    bits = axis_bits("tensor")[:-1]
    if turn % 2:
        bits = bits[::-1]
    order = [0]
    for bit in bits:
        order = order + [bit ^ i for i in order]
    return bits, order


def plane_gather(piece, turn):
    bits, _ = plane_order(turn)
    pieces = [piece]
    for bit in bits:
        pieces = pieces + [swap(p, "tensor", bit) for p in pieces]
    near = jnp.concatenate(pieces, axis=0)
    return near, swap(near, "tensor", 1)


def plane_scatter(near, far, turn):
    bits, _ = plane_order(turn)
    total = near.astype(jnp.float32) + swap(far, "tensor", 1).astype(jnp.float32)
    for bit in bits[::-1]:
        half = total.shape[0] // 2
        sent = total[half:].astype(jnp.bfloat16)
        total = total[:half].astype(jnp.bfloat16).astype(jnp.float32) + swap(
            sent, "tensor", bit
        ).astype(jnp.float32)
    return total


def plane_rows(values, turn, own_rows, sorted_order=False):
    _, order = plane_order(turn)
    if sorted_order:
        order = sorted(order)
    index = lax.axis_index("tensor")

    def block(i):
        return lax.dynamic_slice_in_dim(values, (index ^ i) * own_rows, own_rows, 0)

    near = jnp.concatenate([block(i) for i in order], axis=0)
    far = jnp.concatenate([block(i ^ 1) for i in order], axis=0)
    return near, far


def natural_rows(near, far, turn, own_rows):
    _, order = plane_order(turn)
    index = lax.axis_index("tensor")
    both = jnp.concatenate([near, far], axis=0)
    place = {}
    for at, i in enumerate(order):
        place[i] = at
        place[i ^ 1] = at + len(order)
    table = jnp.array([place[i] for i in range(2 * len(order))], jnp.int32)
    return jnp.concatenate(
        [
            lax.dynamic_slice_in_dim(both, table[index ^ i] * own_rows, own_rows, 0)
            for i in range(2 * len(order))
        ],
        axis=0,
    )


def contract(left, right, left_dim, right_dim):
    return lax.dot_general(
        left, right, (((left_dim,), (right_dim,)), ((), ())), preferred_element_type=jnp.float32
    )


def tie(values, *after):
    return lax.optimization_barrier((values, *after))[0]


def stages(turn, bits):
    if turn % 2:
        bits = bits[::-1]
    found = [[] for _ in bits]
    order = [(0, ())]
    for bit in bits:
        order = order + [(bit ^ i, used + (bit,)) for i, used in order]
    for i, used in order[1:]:
        found[len(used) - 1].append((i, i ^ used[-1], used[-1]))
    return found


def gather_stage(pieces, turn, stage, bits, after=()):
    pieces = dict(pieces)
    for i, source, bit in stages(turn, bits)[stage]:
        sent = pieces[source]
        if after:
            sent = tie(sent, *after)
        pieces[i] = swap(sent, "tensor", bit)
    return pieces


def gather_all(piece, turn, bits):
    pieces = {0: piece}
    for stage in range(len(bits)):
        pieces = gather_stage(pieces, turn, stage, bits)
    return pieces


def scatter_stage(sums, turn, stage, bits, after=()):
    sums = dict(sums)
    for i, target, bit in stages(turn, bits)[len(bits) - 1 - stage]:
        sent = sums.pop(i).astype(jnp.bfloat16)
        if after:
            sent = tie(sent, *after)
        sums[target] = sums[target].astype(jnp.float32) + swap(sent, "tensor", bit).astype(
            jnp.float32
        )
    return sums


MEGABYTE = 1024 * 1024


def kernel_params():
    return pltpu.CompilerParams(vmem_limit_bytes=58 * MEGABYTE)


def cost(flops, moved):
    return pl.CostEstimate(flops=flops, bytes_accessed=moved, transcendentals=0)


def column_of(row):
    n = row.shape[1]
    down = lax.broadcasted_iota(jnp.int32, (n, n), 0)
    across = lax.broadcasted_iota(jnp.int32, (n, n), 1)
    return jnp.sum(jnp.where(down == across, row, 0.0), axis=1, keepdims=True)


def fixed(shape, single=True):
    if single:
        return pl.BlockSpec(
            shape, lambda *_: (0,) * len(shape), pipeline_mode=pl.Buffered(1)
        )
    return pl.BlockSpec(shape, lambda *_: (0,) * len(shape))


def expert_body(indices, dy_count, place, scalars, *refs):
    count = len(indices)
    x_parts, refs = refs[:count], refs[count:]
    dy_parts, refs = refs[:dy_count], refs[dy_count:]
    kept, chosen, router = refs[:3]
    gate_own, gate_other, up_own, up_other, down_own, down_other = refs[3:9]
    scratch = refs[-13:]
    outs = refs[-13 - count - 9 : -13]
    pieces = outs[:count]
    gate_out, dl_all, x_all, dy_all, act_all, own_dp, other_dp, gated_own, gated_other = outs[count:]
    rows, grads, wide, tall, raw, inner, act, slopes, gated, done, probs_ref, dots, sems = scratch
    rows_here, width = rows.shape
    units = gate_own.shape[1]
    own_rows = rows_here // count
    used = []

    def start(source, target):
        copy = pltpu.make_async_copy(source, target, sems.at[len(used)])
        used.append(copy)
        copy.start()
        return copy

    def spread(parts, target):
        size = rows_here // len(parts)
        return [start(part, target.at[pl.ds(at * size, size)]) for at, part in enumerate(parts)]

    x_copies = spread(x_parts, rows)
    order = [gate_own, up_own, gate_other, up_other]
    wide_copies = [
        start(weight, wide.at[:, pl.ds(at * units, units)]) for at, weight in enumerate(order[:2])
    ]
    dy_copies = spread(dy_parts, grads)
    tall_copies = [start(down_own, tall.at[pl.ds(0, units)])]
    wide_copies += [
        start(weight, wide.at[:, pl.ds((at + 2) * units, units)])
        for at, weight in enumerate(order[2:])
    ]
    tall_copies.append(start(down_other, tall.at[pl.ds(units, units)]))

    here_rows = pl.ds(place * rows_here, rows_here)
    for copy in x_copies:
        copy.wait()
    outgoing = [start(rows, x_all.at[here_rows])]
    logits = contract(rows[...], router[...], 1, 0)
    exponent = jnp.exp(logits - jnp.max(logits, axis=-1, keepdims=True))
    probs = exponent / jnp.sum(exponent, axis=-1, keepdims=True)
    kept_column = jnp.concatenate(
        [column_of(kept[pl.ds(scalars[0] ^ i, 1), :]) for i in indices], axis=0
    )
    probs_ref[...] = probs
    gate_out[...] = jnp.sum(probs * chosen[...], axis=-1, keepdims=True) * kept_column
    dots[...] = jnp.zeros_like(dots)

    block = min(64, rows_here)
    for half in range(2):
        columns = pl.ds(half * units, units)
        for part in range(2):
            at = 2 * half + part
            wide_copies[at].wait()
            raw[:, pl.ds(part * units, units)] = contract(
                rows[...], wide[:, pl.ds(at * units, units)], 1, 0
            )
        if half == 0:
            for copy in dy_copies:
                copy.wait()
            outgoing.append(start(grads, dy_all.at[here_rows]))
        tall_copies[half].wait()
        inner[...] = contract(grads[...], tall[columns, :], 1, 1)

        @pl.loop(0, rows_here // block)
        def _(at):
            here = pl.ds(at * block, block)
            pre_gate = raw[here, pl.ds(0, units)]
            pre_up = raw[here, pl.ds(units, units)]
            inward = inner[here, :]
            gate = gate_out[here, :]
            sigmoid_gate = 1.0 / (1.0 + jnp.exp(-pre_gate))
            silu_gate = pre_gate * sigmoid_gate
            active = (silu_gate * pre_up).astype(jnp.bfloat16)
            act[here, columns] = active
            active = active.astype(jnp.float32)
            gated[here, columns] = (gate * active).astype(jnp.bfloat16)
            dots[here, :] += jnp.sum(inward * active, axis=-1, keepdims=True)
            grad_active = gate * inward
            slopes[here, pl.ds(2 * half * units, units)] = (
                grad_active * pre_up * sigmoid_gate * (1.0 + pre_gate * (1.0 - sigmoid_gate))
            ).astype(jnp.bfloat16)
            slopes[here, pl.ds((2 * half + 1) * units, units)] = (grad_active * silu_gate).astype(
                jnp.bfloat16
            )

    outgoing += [
        start(act, act_all.at[here_rows]),
        start(slopes.at[:, pl.ds(0, 2 * units)], own_dp.at[here_rows]),
        start(slopes.at[:, pl.ds(2 * units, 2 * units)], other_dp.at[here_rows]),
        start(gated.at[:, pl.ds(0, units)], gated_own.at[here_rows]),
        start(gated.at[:, pl.ds(units, units)], gated_other.at[here_rows]),
    ]
    grad_logits = (dots[...] * gate_out[...] * (chosen[...] - probs_ref[...])).astype(jnp.bfloat16)
    dl_all[...] = grad_logits
    step = min(512, width)
    for at in range(width // step):
        columns = pl.ds(at * step, step)
        done[:, columns] = (
            contract(slopes[...], wide[columns, :], 1, 1)
            + contract(grad_logits, router[columns, :], 1, 1)
        ).astype(jnp.bfloat16)
    for at, piece in enumerate(pieces):
        outgoing.append(start(done.at[pl.ds(at * own_rows, own_rows)], piece))
    for copy in outgoing:
        copy.wait()


def expert_chunk(place, places, x_pieces, dy_parts, here, kept, chosen, router, gates, ups, downs, chain):
    indices = sorted(x_pieces)
    count = len(indices)
    own_rows, width = x_pieces[0].shape
    rows = own_rows * count
    units = gates[0].shape[1]
    experts = router.shape[1]
    extra = () if chain is None else tuple(chain)
    hbm = pl.BlockSpec(memory_space=pl.ANY)
    first = count + len(dy_parts) + 10
    kept_shapes = [
        (rows * places, experts),
        (rows * places, width),
        (rows * places, width),
        (rows * places, 2 * units),
        (rows * places, 2 * units),
        (rows * places, 2 * units),
        (rows * places, units),
        (rows * places, units),
    ]
    results = pl.pallas_call(
        lambda *refs: expert_body(indices, len(dy_parts), place, *refs),
        grid_spec=pltpu.PrefetchScalarGridSpec(
            num_scalar_prefetch=1,
            grid=(1,),
            in_specs=[hbm] * (count + len(dy_parts))
            + [fixed(kept.shape), fixed((1, experts)), fixed((width, experts))]
            + [hbm] * (6 + len(extra)),
            out_specs=[hbm] * count
            + [
                fixed((rows, 1), False),
                pl.BlockSpec((rows, experts), lambda j, *_: (place, 0)),
            ]
            + [hbm] * 7,
            scratch_shapes=[
                pltpu.VMEM((rows, width), jnp.bfloat16),
                pltpu.VMEM((rows, width), jnp.bfloat16),
                pltpu.VMEM((width, 4 * units), jnp.bfloat16),
                pltpu.VMEM((2 * units, width), jnp.bfloat16),
                pltpu.VMEM((rows, 2 * units), jnp.float32),
                pltpu.VMEM((rows, units), jnp.float32),
                pltpu.VMEM((rows, 2 * units), jnp.bfloat16),
                pltpu.VMEM((rows, 4 * units), jnp.bfloat16),
                pltpu.VMEM((rows, 2 * units), jnp.bfloat16),
                pltpu.VMEM((rows, width), jnp.bfloat16),
                pltpu.VMEM((rows, experts), jnp.float32),
                pltpu.VMEM((rows, 1), jnp.float32),
                pltpu.SemaphoreType.DMA((2 * count + len(dy_parts) + 13,)),
            ],
        ),
        out_shape=[jax.ShapeDtypeStruct((own_rows, width), jnp.bfloat16)] * count
        + [jax.ShapeDtypeStruct((rows, 1), jnp.float32)]
        + [jax.ShapeDtypeStruct(shape, jnp.bfloat16) for shape in kept_shapes],
        input_output_aliases={first + i: count + 1 + i for i in range(len(extra))},
        compiler_params=kernel_params(),
        cost_estimate=cost(20 * rows * width * units, 10 * rows * width + 12 * width * units),
        name="expert_chunk",
    )(
        here,
        *[x_pieces[i] for i in indices],
        *dy_parts,
        kept,
        chosen,
        router,
        *gates,
        *ups,
        *downs,
        *extra,
    )
    return dict(zip(indices, results[:count])), results[count], results[count + 1 :]


def input_grad_body(indices, own_rows, scalars, query_low, key_low, value_low, *refs):
    weights = refs[:3]
    pieces = refs[3:]
    for at, i in enumerate(indices):
        here = pl.ds(pl.multiple_of((scalars[0] ^ i) * own_rows, own_rows), own_rows)
        pieces[at][...] = (
            contract(query_low[here, :], weights[0][...], 1, 1)
            + contract(key_low[here, :], weights[1][...], 1, 1)
            + contract(value_low[here, :], weights[2][...], 1, 1)
        ).astype(jnp.bfloat16)


def input_grad(here, indices, own_rows, lows, weights):
    width = weights[0].shape[0]
    results = pl.pallas_call(
        lambda *refs: input_grad_body(indices, own_rows, *refs),
        grid_spec=pltpu.PrefetchScalarGridSpec(
            num_scalar_prefetch=1,
            grid=(1,),
            in_specs=[fixed(low.shape) for low in lows] + [fixed(w.shape) for w in weights],
            out_specs=[fixed((own_rows, width), False)] * len(indices),
        ),
        out_shape=[jax.ShapeDtypeStruct((own_rows, width), jnp.bfloat16)] * len(indices),
        compiler_params=kernel_params(),
        cost_estimate=cost(6 * lows[0].size * width, 8 * lows[0].size * 8),
        name="input_grad",
    )(here, *lows, *weights)
    return dict(zip(indices, results))


def place_body(indices, own_rows, scalars, *refs):
    pieces, out, sems = refs[: len(indices)], refs[-2], refs[-1]
    copies = []
    for at, i in enumerate(indices):
        here = pl.ds(pl.multiple_of((scalars[0] ^ i) * own_rows, own_rows), own_rows)
        copies.append(pltpu.make_async_copy(pieces[at], out.at[here], sems.at[at]))
        copies[-1].start()
    for copy in copies:
        copy.wait()


def place_rows(here, pieces):
    indices = sorted(pieces)
    own_rows, width = pieces[0].shape
    hbm = pl.BlockSpec(memory_space=pl.ANY)
    return pl.pallas_call(
        lambda *refs: place_body(indices, own_rows, *refs),
        grid_spec=pltpu.PrefetchScalarGridSpec(
            num_scalar_prefetch=1,
            grid=(1,),
            in_specs=[hbm] * len(indices),
            out_specs=hbm,
            scratch_shapes=[pltpu.SemaphoreType.DMA((len(indices),))],
        ),
        out_shape=jax.ShapeDtypeStruct((own_rows * len(indices), width), pieces[0].dtype),
        compiler_params=kernel_params(),
        cost_estimate=cost(0, 4 * own_rows * len(indices) * width),
        name="place_rows",
    )(here, *[pieces[i] for i in indices])


def line_sum(part, after=()):
    index = lax.axis_index("expert")
    bits = axis_bits("expert")[::-1]
    for bit in bits:
        half = part.shape[0] // 2
        high = (index // bit) % 2
        kept = lax.dynamic_slice_in_dim(part, high * half, half, 0)
        sent = lax.dynamic_slice_in_dim(part, (1 - high) * half, half, 0)
        if after:
            sent = tie(sent, *after)
            after = ()
        part = (
            kept.astype(jnp.float32) + swap(sent, "expert", bit).astype(jnp.float32)
        ).astype(jnp.bfloat16)
    for bit in bits[::-1]:
        high = (index // bit) % 2 == 1
        other = swap(part, "expert", bit)
        part = jnp.concatenate([jnp.where(high, other, part), jnp.where(high, part, other)], axis=0)
    return part.astype(jnp.float32)


def send_body(act, gate, down_own, down_other, *pieces):
    units = down_own.shape[0]
    value = contract(act[:, :units], down_own[...], 1, 0) + contract(
        act[:, units:], down_other[...], 1, 0
    )
    sent = (gate[...] * value).astype(jnp.bfloat16)
    own_rows = pieces[0].shape[0]
    for at, piece in enumerate(pieces):
        piece[...] = sent[at * own_rows : (at + 1) * own_rows]


def expert_send(place, indices, act_all, gate, downs):
    rows = gate.shape[0]
    count = len(indices)
    units, width = downs[0].shape
    block = min(512, width)
    results = pl.pallas_call(
        send_body,
        grid=(width // block,),
        in_specs=[
            pl.BlockSpec((rows, 2 * units), lambda j: (place, 0)),
            fixed((rows, 1)),
            pl.BlockSpec((units, block), lambda j: (0, j)),
            pl.BlockSpec((units, block), lambda j: (0, j)),
        ],
        out_specs=[pl.BlockSpec((rows // count, block), lambda j: (0, j))] * count,
        out_shape=[jax.ShapeDtypeStruct((rows // count, width), jnp.bfloat16)] * count,
        compiler_params=kernel_params(),
        cost_estimate=cost(4 * rows * width * units, 4 * rows * width + 4 * width * units),
        name="expert_send",
    )(act_all, gate, *downs)
    return dict(zip(indices, results))


def project_body(indices, halves, scalars, mixed, tokens, gain, *refs):
    weights = refs[: len(indices) * halves]
    hidden_out, low_out = refs[-2:]
    total = tokens[...].astype(jnp.float32)
    depth = weights[0].shape[0]
    attn = None
    for at, i in enumerate(indices):
        piece = mixed[scalars[0] ^ i]
        for half in range(halves):
            part = contract(
                piece[:, half * depth : (half + 1) * depth], weights[at * halves + half][...], 1, 0
            )
            attn = part if attn is None else attn + part
    hidden = total + attn
    normal, _ = rms_forward(hidden)
    hidden_out[...] = hidden
    low_out[...] = (normal * gain[...]).astype(jnp.bfloat16)


def project_out(here, indices, mixed, tokens, gain, weights, halves):
    rows, width = tokens.shape
    return pl.pallas_call(
        lambda *refs: project_body(indices, halves, *refs),
        grid_spec=pltpu.PrefetchScalarGridSpec(
            num_scalar_prefetch=1,
            grid=(1,),
            in_specs=[fixed(mixed.shape), fixed(tokens.shape), fixed((1, width))]
            + [fixed(weights[0].shape)] * len(weights),
            out_specs=[fixed((rows, width), False), fixed((rows, width), False)],
        ),
        out_shape=[
            jax.ShapeDtypeStruct((rows, width), jnp.float32),
            jax.ShapeDtypeStruct((rows, width), jnp.bfloat16),
        ],
        compiler_params=kernel_params(),
        cost_estimate=cost(2 * rows * width * width, 2 * width * width),
        name="project_out",
    )(here, mixed, tokens, gain, *weights)


def turn_body(indices, halves, count, scalars, hidden, grad_out, gain, *refs):
    grads = refs[:count]
    weights = refs[count : count + len(indices) * halves]
    grad_hidden_out, low_out, mixed_out, gain_out = refs[-4:]
    grad_ffn = grads[0][...].astype(jnp.float32)
    for part in grads[1:]:
        grad_ffn = grad_ffn + part[...].astype(jnp.float32)
    normal, inverse = rms_forward(hidden[...])
    gain_out[...] = jnp.sum(grad_ffn * normal, axis=0, keepdims=True)
    scaled = grad_ffn * gain[...]
    grad_hidden = grad_out[...].astype(jnp.float32) + inverse * (
        scaled - normal * jnp.mean(scaled * normal, axis=-1, keepdims=True)
    )
    low = grad_hidden.astype(jnp.bfloat16)
    grad_hidden_out[...] = grad_hidden
    low_out[...] = low
    depth = weights[0].shape[0]
    for at, i in enumerate(indices):
        for half in range(halves):
            mixed_out[scalars[0] ^ i, :, half * depth : (half + 1) * depth] = contract(
                low, weights[at * halves + half][...], 1, 1
            ).astype(jnp.bfloat16)


def turn_back(here, indices, hidden, grad_out, gain, grads, weights, halves):
    rows, width = hidden.shape
    depth = weights[0].shape[0] * halves
    return pl.pallas_call(
        lambda *refs: turn_body(indices, halves, len(grads), *refs),
        grid_spec=pltpu.PrefetchScalarGridSpec(
            num_scalar_prefetch=1,
            grid=(1,),
            in_specs=[fixed((rows, width)), fixed((rows, width)), fixed((1, width))]
            + [fixed((rows, width))] * len(grads)
            + [fixed(weights[0].shape)] * len(weights),
            out_specs=[
                fixed((rows, width), False),
                fixed((rows, width), False),
                fixed((len(indices), rows, depth), False),
                fixed((1, width), False),
            ],
        ),
        out_shape=[
            jax.ShapeDtypeStruct((rows, width), jnp.float32),
            jax.ShapeDtypeStruct((rows, width), jnp.bfloat16),
            jax.ShapeDtypeStruct((len(indices), rows, depth), jnp.bfloat16),
            jax.ShapeDtypeStruct((1, width), jnp.float32),
        ],
        compiler_params=kernel_params(),
        cost_estimate=cost(2 * rows * width * width, 2 * width * width),
        name="turn_back",
    )(here, hidden, grad_out, gain, *grads, *weights)


def on_device(
    tokens,
    positions,
    routes,
    slot_ids,
    attn_gain,
    w_query,
    w_key,
    w_value,
    query_gain,
    key_gain,
    w_out,
    ffn_gain,
    router,
    w_gate,
    w_up,
    w_down,
    grad_out,
):
    tensor_size = lax.axis_size("tensor")
    expert_size = lax.axis_size("expert")
    local_count = tensor_size // 2
    tensor_index = lax.axis_index("tensor")
    expert_index = lax.axis_index("expert")
    own_local = tensor_index // 2
    own_expert = expert_index * local_count + own_local
    length, model_width = tokens.shape
    heads_here = w_query.shape[1] // HEAD_DIM
    full_cols = w_query.shape[1] * tensor_size
    expert_count = router.shape[1]
    capacity = 3 * length * TOP // (2 * expert_count)
    own_rows = length // tensor_size
    chunks = [0] + list(range(2, expert_size)) + [1]
    bits = axis_bits("tensor")
    near_bits = bits[:-1]
    last = len(near_bits)

    def own_slice(rows):
        return lax.dynamic_slice_in_dim(rows, tensor_index * own_rows, own_rows, 0)

    def with_sibling(weights):
        return [weights, swap(weights, "tensor", 1)]

    grad_own = own_slice(grad_out)
    grad_near, _ = plane_rows(grad_out, 0, own_rows, sorted_order=True)
    grad_pieces = {}
    for chunk in range(1, expert_size):
        grad_pieces[chunk] = swap(grad_near if chunk == 1 else grad_own, "expert", chunk)
    w_halves = [w_out[: w_out.shape[0] // 2], w_out[w_out.shape[0] // 2 :]]
    out_pieces = [gather_all(half, turn, bits) for turn, half in enumerate(w_halves)]
    all_indices = sorted(out_pieces[0])
    out_weights = [out_pieces[half][i] for i in all_indices for half in range(2)]
    gates, ups, downs = with_sibling(w_gate[0]), with_sibling(w_up[0]), with_sibling(w_down[0])
    expert_iota = jnp.arange(expert_count, dtype=jnp.int32)
    kept_table = jnp.sum(
        (
            (routes.T[:, None, :] == expert_iota[None, :, None]) & (slot_ids.T < capacity)[:, None, :]
        ).astype(jnp.float32),
        axis=0,
    )
    kept_chunks = []
    for chunk in range(expert_size):
        target = (expert_index ^ chunk) * local_count + own_local
        kept_row = lax.dynamic_slice_in_dim(kept_table, target, 1, 0).reshape(tensor_size, own_rows)
        kept_chunks.append(swap(kept_row, "expert", chunk) if chunk else kept_row)

    def here(chunk):
        return jnp.stack([tensor_index, (expert_index ^ chunk) * tensor_size]).astype(jnp.int32)

    grad_parts_of = {0: [grad_near], 1: [grad_pieces[1]]}
    for chunk in range(2, expert_size):
        pieces = {0: tie(grad_pieces[chunk], out_pieces[1][2 * (tensor_size // 2 - 1)])}
        for stage in range(last):
            pieces = gather_stage(pieces, chunk, stage, near_bits)
        grad_parts_of[chunk] = [pieces[i] for i in sorted(pieces)]

    score_scale = HEAD_DIM ** (-0.5)
    half_dim = HEAD_DIM // 2
    frequency = THETA ** (-2.0 * jnp.arange(half_dim, dtype=jnp.float32) / HEAD_DIM)
    angles = positions.astype(jnp.float32)[:, None] * frequency[None, :]
    cosine_table = jnp.cos(angles)[:, None, :]
    sine_table = jnp.sin(angles)[:, None, :]
    token_float = tokens.astype(jnp.float32)
    attn_normal, attn_inverse = rms_forward(token_float)
    attn_in = (attn_normal * attn_gain).astype(jnp.bfloat16)
    head_shape = (length, heads_here, HEAD_DIM)
    query_raw = jnp.dot(attn_in, w_query, preferred_element_type=jnp.float32).reshape(head_shape)
    key_raw = jnp.dot(attn_in, w_key, preferred_element_type=jnp.float32).reshape(head_shape)
    value_rows = (
        jnp.dot(attn_in, w_value, preferred_element_type=jnp.float32)
        .astype(jnp.bfloat16)
        .reshape(head_shape)
    )
    query_scale = query_gain.reshape(heads_here, HEAD_DIM)
    key_scale = key_gain.reshape(heads_here, HEAD_DIM)
    square_sums = spread_sum(
        jnp.stack(
            [jnp.sum(query_raw * query_raw, axis=(1, 2)), jnp.sum(key_raw * key_raw, axis=(1, 2))]
        ),
        "tensor",
    )
    query_inverse = lax.rsqrt(square_sums[0] / full_cols + EPS)[:, None, None]
    key_inverse = lax.rsqrt(square_sums[1] / full_cols + EPS)[:, None, None]
    query_normal = query_raw * query_inverse
    key_normal = key_raw * key_inverse
    query_rows = (
        rotary(query_normal * query_scale, cosine_table, sine_table) * score_scale
    ).astype(jnp.bfloat16)
    key_rows = rotary(key_normal * key_scale, cosine_table, sine_table).astype(jnp.bfloat16)
    mixed_heads, totals = attention_forward(query_rows, key_rows, value_rows)
    mixed_low = mixed_heads.reshape(length, heads_here * HEAD_DIM).astype(jnp.bfloat16)
    mixed_own = lax.all_to_all(
        mixed_low.reshape(tensor_size, own_rows, -1), "tensor", split_axis=0, concat_axis=0, tiled=True
    )
    hidden, ffn_in = project_out(
        here(0), all_indices, mixed_own, own_slice(tokens), ffn_gain[None, :], out_weights, 2
    )
    chosen = (expert_iota == own_expert).astype(jnp.float32)[None, :]
    gathered = [
        {0: ffn_in if chunk == 0 else swap(ffn_in, "expert", chunk)} for chunk in chunks
    ]
    chain = None
    sums = []
    gate_columns = []
    for at, chunk in enumerate(chunks):
        for stage in range(last):
            before = at - last - 1 + stage
            after = (gate_columns[before],) if before >= 0 else ()
            gathered[at] = gather_stage(gathered[at], at, stage, near_bits, after)
        scalars = here(chunk)
        for stage in range(last):
            if at >= stage + 2:
                scalars = tie(scalars, sums[at - stage - 2][0])
        pieces, gate_column, chain = expert_chunk(
            at,
            expert_size,
            gathered[at],
            grad_parts_of[chunk],
            scalars,
            kept_chunks[chunk],
            chosen,
            router,
            gates,
            ups,
            downs,
            chain,
        )
        gate_columns.append(gate_column)
        for stage in range(1, last):
            if at >= stage:
                sums[at - stage] = scatter_stage(
                    sums[at - stage], at - stage, stage, near_bits, (gate_column,)
                )
        sums.append(scatter_stage(pieces, at, 0, near_bits))
    for stage in range(1, last):
        for at in range(expert_size - stage, expert_size):
            sums[at] = scatter_stage(sums[at], at, stage, near_bits)
    grad_parts = [
        sums[at][0] if chunk == 0 else swap(sums[at][0].astype(jnp.bfloat16), "expert", chunk)
        for at, chunk in enumerate(chunks)
    ]
    indices = sorted(gathered[0])
    dl_all, x_all, dy_all, act_all, own_dp, other_dp, gated_own, gated_other = chain
    sent_pieces = [
        expert_send(at, indices, act_all, gate_columns[at], downs) for at in range(expert_size)
    ]
    grad_hidden, hidden_low, grad_mixed_own, grad_ffn_gain = turn_back(
        here(0), all_indices, hidden, grad_own, ffn_gain[None, :], grad_parts, out_weights, 2
    )
    grad_mixed = lax.all_to_all(
        grad_mixed_own, "tensor", split_axis=0, concat_axis=0, tiled=True
    ).reshape(head_shape)

    moe_sum = hidden
    for at, chunk in enumerate(chunks):
        pieces = sent_pieces[at]
        for stage in range(last):
            pieces = scatter_stage(pieces, at, stage, near_bits, (hidden_low,))
        piece = pieces[0]
        if chunk:
            piece = swap(piece.astype(jnp.bfloat16), "expert", chunk).astype(jnp.float32)
        moe_sum = moe_sum + piece
    output = lax.all_gather(moe_sum.astype(jnp.bfloat16), "tensor", axis=0, tiled=True)

    units = own_dp.shape[1] // 2
    other_wide = swap(contract(x_all, other_dp, 0, 0).astype(jnp.bfloat16), "tensor", 1)
    other_down = swap(contract(gated_other, dy_all, 0, 0).astype(jnp.bfloat16), "tensor", 1)
    grad_gate_w = contract(x_all, own_dp[:, :units], 0, 0) + other_wide[:, :units].astype(jnp.float32)
    grad_up_w = contract(x_all, own_dp[:, units:], 0, 0) + other_wide[:, units:].astype(jnp.float32)
    grad_down = contract(gated_own, dy_all, 0, 0) + other_down.astype(jnp.float32)
    grad_router_part = contract(dl_all, x_all, 0, 0)

    hidden_low_all = lax.all_gather(hidden_low, "tensor", axis=0, tiled=True)
    grad_w_out = contract(mixed_low, hidden_low_all, 0, 0)
    grad_query, grad_key, grad_value_attn = attention_backward(
        query_rows, key_rows, value_rows, grad_mixed, totals
    )
    grad_query_normed = rotary(grad_query * score_scale, cosine_table, -sine_table)
    grad_key_normed = rotary(grad_key, cosine_table, -sine_table)
    grad_query_scale = jnp.sum(grad_query_normed * query_normal, axis=0)
    grad_key_scale = jnp.sum(grad_key_normed * key_normal, axis=0)
    query_scaled = grad_query_normed * query_scale
    key_scaled = grad_key_normed * key_scale
    inner_sums = spread_sum(
        jnp.stack(
            [
                jnp.sum(query_scaled * query_normal, axis=(1, 2)),
                jnp.sum(key_scaled * key_normal, axis=(1, 2)),
            ]
        ),
        "tensor",
    )
    grad_query_raw = query_inverse * (
        query_scaled - query_normal * (inner_sums[0] / full_cols)[:, None, None]
    )
    grad_key_raw = key_inverse * (
        key_scaled - key_normal * (inner_sums[1] / full_cols)[:, None, None]
    )
    query_low = grad_query_raw.reshape(length, heads_here * HEAD_DIM).astype(jnp.bfloat16)
    key_low = grad_key_raw.reshape(length, heads_here * HEAD_DIM).astype(jnp.bfloat16)
    value_low = grad_value_attn.reshape(length, heads_here * HEAD_DIM).astype(jnp.bfloat16)
    grad_w_query = jnp.einsum("td,tq->dq", attn_in, query_low, preferred_element_type=jnp.float32)
    grad_w_key = jnp.einsum("td,tq->dq", attn_in, key_low, preferred_element_type=jnp.float32)
    grad_w_value = jnp.einsum("td,tq->dq", attn_in, value_low, preferred_element_type=jnp.float32)
    grad_attn = input_grad(
        here(0), all_indices, own_rows, (query_low, key_low, value_low), (w_query, w_key, w_value)
    )
    for stage in range(len(bits)):
        grad_attn = scatter_stage(grad_attn, 0, stage, bits)
    grad_token_part, grad_attn_gain = rms_backward(
        grad_attn[0], own_slice(attn_normal), own_slice(attn_inverse), attn_gain
    )
    grad_tokens = place_rows(
        here(0), gather_all((grad_hidden + grad_token_part).astype(jnp.bfloat16), 0, bits)
    )
    sum_value = line_sum(grad_w_value.astype(jnp.bfloat16))
    sum_query = line_sum(grad_w_query.astype(jnp.bfloat16))
    sum_key = line_sum(grad_w_key.astype(jnp.bfloat16))
    sum_out = lax.psum(grad_w_out.astype(jnp.bfloat16), "expert").astype(jnp.float32)
    plane_sums = spread_sum(
        jnp.concatenate([grad_router_part, grad_ffn_gain, grad_attn_gain[None, :]], axis=0), "tensor"
    )
    scales = jnp.concatenate([grad_query_scale.reshape(-1), grad_key_scale.reshape(-1)])
    scales = jnp.pad(scales, (0, model_width - scales.shape[0]))
    all_sums = spread_sum(jnp.concatenate([plane_sums, scales[None, :]], axis=0), "expert")
    columns_here = w_query.shape[1]
    return (
        output,
        grad_tokens,
        all_sums[expert_count + 1],
        sum_query,
        sum_key,
        sum_value,
        all_sums[expert_count + 2, :columns_here],
        all_sums[expert_count + 2, columns_here : 2 * columns_here],
        sum_out,
        all_sums[expert_count],
        all_sums[:expert_count].T,
        grad_gate_w[None],
        grad_up_w[None],
        grad_down[None],
    )


def solution(mesh):
    placed = (
        P("expert", None),
        P("expert"),
        P("expert", None),
        P("expert", None),
        P(),
        P(None, "tensor"),
        P(None, "tensor"),
        P(None, "tensor"),
        P("tensor"),
        P("tensor"),
        P("tensor", None),
        P(),
        P(),
        P(("expert", "tensor"), None, None),
        P(("expert", "tensor"), None, None),
        P(("expert", "tensor"), None, None),
        P("expert", None),
    )
    return jax.shard_map(
        on_device,
        mesh=mesh,
        in_specs=placed,
        out_specs=(
            P("expert", None),
            P("expert", None),
            P(),
            P(None, "tensor"),
            P(None, "tensor"),
            P(None, "tensor"),
            P("tensor"),
            P("tensor"),
            P("tensor", None),
            P(),
            P(),
            P(("expert", "tensor"), None, None),
            P(("expert", "tensor"), None, None),
            P(("expert", "tensor"), None, None),
        ),
        check_vma=False,
    )
```

```python
import jax
import jax.numpy as jnp
from jax import lax
from jax.experimental import pallas as pl
from jax.experimental.pallas import tpu as pltpu
from jax.sharding import PartitionSpec as P

HEAD_DIM = 128
TOP = 8


EPS = 1e-05
THETA = 10000.0


def rms_forward(values):
    inverse = lax.rsqrt(jnp.mean(values * values, axis=-1, keepdims=True) + EPS)
    return (values * inverse, inverse)


def rms_backward(grad_normed, normal_rows, inverse, gain_row):
    gain_grad = jnp.sum(grad_normed * normal_rows, axis=0)
    scaled = grad_normed * gain_row
    grad_rows = inverse * (
        scaled - normal_rows * jnp.mean(scaled * normal_rows, axis=-1, keepdims=True)
    )
    return (grad_rows, gain_grad)


def rotary(values, cosine_table, sine_table):
    half_dim = values.shape[-1] // 2
    first_half = values[..., :half_dim]
    second_half = values[..., half_dim:]
    return jnp.concatenate(
        [
            first_half * cosine_table - second_half * sine_table,
            second_half * cosine_table + first_half * sine_table,
        ],
        axis=-1,
    )


def causal_mask(start_row, end_row):
    return (jnp.arange(start_row, end_row)[:, None] >= jnp.arange(end_row)[None, :])[None]


def attention_forward(query_rows, key_rows, value_rows):
    length = query_rows.shape[0]
    block_rows = min(512, length)
    outputs = []
    totals = []
    for block_start in range(0, length, block_rows):
        block_end = block_start + block_rows
        scores = jnp.einsum(
            "qhd,khd->hqk",
            query_rows[block_start:block_end],
            key_rows[:block_end],
            preferred_element_type=jnp.float32,
        )
        scores = jnp.where(causal_mask(block_start, block_end), scores, -1e30)
        row_peak = jnp.max(scores, axis=-1, keepdims=True)
        exponent = jnp.exp(scores - row_peak)
        row_total = jnp.sum(exponent, axis=-1, keepdims=True)
        weights = (exponent / row_total).astype(jnp.bfloat16)
        outputs.append(
            jnp.einsum(
                "hqk,khd->qhd", weights, value_rows[:block_end], preferred_element_type=jnp.float32
            )
        )
        totals.append(row_peak + jnp.log(row_total))
    return (jnp.concatenate(outputs, axis=0), totals)


def attention_backward(query_rows, key_rows, value_rows, grad_mixed, totals):
    length = query_rows.shape[0]
    block_rows = min(512, length)
    grad_keys = jnp.zeros(key_rows.shape, jnp.float32)
    grad_values = jnp.zeros(value_rows.shape, jnp.float32)
    grad_queries = []
    for block_number, block_start in enumerate(range(0, length, block_rows)):
        block_end = block_start + block_rows
        query_block = query_rows[block_start:block_end]
        grad_block = grad_mixed[block_start:block_end]
        scores = jnp.einsum(
            "qhd,khd->hqk", query_block, key_rows[:block_end], preferred_element_type=jnp.float32
        )
        scores = jnp.where(causal_mask(block_start, block_end), scores, -1e30)
        probs_again = jnp.exp(scores - totals[block_number])
        weights = probs_again.astype(jnp.bfloat16)
        grad_probs = jnp.einsum(
            "qhd,khd->hqk", grad_block, value_rows[:block_end], preferred_element_type=jnp.float32
        )
        grad_scores = (
            probs_again * (grad_probs - jnp.sum(probs_again * grad_probs, axis=-1, keepdims=True))
        ).astype(jnp.bfloat16)
        grad_queries.append(
            jnp.einsum(
                "hqk,khd->qhd",
                grad_scores,
                key_rows[:block_end],
                preferred_element_type=jnp.float32,
            )
        )
        grad_keys = grad_keys.at[:block_end].add(
            jnp.einsum("hqk,qhd->khd", grad_scores, query_block, preferred_element_type=jnp.float32)
        )
        grad_values = grad_values.at[:block_end].add(
            jnp.einsum("hqk,qhd->khd", weights, grad_block, preferred_element_type=jnp.float32)
        )
    return (jnp.concatenate(grad_queries, axis=0), grad_keys, grad_values)


def swap(values, axis, bit):
    return lax.ppermute(values, axis, [(i, i ^ bit) for i in range(lax.axis_size(axis))])


def axis_bits(axis):
    size = lax.axis_size(axis)
    return [size >> (k + 1) for k in range(size.bit_length() - 1)]


def spread_sum(values, axis):
    for bit in axis_bits(axis)[::-1]:
        values = values + swap(values, axis, bit)
    return values


def plane_order(turn):
    bits = axis_bits("tensor")[:-1]
    if turn % 2:
        bits = bits[::-1]
    order = [0]
    for bit in bits:
        order = order + [bit ^ i for i in order]
    return bits, order


def plane_gather(piece, turn):
    bits, _ = plane_order(turn)
    pieces = [piece]
    for bit in bits:
        pieces = pieces + [swap(p, "tensor", bit) for p in pieces]
    near = jnp.concatenate(pieces, axis=0)
    return near, swap(near, "tensor", 1)


def plane_scatter(near, far, turn):
    bits, _ = plane_order(turn)
    total = near.astype(jnp.float32) + swap(far, "tensor", 1).astype(jnp.float32)
    for bit in bits[::-1]:
        half = total.shape[0] // 2
        sent = total[half:].astype(jnp.bfloat16)
        total = total[:half].astype(jnp.bfloat16).astype(jnp.float32) + swap(
            sent, "tensor", bit
        ).astype(jnp.float32)
    return total


def plane_rows(values, turn, own_rows, sorted_order=False):
    _, order = plane_order(turn)
    if sorted_order:
        order = sorted(order)
    index = lax.axis_index("tensor")

    def block(i):
        return lax.dynamic_slice_in_dim(values, (index ^ i) * own_rows, own_rows, 0)

    near = jnp.concatenate([block(i) for i in order], axis=0)
    far = jnp.concatenate([block(i ^ 1) for i in order], axis=0)
    return near, far


def natural_rows(near, far, turn, own_rows):
    _, order = plane_order(turn)
    index = lax.axis_index("tensor")
    both = jnp.concatenate([near, far], axis=0)
    place = {}
    for at, i in enumerate(order):
        place[i] = at
        place[i ^ 1] = at + len(order)
    table = jnp.array([place[i] for i in range(2 * len(order))], jnp.int32)
    return jnp.concatenate(
        [
            lax.dynamic_slice_in_dim(both, table[index ^ i] * own_rows, own_rows, 0)
            for i in range(2 * len(order))
        ],
        axis=0,
    )


def contract(left, right, left_dim, right_dim):
    return lax.dot_general(
        left, right, (((left_dim,), (right_dim,)), ((), ())), preferred_element_type=jnp.float32
    )


def tie(values, *after):
    return lax.optimization_barrier((values, *after))[0]


def stages(turn, bits):
    if turn % 2:
        bits = bits[::-1]
    found = [[] for _ in bits]
    order = [(0, ())]
    for bit in bits:
        order = order + [(bit ^ i, used + (bit,)) for i, used in order]
    for i, used in order[1:]:
        found[len(used) - 1].append((i, i ^ used[-1], used[-1]))
    return found


def gather_stage(pieces, turn, stage, bits, after=()):
    pieces = dict(pieces)
    for i, source, bit in stages(turn, bits)[stage]:
        sent = pieces[source]
        if after:
            sent = tie(sent, *after)
        pieces[i] = swap(sent, "tensor", bit)
    return pieces


def gather_all(piece, turn, bits):
    pieces = {0: piece}
    for stage in range(len(bits)):
        pieces = gather_stage(pieces, turn, stage, bits)
    return pieces


def scatter_stage(sums, turn, stage, bits, after=()):
    sums = dict(sums)
    for i, target, bit in stages(turn, bits)[len(bits) - 1 - stage]:
        sent = sums.pop(i).astype(jnp.bfloat16)
        if after:
            sent = tie(sent, *after)
        sums[target] = sums[target].astype(jnp.float32) + swap(sent, "tensor", bit).astype(
            jnp.float32
        )
    return sums


MEGABYTE = 1024 * 1024


def kernel_params():
    return pltpu.CompilerParams(vmem_limit_bytes=58 * MEGABYTE)


def cost(flops, moved):
    return pl.CostEstimate(flops=flops, bytes_accessed=moved, transcendentals=0)


def column_of(row):
    n = row.shape[1]
    down = lax.broadcasted_iota(jnp.int32, (n, n), 0)
    across = lax.broadcasted_iota(jnp.int32, (n, n), 1)
    return jnp.sum(jnp.where(down == across, row, 0.0), axis=1, keepdims=True)


def fixed(shape, single=True):
    if single:
        return pl.BlockSpec(
            shape, lambda *_: (0,) * len(shape), pipeline_mode=pl.Buffered(1)
        )
    return pl.BlockSpec(shape, lambda *_: (0,) * len(shape))


def expert_body(indices, dy_count, place, scalars, *refs):
    count = len(indices)
    x_parts, refs = refs[:count], refs[count:]
    dy_parts, refs = refs[:dy_count], refs[dy_count:]
    kept, chosen, router = refs[:3]
    gate_own, gate_other, up_own, up_other, down_own, down_other = refs[3:9]
    scratch = refs[-13:]
    pieces, gate_out, dl_all, x_all, dy_all, act_all, own_dp, other_dp, gated_own, gated_other = refs[
        -23:-13
    ]
    rows, grads, wide, tall, raw, inner, act, slopes, gated, done, probs_ref, dots, sems = scratch
    rows_here, width = rows.shape
    units = gate_own.shape[1]
    own_rows = rows_here // count
    used = []

    def start(source, target):
        copy = pltpu.make_async_copy(source, target, sems.at[len(used)])
        used.append(copy)
        copy.start()
        return copy

    def spread(parts, target):
        size = rows_here // len(parts)
        return [start(part, target.at[pl.ds(at * size, size)]) for at, part in enumerate(parts)]

    x_copies = spread(x_parts, rows)
    order = [gate_own, up_own, gate_other, up_other]
    wide_copies = [
        start(weight, wide.at[:, pl.ds(at * units, units)]) for at, weight in enumerate(order[:2])
    ]
    dy_copies = spread(dy_parts, grads)
    tall_copies = [start(down_own, tall.at[pl.ds(0, units)])]
    wide_copies += [
        start(weight, wide.at[:, pl.ds((at + 2) * units, units)])
        for at, weight in enumerate(order[2:])
    ]
    tall_copies.append(start(down_other, tall.at[pl.ds(units, units)]))

    here_rows = pl.ds(place * rows_here, rows_here)
    for copy in x_copies:
        copy.wait()
    outgoing = [start(rows, x_all.at[here_rows])]
    logits = contract(rows[...], router[...], 1, 0)
    exponent = jnp.exp(logits - jnp.max(logits, axis=-1, keepdims=True))
    probs = exponent / jnp.sum(exponent, axis=-1, keepdims=True)
    kept_column = jnp.concatenate(
        [column_of(kept[pl.ds(scalars[0] ^ i, 1), :]) for i in indices], axis=0
    )
    probs_ref[...] = probs
    gate_out[...] = jnp.sum(probs * chosen[...], axis=-1, keepdims=True) * kept_column
    dots[...] = jnp.zeros_like(dots)

    block = min(64, rows_here)
    for half in range(2):
        columns = pl.ds(half * units, units)
        for part in range(2):
            at = 2 * half + part
            wide_copies[at].wait()
            raw[:, pl.ds(part * units, units)] = contract(
                rows[...], wide[:, pl.ds(at * units, units)], 1, 0
            )
        if half == 0:
            for copy in dy_copies:
                copy.wait()
            outgoing.append(start(grads, dy_all.at[here_rows]))
        tall_copies[half].wait()
        inner[...] = contract(grads[...], tall[columns, :], 1, 1)

        @pl.loop(0, rows_here // block)
        def _(at):
            here = pl.ds(at * block, block)
            pre_gate = raw[here, pl.ds(0, units)]
            pre_up = raw[here, pl.ds(units, units)]
            inward = inner[here, :]
            gate = gate_out[here, :]
            sigmoid_gate = 1.0 / (1.0 + jnp.exp(-pre_gate))
            silu_gate = pre_gate * sigmoid_gate
            active = (silu_gate * pre_up).astype(jnp.bfloat16)
            act[here, columns] = active
            active = active.astype(jnp.float32)
            gated[here, columns] = (gate * active).astype(jnp.bfloat16)
            dots[here, :] += jnp.sum(inward * active, axis=-1, keepdims=True)
            grad_active = gate * inward
            slopes[here, pl.ds(2 * half * units, units)] = (
                grad_active * pre_up * sigmoid_gate * (1.0 + pre_gate * (1.0 - sigmoid_gate))
            ).astype(jnp.bfloat16)
            slopes[here, pl.ds((2 * half + 1) * units, units)] = (grad_active * silu_gate).astype(
                jnp.bfloat16
            )

    outgoing += [
        start(act, act_all.at[here_rows]),
        start(slopes.at[:, pl.ds(0, 2 * units)], own_dp.at[here_rows]),
        start(slopes.at[:, pl.ds(2 * units, 2 * units)], other_dp.at[here_rows]),
        start(gated.at[:, pl.ds(0, units)], gated_own.at[here_rows]),
        start(gated.at[:, pl.ds(units, units)], gated_other.at[here_rows]),
    ]
    grad_logits = (dots[...] * gate_out[...] * (chosen[...] - probs_ref[...])).astype(jnp.bfloat16)
    dl_all[...] = grad_logits
    step = min(512, width)
    for at in range(width // step):
        columns = pl.ds(at * step, step)
        done[:, columns] = (
            contract(slopes[...], wide[columns, :], 1, 1)
            + contract(grad_logits, router[columns, :], 1, 1)
        ).astype(jnp.bfloat16)
    for at, i in enumerate(indices):
        to = (scalars[0] ^ i) // 2
        outgoing.append(start(done.at[pl.ds(at * own_rows, own_rows)], pieces.at[to]))
    for copy in outgoing:
        copy.wait()


def expert_chunk(place, places, x_pieces, dy_parts, here, kept, chosen, router, gates, ups, downs, chain):
    indices = sorted(x_pieces)
    count = len(indices)
    own_rows, width = x_pieces[0].shape
    rows = own_rows * count
    units = gates[0].shape[1]
    experts = router.shape[1]
    extra = () if chain is None else tuple(chain)
    hbm = pl.BlockSpec(memory_space=pl.ANY)
    first = count + len(dy_parts) + 10
    kept_shapes = [
        (rows * places, experts),
        (rows * places, width),
        (rows * places, width),
        (rows * places, 2 * units),
        (rows * places, 2 * units),
        (rows * places, 2 * units),
        (rows * places, units),
        (rows * places, units),
    ]
    results = pl.pallas_call(
        lambda *refs: expert_body(indices, len(dy_parts), place, *refs),
        grid_spec=pltpu.PrefetchScalarGridSpec(
            num_scalar_prefetch=1,
            grid=(1,),
            in_specs=[hbm] * (count + len(dy_parts))
            + [fixed(kept.shape), fixed((1, experts)), fixed((width, experts))]
            + [hbm] * (6 + len(extra)),
            out_specs=[hbm]
            + [
                fixed((rows, 1), False),
                pl.BlockSpec((rows, experts), lambda j, *_: (place, 0)),
            ]
            + [hbm] * 7,
            scratch_shapes=[
                pltpu.VMEM((rows, width), jnp.bfloat16),
                pltpu.VMEM((rows, width), jnp.bfloat16),
                pltpu.VMEM((width, 4 * units), jnp.bfloat16),
                pltpu.VMEM((2 * units, width), jnp.bfloat16),
                pltpu.VMEM((rows, 2 * units), jnp.float32),
                pltpu.VMEM((rows, units), jnp.float32),
                pltpu.VMEM((rows, 2 * units), jnp.bfloat16),
                pltpu.VMEM((rows, 4 * units), jnp.bfloat16),
                pltpu.VMEM((rows, 2 * units), jnp.bfloat16),
                pltpu.VMEM((rows, width), jnp.bfloat16),
                pltpu.VMEM((rows, experts), jnp.float32),
                pltpu.VMEM((rows, 1), jnp.float32),
                pltpu.SemaphoreType.DMA((2 * count + len(dy_parts) + 13,)),
            ],
        ),
        out_shape=[jax.ShapeDtypeStruct((count, own_rows, width), jnp.bfloat16)]
        + [jax.ShapeDtypeStruct((rows, 1), jnp.float32)]
        + [jax.ShapeDtypeStruct(shape, jnp.bfloat16) for shape in kept_shapes],
        input_output_aliases={first + i: 2 + i for i in range(len(extra))},
        compiler_params=kernel_params(),
        cost_estimate=cost(20 * rows * width * units, 10 * rows * width + 12 * width * units),
        name="expert_chunk",
    )(
        here,
        *[x_pieces[i] for i in indices],
        *dy_parts,
        kept,
        chosen,
        router,
        *gates,
        *ups,
        *downs,
        *extra,
    )
    return results[0], results[1], results[2:]


def input_grad_body(indices, own_rows, scalars, query_low, key_low, value_low, *refs):
    weights = refs[:3]
    pieces = refs[3:-2]
    done, sems = refs[-2:]
    width = done.shape[1]
    step = min(512, width)
    for at in range(width // step):
        columns = pl.ds(at * step, step)
        done[:, columns] = (
            contract(query_low[...], weights[0][columns, :], 1, 1)
            + contract(key_low[...], weights[1][columns, :], 1, 1)
            + contract(value_low[...], weights[2][columns, :], 1, 1)
        ).astype(jnp.bfloat16)
    copies = []
    for at, i in enumerate(indices):
        here = pl.ds(pl.multiple_of((scalars[0] ^ i) * own_rows, own_rows), own_rows)
        copies.append(pltpu.make_async_copy(done.at[here], pieces[at], sems.at[at]))
        copies[-1].start()
    for copy in copies:
        copy.wait()


def input_grad(here, indices, own_rows, lows, weights):
    width = weights[0].shape[0]
    rows = lows[0].shape[0]
    results = pl.pallas_call(
        lambda *refs: input_grad_body(indices, own_rows, *refs),
        grid_spec=pltpu.PrefetchScalarGridSpec(
            num_scalar_prefetch=1,
            grid=(1,),
            in_specs=[fixed(low.shape) for low in lows] + [fixed(w.shape) for w in weights],
            out_specs=[pl.BlockSpec(memory_space=pl.ANY)] * len(indices),
            scratch_shapes=[
                pltpu.VMEM((rows, width), jnp.bfloat16),
                pltpu.SemaphoreType.DMA((len(indices),)),
            ],
        ),
        out_shape=[jax.ShapeDtypeStruct((own_rows, width), jnp.bfloat16)] * len(indices),
        compiler_params=kernel_params(),
        cost_estimate=cost(6 * lows[0].size * width, 8 * lows[0].size * 8),
        name="input_grad",
    )(here, *lows, *weights)
    return dict(zip(indices, results))


def place_body(indices, own_rows, scalars, *refs):
    pieces, out, sems = refs[: len(indices)], refs[-2], refs[-1]
    copies = []
    for at, i in enumerate(indices):
        here = pl.ds(pl.multiple_of((scalars[0] ^ i) * own_rows, own_rows), own_rows)
        copies.append(pltpu.make_async_copy(pieces[at], out.at[here], sems.at[at]))
        copies[-1].start()
    for copy in copies:
        copy.wait()


def place_rows(here, pieces):
    indices = sorted(pieces)
    own_rows, width = pieces[0].shape
    return pl.pallas_call(
        lambda *refs: place_body(indices, own_rows, *refs),
        grid_spec=pltpu.PrefetchScalarGridSpec(
            num_scalar_prefetch=1,
            grid=(1,),
            in_specs=[fixed((own_rows, width))] * len(indices),
            out_specs=pl.BlockSpec(memory_space=pl.ANY),
            scratch_shapes=[pltpu.SemaphoreType.DMA((len(indices),))],
        ),
        out_shape=jax.ShapeDtypeStruct((own_rows * len(indices), width), pieces[0].dtype),
        compiler_params=kernel_params(),
        cost_estimate=cost(0, 4 * own_rows * len(indices) * width),
        name="place_rows",
    )(here, *[pieces[i] for i in indices])


def near_scatter(pieces):
    size = lax.axis_size("tensor")
    groups = [list(range(core, size, 2)) for core in range(2)]
    return lax.all_to_all(
        pieces, "tensor", split_axis=0, concat_axis=0, axis_index_groups=groups, tiled=True
    )


def line_sum(part, after=()):
    index = lax.axis_index("expert")
    bits = axis_bits("expert")[::-1]
    for bit in bits:
        half = part.shape[0] // 2
        high = (index // bit) % 2
        kept = lax.dynamic_slice_in_dim(part, high * half, half, 0)
        sent = lax.dynamic_slice_in_dim(part, (1 - high) * half, half, 0)
        if after:
            sent = tie(sent, *after)
            after = ()
        part = (
            kept.astype(jnp.float32) + swap(sent, "expert", bit).astype(jnp.float32)
        ).astype(jnp.bfloat16)
    for bit in bits[::-1]:
        high = (index // bit) % 2 == 1
        other = swap(part, "expert", bit)
        part = jnp.concatenate([jnp.where(high, other, part), jnp.where(high, part, other)], axis=0)
    return part.astype(jnp.float32)


def send_body(indices, scalars, act, gate, down_own, down_other, pieces):
    units = down_own.shape[0]
    value = contract(act[:, :units], down_own[...], 1, 0) + contract(
        act[:, units:], down_other[...], 1, 0
    )
    sent = (gate[...] * value).astype(jnp.bfloat16)
    own_rows = pieces.shape[1]
    for at, i in enumerate(indices):
        pieces[(scalars[0] ^ i) // 2] = sent[at * own_rows : (at + 1) * own_rows]


def expert_send(here, place, indices, act_all, gate, downs):
    rows = gate.shape[0]
    count = len(indices)
    units, width = downs[0].shape
    block = min(512, width)
    return pl.pallas_call(
        lambda *refs: send_body(indices, *refs),
        grid_spec=pltpu.PrefetchScalarGridSpec(
            num_scalar_prefetch=1,
            grid=(width // block,),
            in_specs=[
                pl.BlockSpec((rows, 2 * units), lambda j, *_: (place, 0)),
                fixed((rows, 1)),
                pl.BlockSpec((units, block), lambda j, *_: (0, j)),
                pl.BlockSpec((units, block), lambda j, *_: (0, j)),
            ],
            out_specs=pl.BlockSpec((count, rows // count, block), lambda j, *_: (0, 0, j)),
        ),
        out_shape=jax.ShapeDtypeStruct((count, rows // count, width), jnp.bfloat16),
        compiler_params=kernel_params(),
        cost_estimate=cost(4 * rows * width * units, 4 * rows * width + 4 * width * units),
        name="expert_send",
    )(here, act_all, gate, *downs)


def project_body(indices, halves, scalars, mixed, tokens, gain, *refs):
    weights = refs[: len(indices) * halves]
    hidden_out, low_out = refs[-2:]
    total = tokens[...].astype(jnp.float32)
    depth = weights[0].shape[0]
    attn = None
    for at, i in enumerate(indices):
        piece = mixed[scalars[0] ^ i]
        for half in range(halves):
            part = contract(
                piece[:, half * depth : (half + 1) * depth], weights[at * halves + half][...], 1, 0
            )
            attn = part if attn is None else attn + part
    hidden = total + attn
    normal, _ = rms_forward(hidden)
    hidden_out[...] = hidden
    low_out[...] = (normal * gain[...]).astype(jnp.bfloat16)


def project_out(here, indices, mixed, tokens, gain, weights, halves):
    rows, width = tokens.shape
    return pl.pallas_call(
        lambda *refs: project_body(indices, halves, *refs),
        grid_spec=pltpu.PrefetchScalarGridSpec(
            num_scalar_prefetch=1,
            grid=(1,),
            in_specs=[fixed(mixed.shape), fixed(tokens.shape), fixed((1, width))]
            + [fixed(weights[0].shape)] * len(weights),
            out_specs=[fixed((rows, width), False), fixed((rows, width), False)],
        ),
        out_shape=[
            jax.ShapeDtypeStruct((rows, width), jnp.float32),
            jax.ShapeDtypeStruct((rows, width), jnp.bfloat16),
        ],
        compiler_params=kernel_params(),
        cost_estimate=cost(2 * rows * width * width, 2 * width * width),
        name="project_out",
    )(here, mixed, tokens, gain, *weights)


def turn_body(indices, halves, count, scalars, hidden, grad_out, gain, *refs):
    grads = refs[:count]
    weights = refs[count : count + len(indices) * halves]
    grad_hidden_out, low_out, mixed_out, gain_out = refs[-4:]
    grad_ffn = jnp.sum(grads[0][...].astype(jnp.float32), axis=0)
    for part in grads[1:]:
        grad_ffn = grad_ffn + part[...].astype(jnp.float32)
    normal, inverse = rms_forward(hidden[...])
    gain_out[...] = jnp.sum(grad_ffn * normal, axis=0, keepdims=True)
    scaled = grad_ffn * gain[...]
    grad_hidden = grad_out[...].astype(jnp.float32) + inverse * (
        scaled - normal * jnp.mean(scaled * normal, axis=-1, keepdims=True)
    )
    low = grad_hidden.astype(jnp.bfloat16)
    grad_hidden_out[...] = grad_hidden
    low_out[...] = low
    depth = weights[0].shape[0]
    for at, i in enumerate(indices):
        for half in range(halves):
            mixed_out[scalars[0] ^ i, :, half * depth : (half + 1) * depth] = contract(
                low, weights[at * halves + half][...], 1, 1
            ).astype(jnp.bfloat16)


def turn_back(here, indices, hidden, grad_out, gain, grads, weights, halves):
    rows, width = hidden.shape
    depth = weights[0].shape[0] * halves
    return pl.pallas_call(
        lambda *refs: turn_body(indices, halves, len(grads), *refs),
        grid_spec=pltpu.PrefetchScalarGridSpec(
            num_scalar_prefetch=1,
            grid=(1,),
            in_specs=[fixed((rows, width)), fixed((rows, width)), fixed((1, width))]
            + [fixed(part.shape) for part in grads]
            + [fixed(weights[0].shape)] * len(weights),
            out_specs=[
                fixed((rows, width), False),
                fixed((rows, width), False),
                fixed((len(indices), rows, depth), False),
                fixed((1, width), False),
            ],
        ),
        out_shape=[
            jax.ShapeDtypeStruct((rows, width), jnp.float32),
            jax.ShapeDtypeStruct((rows, width), jnp.bfloat16),
            jax.ShapeDtypeStruct((len(indices), rows, depth), jnp.bfloat16),
            jax.ShapeDtypeStruct((1, width), jnp.float32),
        ],
        compiler_params=kernel_params(),
        cost_estimate=cost(2 * rows * width * width, 2 * width * width),
        name="turn_back",
    )(here, hidden, grad_out, gain, *grads, *weights)


def on_device(
    tokens,
    positions,
    routes,
    slot_ids,
    attn_gain,
    w_query,
    w_key,
    w_value,
    query_gain,
    key_gain,
    w_out,
    ffn_gain,
    router,
    w_gate,
    w_up,
    w_down,
    grad_out,
):
    tensor_size = lax.axis_size("tensor")
    expert_size = lax.axis_size("expert")
    local_count = tensor_size // 2
    tensor_index = lax.axis_index("tensor")
    expert_index = lax.axis_index("expert")
    own_local = tensor_index // 2
    own_expert = expert_index * local_count + own_local
    length, model_width = tokens.shape
    heads_here = w_query.shape[1] // HEAD_DIM
    full_cols = w_query.shape[1] * tensor_size
    expert_count = router.shape[1]
    capacity = 3 * length * TOP // (2 * expert_count)
    own_rows = length // tensor_size
    chunks = [0] + list(range(2, expert_size)) + [1]
    bits = axis_bits("tensor")
    near_bits = bits[:-1]
    last = len(near_bits)

    def own_slice(rows):
        return lax.dynamic_slice_in_dim(rows, tensor_index * own_rows, own_rows, 0)

    def with_sibling(weights):
        return [weights, swap(weights, "tensor", 1)]

    grad_own = own_slice(grad_out)
    grad_near, _ = plane_rows(grad_out, 0, own_rows, sorted_order=True)
    grad_pieces = {}
    for chunk in range(1, expert_size):
        grad_pieces[chunk] = swap(grad_near if chunk == 1 else grad_own, "expert", chunk)
    out_pieces = {0: w_out}
    for stage in range(len(bits)):
        out_pieces = gather_stage(out_pieces, 0, stage, bits)
    all_indices = sorted(out_pieces)
    out_weights = [out_pieces[i] for i in all_indices]
    first_out = [out_pieces[i] for i in all_indices if i in near_bits]
    last_out = out_pieces[2 * (tensor_size // 2 - 1)]
    gates, ups, downs = with_sibling(w_gate[0]), with_sibling(w_up[0]), with_sibling(w_down[0])
    expert_iota = jnp.arange(expert_count, dtype=jnp.int32)
    kept_table = jnp.sum(
        (
            (routes.T[:, None, :] == expert_iota[None, :, None]) & (slot_ids.T < capacity)[:, None, :]
        ).astype(jnp.float32),
        axis=0,
    )
    kept_chunks = []
    for chunk in range(expert_size):
        target = (expert_index ^ chunk) * local_count + own_local
        kept_row = lax.dynamic_slice_in_dim(kept_table, target, 1, 0).reshape(tensor_size, own_rows)
        kept_chunks.append(swap(kept_row, "expert", chunk) if chunk else kept_row)

    def here(chunk):
        return jnp.stack([tensor_index, (expert_index ^ chunk) * tensor_size]).astype(jnp.int32)

    grad_parts_of = {0: [grad_near], 1: [grad_pieces[1]]}
    for chunk in range(2, expert_size):
        pieces = {0: tie(grad_pieces[chunk], last_out)}
        for stage in range(last):
            pieces = gather_stage(pieces, chunk, stage, near_bits)
        grad_parts_of[chunk] = [pieces[i] for i in sorted(pieces)]

    score_scale = HEAD_DIM ** (-0.5)
    half_dim = HEAD_DIM // 2
    frequency = THETA ** (-2.0 * jnp.arange(half_dim, dtype=jnp.float32) / HEAD_DIM)
    angles = positions.astype(jnp.float32)[:, None] * frequency[None, :]
    cosine_table = jnp.cos(angles)[:, None, :]
    sine_table = jnp.sin(angles)[:, None, :]
    token_float = tokens.astype(jnp.float32)
    attn_normal, attn_inverse = rms_forward(token_float)
    attn_in = (attn_normal * attn_gain).astype(jnp.bfloat16)
    head_shape = (length, heads_here, HEAD_DIM)
    query_raw = jnp.dot(attn_in, w_query, preferred_element_type=jnp.float32).reshape(head_shape)
    key_raw = jnp.dot(attn_in, w_key, preferred_element_type=jnp.float32).reshape(head_shape)
    value_rows = (
        jnp.dot(attn_in, w_value, preferred_element_type=jnp.float32)
        .astype(jnp.bfloat16)
        .reshape(head_shape)
    )
    query_scale = query_gain.reshape(heads_here, HEAD_DIM)
    key_scale = key_gain.reshape(heads_here, HEAD_DIM)
    square_sums = spread_sum(
        jnp.stack(
            [jnp.sum(query_raw * query_raw, axis=(1, 2)), jnp.sum(key_raw * key_raw, axis=(1, 2))]
        ),
        "tensor",
    )
    square_sums = tie(square_sums, *first_out)
    query_inverse = lax.rsqrt(square_sums[0] / full_cols + EPS)[:, None, None]
    key_inverse = lax.rsqrt(square_sums[1] / full_cols + EPS)[:, None, None]
    query_normal = query_raw * query_inverse
    key_normal = key_raw * key_inverse
    query_rows = (
        rotary(query_normal * query_scale, cosine_table, sine_table) * score_scale
    ).astype(jnp.bfloat16)
    key_rows = rotary(key_normal * key_scale, cosine_table, sine_table).astype(jnp.bfloat16)
    mixed_heads, totals = attention_forward(query_rows, key_rows, value_rows)
    mixed_low = mixed_heads.reshape(length, heads_here * HEAD_DIM).astype(jnp.bfloat16)
    mixed_low = tie(mixed_low, last_out)
    mixed_own = lax.all_to_all(
        mixed_low.reshape(tensor_size, own_rows, -1), "tensor", split_axis=0, concat_axis=0, tiled=True
    )
    hidden, ffn_in = project_out(
        here(0), all_indices, mixed_own, own_slice(tokens), ffn_gain[None, :], out_weights, 1
    )
    chosen = (expert_iota == own_expert).astype(jnp.float32)[None, :]
    gathered = [
        {0: ffn_in if chunk == 0 else swap(ffn_in, "expert", chunk)} for chunk in chunks
    ]
    chain = None
    sums = []
    gate_columns = []
    for at, chunk in enumerate(chunks):
        for stage in range(last):
            before = at - last - 1 + stage
            after = (gate_columns[before],) if before >= 0 else ()
            gathered[at] = gather_stage(gathered[at], at, stage, near_bits, after)
        scalars = here(chunk)
        if at >= 2:
            scalars = tie(scalars, sums[at - 2])
        pieces, gate_column, chain = expert_chunk(
            at,
            expert_size,
            gathered[at],
            grad_parts_of[chunk],
            scalars,
            kept_chunks[chunk],
            chosen,
            router,
            gates,
            ups,
            downs,
            chain,
        )
        gate_columns.append(gate_column)
        sums.append(near_scatter(pieces))

    def to_owner(near, chunk):
        total = jnp.sum(near.astype(jnp.float32), axis=0)
        return swap(total.astype(jnp.bfloat16), "expert", chunk)

    grad_parts = [sums[0]] + [to_owner(sums[at], chunk) for at, chunk in enumerate(chunks) if chunk]
    indices = sorted(gathered[0])
    dl_all, x_all, dy_all, act_all, own_dp, other_dp, gated_own, gated_other = chain
    sent_pieces = [
        expert_send(here(0), at, indices, act_all, gate_columns[at], downs)
        for at in range(expert_size)
    ]
    grad_hidden, hidden_low, grad_mixed_own, grad_ffn_gain = turn_back(
        here(0), all_indices, hidden, grad_own, ffn_gain[None, :], grad_parts, out_weights, 1
    )
    grad_mixed = lax.all_to_all(
        grad_mixed_own, "tensor", split_axis=0, concat_axis=0, tiled=True
    ).reshape(head_shape)

    sent_near = [near_scatter(tie(pieces, hidden_low)) for pieces in sent_pieces]
    units = own_dp.shape[1] // 2
    other_wide = swap(contract(x_all, other_dp, 0, 0).astype(jnp.bfloat16), "tensor", 1)
    other_down = swap(contract(gated_other, dy_all, 0, 0).astype(jnp.bfloat16), "tensor", 1)
    grad_gate_w = contract(x_all, own_dp[:, :units], 0, 0) + other_wide[:, :units].astype(jnp.float32)
    grad_up_w = contract(x_all, own_dp[:, units:], 0, 0) + other_wide[:, units:].astype(jnp.float32)
    grad_down = contract(gated_own, dy_all, 0, 0) + other_down.astype(jnp.float32)
    grad_router_part = contract(dl_all, x_all, 0, 0)

    hidden_low_all = lax.all_gather(hidden_low, "tensor", axis=0, tiled=True)
    grad_w_out = contract(mixed_low, hidden_low_all, 0, 0)
    grad_query, grad_key, grad_value_attn = attention_backward(
        query_rows, key_rows, value_rows, grad_mixed, totals
    )
    grad_query_normed = rotary(grad_query * score_scale, cosine_table, -sine_table)
    grad_key_normed = rotary(grad_key, cosine_table, -sine_table)
    grad_query_scale = jnp.sum(grad_query_normed * query_normal, axis=0)
    grad_key_scale = jnp.sum(grad_key_normed * key_normal, axis=0)
    query_scaled = grad_query_normed * query_scale
    key_scaled = grad_key_normed * key_scale
    inner_sums = spread_sum(
        jnp.stack(
            [
                jnp.sum(query_scaled * query_normal, axis=(1, 2)),
                jnp.sum(key_scaled * key_normal, axis=(1, 2)),
            ]
        ),
        "tensor",
    )
    grad_query_raw = query_inverse * (
        query_scaled - query_normal * (inner_sums[0] / full_cols)[:, None, None]
    )
    grad_key_raw = key_inverse * (
        key_scaled - key_normal * (inner_sums[1] / full_cols)[:, None, None]
    )
    query_low = grad_query_raw.reshape(length, heads_here * HEAD_DIM).astype(jnp.bfloat16)
    key_low = grad_key_raw.reshape(length, heads_here * HEAD_DIM).astype(jnp.bfloat16)
    value_low = grad_value_attn.reshape(length, heads_here * HEAD_DIM).astype(jnp.bfloat16)
    grad_w_query = jnp.einsum("td,tq->dq", attn_in, query_low, preferred_element_type=jnp.float32)
    grad_w_key = jnp.einsum("td,tq->dq", attn_in, key_low, preferred_element_type=jnp.float32)
    grad_w_value = jnp.einsum("td,tq->dq", attn_in, value_low, preferred_element_type=jnp.float32)
    grad_attn = input_grad(
        here(0), all_indices, own_rows, (query_low, key_low, value_low), (w_query, w_key, w_value)
    )
    for stage in range(len(bits)):
        grad_attn = scatter_stage(grad_attn, 0, stage, bits)
    grad_token_part, grad_attn_gain = rms_backward(
        grad_attn[0], own_slice(attn_normal), own_slice(attn_inverse), attn_gain
    )
    grad_tokens = place_rows(
        here(0), gather_all((grad_hidden + grad_token_part).astype(jnp.bfloat16), 0, bits)
    )
    moe_sum = hidden
    for at, chunk in enumerate(chunks):
        near = tie(sent_near[at], query_low)
        if chunk:
            moe_sum = moe_sum + to_owner(near, chunk).astype(jnp.float32)
        else:
            moe_sum = moe_sum + jnp.sum(near.astype(jnp.float32), axis=0)
    output = place_rows(here(0), gather_all(moe_sum.astype(jnp.bfloat16), 1, bits))
    sum_query = line_sum(grad_w_query.astype(jnp.bfloat16))
    sum_key = line_sum(grad_w_key.astype(jnp.bfloat16))
    sum_value, sum_out = [
        part.astype(jnp.float32)
        for part in lax.psum(
            (grad_w_value.astype(jnp.bfloat16), grad_w_out.astype(jnp.bfloat16)), "expert"
        )
    ]
    plane_sums = spread_sum(
        jnp.concatenate([grad_router_part, grad_ffn_gain, grad_attn_gain[None, :]], axis=0), "tensor"
    )
    scales = jnp.concatenate([grad_query_scale.reshape(-1), grad_key_scale.reshape(-1)])
    scales = jnp.pad(scales, (0, model_width - scales.shape[0]))
    all_sums = spread_sum(jnp.concatenate([plane_sums, scales[None, :]], axis=0), "expert")
    columns_here = w_query.shape[1]
    return (
        output,
        grad_tokens,
        all_sums[expert_count + 1],
        sum_query,
        sum_key,
        sum_value,
        all_sums[expert_count + 2, :columns_here],
        all_sums[expert_count + 2, columns_here : 2 * columns_here],
        sum_out,
        all_sums[expert_count],
        all_sums[:expert_count].T,
        grad_gate_w[None],
        grad_up_w[None],
        grad_down[None],
    )


def solution(mesh):
    placed = (
        P("expert", None),
        P("expert"),
        P("expert", None),
        P("expert", None),
        P(),
        P(None, "tensor"),
        P(None, "tensor"),
        P(None, "tensor"),
        P("tensor"),
        P("tensor"),
        P("tensor", None),
        P(),
        P(),
        P(("expert", "tensor"), None, None),
        P(("expert", "tensor"), None, None),
        P(("expert", "tensor"), None, None),
        P("expert", None),
    )
    return jax.shard_map(
        on_device,
        mesh=mesh,
        in_specs=placed,
        out_specs=(
            P("expert", None),
            P("expert", None),
            P(),
            P(None, "tensor"),
            P(None, "tensor"),
            P(None, "tensor"),
            P("tensor"),
            P("tensor"),
            P("tensor", None),
            P(),
            P(),
            P(("expert", "tensor"), None, None),
            P(("expert", "tensor"), None, None),
            P(("expert", "tensor"), None, None),
        ),
        check_vma=False,
    )
```

```python
import jax
import jax.numpy as jnp
from jax import lax
from jax.experimental import pallas as pl
from jax.experimental.pallas import tpu as pltpu
from jax.sharding import PartitionSpec as P

HEAD_DIM = 128
TOP = 8


EPS = 1e-05
THETA = 10000.0


def rms_forward(values):
    inverse = lax.rsqrt(jnp.mean(values * values, axis=-1, keepdims=True) + EPS)
    return (values * inverse, inverse)


def rms_backward(grad_normed, normal_rows, inverse, gain_row):
    gain_grad = jnp.sum(grad_normed * normal_rows, axis=0)
    scaled = grad_normed * gain_row
    grad_rows = inverse * (
        scaled - normal_rows * jnp.mean(scaled * normal_rows, axis=-1, keepdims=True)
    )
    return (grad_rows, gain_grad)


def rotary(values, cosine_table, sine_table):
    half_dim = values.shape[-1] // 2
    first_half = values[..., :half_dim]
    second_half = values[..., half_dim:]
    return jnp.concatenate(
        [
            first_half * cosine_table - second_half * sine_table,
            second_half * cosine_table + first_half * sine_table,
        ],
        axis=-1,
    )


def causal_mask(start_row, end_row):
    return (jnp.arange(start_row, end_row)[:, None] >= jnp.arange(end_row)[None, :])[None]


def attention_forward(query_rows, key_rows, value_rows):
    length = query_rows.shape[0]
    block_rows = min(512, length)
    outputs = []
    totals = []
    for block_start in range(0, length, block_rows):
        block_end = block_start + block_rows
        scores = jnp.einsum(
            "qhd,khd->hqk",
            query_rows[block_start:block_end],
            key_rows[:block_end],
            preferred_element_type=jnp.float32,
        )
        scores = jnp.where(causal_mask(block_start, block_end), scores, -1e30)
        row_peak = jnp.max(scores, axis=-1, keepdims=True)
        exponent = jnp.exp(scores - row_peak)
        row_total = jnp.sum(exponent, axis=-1, keepdims=True)
        weights = (exponent / row_total).astype(jnp.bfloat16)
        outputs.append(
            jnp.einsum(
                "hqk,khd->qhd", weights, value_rows[:block_end], preferred_element_type=jnp.float32
            )
        )
        totals.append(row_peak + jnp.log(row_total))
    return (jnp.concatenate(outputs, axis=0), totals)


def attention_backward(query_rows, key_rows, value_rows, grad_mixed, totals):
    length = query_rows.shape[0]
    block_rows = min(512, length)
    grad_keys = jnp.zeros(key_rows.shape, jnp.float32)
    grad_values = jnp.zeros(value_rows.shape, jnp.float32)
    grad_queries = []
    for block_number, block_start in enumerate(range(0, length, block_rows)):
        block_end = block_start + block_rows
        query_block = query_rows[block_start:block_end]
        grad_block = grad_mixed[block_start:block_end]
        scores = jnp.einsum(
            "qhd,khd->hqk", query_block, key_rows[:block_end], preferred_element_type=jnp.float32
        )
        scores = jnp.where(causal_mask(block_start, block_end), scores, -1e30)
        probs_again = jnp.exp(scores - totals[block_number])
        weights = probs_again.astype(jnp.bfloat16)
        grad_probs = jnp.einsum(
            "qhd,khd->hqk", grad_block, value_rows[:block_end], preferred_element_type=jnp.float32
        )
        grad_scores = (
            probs_again * (grad_probs - jnp.sum(probs_again * grad_probs, axis=-1, keepdims=True))
        ).astype(jnp.bfloat16)
        grad_queries.append(
            jnp.einsum(
                "hqk,khd->qhd",
                grad_scores,
                key_rows[:block_end],
                preferred_element_type=jnp.float32,
            )
        )
        grad_keys = grad_keys.at[:block_end].add(
            jnp.einsum("hqk,qhd->khd", grad_scores, query_block, preferred_element_type=jnp.float32)
        )
        grad_values = grad_values.at[:block_end].add(
            jnp.einsum("hqk,qhd->khd", weights, grad_block, preferred_element_type=jnp.float32)
        )
    return (jnp.concatenate(grad_queries, axis=0), grad_keys, grad_values)


def swap(values, axis, bit):
    return lax.ppermute(values, axis, [(i, i ^ bit) for i in range(lax.axis_size(axis))])


def axis_bits(axis):
    size = lax.axis_size(axis)
    return [size >> (k + 1) for k in range(size.bit_length() - 1)]


def spread_sum(values, axis):
    for bit in axis_bits(axis)[::-1]:
        values = values + swap(values, axis, bit)
    return values


def plane_order(turn):
    bits = axis_bits("tensor")[:-1]
    if turn % 2:
        bits = bits[::-1]
    order = [0]
    for bit in bits:
        order = order + [bit ^ i for i in order]
    return bits, order


def plane_gather(piece, turn):
    bits, _ = plane_order(turn)
    pieces = [piece]
    for bit in bits:
        pieces = pieces + [swap(p, "tensor", bit) for p in pieces]
    near = jnp.concatenate(pieces, axis=0)
    return near, swap(near, "tensor", 1)


def plane_scatter(near, far, turn):
    bits, _ = plane_order(turn)
    total = near.astype(jnp.float32) + swap(far, "tensor", 1).astype(jnp.float32)
    for bit in bits[::-1]:
        half = total.shape[0] // 2
        sent = total[half:].astype(jnp.bfloat16)
        total = total[:half].astype(jnp.bfloat16).astype(jnp.float32) + swap(
            sent, "tensor", bit
        ).astype(jnp.float32)
    return total


def plane_rows(values, turn, own_rows, sorted_order=False):
    _, order = plane_order(turn)
    if sorted_order:
        order = sorted(order)
    index = lax.axis_index("tensor")

    def block(i):
        return lax.dynamic_slice_in_dim(values, (index ^ i) * own_rows, own_rows, 0)

    near = jnp.concatenate([block(i) for i in order], axis=0)
    far = jnp.concatenate([block(i ^ 1) for i in order], axis=0)
    return near, far


def natural_rows(near, far, turn, own_rows):
    _, order = plane_order(turn)
    index = lax.axis_index("tensor")
    both = jnp.concatenate([near, far], axis=0)
    place = {}
    for at, i in enumerate(order):
        place[i] = at
        place[i ^ 1] = at + len(order)
    table = jnp.array([place[i] for i in range(2 * len(order))], jnp.int32)
    return jnp.concatenate(
        [
            lax.dynamic_slice_in_dim(both, table[index ^ i] * own_rows, own_rows, 0)
            for i in range(2 * len(order))
        ],
        axis=0,
    )


def contract(left, right, left_dim, right_dim):
    return lax.dot_general(
        left, right, (((left_dim,), (right_dim,)), ((), ())), preferred_element_type=jnp.float32
    )


def tie(values, *after):
    return lax.optimization_barrier((values, *after))[0]


def stages(turn, bits):
    if turn % 2:
        bits = bits[::-1]
    found = [[] for _ in bits]
    order = [(0, ())]
    for bit in bits:
        order = order + [(bit ^ i, used + (bit,)) for i, used in order]
    for i, used in order[1:]:
        found[len(used) - 1].append((i, i ^ used[-1], used[-1]))
    return found


def gather_stage(pieces, turn, stage, bits, after=()):
    pieces = dict(pieces)
    for i, source, bit in stages(turn, bits)[stage]:
        sent = pieces[source]
        if after:
            sent = tie(sent, *after)
        pieces[i] = swap(sent, "tensor", bit)
    return pieces


def gather_all(piece, turn, bits):
    pieces = {0: piece}
    for stage in range(len(bits)):
        pieces = gather_stage(pieces, turn, stage, bits)
    return pieces


def scatter_stage(sums, turn, stage, bits, after=()):
    sums = dict(sums)
    for i, target, bit in stages(turn, bits)[len(bits) - 1 - stage]:
        sent = sums.pop(i).astype(jnp.bfloat16)
        if after:
            sent = tie(sent, *after)
        sums[target] = sums[target].astype(jnp.float32) + swap(sent, "tensor", bit).astype(
            jnp.float32
        )
    return sums


MEGABYTE = 1024 * 1024


def kernel_params():
    return pltpu.CompilerParams(vmem_limit_bytes=58 * MEGABYTE)


def cost(flops, moved):
    return pl.CostEstimate(flops=flops, bytes_accessed=moved, transcendentals=0)


def column_of(row):
    n = row.shape[1]
    down = lax.broadcasted_iota(jnp.int32, (n, n), 0)
    across = lax.broadcasted_iota(jnp.int32, (n, n), 1)
    return jnp.sum(jnp.where(down == across, row, 0.0), axis=1, keepdims=True)


def fixed(shape, single=True):
    if single:
        return pl.BlockSpec(
            shape, lambda *_: (0,) * len(shape), pipeline_mode=pl.Buffered(1)
        )
    return pl.BlockSpec(shape, lambda *_: (0,) * len(shape))


def expert_body(indices, local, place, scalars, *refs):
    count = len(indices)
    x_parts, refs = refs[:count], refs[count:]
    dy_source, kept, chosen, router, gates, ups, downs = refs[:7]
    core = scalars[0] & 1
    gate_own, gate_other = gates.at[core], gates.at[1 - core]
    up_own, up_other = ups.at[core], ups.at[1 - core]
    down_own, down_other = downs.at[core], downs.at[1 - core]
    scratch = refs[-13:]
    pieces, gate_out, dl_all, x_all, dy_all, act_all, own_dp, other_dp, gated_own, gated_other = refs[
        -23:-13
    ]
    rows, grads, wide, tall, raw, inner, act, slopes, gated, done, probs_ref, dots, sems = scratch
    rows_here, width = rows.shape
    units = gate_own.shape[1]
    own_rows = rows_here // count
    used = []
    dy_parts = []
    for i in indices:
        if local:
            at = pl.multiple_of((scalars[0] ^ i) * own_rows, own_rows)
            dy_parts.append(dy_source.at[pl.ds(at, own_rows)])
        else:
            dy_parts.append(dy_source.at[(scalars[0] ^ i) // 2, scalars[1]])

    def start(source, target):
        copy = pltpu.make_async_copy(source, target, sems.at[len(used)])
        used.append(copy)
        copy.start()
        return copy

    def spread(parts, target):
        size = rows_here // len(parts)
        return [start(part, target.at[pl.ds(at * size, size)]) for at, part in enumerate(parts)]

    x_copies = spread(x_parts, rows)
    order = [gate_own, up_own, gate_other, up_other]
    wide_copies = [
        start(weight, wide.at[:, pl.ds(at * units, units)]) for at, weight in enumerate(order[:2])
    ]
    dy_copies = spread(dy_parts, grads)
    tall_copies = [start(down_own, tall.at[pl.ds(0, units)])]
    wide_copies += [
        start(weight, wide.at[:, pl.ds((at + 2) * units, units)])
        for at, weight in enumerate(order[2:])
    ]
    tall_copies.append(start(down_other, tall.at[pl.ds(units, units)]))

    here_rows = pl.ds(place * rows_here, rows_here)
    for copy in x_copies:
        copy.wait()
    outgoing = [start(rows, x_all.at[here_rows])]
    logits = contract(rows[...], router[...], 1, 0)
    exponent = jnp.exp(logits - jnp.max(logits, axis=-1, keepdims=True))
    probs = exponent / jnp.sum(exponent, axis=-1, keepdims=True)
    kept_column = jnp.concatenate(
        [column_of(kept[scalars[1], pl.ds(scalars[0] ^ i, 1), :]) for i in indices], axis=0
    )
    probs_ref[...] = probs
    gate_out[...] = jnp.sum(probs * chosen[...], axis=-1, keepdims=True) * kept_column
    dots[...] = jnp.zeros_like(dots)

    block = min(64, rows_here)
    for half in range(2):
        columns = pl.ds(half * units, units)
        for part in range(2):
            at = 2 * half + part
            wide_copies[at].wait()
            raw[:, pl.ds(part * units, units)] = contract(
                rows[...], wide[:, pl.ds(at * units, units)], 1, 0
            )
        if half == 0:
            for copy in dy_copies:
                copy.wait()
            outgoing.append(start(grads, dy_all.at[here_rows]))
        tall_copies[half].wait()
        inner[...] = contract(grads[...], tall[columns, :], 1, 1)

        @pl.loop(0, rows_here // block)
        def _(at):
            here = pl.ds(at * block, block)
            pre_gate = raw[here, pl.ds(0, units)]
            pre_up = raw[here, pl.ds(units, units)]
            inward = inner[here, :]
            gate = gate_out[here, :]
            sigmoid_gate = 1.0 / (1.0 + jnp.exp(-pre_gate))
            silu_gate = pre_gate * sigmoid_gate
            active = (silu_gate * pre_up).astype(jnp.bfloat16)
            act[here, columns] = active
            active = active.astype(jnp.float32)
            gated[here, columns] = (gate * active).astype(jnp.bfloat16)
            dots[here, :] += jnp.sum(inward * active, axis=-1, keepdims=True)
            grad_active = gate * inward
            slopes[here, pl.ds(2 * half * units, units)] = (
                grad_active * pre_up * sigmoid_gate * (1.0 + pre_gate * (1.0 - sigmoid_gate))
            ).astype(jnp.bfloat16)
            slopes[here, pl.ds((2 * half + 1) * units, units)] = (grad_active * silu_gate).astype(
                jnp.bfloat16
            )

    outgoing += [
        start(act, act_all.at[here_rows]),
        start(slopes.at[:, pl.ds(0, 2 * units)], own_dp.at[here_rows]),
        start(slopes.at[:, pl.ds(2 * units, 2 * units)], other_dp.at[here_rows]),
        start(gated.at[:, pl.ds(0, units)], gated_own.at[here_rows]),
        start(gated.at[:, pl.ds(units, units)], gated_other.at[here_rows]),
    ]
    grad_logits = (dots[...] * gate_out[...] * (chosen[...] - probs_ref[...])).astype(jnp.bfloat16)
    dl_all[...] = grad_logits
    step = min(512, width)
    for at in range(width // step):
        columns = pl.ds(at * step, step)
        done[:, columns] = (
            contract(slopes[...], wide[columns, :], 1, 1)
            + contract(grad_logits, router[columns, :], 1, 1)
        ).astype(jnp.bfloat16)
    for at, i in enumerate(indices):
        to = (scalars[0] ^ i) // 2
        outgoing.append(start(done.at[pl.ds(at * own_rows, own_rows)], pieces.at[to]))
    for copy in outgoing:
        copy.wait()


def expert_chunk(
    place, places, x_pieces, dy_source, here, kept, chosen, router, gates, ups, downs, chain
):
    indices = sorted(x_pieces)
    count = len(indices)
    own_rows, width = x_pieces[0].shape
    rows = own_rows * count
    units = gates.shape[2]
    experts = router.shape[1]
    extra = () if chain is None else tuple(chain)
    hbm = pl.BlockSpec(memory_space=pl.ANY)
    first = count + 8
    kept_shapes = [
        (rows * places, experts),
        (rows * places, width),
        (rows * places, width),
        (rows * places, 2 * units),
        (rows * places, 2 * units),
        (rows * places, 2 * units),
        (rows * places, units),
        (rows * places, units),
    ]
    results = pl.pallas_call(
        lambda *refs: expert_body(indices, dy_source.ndim == 2, place, *refs),
        grid_spec=pltpu.PrefetchScalarGridSpec(
            num_scalar_prefetch=1,
            grid=(1,),
            in_specs=[hbm] * (count + 1)
            + [fixed(kept.shape), fixed((1, experts)), fixed((width, experts))]
            + [hbm] * (3 + len(extra)),
            out_specs=[hbm]
            + [
                fixed((rows, 1), False),
                pl.BlockSpec((rows, experts), lambda j, *_: (place, 0)),
            ]
            + [hbm] * 7,
            scratch_shapes=[
                pltpu.VMEM((rows, width), jnp.bfloat16),
                pltpu.VMEM((rows, width), jnp.bfloat16),
                pltpu.VMEM((width, 4 * units), jnp.bfloat16),
                pltpu.VMEM((2 * units, width), jnp.bfloat16),
                pltpu.VMEM((rows, 2 * units), jnp.float32),
                pltpu.VMEM((rows, units), jnp.float32),
                pltpu.VMEM((rows, 2 * units), jnp.bfloat16),
                pltpu.VMEM((rows, 4 * units), jnp.bfloat16),
                pltpu.VMEM((rows, 2 * units), jnp.bfloat16),
                pltpu.VMEM((rows, width), jnp.bfloat16),
                pltpu.VMEM((rows, experts), jnp.float32),
                pltpu.VMEM((rows, 1), jnp.float32),
                pltpu.SemaphoreType.DMA((3 * count + 13,)),
            ],
        ),
        out_shape=[jax.ShapeDtypeStruct((count, own_rows, width), jnp.bfloat16)]
        + [jax.ShapeDtypeStruct((rows, 1), jnp.float32)]
        + [jax.ShapeDtypeStruct(shape, jnp.bfloat16) for shape in kept_shapes],
        input_output_aliases={first + i: 2 + i for i in range(len(extra))},
        compiler_params=kernel_params(),
        cost_estimate=cost(20 * rows * width * units, 10 * rows * width + 12 * width * units),
        name="expert_chunk",
    )(
        here,
        *[x_pieces[i] for i in indices],
        dy_source,
        kept,
        chosen,
        router,
        gates,
        ups,
        downs,
        *extra,
    )
    return results[0], results[1], results[2:]


def input_grad_body(indices, own_rows, scalars, query_low, key_low, value_low, *refs):
    weights = refs[:3]
    pieces = refs[3:-2]
    done, sems = refs[-2:]
    width = done.shape[1]
    step = min(512, width)
    for at in range(width // step):
        columns = pl.ds(at * step, step)
        done[:, columns] = (
            contract(query_low[...], weights[0][columns, :], 1, 1)
            + contract(key_low[...], weights[1][columns, :], 1, 1)
            + contract(value_low[...], weights[2][columns, :], 1, 1)
        ).astype(jnp.bfloat16)
    copies = []
    for at, i in enumerate(indices):
        here = pl.ds(pl.multiple_of((scalars[0] ^ i) * own_rows, own_rows), own_rows)
        copies.append(pltpu.make_async_copy(done.at[here], pieces[at], sems.at[at]))
        copies[-1].start()
    for copy in copies:
        copy.wait()


def input_grad(here, indices, own_rows, lows, weights):
    width = weights[0].shape[0]
    rows = lows[0].shape[0]
    results = pl.pallas_call(
        lambda *refs: input_grad_body(indices, own_rows, *refs),
        grid_spec=pltpu.PrefetchScalarGridSpec(
            num_scalar_prefetch=1,
            grid=(1,),
            in_specs=[fixed(low.shape) for low in lows] + [fixed(w.shape) for w in weights],
            out_specs=[pl.BlockSpec(memory_space=pl.ANY)] * len(indices),
            scratch_shapes=[
                pltpu.VMEM((rows, width), jnp.bfloat16),
                pltpu.SemaphoreType.DMA((len(indices),)),
            ],
        ),
        out_shape=[jax.ShapeDtypeStruct((own_rows, width), jnp.bfloat16)] * len(indices),
        compiler_params=kernel_params(),
        cost_estimate=cost(6 * lows[0].size * width, 8 * lows[0].size * 8),
        name="input_grad",
    )(here, *lows, *weights)
    return dict(zip(indices, results))


def place_body(indices, own_rows, scalars, *refs):
    pieces, out, sems = refs[: len(indices)], refs[-2], refs[-1]
    copies = []
    for at, i in enumerate(indices):
        here = pl.ds(pl.multiple_of((scalars[0] ^ i) * own_rows, own_rows), own_rows)
        copies.append(pltpu.make_async_copy(pieces[at], out.at[here], sems.at[at]))
        copies[-1].start()
    for copy in copies:
        copy.wait()


def place_rows(here, pieces):
    indices = sorted(pieces)
    own_rows, width = pieces[0].shape
    return pl.pallas_call(
        lambda *refs: place_body(indices, own_rows, *refs),
        grid_spec=pltpu.PrefetchScalarGridSpec(
            num_scalar_prefetch=1,
            grid=(1,),
            in_specs=[fixed((own_rows, width))] * len(indices),
            out_specs=pl.BlockSpec(memory_space=pl.ANY),
            scratch_shapes=[pltpu.SemaphoreType.DMA((len(indices),))],
        ),
        out_shape=jax.ShapeDtypeStruct((own_rows * len(indices), width), pieces[0].dtype),
        compiler_params=kernel_params(),
        cost_estimate=cost(0, 4 * own_rows * len(indices) * width),
        name="place_rows",
    )(here, *[pieces[i] for i in indices])


def near_scatter(pieces):
    size = lax.axis_size("tensor")
    groups = [list(range(core, size, 2)) for core in range(2)]
    return lax.all_to_all(
        pieces, "tensor", split_axis=0, concat_axis=0, axis_index_groups=groups, tiled=True
    )


def line_sum(part, after):
    index = lax.axis_index("expert")
    bits = axis_bits("expert")[::-1]
    after = list(after) + [None] * (2 * len(bits))
    for bit in bits:
        half = part.shape[0] // 2
        high = (index // bit) % 2
        kept = lax.dynamic_slice_in_dim(part, high * half, half, 0)
        sent = lax.dynamic_slice_in_dim(part, (1 - high) * half, half, 0)
        wait = after.pop(0)
        if wait is not None:
            sent = tie(sent, wait)
        part = (
            kept.astype(jnp.float32) + swap(sent, "expert", bit).astype(jnp.float32)
        ).astype(jnp.bfloat16)
    for bit in bits[::-1]:
        high = (index // bit) % 2 == 1
        wait = after.pop(0)
        if wait is not None:
            part = tie(part, wait)
        other = swap(part, "expert", bit)
        part = jnp.concatenate([jnp.where(high, other, part), jnp.where(high, part, other)], axis=0)
    return part.astype(jnp.float32)


def send_body(indices, places, scalars, act, *refs):
    gates, (down_own, down_other), outs = refs[:places], refs[places : places + 2], refs[-places:]
    units = down_own.shape[1]
    value = contract(act[:, :units], down_own[0], 1, 0) + contract(
        act[:, units:], down_other[0], 1, 0
    )
    own_rows = outs[0].shape[1]
    for place in range(places):

        @pl.when(pl.program_id(1) == place)
        def _():
            sent = (gates[place][...] * value).astype(jnp.bfloat16)
            for at, i in enumerate(indices):
                outs[place][(scalars[0] ^ i) // 2] = sent[at * own_rows : (at + 1) * own_rows]


def expert_send(here, indices, act_all, gates, downs):
    rows = gates[0].shape[0]
    count = len(indices)
    places = len(gates)
    _, units, width = downs.shape
    block = min(1024, width // 2)
    return pl.pallas_call(
        lambda *refs: send_body(indices, places, *refs),
        grid_spec=pltpu.PrefetchScalarGridSpec(
            num_scalar_prefetch=1,
            grid=(width // block, places),
            in_specs=[pl.BlockSpec((rows, 2 * units), lambda j, k, *_: (k, 0))]
            + [fixed((rows, 1))] * places
            + [
                pl.BlockSpec((1, units, block), lambda j, k, at: (at[0] & 1, 0, j)),
                pl.BlockSpec((1, units, block), lambda j, k, at: (1 - (at[0] & 1), 0, j)),
            ],
            out_specs=[pl.BlockSpec((count, rows // count, block), lambda j, k, *_: (0, 0, j))]
            * places,
        ),
        out_shape=[jax.ShapeDtypeStruct((count, rows // count, width), jnp.bfloat16)] * places,
        compiler_params=kernel_params(),
        cost_estimate=cost(
            4 * places * rows * width * units, places * 4 * rows * width + 4 * width * units
        ),
        name="expert_send",
    )(here, act_all, *gates, downs, downs)


def project_body(indices, halves, scalars, mixed, tokens, gain, *refs):
    weights = refs[: len(indices) * halves]
    hidden_out, low_out = refs[-2:]
    total = tokens[...].astype(jnp.float32)
    depth = weights[0].shape[0]
    attn = None
    for at, i in enumerate(indices):
        piece = mixed[scalars[0] ^ i]
        for half in range(halves):
            part = contract(
                piece[:, half * depth : (half + 1) * depth], weights[at * halves + half][...], 1, 0
            )
            attn = part if attn is None else attn + part
    hidden = total + attn
    normal, _ = rms_forward(hidden)
    hidden_out[...] = hidden
    low_out[...] = (normal * gain[...]).astype(jnp.bfloat16)


def project_out(here, indices, mixed, tokens, gain, weights, halves):
    rows, width = tokens.shape
    return pl.pallas_call(
        lambda *refs: project_body(indices, halves, *refs),
        grid_spec=pltpu.PrefetchScalarGridSpec(
            num_scalar_prefetch=1,
            grid=(1,),
            in_specs=[fixed(mixed.shape), fixed(tokens.shape), fixed((1, width))]
            + [fixed(weights[0].shape)] * len(weights),
            out_specs=[fixed((rows, width), False), fixed((rows, width), False)],
        ),
        out_shape=[
            jax.ShapeDtypeStruct((rows, width), jnp.float32),
            jax.ShapeDtypeStruct((rows, width), jnp.bfloat16),
        ],
        compiler_params=kernel_params(),
        cost_estimate=cost(2 * rows * width * width, 2 * width * width),
        name="project_out",
    )(here, mixed, tokens, gain, *weights)


def turn_body(indices, halves, count, scalars, hidden, grad_out, gain, *refs):
    grads = refs[:count]
    weights = refs[count : count + len(indices) * halves]
    grad_hidden_out, low_out, mixed_out, gain_out = refs[-4:]
    grad_ffn = jnp.sum(grads[0][...].astype(jnp.float32), axis=0)
    for part in grads[1:]:
        grad_ffn = grad_ffn + part[...].astype(jnp.float32)
    normal, inverse = rms_forward(hidden[...])
    gain_out[...] = jnp.sum(grad_ffn * normal, axis=0, keepdims=True)
    scaled = grad_ffn * gain[...]
    grad_hidden = grad_out[...].astype(jnp.float32) + inverse * (
        scaled - normal * jnp.mean(scaled * normal, axis=-1, keepdims=True)
    )
    low = grad_hidden.astype(jnp.bfloat16)
    grad_hidden_out[...] = grad_hidden
    low_out[...] = low
    depth = weights[0].shape[0]
    for at, i in enumerate(indices):
        for half in range(halves):
            mixed_out[scalars[0] ^ i, :, half * depth : (half + 1) * depth] = contract(
                low, weights[at * halves + half][...], 1, 1
            ).astype(jnp.bfloat16)


def turn_back(here, indices, hidden, grad_out, gain, grads, weights, halves):
    rows, width = hidden.shape
    depth = weights[0].shape[0] * halves
    return pl.pallas_call(
        lambda *refs: turn_body(indices, halves, len(grads), *refs),
        grid_spec=pltpu.PrefetchScalarGridSpec(
            num_scalar_prefetch=1,
            grid=(1,),
            in_specs=[fixed((rows, width)), fixed((rows, width)), fixed((1, width))]
            + [fixed(part.shape) for part in grads]
            + [fixed(weights[0].shape)] * len(weights),
            out_specs=[
                fixed((rows, width), False),
                fixed((rows, width), False),
                fixed((len(indices), rows, depth), False),
                fixed((1, width), False),
            ],
        ),
        out_shape=[
            jax.ShapeDtypeStruct((rows, width), jnp.float32),
            jax.ShapeDtypeStruct((rows, width), jnp.bfloat16),
            jax.ShapeDtypeStruct((len(indices), rows, depth), jnp.bfloat16),
            jax.ShapeDtypeStruct((1, width), jnp.float32),
        ],
        compiler_params=kernel_params(),
        cost_estimate=cost(2 * rows * width * width, 2 * width * width),
        name="turn_back",
    )(here, hidden, grad_out, gain, *grads, *weights)


def on_device(
    tokens,
    positions,
    routes,
    slot_ids,
    attn_gain,
    w_query,
    w_key,
    w_value,
    query_gain,
    key_gain,
    w_out,
    ffn_gain,
    router,
    w_gate,
    w_up,
    w_down,
    grad_out,
):
    tensor_size = lax.axis_size("tensor")
    expert_size = lax.axis_size("expert")
    local_count = tensor_size // 2
    tensor_index = lax.axis_index("tensor")
    expert_index = lax.axis_index("expert")
    own_local = tensor_index // 2
    own_expert = expert_index * local_count + own_local
    length, model_width = tokens.shape
    heads_here = w_query.shape[1] // HEAD_DIM
    full_cols = w_query.shape[1] * tensor_size
    expert_count = router.shape[1]
    capacity = 3 * length * TOP // (2 * expert_count)
    own_rows = length // tensor_size
    chunks = [0] + list(range(2, expert_size)) + [1]
    bits = axis_bits("tensor")
    near_bits = bits[:-1]
    last = len(near_bits)

    def own_slice(rows):
        return lax.dynamic_slice_in_dim(rows, tensor_index * own_rows, own_rows, 0)

    near_groups = [list(range(core, tensor_size, 2)) for core in range(2)]
    pairs = [[2 * i, 2 * i + 1] for i in range(tensor_size // 2)]
    gates, ups, downs = [
        lax.all_gather(weights[0], "tensor", axis_index_groups=pairs)
        for weights in (w_gate, w_up, w_down)
    ]
    grad_own = own_slice(grad_out)
    grad_all = lax.all_gather(
        lax.all_gather(grad_own, "expert"), "tensor", axis_index_groups=near_groups
    )
    out_pieces = {0: w_out}
    for stage in range(len(bits)):
        out_pieces = gather_stage(out_pieces, 0, stage, bits)
    all_indices = sorted(out_pieces)
    out_weights = [out_pieces[i] for i in all_indices]
    first_out = [out_pieces[i] for i in all_indices if i in near_bits]
    last_out = out_pieces[2 * (tensor_size // 2 - 1)]
    expert_iota = jnp.arange(expert_count, dtype=jnp.int32)
    kept_table = jnp.sum(
        (
            (routes.T[:, None, :] == expert_iota[None, :, None]) & (slot_ids.T < capacity)[:, None, :]
        ).astype(jnp.float32),
        axis=0,
    )
    targets = jnp.arange(expert_size, dtype=jnp.int32) * local_count + own_local
    kept_rows = lax.all_to_all(
        jnp.take(kept_table, targets, axis=0).reshape(expert_size, tensor_size, own_rows),
        "expert",
        split_axis=0,
        concat_axis=0,
        tiled=True,
    )

    def here(chunk):
        return jnp.stack([tensor_index, expert_index ^ chunk]).astype(jnp.int32)

    score_scale = HEAD_DIM ** (-0.5)
    half_dim = HEAD_DIM // 2
    frequency = THETA ** (-2.0 * jnp.arange(half_dim, dtype=jnp.float32) / HEAD_DIM)
    angles = positions.astype(jnp.float32)[:, None] * frequency[None, :]
    cosine_table = jnp.cos(angles)[:, None, :]
    sine_table = jnp.sin(angles)[:, None, :]
    token_float = tokens.astype(jnp.float32)
    attn_normal, attn_inverse = rms_forward(token_float)
    attn_in = (attn_normal * attn_gain).astype(jnp.bfloat16)
    head_shape = (length, heads_here, HEAD_DIM)
    query_raw = jnp.dot(attn_in, w_query, preferred_element_type=jnp.float32).reshape(head_shape)
    key_raw = jnp.dot(attn_in, w_key, preferred_element_type=jnp.float32).reshape(head_shape)
    value_rows = (
        jnp.dot(attn_in, w_value, preferred_element_type=jnp.float32)
        .astype(jnp.bfloat16)
        .reshape(head_shape)
    )
    query_scale = query_gain.reshape(heads_here, HEAD_DIM)
    key_scale = key_gain.reshape(heads_here, HEAD_DIM)
    square_sums = jnp.stack(
        [jnp.sum(query_raw * query_raw, axis=(1, 2)), jnp.sum(key_raw * key_raw, axis=(1, 2))]
    )
    for at, bit in enumerate(bits[::-1]):
        if at == len(bits) - 1:
            square_sums = tie(square_sums, *first_out)
        square_sums = square_sums + swap(square_sums, "tensor", bit)
    query_inverse = lax.rsqrt(square_sums[0] / full_cols + EPS)[:, None, None]
    key_inverse = lax.rsqrt(square_sums[1] / full_cols + EPS)[:, None, None]
    query_normal = query_raw * query_inverse
    key_normal = key_raw * key_inverse
    query_rows = (
        rotary(query_normal * query_scale, cosine_table, sine_table) * score_scale
    ).astype(jnp.bfloat16)
    key_rows = rotary(key_normal * key_scale, cosine_table, sine_table).astype(jnp.bfloat16)
    mixed_heads, totals = attention_forward(query_rows, key_rows, value_rows)
    mixed_low = mixed_heads.reshape(length, heads_here * HEAD_DIM).astype(jnp.bfloat16)
    mixed_low = tie(mixed_low, last_out)
    mixed_own = lax.all_to_all(
        mixed_low.reshape(tensor_size, own_rows, -1), "tensor", split_axis=0, concat_axis=0, tiled=True
    )
    hidden, ffn_in = project_out(
        here(0), all_indices, mixed_own, own_slice(tokens), ffn_gain[None, :], out_weights, 1
    )
    chosen = (expert_iota == own_expert).astype(jnp.float32)[None, :]
    gathered = [
        {0: ffn_in if chunk == 0 else swap(ffn_in, "expert", chunk)} for chunk in chunks
    ]
    chain = None
    sums = []
    gate_columns = []
    for at, chunk in enumerate(chunks):
        for stage in range(last):
            before = at - last - 1 + stage
            after = (gate_columns[before],) if before >= 0 else ()
            gathered[at] = gather_stage(gathered[at], at, stage, near_bits, after)
        scalars = here(chunk)
        if at >= 2:
            scalars = tie(scalars, sums[at - 2])
        pieces, gate_column, chain = expert_chunk(
            at,
            expert_size,
            gathered[at],
            grad_all if chunk else grad_out,
            scalars,
            kept_rows,
            chosen,
            router,
            gates,
            ups,
            downs,
            chain,
        )
        gate_columns.append(gate_column)
        sums.append(near_scatter(pieces))

    def plane_total(near):
        return jnp.sum(near.astype(jnp.float32), axis=0).astype(jnp.bfloat16)

    row_totals = [plane_total(near) for near in sums[1:]]
    grad_parts = [sums[0]] + [
        swap(total, "expert", chunk) for total, chunk in zip(row_totals, chunks[1:])
    ]
    indices = sorted(gathered[0])
    dl_all, x_all, dy_all, act_all, own_dp, other_dp, gated_own, gated_other = chain
    sent_pieces = expert_send(tie(here(0), row_totals[-1]), indices, act_all, gate_columns, downs)
    grad_hidden, hidden_low, grad_mixed_own, grad_ffn_gain = turn_back(
        here(0), all_indices, hidden, grad_own, ffn_gain[None, :], grad_parts, out_weights, 1
    )
    grad_mixed = lax.all_to_all(
        grad_mixed_own, "tensor", split_axis=0, concat_axis=0, tiled=True
    ).reshape(head_shape)

    sent_near = []
    for at, pieces in enumerate(sent_pieces):
        sent_near.append(near_scatter(tie(pieces, grad_mixed) if at else pieces))
    units = own_dp.shape[1] // 2
    other_wide = swap(contract(x_all, other_dp, 0, 0).astype(jnp.bfloat16), "tensor", 1)
    other_down = swap(contract(gated_other, dy_all, 0, 0).astype(jnp.bfloat16), "tensor", 1)
    grad_gate_w = contract(x_all, own_dp[:, :units], 0, 0) + other_wide[:, :units].astype(jnp.float32)
    grad_up_w = contract(x_all, own_dp[:, units:], 0, 0) + other_wide[:, units:].astype(jnp.float32)
    grad_down = contract(gated_own, dy_all, 0, 0) + other_down.astype(jnp.float32)
    grad_router_part = contract(dl_all, x_all, 0, 0)

    hidden_low_all = lax.all_gather(hidden_low, "tensor", axis=0, tiled=True)
    grad_w_out = contract(mixed_low, hidden_low_all, 0, 0)
    grad_query, grad_key, grad_value_attn = attention_backward(
        query_rows, key_rows, value_rows, grad_mixed, totals
    )
    grad_query_normed = rotary(grad_query * score_scale, cosine_table, -sine_table)
    grad_key_normed = rotary(grad_key, cosine_table, -sine_table)
    grad_query_scale = jnp.sum(grad_query_normed * query_normal, axis=0)
    grad_key_scale = jnp.sum(grad_key_normed * key_normal, axis=0)
    query_scaled = grad_query_normed * query_scale
    key_scaled = grad_key_normed * key_scale
    inner_sums = spread_sum(
        jnp.stack(
            [
                jnp.sum(query_scaled * query_normal, axis=(1, 2)),
                jnp.sum(key_scaled * key_normal, axis=(1, 2)),
            ]
        ),
        "tensor",
    )
    grad_query_raw = query_inverse * (
        query_scaled - query_normal * (inner_sums[0] / full_cols)[:, None, None]
    )
    grad_key_raw = key_inverse * (
        key_scaled - key_normal * (inner_sums[1] / full_cols)[:, None, None]
    )
    query_low = grad_query_raw.reshape(length, heads_here * HEAD_DIM).astype(jnp.bfloat16)
    key_low = grad_key_raw.reshape(length, heads_here * HEAD_DIM).astype(jnp.bfloat16)
    value_low = grad_value_attn.reshape(length, heads_here * HEAD_DIM).astype(jnp.bfloat16)
    grad_w_query = jnp.einsum("td,tq->dq", attn_in, query_low, preferred_element_type=jnp.float32)
    grad_w_key = jnp.einsum("td,tq->dq", attn_in, key_low, preferred_element_type=jnp.float32)
    grad_w_value = jnp.einsum("td,tq->dq", attn_in, value_low, preferred_element_type=jnp.float32)
    grad_attn = input_grad(
        here(0), all_indices, own_rows, (query_low, key_low, value_low), (w_query, w_key, w_value)
    )
    for stage in range(len(bits)):
        grad_attn = scatter_stage(grad_attn, 0, stage, bits)
    grad_token_part, grad_attn_gain = rms_backward(
        grad_attn[0], own_slice(attn_normal), own_slice(attn_inverse), attn_gain
    )
    token_pieces = [{0: (grad_hidden + grad_token_part).astype(jnp.bfloat16)}]
    for stage in range(len(bits)):
        token_pieces.append(gather_stage(token_pieces[-1], 0, stage, bits))
    grad_tokens = place_rows(here(0), token_pieces[-1])
    late = token_pieces[2][bits[0] ^ bits[1]]
    moe_sum = hidden
    for at, chunk in enumerate(chunks):
        near = tie(sent_near[at], grad_attn[0])
        if chunk:
            moe_sum = moe_sum + swap(plane_total(near), "expert", chunk).astype(jnp.float32)
        else:
            moe_sum = moe_sum + jnp.sum(near.astype(jnp.float32), axis=0)
    output = place_rows(
        here(0), gather_all(tie(moe_sum.astype(jnp.bfloat16), late), 1, bits)
    )
    waits = [None, grad_attn[0], late]
    sum_query = line_sum(grad_w_query.astype(jnp.bfloat16), waits)
    sum_key = line_sum(grad_w_key.astype(jnp.bfloat16), waits)
    sum_value, sum_out = [
        part.astype(jnp.float32)
        for part in lax.psum(
            (grad_w_value.astype(jnp.bfloat16), grad_w_out.astype(jnp.bfloat16)), "expert"
        )
    ]
    plane_sums = spread_sum(
        jnp.concatenate([grad_router_part, grad_ffn_gain, grad_attn_gain[None, :]], axis=0), "tensor"
    )
    scales = jnp.concatenate([grad_query_scale.reshape(-1), grad_key_scale.reshape(-1)])
    scales = jnp.pad(scales, (0, model_width - scales.shape[0]))
    all_sums = spread_sum(jnp.concatenate([plane_sums, scales[None, :]], axis=0), "expert")
    columns_here = w_query.shape[1]
    return (
        output,
        grad_tokens,
        all_sums[expert_count + 1],
        sum_query,
        sum_key,
        sum_value,
        all_sums[expert_count + 2, :columns_here],
        all_sums[expert_count + 2, columns_here : 2 * columns_here],
        sum_out,
        all_sums[expert_count],
        all_sums[:expert_count].T,
        grad_gate_w[None],
        grad_up_w[None],
        grad_down[None],
    )


def solution(mesh):
    placed = (
        P("expert", None),
        P("expert"),
        P("expert", None),
        P("expert", None),
        P(),
        P(None, "tensor"),
        P(None, "tensor"),
        P(None, "tensor"),
        P("tensor"),
        P("tensor"),
        P("tensor", None),
        P(),
        P(),
        P(("expert", "tensor"), None, None),
        P(("expert", "tensor"), None, None),
        P(("expert", "tensor"), None, None),
        P("expert", None),
    )
    return jax.shard_map(
        on_device,
        mesh=mesh,
        in_specs=placed,
        out_specs=(
            P("expert", None),
            P("expert", None),
            P(),
            P(None, "tensor"),
            P(None, "tensor"),
            P(None, "tensor"),
            P("tensor"),
            P("tensor"),
            P("tensor", None),
            P(),
            P(),
            P(("expert", "tensor"), None, None),
            P(("expert", "tensor"), None, None),
            P(("expert", "tensor"), None, None),
        ),
        check_vma=False,
    )
```

```python
import jax
import jax.numpy as jnp
from jax import lax
from jax.experimental import pallas as pl
from jax.experimental.pallas import tpu as pltpu
from jax.sharding import PartitionSpec as P

HEAD_DIM = 128
TOP = 8


EPS = 1e-05
THETA = 10000.0


def rms_forward(values):
    inverse = lax.rsqrt(jnp.mean(values * values, axis=-1, keepdims=True) + EPS)
    return (values * inverse, inverse)


def rms_backward(grad_normed, normal_rows, inverse, gain_row):
    gain_grad = jnp.sum(grad_normed * normal_rows, axis=0)
    scaled = grad_normed * gain_row
    grad_rows = inverse * (
        scaled - normal_rows * jnp.mean(scaled * normal_rows, axis=-1, keepdims=True)
    )
    return (grad_rows, gain_grad)


def swap(values, axis, bit):
    return lax.ppermute(values, axis, [(i, i ^ bit) for i in range(lax.axis_size(axis))])


def axis_bits(axis):
    size = lax.axis_size(axis)
    return [size >> (k + 1) for k in range(size.bit_length() - 1)]


def spread_sum(values, axis):
    for bit in axis_bits(axis)[::-1]:
        values = values + swap(values, axis, bit)
    return values


def plane_order(turn):
    bits = axis_bits("tensor")[:-1]
    if turn % 2:
        bits = bits[::-1]
    order = [0]
    for bit in bits:
        order = order + [bit ^ i for i in order]
    return bits, order


def plane_gather(piece, turn):
    bits, _ = plane_order(turn)
    pieces = [piece]
    for bit in bits:
        pieces = pieces + [swap(p, "tensor", bit) for p in pieces]
    near = jnp.concatenate(pieces, axis=0)
    return near, swap(near, "tensor", 1)


def plane_scatter(near, far, turn):
    bits, _ = plane_order(turn)
    total = near.astype(jnp.float32) + swap(far, "tensor", 1).astype(jnp.float32)
    for bit in bits[::-1]:
        half = total.shape[0] // 2
        sent = total[half:].astype(jnp.bfloat16)
        total = total[:half].astype(jnp.bfloat16).astype(jnp.float32) + swap(
            sent, "tensor", bit
        ).astype(jnp.float32)
    return total


def plane_rows(values, turn, own_rows, sorted_order=False):
    _, order = plane_order(turn)
    if sorted_order:
        order = sorted(order)
    index = lax.axis_index("tensor")

    def block(i):
        return lax.dynamic_slice_in_dim(values, (index ^ i) * own_rows, own_rows, 0)

    near = jnp.concatenate([block(i) for i in order], axis=0)
    far = jnp.concatenate([block(i ^ 1) for i in order], axis=0)
    return near, far


def natural_rows(near, far, turn, own_rows):
    _, order = plane_order(turn)
    index = lax.axis_index("tensor")
    both = jnp.concatenate([near, far], axis=0)
    place = {}
    for at, i in enumerate(order):
        place[i] = at
        place[i ^ 1] = at + len(order)
    table = jnp.array([place[i] for i in range(2 * len(order))], jnp.int32)
    return jnp.concatenate(
        [
            lax.dynamic_slice_in_dim(both, table[index ^ i] * own_rows, own_rows, 0)
            for i in range(2 * len(order))
        ],
        axis=0,
    )


def contract(left, right, left_dim, right_dim):
    return lax.dot_general(
        left, right, (((left_dim,), (right_dim,)), ((), ())), preferred_element_type=jnp.float32
    )


def tie(values, *after):
    return lax.optimization_barrier((values, *after))[0]


def stages(turn, bits):
    if turn % 2:
        bits = bits[::-1]
    found = [[] for _ in bits]
    order = [(0, ())]
    for bit in bits:
        order = order + [(bit ^ i, used + (bit,)) for i, used in order]
    for i, used in order[1:]:
        found[len(used) - 1].append((i, i ^ used[-1], used[-1]))
    return found


def gather_stage(pieces, turn, stage, bits, after=()):
    pieces = dict(pieces)
    for i, source, bit in stages(turn, bits)[stage]:
        sent = pieces[source]
        if after:
            sent = tie(sent, *after)
        pieces[i] = swap(sent, "tensor", bit)
    return pieces


def direct_gather(piece, bits, after=()):
    pieces = {0: piece}
    combos = [0]
    for bit in bits:
        combos = combos + [bit ^ i for i in combos]
    for i in combos[1:]:
        pieces[i] = swap(tie(piece, *after) if after else piece, "tensor", i)
    return pieces


def gather_all(piece, turn, bits):
    pieces = {0: piece}
    for stage in range(len(bits)):
        pieces = gather_stage(pieces, turn, stage, bits)
    return pieces


def scatter_stage(sums, turn, stage, bits, after=()):
    sums = dict(sums)
    for i, target, bit in stages(turn, bits)[len(bits) - 1 - stage]:
        sent = sums.pop(i).astype(jnp.bfloat16)
        if after:
            sent = tie(sent, *after)
        sums[target] = sums[target].astype(jnp.float32) + swap(sent, "tensor", bit).astype(
            jnp.float32
        )
    return sums


MEGABYTE = 1024 * 1024


def kernel_params():
    return pltpu.CompilerParams(vmem_limit_bytes=58 * MEGABYTE)


def cost(flops, moved):
    return pl.CostEstimate(flops=flops, bytes_accessed=moved, transcendentals=0)


def column_of(row):
    n = row.shape[1]
    down = lax.broadcasted_iota(jnp.int32, (n, n), 0)
    across = lax.broadcasted_iota(jnp.int32, (n, n), 1)
    return jnp.sum(jnp.where(down == across, row, 0.0), axis=1, keepdims=True)


def fixed(shape, single=True):
    if single:
        return pl.BlockSpec(
            shape, lambda *_: (0,) * len(shape), pipeline_mode=pl.Buffered(1)
        )
    return pl.BlockSpec(shape, lambda *_: (0,) * len(shape))


def expert_body(indices, local, place, scalars, *refs):
    count = len(indices)
    x_parts, refs = refs[:count], refs[count:]
    dy_source, kept, chosen, router, gates, ups, downs = refs[:7]
    core = scalars[0] & 1
    gate_own, gate_other = gates.at[core], gates.at[1 - core]
    up_own, up_other = ups.at[core], ups.at[1 - core]
    down_own, down_other = downs.at[core], downs.at[1 - core]
    scratch = refs[-13:]
    pieces, gate_out, dl_all, x_all, dy_all, act_all, own_dp, other_dp, gated_own, gated_other = refs[
        -23:-13
    ]
    rows, grads, wide, tall, raw, inner, act, slopes, gated, done, probs_ref, dots, sems = scratch
    rows_here, width = rows.shape
    units = gate_own.shape[1]
    own_rows = rows_here // count
    used = []
    dy_parts = []
    for i in indices:
        if local:
            at = pl.multiple_of((scalars[0] ^ i) * own_rows, own_rows)
            dy_parts.append(dy_source.at[pl.ds(at, own_rows)])
        else:
            dy_parts.append(dy_source.at[scalars[2], pl.ds(len(dy_parts) * own_rows, own_rows)])

    def start(source, target):
        copy = pltpu.make_async_copy(source, target, sems.at[len(used)])
        used.append(copy)
        copy.start()
        return copy

    def spread(parts, target):
        size = rows_here // len(parts)
        return [start(part, target.at[pl.ds(at * size, size)]) for at, part in enumerate(parts)]

    x_copies = spread(x_parts, rows)
    order = [gate_own, up_own, gate_other, up_other]
    wide_copies = [
        start(weight, wide.at[:, pl.ds(at * units, units)]) for at, weight in enumerate(order[:2])
    ]
    dy_copies = spread(dy_parts, grads)
    tall_copies = [start(down_own, tall.at[pl.ds(0, units)])]
    wide_copies += [
        start(weight, wide.at[:, pl.ds((at + 2) * units, units)])
        for at, weight in enumerate(order[2:])
    ]
    tall_copies.append(start(down_other, tall.at[pl.ds(units, units)]))

    here_rows = pl.ds(place * rows_here, rows_here)
    for copy in x_copies:
        copy.wait()
    outgoing = [start(rows, x_all.at[here_rows])]
    logits = contract(rows[...], router[...], 1, 0)
    exponent = jnp.exp(logits - jnp.max(logits, axis=-1, keepdims=True))
    probs = exponent / jnp.sum(exponent, axis=-1, keepdims=True)
    kept_column = jnp.concatenate(
        [column_of(kept[scalars[1], pl.ds(scalars[0] ^ i, 1), :]) for i in indices], axis=0
    )
    probs_ref[...] = probs
    gate_out[...] = jnp.sum(probs * chosen[...], axis=-1, keepdims=True) * kept_column
    dots[...] = jnp.zeros_like(dots)

    block = min(64, rows_here)
    for half in range(2):
        columns = pl.ds(half * units, units)
        for part in range(2):
            at = 2 * half + part
            wide_copies[at].wait()
            raw[:, pl.ds(part * units, units)] = contract(
                rows[...], wide[:, pl.ds(at * units, units)], 1, 0
            )
        if half == 0:
            for copy in dy_copies:
                copy.wait()
            outgoing.append(start(grads, dy_all.at[here_rows]))
        tall_copies[half].wait()
        inner[...] = contract(grads[...], tall[columns, :], 1, 1)

        @pl.loop(0, rows_here // block)
        def _(at):
            here = pl.ds(at * block, block)
            pre_gate = raw[here, pl.ds(0, units)]
            pre_up = raw[here, pl.ds(units, units)]
            inward = inner[here, :]
            gate = gate_out[here, :]
            sigmoid_gate = 1.0 / (1.0 + jnp.exp(-pre_gate))
            silu_gate = pre_gate * sigmoid_gate
            active = (silu_gate * pre_up).astype(jnp.bfloat16)
            act[here, columns] = active
            active = active.astype(jnp.float32)
            gated[here, columns] = (gate * active).astype(jnp.bfloat16)
            dots[here, :] += jnp.sum(inward * active, axis=-1, keepdims=True)
            grad_active = gate * inward
            slopes[here, pl.ds(2 * half * units, units)] = (
                grad_active * pre_up * sigmoid_gate * (1.0 + pre_gate * (1.0 - sigmoid_gate))
            ).astype(jnp.bfloat16)
            slopes[here, pl.ds((2 * half + 1) * units, units)] = (grad_active * silu_gate).astype(
                jnp.bfloat16
            )

    outgoing += [
        start(act, act_all.at[here_rows]),
        start(slopes.at[:, pl.ds(0, 2 * units)], own_dp.at[here_rows]),
        start(slopes.at[:, pl.ds(2 * units, 2 * units)], other_dp.at[here_rows]),
        start(gated.at[:, pl.ds(0, units)], gated_own.at[here_rows]),
        start(gated.at[:, pl.ds(units, units)], gated_other.at[here_rows]),
    ]
    grad_logits = (dots[...] * gate_out[...] * (chosen[...] - probs_ref[...])).astype(jnp.bfloat16)
    dl_all[...] = grad_logits
    step = min(512, width)
    for at in range(width // step):
        columns = pl.ds(at * step, step)
        done[:, columns] = (
            contract(slopes[...], wide[columns, :], 1, 1)
            + contract(grad_logits, router[columns, :], 1, 1)
        ).astype(jnp.bfloat16)
    for at, i in enumerate(indices):
        to = (scalars[0] ^ i) // 2
        outgoing.append(start(done.at[pl.ds(at * own_rows, own_rows)], pieces.at[to]))
    for copy in outgoing:
        copy.wait()


def expert_chunk(
    place, places, x_pieces, dy_source, here, kept, chosen, router, gates, ups, downs, chain
):
    indices = sorted(x_pieces)
    count = len(indices)
    own_rows, width = x_pieces[0].shape
    rows = own_rows * count
    units = gates.shape[2]
    experts = router.shape[1]
    extra = () if chain is None else tuple(chain)
    hbm = pl.BlockSpec(memory_space=pl.ANY)
    first = count + 8
    kept_shapes = [
        (rows * places, experts),
        (rows * places, width),
        (rows * places, width),
        (rows * places, 2 * units),
        (rows * places, 2 * units),
        (rows * places, 2 * units),
        (rows * places, units),
        (rows * places, units),
    ]
    results = pl.pallas_call(
        lambda *refs: expert_body(indices, dy_source.ndim == 2, place, *refs),
        grid_spec=pltpu.PrefetchScalarGridSpec(
            num_scalar_prefetch=1,
            grid=(1,),
            in_specs=[hbm] * (count + 1)
            + [fixed(kept.shape), fixed((1, experts)), fixed((width, experts))]
            + [hbm] * (3 + len(extra)),
            out_specs=[hbm]
            + [
                fixed((rows, 1), False),
                pl.BlockSpec((rows, experts), lambda j, *_: (place, 0)),
            ]
            + [hbm] * 7,
            scratch_shapes=[
                pltpu.VMEM((rows, width), jnp.bfloat16),
                pltpu.VMEM((rows, width), jnp.bfloat16),
                pltpu.VMEM((width, 4 * units), jnp.bfloat16),
                pltpu.VMEM((2 * units, width), jnp.bfloat16),
                pltpu.VMEM((rows, 2 * units), jnp.float32),
                pltpu.VMEM((rows, units), jnp.float32),
                pltpu.VMEM((rows, 2 * units), jnp.bfloat16),
                pltpu.VMEM((rows, 4 * units), jnp.bfloat16),
                pltpu.VMEM((rows, 2 * units), jnp.bfloat16),
                pltpu.VMEM((rows, width), jnp.bfloat16),
                pltpu.VMEM((rows, experts), jnp.float32),
                pltpu.VMEM((rows, 1), jnp.float32),
                pltpu.SemaphoreType.DMA((3 * count + 13,)),
            ],
        ),
        out_shape=[jax.ShapeDtypeStruct((count, own_rows, width), jnp.bfloat16)]
        + [jax.ShapeDtypeStruct((rows, 1), jnp.float32)]
        + [jax.ShapeDtypeStruct(shape, jnp.bfloat16) for shape in kept_shapes],
        input_output_aliases={first + i: 2 + i for i in range(len(extra))},
        compiler_params=kernel_params(),
        cost_estimate=cost(80 * rows * width * units, 10 * rows * width + 12 * width * units),
        name="expert_chunk",
    )(
        here,
        *[x_pieces[i] for i in indices],
        dy_source,
        kept,
        chosen,
        router,
        gates,
        ups,
        downs,
        *extra,
    )
    return results[0], results[1], results[2:]


def input_grad_body(indices, own_rows, full_cols, scalars, *refs):
    (query_scaled, key_scaled, value_low, query_raw, key_raw) = refs[:5]
    query_inv, key_inv, query_inner, key_inner = refs[5:9]
    weights = refs[9:12]
    pieces = refs[12 : 12 + len(indices)]
    query_low, key_low, done, sems = refs[12 + len(indices) :]
    for scaled, raw, inverse, inner, low in (
        (query_scaled, query_raw, query_inv, query_inner, query_low),
        (key_scaled, key_raw, key_inv, key_inner, key_low),
    ):
        normal = raw[...] * inverse[...]
        low[...] = (inverse[...] * (scaled[...] - normal * (inner[...] / full_cols))).astype(
            jnp.bfloat16
        )
    width = done.shape[1]
    step = min(512, width)
    for at in range(width // step):
        columns = pl.ds(at * step, step)
        done[:, columns] = (
            contract(query_low[...], weights[0][columns, :], 1, 1)
            + contract(key_low[...], weights[1][columns, :], 1, 1)
            + contract(value_low[...], weights[2][columns, :], 1, 1)
        ).astype(jnp.bfloat16)
    copies = []
    for at, i in enumerate(indices):
        here = pl.ds(pl.multiple_of((scalars[0] ^ i) * own_rows, own_rows), own_rows)
        copies.append(pltpu.make_async_copy(done.at[here], pieces[at], sems.at[at]))
        copies[-1].start()
    for copy in copies:
        copy.wait()


def input_grad(here, indices, own_rows, full_cols, parts, weights):
    width = weights[0].shape[0]
    rows, columns = parts[0].shape
    low = jax.ShapeDtypeStruct((rows, columns), jnp.bfloat16)
    results = pl.pallas_call(
        lambda *refs: input_grad_body(indices, own_rows, full_cols, *refs),
        grid_spec=pltpu.PrefetchScalarGridSpec(
            num_scalar_prefetch=1,
            grid=(1,),
            in_specs=[fixed(part.shape) for part in parts] + [fixed(w.shape) for w in weights],
            out_specs=[pl.BlockSpec(memory_space=pl.ANY)] * len(indices)
            + [fixed((rows, columns), False)] * 2,
            scratch_shapes=[
                pltpu.VMEM((rows, width), jnp.bfloat16),
                pltpu.SemaphoreType.DMA((len(indices),)),
            ],
        ),
        out_shape=[jax.ShapeDtypeStruct((own_rows, width), jnp.bfloat16)] * len(indices)
        + [low, low],
        compiler_params=kernel_params(),
        cost_estimate=cost(6 * parts[0].size * width, 8 * parts[0].size * 8),
        name="input_grad",
    )(here, *parts, *weights)
    return dict(zip(indices, results[: len(indices)])), results[-2], results[-1]


def place_body(indices, own_rows, scalars, *refs):
    pieces, out, sems = refs[: len(indices)], refs[-2], refs[-1]
    copies = []
    for at, i in enumerate(indices):
        here = pl.ds(pl.multiple_of((scalars[0] ^ i) * own_rows, own_rows), own_rows)
        copies.append(pltpu.make_async_copy(pieces[at], out.at[here], sems.at[at]))
        copies[-1].start()
    for copy in copies:
        copy.wait()


def place_rows(here, pieces):
    indices = sorted(pieces)
    own_rows, width = pieces[0].shape
    return pl.pallas_call(
        lambda *refs: place_body(indices, own_rows, *refs),
        grid_spec=pltpu.PrefetchScalarGridSpec(
            num_scalar_prefetch=1,
            grid=(1,),
            in_specs=[fixed((own_rows, width))] * len(indices),
            out_specs=pl.BlockSpec(memory_space=pl.ANY),
            scratch_shapes=[pltpu.SemaphoreType.DMA((len(indices),))],
        ),
        out_shape=jax.ShapeDtypeStruct((own_rows * len(indices), width), pieces[0].dtype),
        compiler_params=kernel_params(),
        cost_estimate=cost(0, 4 * own_rows * len(indices) * width),
        name="place_rows",
    )(here, *[pieces[i] for i in indices])


def turned(values, cosine, sine):
    return values * cosine + pltpu.roll(values, values.shape[1] // 2, 1) * sine


def head_blocks(length):
    block = min(256, length)
    return [(start, start + block) for start in range(0, length, block)]


def block_probs(queries, keys, start, end):
    scores = contract(queries, keys, 1, 1)
    down = lax.broadcasted_iota(jnp.int32, scores.shape, 0) + start
    across = lax.broadcasted_iota(jnp.int32, scores.shape, 1)
    scores = jnp.where(down >= across, scores, -1e30)
    exponent = jnp.exp(scores - jnp.max(scores, axis=-1, keepdims=True))
    return exponent * (1.0 / jnp.sum(exponent, axis=-1, keepdims=True))


def attend_body(query_raw, key_raw, values, query_inv, key_inv, cosine, sine, gains, q_out, k_out, mixed):
    length, columns = query_raw.shape
    for head in range(columns // HEAD_DIM):
        here = pl.ds(head * HEAD_DIM, HEAD_DIM)
        query_normed = query_raw[:, here] * query_inv[...] * gains[0:1, here]
        key_normed = key_raw[:, here] * key_inv[...] * gains[1:2, here]
        q_out[:, here] = (
            turned(query_normed, cosine[...], sine[...]) * HEAD_DIM ** (-0.5)
        ).astype(jnp.bfloat16)
        k_out[:, here] = turned(key_normed, cosine[...], sine[...]).astype(jnp.bfloat16)
        for start, end in head_blocks(length):
            rows = pl.ds(start, end - start)
            probs = block_probs(q_out[rows, here], k_out[pl.ds(0, end), here], start, end)
            mixed[rows, here] = contract(
                probs.astype(jnp.bfloat16), values[pl.ds(0, end), here], 1, 0
            ).astype(jnp.bfloat16)


def attend(query_raw, key_raw, values, query_inv, key_inv, cosine, sine, gains):
    length, columns = query_raw.shape
    args = (query_raw, key_raw, values, query_inv, key_inv, cosine, sine, gains)
    return pl.pallas_call(
        attend_body,
        grid=(1,),
        in_specs=[fixed(arg.shape) for arg in args],
        out_specs=[fixed((length, columns), False)] * 3,
        out_shape=[jax.ShapeDtypeStruct((length, columns), jnp.bfloat16)] * 3,
        compiler_params=kernel_params(),
        cost_estimate=cost(4 * length * length * columns, 16 * length * columns),
        name="attend",
    )(*args)


def attend_back_body(
    queries, keys, values, grads, query_raw, key_raw, query_inv, key_inv, cosine, sine, gains, *refs
):
    query_scaled, key_scaled, value_low, query_inner, key_inner, gain_out = refs[:6]
    grad_key, grad_value = refs[6:]
    length, columns = queries.shape
    for head in range(columns // HEAD_DIM):
        here = pl.ds(head * HEAD_DIM, HEAD_DIM)
        grad_key[...] = jnp.zeros_like(grad_key)
        grad_value[...] = jnp.zeros_like(grad_value)
        for start, end in head_blocks(length):
            rows, past = pl.ds(start, end - start), pl.ds(0, end)
            probs = block_probs(queries[rows, here], keys[past, here], start, end)
            grad_probs = contract(grads[rows, here], values[past, here], 1, 1)
            grad_scores = (
                probs * (grad_probs - jnp.sum(probs * grad_probs, axis=-1, keepdims=True))
            ).astype(jnp.bfloat16)
            grad_value[past, :] += contract(probs.astype(jnp.bfloat16), grads[rows, here], 0, 0)
            grad_key[past, :] += contract(grad_scores, queries[rows, here], 0, 0)
            query_scaled[rows, here] = contract(grad_scores, keys[past, here], 1, 0)
        value_low[:, here] = grad_value[...].astype(jnp.bfloat16)
        sides = (
            (query_scaled[:, here] * HEAD_DIM ** (-0.5), query_raw, query_inv, query_scaled, query_inner),
            (grad_key[...], key_raw, key_inv, key_scaled, key_inner),
        )
        for side, (grad, raw, inverse, scaled_out, inner_out) in enumerate(sides):
            normed = turned(grad, cosine[...], -sine[...])
            normal = raw[:, here] * inverse[...]
            gain_out[side : side + 1, here] = jnp.sum(normed * normal, axis=0, keepdims=True)
            scaled = normed * gains[side : side + 1, here]
            scaled_out[:, here] = scaled
            inner = jnp.sum(scaled * normal, axis=-1, keepdims=True)
            if head == 0:
                inner_out[...] = inner
            else:
                inner_out[...] += inner


def attend_back(*args):
    length, columns = args[0].shape
    wide = jax.ShapeDtypeStruct((length, columns), jnp.float32)
    column = jax.ShapeDtypeStruct((length, 1), jnp.float32)
    outs = [
        wide,
        wide,
        jax.ShapeDtypeStruct((length, columns), jnp.bfloat16),
        column,
        column,
        jax.ShapeDtypeStruct((2, columns), jnp.float32),
    ]
    return pl.pallas_call(
        attend_back_body,
        grid=(1,),
        in_specs=[fixed(arg.shape) for arg in args],
        out_specs=[fixed(out.shape, False) for out in outs],
        out_shape=outs,
        scratch_shapes=[pltpu.VMEM((length, HEAD_DIM), jnp.float32)] * 2,
        compiler_params=kernel_params(),
        cost_estimate=cost(8 * length * length * columns, 40 * length * columns),
        name="attend_back",
    )(*args)


def near_scatter(pieces):
    size = lax.axis_size("tensor")
    groups = [list(range(core, size, 2)) for core in range(2)]
    return lax.all_to_all(
        pieces, "tensor", split_axis=0, concat_axis=0, axis_index_groups=groups, tiled=True
    )


def line_sum(part, after):
    index = lax.axis_index("expert")
    bits = axis_bits("expert")[::-1]
    after = list(after) + [None] * (2 * len(bits))
    for bit in bits:
        half = part.shape[0] // 2
        high = (index // bit) % 2
        kept = lax.dynamic_slice_in_dim(part, high * half, half, 0)
        sent = lax.dynamic_slice_in_dim(part, (1 - high) * half, half, 0)
        wait = after.pop(0)
        if wait is not None:
            sent = tie(sent, wait)
        part = (
            kept.astype(jnp.float32) + swap(sent, "expert", bit).astype(jnp.float32)
        ).astype(jnp.bfloat16)
    for bit in bits[::-1]:
        high = (index // bit) % 2 == 1
        wait = after.pop(0)
        if wait is not None:
            part = tie(part, wait)
        other = swap(part, "expert", bit)
        part = jnp.concatenate([jnp.where(high, other, part), jnp.where(high, part, other)], axis=0)
    return part.astype(jnp.float32)


def send_body(indices, places, scalars, act, *refs):
    gates, (down_own, down_other), outs = refs[:places], refs[places : places + 2], refs[-places:]
    units = down_own.shape[1]
    value = contract(act[:, :units], down_own[0], 1, 0) + contract(
        act[:, units:], down_other[0], 1, 0
    )
    own_rows = outs[0].shape[1]
    for place in range(places):

        @pl.when(pl.program_id(1) == place)
        def _():
            sent = (gates[place][...] * value).astype(jnp.bfloat16)
            for at, i in enumerate(indices):
                outs[place][(scalars[0] ^ i) // 2] = sent[at * own_rows : (at + 1) * own_rows]


def expert_send(here, indices, act_all, gates, downs):
    rows = gates[0].shape[0]
    count = len(indices)
    places = len(gates)
    _, units, width = downs.shape
    block = min(1024, width // 2)
    return pl.pallas_call(
        lambda *refs: send_body(indices, places, *refs),
        grid_spec=pltpu.PrefetchScalarGridSpec(
            num_scalar_prefetch=1,
            grid=(width // block, places),
            in_specs=[pl.BlockSpec((rows, 2 * units), lambda j, k, *_: (k, 0))]
            + [fixed((rows, 1))] * places
            + [
                pl.BlockSpec((1, units, block), lambda j, k, at: (at[0] & 1, 0, j)),
                pl.BlockSpec((1, units, block), lambda j, k, at: (1 - (at[0] & 1), 0, j)),
            ],
            out_specs=[pl.BlockSpec((count, rows // count, block), lambda j, k, *_: (0, 0, j))]
            * places,
        ),
        out_shape=[jax.ShapeDtypeStruct((count, rows // count, width), jnp.bfloat16)] * places,
        compiler_params=kernel_params(),
        cost_estimate=cost(
            4 * places * rows * width * units, places * 4 * rows * width + 4 * width * units
        ),
        name="expert_send",
    )(here, act_all, *gates, downs, downs)


def project_body(indices, halves, scalars, mixed, tokens, gain, *refs):
    weights = refs[: len(indices) * halves]
    hidden_out, low_out = refs[-2:]
    total = tokens[...].astype(jnp.float32)
    depth = weights[0].shape[0]
    attn = None
    for at, i in enumerate(indices):
        piece = mixed[scalars[0] ^ i]
        for half in range(halves):
            part = contract(
                piece[:, half * depth : (half + 1) * depth], weights[at * halves + half][...], 1, 0
            )
            attn = part if attn is None else attn + part
    hidden = total + attn
    normal, _ = rms_forward(hidden)
    hidden_out[...] = hidden
    low_out[...] = (normal * gain[...]).astype(jnp.bfloat16)


def project_out(here, indices, mixed, tokens, gain, weights, halves):
    rows, width = tokens.shape
    return pl.pallas_call(
        lambda *refs: project_body(indices, halves, *refs),
        grid_spec=pltpu.PrefetchScalarGridSpec(
            num_scalar_prefetch=1,
            grid=(1,),
            in_specs=[fixed(mixed.shape), fixed(tokens.shape), fixed((1, width))]
            + [fixed(weights[0].shape)] * len(weights),
            out_specs=[fixed((rows, width), False), fixed((rows, width), False)],
        ),
        out_shape=[
            jax.ShapeDtypeStruct((rows, width), jnp.float32),
            jax.ShapeDtypeStruct((rows, width), jnp.bfloat16),
        ],
        compiler_params=kernel_params(),
        cost_estimate=cost(2 * rows * width * width, 2 * width * width),
        name="project_out",
    )(here, mixed, tokens, gain, *weights)


def turn_body(indices, halves, count, scalars, hidden, grad_out, gain, *refs):
    grads = refs[:count]
    weights = refs[count : count + len(indices) * halves]
    grad_hidden_out, low_out, mixed_out, gain_out = refs[-4:]
    grad_ffn = jnp.sum(grads[0][...].astype(jnp.float32), axis=0)
    for part in grads[1:]:
        grad_ffn = grad_ffn + part[...].astype(jnp.float32)
    normal, inverse = rms_forward(hidden[...])
    gain_out[...] = jnp.sum(grad_ffn * normal, axis=0, keepdims=True)
    scaled = grad_ffn * gain[...]
    grad_hidden = grad_out[...].astype(jnp.float32) + inverse * (
        scaled - normal * jnp.mean(scaled * normal, axis=-1, keepdims=True)
    )
    low = grad_hidden.astype(jnp.bfloat16)
    grad_hidden_out[...] = grad_hidden
    low_out[...] = low
    depth = weights[0].shape[0]
    for at, i in enumerate(indices):
        for half in range(halves):
            mixed_out[scalars[0] ^ i, :, half * depth : (half + 1) * depth] = contract(
                low, weights[at * halves + half][...], 1, 1
            ).astype(jnp.bfloat16)


def turn_back(here, indices, hidden, grad_out, gain, grads, weights, halves):
    rows, width = hidden.shape
    depth = weights[0].shape[0] * halves
    return pl.pallas_call(
        lambda *refs: turn_body(indices, halves, len(grads), *refs),
        grid_spec=pltpu.PrefetchScalarGridSpec(
            num_scalar_prefetch=1,
            grid=(1,),
            in_specs=[fixed((rows, width)), fixed((rows, width)), fixed((1, width))]
            + [fixed(part.shape) for part in grads]
            + [fixed(weights[0].shape)] * len(weights),
            out_specs=[
                fixed((rows, width), False),
                fixed((rows, width), False),
                fixed((len(indices), rows, depth), False),
                fixed((1, width), False),
            ],
        ),
        out_shape=[
            jax.ShapeDtypeStruct((rows, width), jnp.float32),
            jax.ShapeDtypeStruct((rows, width), jnp.bfloat16),
            jax.ShapeDtypeStruct((len(indices), rows, depth), jnp.bfloat16),
            jax.ShapeDtypeStruct((1, width), jnp.float32),
        ],
        compiler_params=kernel_params(),
        cost_estimate=cost(2 * rows * width * width, 2 * width * width),
        name="turn_back",
    )(here, hidden, grad_out, gain, *grads, *weights)


def on_device(
    tokens,
    positions,
    routes,
    slot_ids,
    attn_gain,
    w_query,
    w_key,
    w_value,
    query_gain,
    key_gain,
    w_out,
    ffn_gain,
    router,
    w_gate,
    w_up,
    w_down,
    grad_out,
):
    tensor_size = lax.axis_size("tensor")
    expert_size = lax.axis_size("expert")
    local_count = tensor_size // 2
    tensor_index = lax.axis_index("tensor")
    expert_index = lax.axis_index("expert")
    own_local = tensor_index // 2
    own_expert = expert_index * local_count + own_local
    length, model_width = tokens.shape
    heads_here = w_query.shape[1] // HEAD_DIM
    full_cols = w_query.shape[1] * tensor_size
    expert_count = router.shape[1]
    capacity = 3 * length * TOP // (2 * expert_count)
    own_rows = length // tensor_size
    chunks = list(range(expert_size))
    bits = axis_bits("tensor")
    near_bits = bits[:-1]
    last = len(near_bits)

    def own_slice(rows):
        return lax.dynamic_slice_in_dim(rows, tensor_index * own_rows, own_rows, 0)

    near_groups = [list(range(core, tensor_size, 2)) for core in range(2)]
    pairs = [[2 * i, 2 * i + 1] for i in range(tensor_size // 2)]
    gates, ups, downs = [
        lax.all_gather(weights[0], "tensor", axis_index_groups=pairs)
        for weights in (w_gate, w_up, w_down)
    ]
    grad_own = own_slice(grad_out)
    grad_near, _ = plane_rows(grad_out, 0, own_rows, sorted_order=True)
    grad_rows_of = {0: grad_out}
    grad_sent = {}
    for chunk in range(1, expert_size):
        if chunk % 2:
            groups = [[i, i ^ chunk] for i in range(expert_size) if i < i ^ chunk]
            grad_rows_of[chunk] = lax.all_gather(grad_near, "expert", axis_index_groups=groups)
        else:
            grad_sent[chunk] = swap(grad_own, "expert", chunk)
    out_pieces = {0: w_out}
    for stage in range(len(bits)):
        out_pieces = gather_stage(out_pieces, 0, stage, bits)
    all_indices = sorted(out_pieces)
    out_weights = [out_pieces[i] for i in all_indices]
    for chunk, piece in grad_sent.items():
        pieces = direct_gather(piece, near_bits, (out_pieces[near_bits[0]],))
        grad_rows_of[chunk] = jnp.concatenate([pieces[i] for i in sorted(pieces)], axis=0)[None]
    first_out = [out_pieces[i] for i in all_indices if i in near_bits]
    last_out = out_pieces[2 * (tensor_size // 2 - 1)]
    expert_iota = jnp.arange(expert_count, dtype=jnp.int32)
    kept_table = jnp.sum(
        (
            (routes.T[:, None, :] == expert_iota[None, :, None]) & (slot_ids.T < capacity)[:, None, :]
        ).astype(jnp.float32),
        axis=0,
    )
    targets = jnp.arange(expert_size, dtype=jnp.int32) * local_count + own_local
    kept_rows = lax.all_to_all(
        jnp.take(kept_table, targets, axis=0).reshape(expert_size, tensor_size, own_rows),
        "expert",
        split_axis=0,
        concat_axis=0,
        tiled=True,
    )

    def here(chunk):
        from_plane = expert_index ^ chunk
        side = jnp.where(from_plane > expert_index, 1, 0) if chunk % 2 else 0 * from_plane
        return jnp.stack([tensor_index, from_plane, side]).astype(jnp.int32)

    score_scale = HEAD_DIM ** (-0.5)
    half_dim = HEAD_DIM // 2
    frequency = THETA ** (-2.0 * jnp.arange(half_dim, dtype=jnp.float32) / HEAD_DIM)
    angles = positions.astype(jnp.float32)[:, None] * frequency[None, :]
    cosine_table = jnp.concatenate([jnp.cos(angles)] * 2, axis=-1)
    sine_half = jnp.sin(angles)
    sine_table = jnp.concatenate([-sine_half, sine_half], axis=-1)
    token_float = tokens.astype(jnp.float32)
    attn_normal, attn_inverse = rms_forward(token_float)
    attn_in = (attn_normal * attn_gain).astype(jnp.bfloat16)
    head_shape = (length, heads_here, HEAD_DIM)
    query_raw = jnp.dot(attn_in, w_query, preferred_element_type=jnp.float32)
    key_raw = jnp.dot(attn_in, w_key, preferred_element_type=jnp.float32)
    value_rows = jnp.dot(attn_in, w_value, preferred_element_type=jnp.float32).astype(jnp.bfloat16)
    gains = jnp.stack([query_gain, key_gain])
    square_sums = jnp.stack(
        [jnp.sum(query_raw * query_raw, axis=1), jnp.sum(key_raw * key_raw, axis=1)]
    )
    for at, bit in enumerate(bits[::-1]):
        if at == len(bits) - 1:
            square_sums = tie(square_sums, *first_out, *grad_sent.values())
        square_sums = square_sums + swap(square_sums, "tensor", bit)
    inverse = lax.rsqrt(square_sums / full_cols + EPS)[:, :, None]
    query_inverse, key_inverse = inverse[0], inverse[1]
    query_rows, key_rows, mixed_low = attend(
        query_raw, key_raw, value_rows, query_inverse, key_inverse, cosine_table, sine_table, gains
    )
    mixed_low = tie(mixed_low, last_out)
    mixed_own = lax.all_to_all(
        mixed_low.reshape(tensor_size, own_rows, -1), "tensor", split_axis=0, concat_axis=0, tiled=True
    )
    hidden, ffn_in = project_out(
        tie(here(0), *[grad_rows_of[chunk] for chunk in grad_sent]), all_indices, mixed_own, own_slice(tokens), ffn_gain[None, :], out_weights, 1
    )
    chosen = (expert_iota == own_expert).astype(jnp.float32)[None, :]
    received = [ffn_in]
    gathered = [direct_gather(ffn_in, near_bits)]
    for chunk in chunks[1:]:
        sent = tie(ffn_in, gathered[0][near_bits[0]]) if chunk > 2 else ffn_in
        received.append(swap(sent, "expert", chunk))
    chain = None
    sums = []
    gate_columns = []
    for at, chunk in enumerate(chunks):
        scalars = here(chunk)
        if at == 0:
            scalars = tie(scalars, *received[1:3])
        elif at + 2 < expert_size:
            scalars = tie(scalars, received[at + 2])
        if at:
            after = [gathered[at - 1][i] for i in gathered[at - 1] if i]
            if at >= 2:
                after.append(gate_columns[at - 2])
            gathered.append(direct_gather(received[at], near_bits, after))
        if at >= 3:
            scalars = tie(scalars, sums[at - 3])
        pieces, gate_column, chain = expert_chunk(
            at,
            expert_size,
            gathered[at],
            grad_rows_of[chunk],
            scalars,
            kept_rows,
            chosen,
            router,
            gates,
            ups,
            downs,
            chain,
        )
        gate_columns.append(gate_column)
        sums.append(near_scatter(pieces))

    def plane_total(near):
        return jnp.sum(near.astype(jnp.float32), axis=0).astype(jnp.bfloat16)

    row_totals = [plane_total(near) for near in sums[1:]]
    grad_parts = [sums[0]] + [
        swap(total, "expert", chunk) for total, chunk in zip(row_totals, chunks[1:])
    ]
    indices = sorted(gathered[0])
    dl_all, x_all, dy_all, act_all, own_dp, other_dp, gated_own, gated_other = chain
    sent_pieces = expert_send(tie(here(0), row_totals[-1]), indices, act_all, gate_columns, downs)
    grad_hidden, hidden_low, grad_mixed_own, grad_ffn_gain = turn_back(
        here(0), all_indices, hidden, grad_own, ffn_gain[None, :], grad_parts, out_weights, 1
    )
    grad_mixed = lax.all_to_all(
        grad_mixed_own, "tensor", split_axis=0, concat_axis=0, tiled=True
    ).reshape(length, -1)

    sent_near = []
    for at, pieces in enumerate(sent_pieces):
        sent_near.append(near_scatter(tie(pieces, grad_mixed) if at else pieces))
    units = own_dp.shape[1] // 2
    other_wide = swap(contract(x_all, other_dp, 0, 0).astype(jnp.bfloat16), "tensor", 1)
    other_down = swap(contract(gated_other, dy_all, 0, 0).astype(jnp.bfloat16), "tensor", 1)
    grad_gate_w = contract(x_all, own_dp[:, :units], 0, 0) + other_wide[:, :units].astype(jnp.float32)
    grad_up_w = contract(x_all, own_dp[:, units:], 0, 0) + other_wide[:, units:].astype(jnp.float32)
    grad_down = contract(gated_own, dy_all, 0, 0) + other_down.astype(jnp.float32)
    grad_router_part = contract(dl_all, x_all, 0, 0)

    hidden_low_all = lax.all_gather(hidden_low, "tensor", axis=0, tiled=True)
    grad_w_out = contract(mixed_low, hidden_low_all, 0, 0)
    grad_w_out_low = grad_w_out.astype(jnp.bfloat16)
    query_scaled, key_scaled, value_low, query_inner, key_inner, gain_parts = attend_back(
        query_rows,
        key_rows,
        value_rows,
        grad_mixed,
        query_raw,
        key_raw,
        query_inverse,
        key_inverse,
        cosine_table,
        sine_table,
        gains,
    )
    inner_sums = spread_sum(jnp.stack([query_inner[:, 0], key_inner[:, 0]]), "tensor")
    inner_sums = tie(inner_sums, grad_w_out_low, *sent_near)[:, :, None]
    grad_attn, query_low, key_low = input_grad(
        here(0),
        all_indices,
        own_rows,
        full_cols,
        (
            query_scaled,
            key_scaled,
            value_low,
            query_raw,
            key_raw,
            query_inverse,
            key_inverse,
            inner_sums[0],
            inner_sums[1],
        ),
        (w_query, w_key, w_value),
    )
    grad_w_query = jnp.einsum("td,tq->dq", attn_in, query_low, preferred_element_type=jnp.float32)
    grad_w_key = jnp.einsum("td,tq->dq", attn_in, key_low, preferred_element_type=jnp.float32)
    grad_w_value = jnp.einsum("td,tq->dq", attn_in, value_low, preferred_element_type=jnp.float32)
    for stage in range(len(bits)):
        grad_attn = scatter_stage(grad_attn, 0, stage, bits)
    grad_token_part, grad_attn_gain = rms_backward(
        grad_attn[0], own_slice(attn_normal), own_slice(attn_inverse), attn_gain
    )
    token_pieces = [{0: (grad_hidden + grad_token_part).astype(jnp.bfloat16)}]
    for stage in range(len(bits)):
        token_pieces.append(gather_stage(token_pieces[-1], 0, stage, bits))
    grad_tokens = place_rows(here(0), token_pieces[-1])
    late = token_pieces[2][bits[0] ^ bits[1]]
    moe_sum = hidden
    for at, chunk in enumerate(chunks):
        near = tie(sent_near[at], grad_attn[0])
        if chunk:
            moe_sum = moe_sum + swap(plane_total(near), "expert", chunk).astype(jnp.float32)
        else:
            moe_sum = moe_sum + jnp.sum(near.astype(jnp.float32), axis=0)
    output = place_rows(
        here(0), gather_all(tie(moe_sum.astype(jnp.bfloat16), late), 1, bits)
    )
    waits = [None, grad_attn[0], late]
    sum_query = line_sum(grad_w_query.astype(jnp.bfloat16), waits)
    sum_key = line_sum(grad_w_key.astype(jnp.bfloat16), waits)
    sum_value, sum_out = [
        part.astype(jnp.float32)
        for part in lax.psum(
            (grad_w_value.astype(jnp.bfloat16), grad_w_out_low), "expert"
        )
    ]
    plane_sums = spread_sum(
        jnp.concatenate([grad_router_part, grad_ffn_gain, grad_attn_gain[None, :]], axis=0), "tensor"
    )
    scales = gain_parts.reshape(-1)
    scales = jnp.pad(scales, (0, model_width - scales.shape[0]))
    all_sums = spread_sum(jnp.concatenate([plane_sums, scales[None, :]], axis=0), "expert")
    columns_here = w_query.shape[1]
    return (
        output,
        grad_tokens,
        all_sums[expert_count + 1],
        sum_query,
        sum_key,
        sum_value,
        all_sums[expert_count + 2, :columns_here],
        all_sums[expert_count + 2, columns_here : 2 * columns_here],
        sum_out,
        all_sums[expert_count],
        all_sums[:expert_count].T,
        grad_gate_w[None],
        grad_up_w[None],
        grad_down[None],
    )


def solution(mesh):
    placed = (
        P("expert", None),
        P("expert"),
        P("expert", None),
        P("expert", None),
        P(),
        P(None, "tensor"),
        P(None, "tensor"),
        P(None, "tensor"),
        P("tensor"),
        P("tensor"),
        P("tensor", None),
        P(),
        P(),
        P(("expert", "tensor"), None, None),
        P(("expert", "tensor"), None, None),
        P(("expert", "tensor"), None, None),
        P("expert", None),
    )
    return jax.shard_map(
        on_device,
        mesh=mesh,
        in_specs=placed,
        out_specs=(
            P("expert", None),
            P("expert", None),
            P(),
            P(None, "tensor"),
            P(None, "tensor"),
            P(None, "tensor"),
            P("tensor"),
            P("tensor"),
            P("tensor", None),
            P(),
            P(),
            P(("expert", "tensor"), None, None),
            P(("expert", "tensor"), None, None),
            P(("expert", "tensor"), None, None),
        ),
        check_vma=False,
    )
```

```python
import jax
import jax.numpy as jnp
from jax import lax
from jax.experimental import pallas as pl
from jax.experimental.pallas import tpu as pltpu
from jax.sharding import PartitionSpec as P

HEAD_DIM = 128
TOP = 8


EPS = 1e-05
THETA = 10000.0


def rms_forward(values):
    inverse = lax.rsqrt(jnp.mean(values * values, axis=-1, keepdims=True) + EPS)
    return (values * inverse, inverse)


def rms_backward(grad_normed, normal_rows, inverse, gain_row):
    gain_grad = jnp.sum(grad_normed * normal_rows, axis=0)
    scaled = grad_normed * gain_row
    grad_rows = inverse * (
        scaled - normal_rows * jnp.mean(scaled * normal_rows, axis=-1, keepdims=True)
    )
    return (grad_rows, gain_grad)


def swap(values, axis, bit):
    return lax.ppermute(values, axis, [(i, i ^ bit) for i in range(lax.axis_size(axis))])


def axis_bits(axis):
    size = lax.axis_size(axis)
    return [size >> (k + 1) for k in range(size.bit_length() - 1)]


def spread_sum(values, axis):
    for bit in axis_bits(axis)[::-1]:
        values = values + swap(values, axis, bit)
    return values


def plane_order(turn):
    bits = axis_bits("tensor")[:-1]
    if turn % 2:
        bits = bits[::-1]
    order = [0]
    for bit in bits:
        order = order + [bit ^ i for i in order]
    return bits, order


def plane_gather(piece, turn):
    bits, _ = plane_order(turn)
    pieces = [piece]
    for bit in bits:
        pieces = pieces + [swap(p, "tensor", bit) for p in pieces]
    near = jnp.concatenate(pieces, axis=0)
    return near, swap(near, "tensor", 1)


def plane_scatter(near, far, turn):
    bits, _ = plane_order(turn)
    total = near.astype(jnp.float32) + swap(far, "tensor", 1).astype(jnp.float32)
    for bit in bits[::-1]:
        half = total.shape[0] // 2
        sent = total[half:].astype(jnp.bfloat16)
        total = total[:half].astype(jnp.bfloat16).astype(jnp.float32) + swap(
            sent, "tensor", bit
        ).astype(jnp.float32)
    return total


def plane_rows(values, turn, own_rows, sorted_order=False):
    _, order = plane_order(turn)
    if sorted_order:
        order = sorted(order)
    index = lax.axis_index("tensor")

    def block(i):
        return lax.dynamic_slice_in_dim(values, (index ^ i) * own_rows, own_rows, 0)

    near = jnp.concatenate([block(i) for i in order], axis=0)
    far = jnp.concatenate([block(i ^ 1) for i in order], axis=0)
    return near, far


def natural_rows(near, far, turn, own_rows):
    _, order = plane_order(turn)
    index = lax.axis_index("tensor")
    both = jnp.concatenate([near, far], axis=0)
    place = {}
    for at, i in enumerate(order):
        place[i] = at
        place[i ^ 1] = at + len(order)
    table = jnp.array([place[i] for i in range(2 * len(order))], jnp.int32)
    return jnp.concatenate(
        [
            lax.dynamic_slice_in_dim(both, table[index ^ i] * own_rows, own_rows, 0)
            for i in range(2 * len(order))
        ],
        axis=0,
    )


def contract(left, right, left_dim, right_dim):
    return lax.dot_general(
        left, right, (((left_dim,), (right_dim,)), ((), ())), preferred_element_type=jnp.float32
    )


def tie(values, *after):
    return lax.optimization_barrier((values, *after))[0]


def stages(turn, bits):
    if turn % 2:
        bits = bits[::-1]
    found = [[] for _ in bits]
    order = [(0, ())]
    for bit in bits:
        order = order + [(bit ^ i, used + (bit,)) for i, used in order]
    for i, used in order[1:]:
        found[len(used) - 1].append((i, i ^ used[-1], used[-1]))
    return found


def gather_stage(pieces, turn, stage, bits, after=()):
    pieces = dict(pieces)
    for i, source, bit in stages(turn, bits)[stage]:
        sent = pieces[source]
        if after:
            sent = tie(sent, *after)
        pieces[i] = swap(sent, "tensor", bit)
    return pieces


def direct_combos(bits):
    combos = [0]
    for bit in bits:
        combos = combos + [bit ^ i for i in combos]
    return combos


def direct_gather(piece, bits, after=()):
    pieces = {0: piece}
    for i in direct_combos(bits)[1:]:
        pieces[i] = swap(tie(piece, *after) if after else piece, "tensor", i)
    return pieces


def gather_all(piece, turn, bits):
    pieces = {0: piece}
    for stage in range(len(bits)):
        pieces = gather_stage(pieces, turn, stage, bits)
    return pieces


def scatter_stage(sums, turn, stage, bits, after=()):
    sums = dict(sums)
    for i, target, bit in stages(turn, bits)[len(bits) - 1 - stage]:
        sent = sums.pop(i).astype(jnp.bfloat16)
        if after:
            sent = tie(sent, *after)
        sums[target] = sums[target].astype(jnp.float32) + swap(sent, "tensor", bit).astype(
            jnp.float32
        )
    return sums


MEGABYTE = 1024 * 1024


def kernel_params():
    return pltpu.CompilerParams(vmem_limit_bytes=58 * MEGABYTE)


def cost(flops, moved):
    return pl.CostEstimate(flops=flops, bytes_accessed=moved, transcendentals=0)


def column_of(row):
    n = row.shape[1]
    down = lax.broadcasted_iota(jnp.int32, (n, n), 0)
    across = lax.broadcasted_iota(jnp.int32, (n, n), 1)
    return jnp.sum(jnp.where(down == across, row, 0.0), axis=1, keepdims=True)


def fixed(shape, single=True):
    if single:
        return pl.BlockSpec(
            shape, lambda *_: (0,) * len(shape), pipeline_mode=pl.Buffered(1)
        )
    return pl.BlockSpec(shape, lambda *_: (0,) * len(shape))


def expert_body(indices, local, place, scalars, *refs):
    count = len(indices)
    x_parts, refs = refs[:count], refs[count:]
    dy_source, kept, chosen, router, gates, ups, downs = refs[:7]
    core = scalars[0] & 1
    gate_own, gate_other = gates.at[core], gates.at[1 - core]
    up_own, up_other = ups.at[core], ups.at[1 - core]
    down_own, down_other = downs.at[core], downs.at[1 - core]
    scratch = refs[-13:]
    pieces, gate_out, dl_all, x_all, dy_all, act_all, own_dp, other_dp, gated_own, gated_other = refs[
        -23:-13
    ]
    rows, grads, wide, tall, raw, inner, act, slopes, gated, done, probs_ref, dots, sems = scratch
    rows_here, width = rows.shape
    units = gate_own.shape[1]
    own_rows = rows_here // count
    used = []
    dy_parts = []
    for i in indices:
        if local:
            at = pl.multiple_of((scalars[0] ^ i) * own_rows, own_rows)
            dy_parts.append(dy_source.at[pl.ds(at, own_rows)])
        else:
            dy_parts.append(dy_source.at[scalars[2], pl.ds(len(dy_parts) * own_rows, own_rows)])

    def start(source, target):
        copy = pltpu.make_async_copy(source, target, sems.at[len(used)])
        used.append(copy)
        copy.start()
        return copy

    def spread(parts, target):
        size = rows_here // len(parts)
        return [start(part, target.at[pl.ds(at * size, size)]) for at, part in enumerate(parts)]

    x_copies = spread(x_parts, rows)
    order = [gate_own, up_own, gate_other, up_other]
    wide_copies = [
        start(weight, wide.at[:, pl.ds(at * units, units)]) for at, weight in enumerate(order[:2])
    ]
    dy_copies = spread(dy_parts, grads)
    tall_copies = [start(down_own, tall.at[pl.ds(0, units)])]
    wide_copies += [
        start(weight, wide.at[:, pl.ds((at + 2) * units, units)])
        for at, weight in enumerate(order[2:])
    ]
    tall_copies.append(start(down_other, tall.at[pl.ds(units, units)]))

    here_rows = pl.ds(place * rows_here, rows_here)
    for copy in x_copies:
        copy.wait()
    outgoing = [start(rows, x_all.at[here_rows])]
    logits = contract(rows[...], router[...], 1, 0)
    exponent = jnp.exp(logits - jnp.max(logits, axis=-1, keepdims=True))
    probs = exponent / jnp.sum(exponent, axis=-1, keepdims=True)
    kept_column = jnp.concatenate(
        [column_of(kept[scalars[1], pl.ds(scalars[0] ^ i, 1), :]) for i in indices], axis=0
    )
    probs_ref[...] = probs
    gate_out[...] = jnp.sum(probs * chosen[...], axis=-1, keepdims=True) * kept_column
    dots[...] = jnp.zeros_like(dots)

    block = min(64, rows_here)
    for half in range(2):
        columns = pl.ds(half * units, units)
        for part in range(2):
            at = 2 * half + part
            wide_copies[at].wait()
            raw[:, pl.ds(part * units, units)] = contract(
                rows[...], wide[:, pl.ds(at * units, units)], 1, 0
            )
        if half == 0:
            for copy in dy_copies:
                copy.wait()
            outgoing.append(start(grads, dy_all.at[here_rows]))
        tall_copies[half].wait()
        inner[...] = contract(grads[...], tall[columns, :], 1, 1)

        @pl.loop(0, rows_here // block)
        def _(at):
            here = pl.ds(at * block, block)
            pre_gate = raw[here, pl.ds(0, units)]
            pre_up = raw[here, pl.ds(units, units)]
            inward = inner[here, :]
            gate = gate_out[here, :]
            sigmoid_gate = 1.0 / (1.0 + jnp.exp(-pre_gate))
            silu_gate = pre_gate * sigmoid_gate
            active = (silu_gate * pre_up).astype(jnp.bfloat16)
            act[here, columns] = active
            active = active.astype(jnp.float32)
            gated[here, columns] = (gate * active).astype(jnp.bfloat16)
            dots[here, :] += jnp.sum(inward * active, axis=-1, keepdims=True)
            grad_active = gate * inward
            slopes[here, pl.ds(2 * half * units, units)] = (
                grad_active * pre_up * sigmoid_gate * (1.0 + pre_gate * (1.0 - sigmoid_gate))
            ).astype(jnp.bfloat16)
            slopes[here, pl.ds((2 * half + 1) * units, units)] = (grad_active * silu_gate).astype(
                jnp.bfloat16
            )

    outgoing += [
        start(act, act_all.at[here_rows]),
        start(slopes.at[:, pl.ds(0, 2 * units)], own_dp.at[here_rows]),
        start(slopes.at[:, pl.ds(2 * units, 2 * units)], other_dp.at[here_rows]),
        start(gated.at[:, pl.ds(0, units)], gated_own.at[here_rows]),
        start(gated.at[:, pl.ds(units, units)], gated_other.at[here_rows]),
    ]
    grad_logits = (dots[...] * gate_out[...] * (chosen[...] - probs_ref[...])).astype(jnp.bfloat16)
    dl_all[...] = grad_logits
    step = min(512, width)
    for at in range(width // step):
        columns = pl.ds(at * step, step)
        done[:, columns] = (
            contract(slopes[...], wide[columns, :], 1, 1)
            + contract(grad_logits, router[columns, :], 1, 1)
        ).astype(jnp.bfloat16)
    for at, i in enumerate(indices):
        to = (scalars[0] ^ i) // 2
        outgoing.append(start(done.at[pl.ds(at * own_rows, own_rows)], pieces.at[to]))
    for copy in outgoing:
        copy.wait()


def expert_chunk(
    place, places, x_pieces, dy_source, here, kept, chosen, router, gates, ups, downs, chain
):
    indices = sorted(x_pieces)
    count = len(indices)
    own_rows, width = x_pieces[0].shape
    rows = own_rows * count
    units = gates.shape[2]
    experts = router.shape[1]
    extra = () if chain is None else tuple(chain)
    hbm = pl.BlockSpec(memory_space=pl.ANY)
    first = count + 8
    kept_shapes = [
        (rows * places, experts),
        (rows * places, width),
        (rows * places, width),
        (rows * places, 2 * units),
        (rows * places, 2 * units),
        (rows * places, 2 * units),
        (rows * places, units),
        (rows * places, units),
    ]
    results = pl.pallas_call(
        lambda *refs: expert_body(indices, dy_source.ndim == 2, place, *refs),
        grid_spec=pltpu.PrefetchScalarGridSpec(
            num_scalar_prefetch=1,
            grid=(1,),
            in_specs=[hbm] * (count + 1)
            + [fixed(kept.shape), fixed((1, experts)), fixed((width, experts))]
            + [hbm] * (3 + len(extra)),
            out_specs=[hbm]
            + [
                fixed((rows, 1), False),
                pl.BlockSpec((rows, experts), lambda j, *_: (place, 0)),
            ]
            + [hbm] * 7,
            scratch_shapes=[
                pltpu.VMEM((rows, width), jnp.bfloat16),
                pltpu.VMEM((rows, width), jnp.bfloat16),
                pltpu.VMEM((width, 4 * units), jnp.bfloat16),
                pltpu.VMEM((2 * units, width), jnp.bfloat16),
                pltpu.VMEM((rows, 2 * units), jnp.float32),
                pltpu.VMEM((rows, units), jnp.float32),
                pltpu.VMEM((rows, 2 * units), jnp.bfloat16),
                pltpu.VMEM((rows, 4 * units), jnp.bfloat16),
                pltpu.VMEM((rows, 2 * units), jnp.bfloat16),
                pltpu.VMEM((rows, width), jnp.bfloat16),
                pltpu.VMEM((rows, experts), jnp.float32),
                pltpu.VMEM((rows, 1), jnp.float32),
                pltpu.SemaphoreType.DMA((3 * count + 13,)),
            ],
        ),
        out_shape=[jax.ShapeDtypeStruct((count, own_rows, width), jnp.bfloat16)]
        + [jax.ShapeDtypeStruct((rows, 1), jnp.float32)]
        + [jax.ShapeDtypeStruct(shape, jnp.bfloat16) for shape in kept_shapes],
        input_output_aliases={first + i: 2 + i for i in range(len(extra))},
        compiler_params=kernel_params(),
        cost_estimate=cost(80 * rows * width * units, 10 * rows * width + 12 * width * units),
        name="expert_chunk",
    )(
        here,
        *[x_pieces[i] for i in indices],
        dy_source,
        kept,
        chosen,
        router,
        gates,
        ups,
        downs,
        *extra,
    )
    return results[0], results[1], results[2:]


def finish_body(own_rows, full_cols, scalars, *refs):
    (query_scaled, key_scaled, value_low, query_raw, key_raw) = refs[:5]
    query_inv, key_inv, query_inner, key_inner, low_out, near_out, far_out = refs[5:]
    columns = value_low.shape[1]
    core = scalars[0] & 1
    for side, (scaled, raw, inverse, inner) in enumerate(
        (
            (query_scaled, query_raw, query_inv, query_inner),
            (key_scaled, key_raw, key_inv, key_inner),
        )
    ):
        normal = raw[...] * inverse[...]
        low_out[:, side * columns : (side + 1) * columns] = (
            inverse[...] * (scaled[...] - normal * (inner[...] / full_cols))
        ).astype(jnp.bfloat16)
    low_out[:, 2 * columns :] = value_low[...]
    for at in range(low_out.shape[0] // (2 * own_rows)):
        first = low_out[pl.ds(2 * at * own_rows, own_rows), :]
        second = low_out[pl.ds((2 * at + 1) * own_rows, own_rows), :]
        near_out[pl.ds(at * own_rows, own_rows), :] = jnp.where(core == 0, first, second)
        far_out[pl.ds(at * own_rows, own_rows), :] = jnp.where(core == 0, second, first)


def finish(here, own_rows, full_cols, *args):
    rows, columns = args[0].shape
    shapes = [(rows, 3 * columns)] + [(rows // 2, 3 * columns)] * 2
    return pl.pallas_call(
        lambda *refs: finish_body(own_rows, full_cols, *refs),
        grid_spec=pltpu.PrefetchScalarGridSpec(
            num_scalar_prefetch=1,
            grid=(1,),
            in_specs=[fixed(arg.shape) for arg in args],
            out_specs=[fixed(shape, False) for shape in shapes],
        ),
        out_shape=[jax.ShapeDtypeStruct(shape, jnp.bfloat16) for shape in shapes],
        compiler_params=kernel_params(),
        cost_estimate=cost(20 * rows * columns, 24 * rows * columns),
        name="finish",
    )(here, *args)


def near_product_body(indices, transposed, scalars, own, other, own_weight, other_weight, *refs):
    pieces, value = refs[:-1], refs[-1]
    side = 1 if transposed else 0
    value[...] = contract(own[...], own_weight[...], 1, side) + contract(
        other[...], other_weight[0], 1, side
    )
    own_rows = pieces[0].shape[0]
    for at, i in enumerate(indices):
        here = pl.ds(pl.multiple_of((scalars[0] ^ i) // 2 * own_rows, own_rows), own_rows)
        pieces[at][...] = value[here, :].astype(jnp.bfloat16)


def near_product(here, indices, own, other, own_weight, pair_weight, transposed):
    rows, depth = own.shape
    width = own_weight.shape[0 if transposed else 1]
    block = min(512, width // 2)
    count = len(indices)
    if transposed:
        mine = pl.BlockSpec((block, depth), lambda j, at: (j, 0))
        theirs = pl.BlockSpec((1, block, depth), lambda j, at: (1 - (at[0] & 1), j, 0))
    else:
        mine = pl.BlockSpec((depth, block), lambda j, at: (0, j))
        theirs = pl.BlockSpec((1, depth, block), lambda j, at: (1 - (at[0] & 1), 0, j))
    results = pl.pallas_call(
        lambda *refs: near_product_body(indices, transposed, *refs),
        grid_spec=pltpu.PrefetchScalarGridSpec(
            num_scalar_prefetch=1,
            grid=(width // block,),
            in_specs=[fixed(own.shape), fixed(other.shape), mine, theirs],
            out_specs=[pl.BlockSpec((rows // count, block), lambda j, at: (0, j))] * count,
            scratch_shapes=[pltpu.VMEM((rows, block), jnp.float32)],
        ),
        out_shape=[jax.ShapeDtypeStruct((rows // count, width), jnp.bfloat16)] * count,
        compiler_params=kernel_params(),
        cost_estimate=cost(4 * rows * depth * width, 2 * rows * width + 4 * depth * width),
        name="near_product",
    )(here, own, other, own_weight, pair_weight)
    return dict(zip(indices, results))


def total_of(parts):
    total = parts[0][...].astype(jnp.float32)
    for part in parts[1:]:
        total = total + part[...].astype(jnp.float32)
    return jnp.sum(total, axis=0) if total.ndim == 3 else total


def residual_body(tokens, gain, *refs):
    hidden_out, low_out = refs[-2:]
    hidden = tokens[...].astype(jnp.float32) + total_of(refs[:-2])
    normal, _ = rms_forward(hidden)
    hidden_out[...] = hidden
    low_out[...] = (normal * gain[...]).astype(jnp.bfloat16)


def residual(tokens, gain, parts):
    rows, width = tokens.shape
    return pl.pallas_call(
        residual_body,
        grid=(1,),
        in_specs=[fixed(tokens.shape), fixed((1, width))] + [fixed(part.shape) for part in parts],
        out_specs=[fixed((rows, width), False)] * 2,
        out_shape=[
            jax.ShapeDtypeStruct((rows, width), jnp.float32),
            jax.ShapeDtypeStruct((rows, width), jnp.bfloat16),
        ],
        compiler_params=kernel_params(),
        cost_estimate=cost(10 * rows * width, 20 * rows * width),
        name="residual",
    )(tokens, gain, *parts)


def norm_back_body(values, passed, gain, near, *refs):
    grad_out, low_out, gain_out = refs[-3:]
    grad = total_of([near]) + total_of(refs[:-3]) if len(refs) > 3 else total_of([near])
    normal, inverse = rms_forward(values[...].astype(jnp.float32))
    gain_out[...] = jnp.sum(grad * normal, axis=0, keepdims=True)
    scaled = grad * gain[...]
    result = passed[...].astype(jnp.float32) + inverse * (
        scaled - normal * jnp.mean(scaled * normal, axis=-1, keepdims=True)
    )
    grad_out[...] = result
    low_out[...] = result.astype(jnp.bfloat16)


def norm_back(values, passed, gain, near, parts):
    rows, width = values.shape
    args = (values, passed, gain, near, *parts)
    return pl.pallas_call(
        norm_back_body,
        grid=(1,),
        in_specs=[fixed(arg.shape) for arg in args],
        out_specs=[fixed((rows, width), False)] * 2 + [fixed((1, width), False)],
        out_shape=[
            jax.ShapeDtypeStruct((rows, width), jnp.float32),
            jax.ShapeDtypeStruct((rows, width), jnp.bfloat16),
            jax.ShapeDtypeStruct((1, width), jnp.float32),
        ],
        compiler_params=kernel_params(),
        cost_estimate=cost(20 * rows * width, 20 * rows * width),
        name="norm_back",
    )(*args)


def mixed_back_body(indices, scalars, own_weight, other_weight, *refs):
    count = len(indices)
    pieces = refs[:count]
    rows_out, own_out, other_out, lows = refs[count:]
    own_rows = pieces[0].shape[0]
    for at, i in enumerate(indices):
        here = pl.ds(pl.multiple_of((scalars[0] ^ i) // 2 * own_rows, own_rows), own_rows)
        lows[here, :] = pieces[at][...]
    rows_out[...] = lows[...]
    own_out[...] = contract(lows[...], own_weight[...], 1, 1).astype(jnp.bfloat16)
    other_out[...] = contract(lows[...], other_weight[0], 1, 1).astype(jnp.bfloat16)


def mixed_back(here, pieces, own_weight, pair_weight):
    indices = sorted(pieces)
    own_rows, width = pieces[0].shape
    rows = own_rows * len(indices)
    depth = own_weight.shape[0]
    shapes = [(rows, width), (rows, depth), (rows, depth)]
    return pl.pallas_call(
        lambda *refs: mixed_back_body(indices, *refs),
        grid_spec=pltpu.PrefetchScalarGridSpec(
            num_scalar_prefetch=1,
            grid=(1,),
            in_specs=[
                fixed(own_weight.shape),
                pl.BlockSpec((1, depth, width), lambda j, at: (1 - (at[0] & 1), 0, 0)),
            ]
            + [fixed((own_rows, width))] * len(indices),
            out_specs=[fixed(shape, False) for shape in shapes],
            scratch_shapes=[pltpu.VMEM((rows, width), jnp.bfloat16)],
        ),
        out_shape=[jax.ShapeDtypeStruct(shape, jnp.bfloat16) for shape in shapes],
        compiler_params=kernel_params(),
        cost_estimate=cost(4 * rows * depth * width, 4 * rows * width + 4 * depth * width),
        name="mixed_back",
    )(here, own_weight, pair_weight, *[pieces[i] for i in indices])


def place_body(indices, own_rows, scalars, *refs):
    pieces, out, sems = refs[: len(indices)], refs[-2], refs[-1]
    copies = []
    for at, i in enumerate(indices):
        here = pl.ds(pl.multiple_of((scalars[0] ^ i) * own_rows, own_rows), own_rows)
        copies.append(pltpu.make_async_copy(pieces[at], out.at[here], sems.at[at]))
        copies[-1].start()
    for copy in copies:
        copy.wait()


def place_rows(here, pieces):
    indices = sorted(pieces)
    own_rows, width = pieces[0].shape
    return pl.pallas_call(
        lambda *refs: place_body(indices, own_rows, *refs),
        grid_spec=pltpu.PrefetchScalarGridSpec(
            num_scalar_prefetch=1,
            grid=(1,),
            in_specs=[fixed((own_rows, width))] * len(indices),
            out_specs=pl.BlockSpec(memory_space=pl.ANY),
            scratch_shapes=[pltpu.SemaphoreType.DMA((len(indices),))],
        ),
        out_shape=jax.ShapeDtypeStruct((own_rows * len(indices), width), pieces[0].dtype),
        compiler_params=kernel_params(),
        cost_estimate=cost(0, 4 * own_rows * len(indices) * width),
        name="place_rows",
    )(here, *[pieces[i] for i in indices])


def turned(values, cosine, sine):
    return values * cosine + pltpu.roll(values, values.shape[1] // 2, 1) * sine


def head_blocks(length):
    block = min(256, length)
    return [(start, start + block) for start in range(0, length, block)]


def block_probs(queries, keys, start, end):
    scores = contract(queries, keys, 1, 1)
    down = lax.broadcasted_iota(jnp.int32, scores.shape, 0) + start
    across = lax.broadcasted_iota(jnp.int32, scores.shape, 1)
    scores = jnp.where(down >= across, scores, -1e30)
    exponent = jnp.exp(scores - jnp.max(scores, axis=-1, keepdims=True))
    return exponent * (1.0 / jnp.sum(exponent, axis=-1, keepdims=True))


def pair_split(rows, core, own_rows):
    low = jnp.concatenate(
        [rows[at : at + own_rows] for at in range(0, rows.shape[0], 2 * own_rows)], axis=0
    )
    high = jnp.concatenate(
        [rows[at : at + own_rows] for at in range(own_rows, rows.shape[0], 2 * own_rows)], axis=0
    )
    return jnp.where(core == 0, low, high), jnp.where(core == 0, high, low)


def attend_body(
    own_rows,
    scalars,
    query_raw,
    key_raw,
    values,
    query_inv,
    key_inv,
    cosine,
    sine,
    gains,
    q_out,
    k_out,
    near_out,
    far_out,
):
    length, columns = query_raw.shape
    core = scalars[0] & 1
    for head in range(columns // HEAD_DIM):
        here = pl.ds(head * HEAD_DIM, HEAD_DIM)
        query_normed = query_raw[:, here] * query_inv[...] * gains[0:1, here]
        key_normed = key_raw[:, here] * key_inv[...] * gains[1:2, here]
        q_out[:, here] = (
            turned(query_normed, cosine[...], sine[...]) * HEAD_DIM ** (-0.5)
        ).astype(jnp.bfloat16)
        k_out[:, here] = turned(key_normed, cosine[...], sine[...]).astype(jnp.bfloat16)
        for start, end in head_blocks(length):
            rows = pl.ds(start, end - start)
            probs = block_probs(q_out[rows, here], k_out[pl.ds(0, end), here], start, end)
            near, far = pair_split(
                contract(probs.astype(jnp.bfloat16), values[pl.ds(0, end), here], 1, 0),
                core,
                own_rows,
            )
            half = pl.ds(start // 2, (end - start) // 2)
            near_out[half, here] = near.astype(jnp.bfloat16)
            far_out[half, here] = far.astype(jnp.bfloat16)


def attend(here, own_rows, *args):
    length, columns = args[0].shape
    shapes = [(length, columns)] * 2 + [(length // 2, columns)] * 2
    return pl.pallas_call(
        lambda *refs: attend_body(own_rows, *refs),
        grid_spec=pltpu.PrefetchScalarGridSpec(
            num_scalar_prefetch=1,
            grid=(1,),
            in_specs=[fixed(arg.shape) for arg in args],
            out_specs=[fixed(shape, False) for shape in shapes],
        ),
        out_shape=[jax.ShapeDtypeStruct(shape, jnp.bfloat16) for shape in shapes],
        compiler_params=kernel_params(),
        cost_estimate=cost(4 * length * length * columns, 16 * length * columns),
        name="attend",
    )(here, *args)


def attend_back_body(
    own_rows,
    scalars,
    near,
    far,
    queries,
    keys,
    values,
    query_raw,
    key_raw,
    query_inv,
    key_inv,
    cosine,
    sine,
    gains,
    *refs,
):
    query_scaled, key_scaled, value_low, query_inner, key_inner, gain_out = refs[:6]
    grads, grad_key, grad_value = refs[6:]
    length, columns = queries.shape
    core = scalars[0] & 1
    for at in range(length // (2 * own_rows)):
        mine, other = near[pl.ds(at * own_rows, own_rows), :], far[pl.ds(at * own_rows, own_rows), :]
        first = pl.ds(2 * at * own_rows, own_rows)
        second = pl.ds((2 * at + 1) * own_rows, own_rows)
        grads[first, :] = jnp.where(core == 0, mine, other)
        grads[second, :] = jnp.where(core == 0, other, mine)
    for head in range(columns // HEAD_DIM):
        here = pl.ds(head * HEAD_DIM, HEAD_DIM)
        grad_key[...] = jnp.zeros_like(grad_key)
        grad_value[...] = jnp.zeros_like(grad_value)
        for start, end in head_blocks(length):
            rows, past = pl.ds(start, end - start), pl.ds(0, end)
            probs = block_probs(queries[rows, here], keys[past, here], start, end)
            grad_probs = contract(grads[rows, here], values[past, here], 1, 1)
            grad_scores = (
                probs * (grad_probs - jnp.sum(probs * grad_probs, axis=-1, keepdims=True))
            ).astype(jnp.bfloat16)
            grad_value[past, :] += contract(probs.astype(jnp.bfloat16), grads[rows, here], 0, 0)
            grad_key[past, :] += contract(grad_scores, queries[rows, here], 0, 0)
            query_scaled[rows, here] = contract(grad_scores, keys[past, here], 1, 0)
        value_low[:, here] = grad_value[...].astype(jnp.bfloat16)
        sides = (
            (query_scaled[:, here] * HEAD_DIM ** (-0.5), query_raw, query_inv, query_scaled, query_inner),
            (grad_key[...], key_raw, key_inv, key_scaled, key_inner),
        )
        for side, (grad, raw, inverse, scaled_out, inner_out) in enumerate(sides):
            normed = turned(grad, cosine[...], -sine[...])
            normal = raw[:, here] * inverse[...]
            gain_out[side : side + 1, here] = jnp.sum(normed * normal, axis=0, keepdims=True)
            scaled = normed * gains[side : side + 1, here]
            scaled_out[:, here] = scaled
            inner = jnp.sum(scaled * normal, axis=-1, keepdims=True)
            if head == 0:
                inner_out[...] = inner
            else:
                inner_out[...] += inner


def attend_back(here, own_rows, *args):
    length, columns = args[2].shape
    wide = jax.ShapeDtypeStruct((length, columns), jnp.float32)
    column = jax.ShapeDtypeStruct((length, 1), jnp.float32)
    outs = [
        wide,
        wide,
        jax.ShapeDtypeStruct((length, columns), jnp.bfloat16),
        column,
        column,
        jax.ShapeDtypeStruct((2, columns), jnp.float32),
    ]
    return pl.pallas_call(
        lambda *refs: attend_back_body(own_rows, *refs),
        grid_spec=pltpu.PrefetchScalarGridSpec(
            num_scalar_prefetch=1,
            grid=(1,),
            in_specs=[fixed(arg.shape) for arg in args],
            out_specs=[fixed(out.shape, False) for out in outs],
            scratch_shapes=[pltpu.VMEM((length, columns), jnp.bfloat16)]
            + [pltpu.VMEM((length, HEAD_DIM), jnp.float32)] * 2,
        ),
        out_shape=outs,
        compiler_params=kernel_params(),
        cost_estimate=cost(8 * length * length * columns, 40 * length * columns),
        name="attend_back",
    )(here, *args)


def near_scatter(pieces):
    size = lax.axis_size("tensor")
    groups = [list(range(core, size, 2)) for core in range(2)]
    return lax.all_to_all(
        pieces, "tensor", split_axis=0, concat_axis=0, axis_index_groups=groups, tiled=True
    )


def line_sum(part, after):
    index = lax.axis_index("expert")
    bits = axis_bits("expert")[::-1]
    after = list(after) + [None] * (2 * len(bits))
    for bit in bits:
        half = part.shape[0] // 2
        high = (index // bit) % 2
        kept = lax.dynamic_slice_in_dim(part, high * half, half, 0)
        sent = lax.dynamic_slice_in_dim(part, (1 - high) * half, half, 0)
        wait = after.pop(0)
        if wait is not None:
            sent = tie(sent, wait)
        part = (
            kept.astype(jnp.float32) + swap(sent, "expert", bit).astype(jnp.float32)
        ).astype(jnp.bfloat16)
    for bit in bits[::-1]:
        high = (index // bit) % 2 == 1
        wait = after.pop(0)
        if wait is not None:
            part = tie(part, wait)
        other = swap(part, "expert", bit)
        part = jnp.concatenate([jnp.where(high, other, part), jnp.where(high, part, other)], axis=0)
    return part.astype(jnp.float32)


def send_body(indices, places, scalars, act, *refs):
    gates, (down_own, down_other), outs = refs[:places], refs[places : places + 2], refs[-places:]
    units = down_own.shape[1]
    value = contract(act[:, :units], down_own[0], 1, 0) + contract(
        act[:, units:], down_other[0], 1, 0
    )
    own_rows = outs[0].shape[1]
    for place in range(places):

        @pl.when(pl.program_id(1) == place)
        def _():
            sent = (gates[place][...] * value).astype(jnp.bfloat16)
            for at, i in enumerate(indices):
                outs[place][(scalars[0] ^ i) // 2] = sent[at * own_rows : (at + 1) * own_rows]


def expert_send(here, indices, act_all, gates, downs):
    rows = gates[0].shape[0]
    count = len(indices)
    places = len(gates)
    _, units, width = downs.shape
    block = min(1024, width // 2)
    return pl.pallas_call(
        lambda *refs: send_body(indices, places, *refs),
        grid_spec=pltpu.PrefetchScalarGridSpec(
            num_scalar_prefetch=1,
            grid=(width // block, places),
            in_specs=[pl.BlockSpec((rows, 2 * units), lambda j, k, *_: (k, 0))]
            + [fixed((rows, 1))] * places
            + [
                pl.BlockSpec((1, units, block), lambda j, k, at: (at[0] & 1, 0, j)),
                pl.BlockSpec((1, units, block), lambda j, k, at: (1 - (at[0] & 1), 0, j)),
            ],
            out_specs=[pl.BlockSpec((count, rows // count, block), lambda j, k, *_: (0, 0, j))]
            * places,
        ),
        out_shape=[jax.ShapeDtypeStruct((count, rows // count, width), jnp.bfloat16)] * places,
        compiler_params=kernel_params(),
        cost_estimate=cost(
            4 * places * rows * width * units, places * 4 * rows * width + 4 * width * units
        ),
        name="expert_send",
    )(here, act_all, *gates, downs, downs)


def on_device(
    tokens,
    positions,
    routes,
    slot_ids,
    attn_gain,
    w_query,
    w_key,
    w_value,
    query_gain,
    key_gain,
    w_out,
    ffn_gain,
    router,
    w_gate,
    w_up,
    w_down,
    grad_out,
):
    tensor_size = lax.axis_size("tensor")
    expert_size = lax.axis_size("expert")
    local_count = tensor_size // 2
    tensor_index = lax.axis_index("tensor")
    expert_index = lax.axis_index("expert")
    own_local = tensor_index // 2
    own_expert = expert_index * local_count + own_local
    length, model_width = tokens.shape
    heads_here = w_query.shape[1] // HEAD_DIM
    full_cols = w_query.shape[1] * tensor_size
    expert_count = router.shape[1]
    capacity = 3 * length * TOP // (2 * expert_count)
    own_rows = length // tensor_size
    chunks = list(range(expert_size))
    bits = axis_bits("tensor")
    near_bits = bits[:-1]
    last = len(near_bits)

    def own_slice(rows):
        return lax.dynamic_slice_in_dim(rows, tensor_index * own_rows, own_rows, 0)

    pairs = [[2 * i, 2 * i + 1] for i in range(tensor_size // 2)]

    def pair_gather(values):
        return lax.all_gather(values, "tensor", axis_index_groups=pairs)

    grad_own = own_slice(grad_out)
    grad_near, _ = plane_rows(grad_out, 0, own_rows, sorted_order=True)
    grad_rows_of = {0: grad_out}
    grad_sent = {}
    for chunk in range(1, expert_size):
        if chunk == 1 or chunk % 4 == 1:
            groups = [[i, i ^ chunk] for i in range(expert_size) if i < i ^ chunk]
            grad_rows_of[chunk] = lax.all_gather(grad_near, "expert", axis_index_groups=groups)
        else:
            grad_sent[chunk] = swap(grad_own, "expert", chunk)
    out_pair = jnp.where(
        jnp.arange(2)[:, None, None] == tensor_index % 2,
        w_out[None],
        swap(w_out, "tensor", 1)[None],
    )
    expert_iota = jnp.arange(expert_count, dtype=jnp.int32)
    kept_table = jnp.sum(
        (
            (routes.T[:, None, :] == expert_iota[None, :, None]) & (slot_ids.T < capacity)[:, None, :]
        ).astype(jnp.float32),
        axis=0,
    )
    targets = jnp.arange(expert_size, dtype=jnp.int32) * local_count + own_local
    kept_rows = lax.all_to_all(
        jnp.take(kept_table, targets, axis=0).reshape(expert_size, tensor_size, own_rows),
        "expert",
        split_axis=0,
        concat_axis=0,
        tiled=True,
    )

    def here(chunk):
        from_plane = expert_index ^ chunk
        paired = chunk % 4 == 1
        side = jnp.where(from_plane > expert_index, 1, 0) if paired else 0 * from_plane
        return jnp.stack([tensor_index, from_plane, side]).astype(jnp.int32)

    score_scale = HEAD_DIM ** (-0.5)
    half_dim = HEAD_DIM // 2
    frequency = THETA ** (-2.0 * jnp.arange(half_dim, dtype=jnp.float32) / HEAD_DIM)
    angles = positions.astype(jnp.float32)[:, None] * frequency[None, :]
    cosine_table = jnp.concatenate([jnp.cos(angles)] * 2, axis=-1)
    sine_half = jnp.sin(angles)
    sine_table = jnp.concatenate([-sine_half, sine_half], axis=-1)
    token_float = tokens.astype(jnp.float32)
    attn_normal, attn_inverse = rms_forward(token_float)
    attn_in = (attn_normal * attn_gain).astype(jnp.bfloat16)
    head_shape = (length, heads_here, HEAD_DIM)
    w_all = jnp.concatenate([w_query, w_key, w_value], axis=1)
    query_raw = jnp.dot(attn_in, w_query, preferred_element_type=jnp.float32)
    key_raw = jnp.dot(attn_in, w_key, preferred_element_type=jnp.float32)
    value_rows = jnp.dot(attn_in, w_value, preferred_element_type=jnp.float32).astype(jnp.bfloat16)
    gains = jnp.stack([query_gain, key_gain])
    square_sums = spread_sum(
        jnp.stack([jnp.sum(query_raw * query_raw, axis=1), jnp.sum(key_raw * key_raw, axis=1)]),
        "tensor",
    )
    indices = sorted(direct_combos(near_bits))
    for chunk, piece in grad_sent.items():
        if chunk == 2:
            pieces = direct_gather(piece, near_bits, (square_sums,))
            grad_rows_of[chunk] = jnp.concatenate([pieces[i] for i in indices], axis=0)[None]
    gates, ups, downs, w_pair = [
        pair_gather(tie(weights, attn_in)) for weights in (w_gate[0], w_up[0], w_down[0], w_all)
    ]
    inverse = lax.rsqrt(square_sums / full_cols + EPS)[:, :, None]
    query_inverse, key_inverse = inverse[0], inverse[1]
    query_rows, key_rows, mixed_near, mixed_far = attend(
        here(0),
        own_rows,
        query_raw,
        key_raw,
        value_rows,
        query_inverse,
        key_inverse,
        cosine_table,
        sine_table,
        gains,
    )
    mixed_other = swap(mixed_far, "tensor", 1)
    ready = tie(here(0), *[grad_rows_of[chunk] for chunk in grad_sent if chunk == 2])
    attn_parts = near_product(
        ready, indices, mixed_near, mixed_other, w_out, out_pair, False
    )
    attn_moved = [swap(attn_parts[i], "tensor", i) for i in indices if i]
    hidden, ffn_in = residual(
        own_slice(tokens), ffn_gain[None, :], [attn_parts[0]] + attn_moved
    )
    chosen = (expert_iota == own_expert).astype(jnp.float32)[None, :]
    received = [ffn_in]
    gathered = [direct_gather(ffn_in, near_bits)]
    for chunk in chunks[1:]:
        sent = tie(ffn_in, gathered[0][near_bits[0]]) if chunk > 2 else ffn_in
        received.append(swap(sent, "expert", chunk))
    chain = None
    sums = []
    gate_columns = []
    late_pieces = {}
    for at, chunk in enumerate(chunks):
        scalars = here(chunk)
        if at == 0:
            scalars = tie(scalars, *received[1:3])
        elif at + 2 < expert_size:
            scalars = tie(scalars, received[at + 2])
        if at:
            after = [gathered[at - 1][i] for i in gathered[at - 1] if i]
            if at >= 2:
                after.append(gate_columns[at - 2])
            gathered.append(direct_gather(received[at], near_bits, after))
        if at >= 3:
            scalars = tie(scalars, sums[at - 3])
        here_now = [gathered[at][i] for i in indices if i]
        if at and chunk + 2 in grad_sent:
            late_pieces[chunk + 2] = gather_stage(
                {0: grad_sent[chunk + 2]}, 0, 0, near_bits, here_now
            )
        if chunk + 1 in late_pieces:
            pieces = late_pieces[chunk + 1]
            for stage in range(1, last):
                pieces = gather_stage(pieces, 0, stage, near_bits, here_now)
            grad_rows_of[chunk + 1] = jnp.concatenate([pieces[i] for i in indices], axis=0)[None]
        pieces, gate_column, chain = expert_chunk(
            at,
            expert_size,
            gathered[at],
            grad_rows_of[chunk],
            scalars,
            kept_rows,
            chosen,
            router,
            gates,
            ups,
            downs,
            chain,
        )
        gate_columns.append(gate_column)
        sums.append(near_scatter(pieces))

    def plane_total(near):
        return jnp.sum(near.astype(jnp.float32), axis=0).astype(jnp.bfloat16)

    row_totals = [plane_total(near) for near in sums[1:]]
    grad_parts = [sums[0]] + [
        swap(total, "expert", chunk) for total, chunk in zip(row_totals, chunks[1:])
    ]
    dl_all, x_all, dy_all, act_all, own_dp, other_dp, gated_own, gated_other = chain
    sent_pieces = expert_send(tie(here(0), row_totals[-1]), indices, act_all, gate_columns, downs)
    grad_hidden, hidden_low, grad_ffn_gain = norm_back(
        hidden, grad_own, ffn_gain[None, :], grad_parts[0], grad_parts[1:]
    )
    hidden_near, back_own, back_other = mixed_back(
        here(0), direct_gather(hidden_low, near_bits), w_out, out_pair
    )
    back_far = swap(back_other, "tensor", 1)
    sent_near = [
        near_scatter(tie(pieces, back_far) if at else pieces)
        for at, pieces in enumerate(sent_pieces)
    ]

    units = own_dp.shape[1] // 2
    other_wide = swap(contract(x_all, other_dp, 0, 0).astype(jnp.bfloat16), "tensor", 1)
    other_down = swap(contract(gated_other, dy_all, 0, 0).astype(jnp.bfloat16), "tensor", 1)
    grad_gate_w = contract(x_all, own_dp[:, :units], 0, 0) + other_wide[:, :units].astype(jnp.float32)
    grad_up_w = contract(x_all, own_dp[:, units:], 0, 0) + other_wide[:, units:].astype(jnp.float32)
    grad_down = contract(gated_own, dy_all, 0, 0) + other_down.astype(jnp.float32)
    grad_router_part = contract(dl_all, x_all, 0, 0)

    grad_w_out = contract(mixed_near, hidden_near, 0, 0)
    grad_w_out_other = contract(mixed_other, hidden_near, 0, 0).astype(jnp.bfloat16)
    grad_w_out_low = (
        grad_w_out + swap(grad_w_out_other, "tensor", 1).astype(jnp.float32)
    ).astype(jnp.bfloat16)
    query_scaled, key_scaled, value_low, query_inner, key_inner, gain_parts = attend_back(
        here(0),
        own_rows,
        back_own,
        back_far,
        query_rows,
        key_rows,
        value_rows,
        query_raw,
        key_raw,
        query_inverse,
        key_inverse,
        cosine_table,
        sine_table,
        gains,
    )
    inner_sums = spread_sum(jnp.stack([query_inner[:, 0], key_inner[:, 0]]), "tensor")
    inner_sums = tie(inner_sums, grad_w_out_low)[:, :, None]
    low_all, low_near, low_far = finish(
        here(0),
        own_rows,
        full_cols,
        query_scaled,
        key_scaled,
        value_low,
        query_raw,
        key_raw,
        query_inverse,
        key_inverse,
        inner_sums[0],
        inner_sums[1],
    )
    grad_attn = near_product(
        here(0), indices, low_near, swap(low_far, "tensor", 1), w_all, w_pair, True
    )
    columns_here = w_query.shape[1]
    grad_w_all = contract(attn_in, low_all, 0, 0).astype(jnp.bfloat16)
    grad_attn_moved = [swap(grad_attn[i], "tensor", i) for i in indices if i]
    _, token_low, grad_attn_gain = norm_back(
        own_slice(tokens), grad_hidden, attn_gain[None, :], grad_attn[0], grad_attn_moved
    )

    def gather_rows(piece):
        pieces = direct_gather(piece, near_bits)
        return {**pieces, **{i ^ 1: swap(near, "tensor", 1) for i, near in pieces.items()}}

    token_pieces = gather_rows(token_low)
    grad_tokens = place_rows(here(0), token_pieces)
    late = token_pieces[indices[-1]]
    moe_sum = hidden
    for at, chunk in enumerate(chunks):
        near = tie(sent_near[at], token_low)
        if chunk:
            moe_sum = moe_sum + swap(plane_total(near), "expert", chunk).astype(jnp.float32)
        else:
            moe_sum = moe_sum + jnp.sum(near.astype(jnp.float32), axis=0)
    output = place_rows(here(0), gather_rows(tie(moe_sum.astype(jnp.bfloat16), late)))
    sum_both = line_sum(grad_w_all[:, : 2 * columns_here], [None, token_low, late])
    sum_query, sum_key = sum_both[:, :columns_here], sum_both[:, columns_here:]
    sum_value, sum_out = [
        part.astype(jnp.float32)
        for part in lax.psum(
            (grad_w_all[:, 2 * columns_here :], grad_w_out_low), "expert"
        )
    ]
    plane_sums = spread_sum(
        jnp.concatenate([grad_router_part, grad_ffn_gain, grad_attn_gain], axis=0), "tensor"
    )
    scales = gain_parts.reshape(-1)
    scales = jnp.pad(scales, (0, model_width - scales.shape[0]))
    all_sums = spread_sum(jnp.concatenate([plane_sums, scales[None, :]], axis=0), "expert")
    return (
        output,
        grad_tokens,
        all_sums[expert_count + 1],
        sum_query,
        sum_key,
        sum_value,
        all_sums[expert_count + 2, :columns_here],
        all_sums[expert_count + 2, columns_here : 2 * columns_here],
        sum_out,
        all_sums[expert_count],
        all_sums[:expert_count].T,
        grad_gate_w[None],
        grad_up_w[None],
        grad_down[None],
    )


def solution(mesh):
    placed = (
        P("expert", None),
        P("expert"),
        P("expert", None),
        P("expert", None),
        P(),
        P(None, "tensor"),
        P(None, "tensor"),
        P(None, "tensor"),
        P("tensor"),
        P("tensor"),
        P("tensor", None),
        P(),
        P(),
        P(("expert", "tensor"), None, None),
        P(("expert", "tensor"), None, None),
        P(("expert", "tensor"), None, None),
        P("expert", None),
    )
    return jax.shard_map(
        on_device,
        mesh=mesh,
        in_specs=placed,
        out_specs=(
            P("expert", None),
            P("expert", None),
            P(),
            P(None, "tensor"),
            P(None, "tensor"),
            P(None, "tensor"),
            P("tensor"),
            P("tensor"),
            P("tensor", None),
            P(),
            P(),
            P(("expert", "tensor"), None, None),
            P(("expert", "tensor"), None, None),
            P(("expert", "tensor"), None, None),
        ),
        check_vma=False,
    )
```

```python
import jax
import jax.numpy as jnp
from jax import lax
from jax.experimental import pallas as pl
from jax.experimental.pallas import tpu as pltpu
from jax.sharding import PartitionSpec as P

HEAD_DIM = 128
TOP = 8


EPS = 1e-05
THETA = 10000.0


def rms_forward(values):
    inverse = lax.rsqrt(jnp.mean(values * values, axis=-1, keepdims=True) + EPS)
    return (values * inverse, inverse)


def rms_backward(grad_normed, normal_rows, inverse, gain_row):
    gain_grad = jnp.sum(grad_normed * normal_rows, axis=0)
    scaled = grad_normed * gain_row
    grad_rows = inverse * (
        scaled - normal_rows * jnp.mean(scaled * normal_rows, axis=-1, keepdims=True)
    )
    return (grad_rows, gain_grad)


def swap(values, axis, bit):
    return lax.ppermute(values, axis, [(i, i ^ bit) for i in range(lax.axis_size(axis))])


def axis_bits(axis):
    size = lax.axis_size(axis)
    return [size >> (k + 1) for k in range(size.bit_length() - 1)]


def spread_sum(values, axis):
    for bit in axis_bits(axis)[::-1]:
        values = values + swap(values, axis, bit)
    return values


def plane_order(turn):
    bits = axis_bits("tensor")[:-1]
    if turn % 2:
        bits = bits[::-1]
    order = [0]
    for bit in bits:
        order = order + [bit ^ i for i in order]
    return bits, order


def plane_gather(piece, turn):
    bits, _ = plane_order(turn)
    pieces = [piece]
    for bit in bits:
        pieces = pieces + [swap(p, "tensor", bit) for p in pieces]
    near = jnp.concatenate(pieces, axis=0)
    return near, swap(near, "tensor", 1)


def plane_scatter(near, far, turn):
    bits, _ = plane_order(turn)
    total = near.astype(jnp.float32) + swap(far, "tensor", 1).astype(jnp.float32)
    for bit in bits[::-1]:
        half = total.shape[0] // 2
        sent = total[half:].astype(jnp.bfloat16)
        total = total[:half].astype(jnp.bfloat16).astype(jnp.float32) + swap(
            sent, "tensor", bit
        ).astype(jnp.float32)
    return total


def plane_rows(values, turn, own_rows, sorted_order=False):
    _, order = plane_order(turn)
    if sorted_order:
        order = sorted(order)
    index = lax.axis_index("tensor")

    def block(i):
        return lax.dynamic_slice_in_dim(values, (index ^ i) * own_rows, own_rows, 0)

    near = jnp.concatenate([block(i) for i in order], axis=0)
    far = jnp.concatenate([block(i ^ 1) for i in order], axis=0)
    return near, far


def natural_rows(near, far, turn, own_rows):
    _, order = plane_order(turn)
    index = lax.axis_index("tensor")
    both = jnp.concatenate([near, far], axis=0)
    place = {}
    for at, i in enumerate(order):
        place[i] = at
        place[i ^ 1] = at + len(order)
    table = jnp.array([place[i] for i in range(2 * len(order))], jnp.int32)
    return jnp.concatenate(
        [
            lax.dynamic_slice_in_dim(both, table[index ^ i] * own_rows, own_rows, 0)
            for i in range(2 * len(order))
        ],
        axis=0,
    )


def contract(left, right, left_dim, right_dim):
    return lax.dot_general(
        left, right, (((left_dim,), (right_dim,)), ((), ())), preferred_element_type=jnp.float32
    )


def tie(values, *after):
    return lax.optimization_barrier((values, *after))[0]


def stages(turn, bits):
    if turn % 2:
        bits = bits[::-1]
    found = [[] for _ in bits]
    order = [(0, ())]
    for bit in bits:
        order = order + [(bit ^ i, used + (bit,)) for i, used in order]
    for i, used in order[1:]:
        found[len(used) - 1].append((i, i ^ used[-1], used[-1]))
    return found


def gather_stage(pieces, turn, stage, bits, after=()):
    pieces = dict(pieces)
    for i, source, bit in stages(turn, bits)[stage]:
        sent = pieces[source]
        if after:
            sent = tie(sent, *after)
        pieces[i] = swap(sent, "tensor", bit)
    return pieces


def direct_combos(bits):
    combos = [0]
    for bit in bits:
        combos = combos + [bit ^ i for i in combos]
    return combos


def direct_gather(piece, bits, after=()):
    pieces = {0: piece}
    for i in direct_combos(bits)[1:]:
        pieces[i] = swap(tie(piece, *after) if after else piece, "tensor", i)
    return pieces


def gather_all(piece, turn, bits):
    pieces = {0: piece}
    for stage in range(len(bits)):
        pieces = gather_stage(pieces, turn, stage, bits)
    return pieces


def scatter_stage(sums, turn, stage, bits, after=()):
    sums = dict(sums)
    for i, target, bit in stages(turn, bits)[len(bits) - 1 - stage]:
        sent = sums.pop(i).astype(jnp.bfloat16)
        if after:
            sent = tie(sent, *after)
        sums[target] = sums[target].astype(jnp.float32) + swap(sent, "tensor", bit).astype(
            jnp.float32
        )
    return sums


MEGABYTE = 1024 * 1024


def kernel_params():
    return pltpu.CompilerParams(vmem_limit_bytes=58 * MEGABYTE)


def cost(flops, moved):
    return pl.CostEstimate(flops=flops, bytes_accessed=moved, transcendentals=0)


def column_of(row):
    n = row.shape[1]
    down = lax.broadcasted_iota(jnp.int32, (n, n), 0)
    across = lax.broadcasted_iota(jnp.int32, (n, n), 1)
    return jnp.sum(jnp.where(down == across, row, 0.0), axis=1, keepdims=True)


def fixed(shape, single=True):
    if single:
        return pl.BlockSpec(
            shape, lambda *_: (0,) * len(shape), pipeline_mode=pl.Buffered(1)
        )
    return pl.BlockSpec(shape, lambda *_: (0,) * len(shape))


def expert_body(indices, local, place, scalars, *refs):
    count = len(indices)
    x_parts, refs = refs[:count], refs[count:]
    dy_source, kept, chosen, router, gates, ups, downs = refs[:7]
    core = scalars[0] & 1
    gate_own, gate_other = gates.at[core], gates.at[1 - core]
    up_own, up_other = ups.at[core], ups.at[1 - core]
    down_own, down_other = downs.at[core], downs.at[1 - core]
    scratch = refs[-13:]
    pieces, gate_out, dl_all, x_all, dy_all, act_all, own_dp, other_dp, gated_own, gated_other = refs[
        -23:-13
    ]
    rows, grads, wide, tall, raw, inner, act, slopes, gated, done, probs_ref, dots, sems = scratch
    rows_here, width = rows.shape
    units = gate_own.shape[1]
    own_rows = rows_here // count
    used = []
    dy_parts = []
    for i in indices:
        if local:
            at = pl.multiple_of((scalars[0] ^ i) * own_rows, own_rows)
            dy_parts.append(dy_source.at[pl.ds(at, own_rows)])
        else:
            dy_parts.append(dy_source.at[scalars[2], pl.ds(len(dy_parts) * own_rows, own_rows)])

    def start(source, target):
        copy = pltpu.make_async_copy(source, target, sems.at[len(used)])
        used.append(copy)
        copy.start()
        return copy

    def spread(parts, target):
        size = rows_here // len(parts)
        return [start(part, target.at[pl.ds(at * size, size)]) for at, part in enumerate(parts)]

    x_copies = spread(x_parts, rows)
    order = [gate_own, up_own, gate_other, up_other]
    wide_copies = [
        start(weight, wide.at[:, pl.ds(at * units, units)]) for at, weight in enumerate(order[:2])
    ]
    dy_copies = spread(dy_parts, grads)
    tall_copies = [start(down_own, tall.at[pl.ds(0, units)])]
    wide_copies += [
        start(weight, wide.at[:, pl.ds((at + 2) * units, units)])
        for at, weight in enumerate(order[2:])
    ]
    tall_copies.append(start(down_other, tall.at[pl.ds(units, units)]))

    here_rows = pl.ds(place * rows_here, rows_here)
    for copy in x_copies:
        copy.wait()
    outgoing = [start(rows, x_all.at[here_rows])]
    logits = contract(rows[...], router[...], 1, 0)
    exponent = jnp.exp(logits - jnp.max(logits, axis=-1, keepdims=True))
    probs = exponent / jnp.sum(exponent, axis=-1, keepdims=True)
    kept_column = jnp.concatenate(
        [column_of(kept[scalars[1], pl.ds(scalars[0] ^ i, 1), :]) for i in indices], axis=0
    )
    probs_ref[...] = probs
    gate_out[...] = jnp.sum(probs * chosen[...], axis=-1, keepdims=True) * kept_column
    dots[...] = jnp.zeros_like(dots)

    block = min(64, rows_here)
    for half in range(2):
        columns = pl.ds(half * units, units)
        for part in range(2):
            at = 2 * half + part
            wide_copies[at].wait()
            raw[:, pl.ds(part * units, units)] = contract(
                rows[...], wide[:, pl.ds(at * units, units)], 1, 0
            )
        if half == 0:
            for copy in dy_copies:
                copy.wait()
            outgoing.append(start(grads, dy_all.at[here_rows]))
        tall_copies[half].wait()
        inner[...] = contract(grads[...], tall[columns, :], 1, 1)

        @pl.loop(0, rows_here // block)
        def _(at):
            here = pl.ds(at * block, block)
            pre_gate = raw[here, pl.ds(0, units)]
            pre_up = raw[here, pl.ds(units, units)]
            inward = inner[here, :]
            gate = gate_out[here, :]
            sigmoid_gate = 1.0 / (1.0 + jnp.exp(-pre_gate))
            silu_gate = pre_gate * sigmoid_gate
            active = (silu_gate * pre_up).astype(jnp.bfloat16)
            act[here, columns] = active
            active = active.astype(jnp.float32)
            gated[here, columns] = (gate * active).astype(jnp.bfloat16)
            dots[here, :] += jnp.sum(inward * active, axis=-1, keepdims=True)
            grad_active = gate * inward
            slopes[here, pl.ds(2 * half * units, units)] = (
                grad_active * pre_up * sigmoid_gate * (1.0 + pre_gate * (1.0 - sigmoid_gate))
            ).astype(jnp.bfloat16)
            slopes[here, pl.ds((2 * half + 1) * units, units)] = (grad_active * silu_gate).astype(
                jnp.bfloat16
            )

    outgoing += [
        start(act, act_all.at[here_rows]),
        start(slopes.at[:, pl.ds(0, 2 * units)], own_dp.at[here_rows]),
        start(slopes.at[:, pl.ds(2 * units, 2 * units)], other_dp.at[here_rows]),
        start(gated.at[:, pl.ds(0, units)], gated_own.at[here_rows]),
        start(gated.at[:, pl.ds(units, units)], gated_other.at[here_rows]),
    ]
    grad_logits = (dots[...] * gate_out[...] * (chosen[...] - probs_ref[...])).astype(jnp.bfloat16)
    dl_all[...] = grad_logits
    step = min(512, width)
    for at in range(width // step):
        columns = pl.ds(at * step, step)
        done[:, columns] = (
            contract(slopes[...], wide[columns, :], 1, 1)
            + contract(grad_logits, router[columns, :], 1, 1)
        ).astype(jnp.bfloat16)
    for at, i in enumerate(indices):
        to = (scalars[0] ^ i) // 2
        outgoing.append(start(done.at[pl.ds(at * own_rows, own_rows)], pieces.at[to]))
    for copy in outgoing:
        copy.wait()


def expert_chunk(
    place, places, x_pieces, dy_source, here, kept, chosen, router, gates, ups, downs, chain
):
    indices = sorted(x_pieces)
    count = len(indices)
    own_rows, width = x_pieces[0].shape
    rows = own_rows * count
    units = gates.shape[2]
    experts = router.shape[1]
    extra = () if chain is None else tuple(chain)
    hbm = pl.BlockSpec(memory_space=pl.ANY)
    first = count + 8
    kept_shapes = [
        (rows * places, experts),
        (rows * places, width),
        (rows * places, width),
        (rows * places, 2 * units),
        (rows * places, 2 * units),
        (rows * places, 2 * units),
        (rows * places, units),
        (rows * places, units),
    ]
    results = pl.pallas_call(
        lambda *refs: expert_body(indices, dy_source.ndim == 2, place, *refs),
        grid_spec=pltpu.PrefetchScalarGridSpec(
            num_scalar_prefetch=1,
            grid=(1,),
            in_specs=[hbm] * (count + 1)
            + [fixed(kept.shape), fixed((1, experts)), fixed((width, experts))]
            + [hbm] * (3 + len(extra)),
            out_specs=[hbm]
            + [
                fixed((rows, 1), False),
                pl.BlockSpec((rows, experts), lambda j, *_: (place, 0)),
            ]
            + [hbm] * 7,
            scratch_shapes=[
                pltpu.VMEM((rows, width), jnp.bfloat16),
                pltpu.VMEM((rows, width), jnp.bfloat16),
                pltpu.VMEM((width, 4 * units), jnp.bfloat16),
                pltpu.VMEM((2 * units, width), jnp.bfloat16),
                pltpu.VMEM((rows, 2 * units), jnp.float32),
                pltpu.VMEM((rows, units), jnp.float32),
                pltpu.VMEM((rows, 2 * units), jnp.bfloat16),
                pltpu.VMEM((rows, 4 * units), jnp.bfloat16),
                pltpu.VMEM((rows, 2 * units), jnp.bfloat16),
                pltpu.VMEM((rows, width), jnp.bfloat16),
                pltpu.VMEM((rows, experts), jnp.float32),
                pltpu.VMEM((rows, 1), jnp.float32),
                pltpu.SemaphoreType.DMA((3 * count + 13,)),
            ],
        ),
        out_shape=[jax.ShapeDtypeStruct((count, own_rows, width), jnp.bfloat16)]
        + [jax.ShapeDtypeStruct((rows, 1), jnp.float32)]
        + [jax.ShapeDtypeStruct(shape, jnp.bfloat16) for shape in kept_shapes],
        input_output_aliases={first + i: 2 + i for i in range(len(extra))},
        compiler_params=kernel_params(),
        cost_estimate=cost(80 * rows * width * units, 10 * rows * width + 12 * width * units),
        name="expert_chunk",
    )(
        here,
        *[x_pieces[i] for i in indices],
        dy_source,
        kept,
        chosen,
        router,
        gates,
        ups,
        downs,
        *extra,
    )
    return results[0], results[1], results[2:]


def finish_body(own_rows, full_cols, scalars, *refs):
    (query_scaled, key_scaled, value_low, query_raw, key_raw) = refs[:5]
    sums, inner_sums, low_out, near_out, far_out = refs[5:]
    columns = value_low.shape[1]
    core = scalars[0] & 1
    for side, (scaled, raw) in enumerate(((query_scaled, query_raw), (key_scaled, key_raw))):
        inverse = inverse_norm(sums, side, full_cols)
        normal = raw[...] * inverse
        low_out[:, side * columns : (side + 1) * columns] = (
            inverse * (scaled[...] - normal * (tall_column(inner_sums[...], side) / full_cols))
        ).astype(jnp.bfloat16)
    low_out[:, 2 * columns :] = value_low[...]
    for at in range(low_out.shape[0] // (2 * own_rows)):
        first = low_out[pl.ds(2 * at * own_rows, own_rows), :]
        second = low_out[pl.ds((2 * at + 1) * own_rows, own_rows), :]
        near_out[pl.ds(at * own_rows, own_rows), :] = jnp.where(core == 0, first, second)
        far_out[pl.ds(at * own_rows, own_rows), :] = jnp.where(core == 0, second, first)


def finish(here, own_rows, full_cols, *args):
    rows, columns = args[0].shape
    shapes = [(rows, 3 * columns)] + [(rows // 2, 3 * columns)] * 2
    return pl.pallas_call(
        lambda *refs: finish_body(own_rows, full_cols, *refs),
        grid_spec=pltpu.PrefetchScalarGridSpec(
            num_scalar_prefetch=1,
            grid=(1,),
            in_specs=[fixed(arg.shape) for arg in args],
            out_specs=[fixed(shape, False) for shape in shapes],
        ),
        out_shape=[jax.ShapeDtypeStruct(shape, jnp.bfloat16) for shape in shapes],
        compiler_params=kernel_params(),
        cost_estimate=cost(20 * rows * columns, 24 * rows * columns),
        name="finish",
    )(here, *args)


def near_product_body(indices, transposed, scalars, own, other, own_weight, other_weight, *refs):
    pieces, value = refs[:-1], refs[-1]
    side = 1 if transposed else 0
    value[...] = contract(own[...], own_weight[...], 1, side) + contract(
        other[...], other_weight[0], 1, side
    )
    own_rows = pieces[0].shape[0]
    for at, i in enumerate(indices):
        here = pl.ds(pl.multiple_of((scalars[0] ^ i) // 2 * own_rows, own_rows), own_rows)
        pieces[at][...] = value[here, :].astype(jnp.bfloat16)


def near_product(here, indices, own, other, own_weight, pair_weight, transposed):
    rows, depth = own.shape
    width = own_weight.shape[0 if transposed else 1]
    block = min(512, width // 2)
    count = len(indices)
    if transposed:
        mine = pl.BlockSpec((block, depth), lambda j, at: (j, 0))
        theirs = pl.BlockSpec((1, block, depth), lambda j, at: (1 - (at[0] & 1), j, 0))
    else:
        mine = pl.BlockSpec((depth, block), lambda j, at: (0, j))
        theirs = pl.BlockSpec((1, depth, block), lambda j, at: (1 - (at[0] & 1), 0, j))
    results = pl.pallas_call(
        lambda *refs: near_product_body(indices, transposed, *refs),
        grid_spec=pltpu.PrefetchScalarGridSpec(
            num_scalar_prefetch=1,
            grid=(width // block,),
            in_specs=[fixed(own.shape), fixed(other.shape), mine, theirs],
            out_specs=[pl.BlockSpec((rows // count, block), lambda j, at: (0, j))] * count,
            scratch_shapes=[pltpu.VMEM((rows, block), jnp.float32)],
        ),
        out_shape=[jax.ShapeDtypeStruct((rows // count, width), jnp.bfloat16)] * count,
        compiler_params=kernel_params(),
        cost_estimate=cost(4 * rows * depth * width, 2 * rows * width + 4 * depth * width),
        name="near_product",
    )(here, own, other, own_weight, pair_weight)
    return dict(zip(indices, results))


def total_of(parts):
    total = parts[0][...].astype(jnp.float32)
    for part in parts[1:]:
        total = total + part[...].astype(jnp.float32)
    return jnp.sum(total, axis=0) if total.ndim == 3 else total


def residual_body(tokens, gain, *refs):
    hidden_out, low_out = refs[-2:]
    hidden = tokens[...].astype(jnp.float32) + total_of(refs[:-2])
    normal, _ = rms_forward(hidden)
    hidden_out[...] = hidden
    low_out[...] = (normal * gain[...]).astype(jnp.bfloat16)


def residual(tokens, gain, parts):
    rows, width = tokens.shape
    return pl.pallas_call(
        residual_body,
        grid=(1,),
        in_specs=[fixed(tokens.shape), fixed((1, width))] + [fixed(part.shape) for part in parts],
        out_specs=[fixed((rows, width), False)] * 2,
        out_shape=[
            jax.ShapeDtypeStruct((rows, width), jnp.float32),
            jax.ShapeDtypeStruct((rows, width), jnp.bfloat16),
        ],
        compiler_params=kernel_params(),
        cost_estimate=cost(10 * rows * width, 20 * rows * width),
        name="residual",
    )(tokens, gain, *parts)


def norm_back_body(values, passed, gain, near, *refs):
    grad_out, low_out, gain_out = refs[-3:]
    grad = total_of([near]) + total_of(refs[:-3]) if len(refs) > 3 else total_of([near])
    normal, inverse = rms_forward(values[...].astype(jnp.float32))
    gain_out[...] = jnp.sum(grad * normal, axis=0, keepdims=True)
    scaled = grad * gain[...]
    result = passed[...].astype(jnp.float32) + inverse * (
        scaled - normal * jnp.mean(scaled * normal, axis=-1, keepdims=True)
    )
    grad_out[...] = result
    low_out[...] = result.astype(jnp.bfloat16)


def norm_back(values, passed, gain, near, parts):
    rows, width = values.shape
    args = (values, passed, gain, near, *parts)
    return pl.pallas_call(
        norm_back_body,
        grid=(1,),
        in_specs=[fixed(arg.shape) for arg in args],
        out_specs=[fixed((rows, width), False)] * 2 + [fixed((1, width), False)],
        out_shape=[
            jax.ShapeDtypeStruct((rows, width), jnp.float32),
            jax.ShapeDtypeStruct((rows, width), jnp.bfloat16),
            jax.ShapeDtypeStruct((1, width), jnp.float32),
        ],
        compiler_params=kernel_params(),
        cost_estimate=cost(20 * rows * width, 20 * rows * width),
        name="norm_back",
    )(*args)


def mixed_back_body(indices, scalars, own_weight, other_weight, *refs):
    count = len(indices)
    pieces = refs[:count]
    rows_out, own_out, other_out, lows = refs[count:]
    own_rows = pieces[0].shape[0]
    for at, i in enumerate(indices):
        here = pl.ds(pl.multiple_of((scalars[0] ^ i) // 2 * own_rows, own_rows), own_rows)
        lows[here, :] = pieces[at][...]
    rows_out[...] = lows[...]
    own_out[...] = contract(lows[...], own_weight[...], 1, 1).astype(jnp.bfloat16)
    other_out[...] = contract(lows[...], other_weight[0], 1, 1).astype(jnp.bfloat16)


def mixed_back(here, pieces, own_weight, pair_weight):
    indices = sorted(pieces)
    own_rows, width = pieces[0].shape
    rows = own_rows * len(indices)
    depth = own_weight.shape[0]
    shapes = [(rows, width), (rows, depth), (rows, depth)]
    return pl.pallas_call(
        lambda *refs: mixed_back_body(indices, *refs),
        grid_spec=pltpu.PrefetchScalarGridSpec(
            num_scalar_prefetch=1,
            grid=(1,),
            in_specs=[
                fixed(own_weight.shape),
                pl.BlockSpec((1, depth, width), lambda j, at: (1 - (at[0] & 1), 0, 0)),
            ]
            + [fixed((own_rows, width))] * len(indices),
            out_specs=[fixed(shape, False) for shape in shapes],
            scratch_shapes=[pltpu.VMEM((rows, width), jnp.bfloat16)],
        ),
        out_shape=[jax.ShapeDtypeStruct(shape, jnp.bfloat16) for shape in shapes],
        compiler_params=kernel_params(),
        cost_estimate=cost(4 * rows * depth * width, 4 * rows * width + 4 * depth * width),
        name="mixed_back",
    )(here, own_weight, pair_weight, *[pieces[i] for i in indices])


def place_body(indices, own_rows, scalars, *refs):
    pieces, out, sems = refs[: len(indices)], refs[-2], refs[-1]
    copies = []
    for at, i in enumerate(indices):
        here = pl.ds(pl.multiple_of((scalars[0] ^ i) * own_rows, own_rows), own_rows)
        copies.append(pltpu.make_async_copy(pieces[at], out.at[here], sems.at[at]))
        copies[-1].start()
    for copy in copies:
        copy.wait()


def place_rows(here, pieces):
    indices = sorted(pieces)
    own_rows, width = pieces[0].shape
    return pl.pallas_call(
        lambda *refs: place_body(indices, own_rows, *refs),
        grid_spec=pltpu.PrefetchScalarGridSpec(
            num_scalar_prefetch=1,
            grid=(1,),
            in_specs=[fixed((own_rows, width))] * len(indices),
            out_specs=pl.BlockSpec(memory_space=pl.ANY),
            scratch_shapes=[pltpu.SemaphoreType.DMA((len(indices),))],
        ),
        out_shape=jax.ShapeDtypeStruct((own_rows * len(indices), width), pieces[0].dtype),
        compiler_params=kernel_params(),
        cost_estimate=cost(0, 4 * own_rows * len(indices) * width),
        name="place_rows",
    )(here, *[pieces[i] for i in indices])


def row_of(column):
    n = column.shape[0]
    down = lax.broadcasted_iota(jnp.int32, (n, n), 0)
    across = lax.broadcasted_iota(jnp.int32, (n, n), 1)
    return jnp.sum(jnp.where(down == across, column, 0.0), axis=0, keepdims=True)


def tall_column(rows, side):
    block = min(256, rows.shape[1])
    return jnp.concatenate(
        [
            column_of(rows[side : side + 1, at : at + block])
            for at in range(0, rows.shape[1], block)
        ],
        axis=0,
    )


def inverse_norm(sums, side, full_cols):
    return lax.rsqrt(tall_column(sums[...], side) / full_cols + EPS)


def project_in_body(tokens, gain, w_query, w_key, w_value, low_out, q_out, k_out, v_out, sums_out):
    normal, _ = rms_forward(tokens[...].astype(jnp.float32))
    low = (normal * gain[...]).astype(jnp.bfloat16)
    low_out[...] = low
    for side, (weight, out) in enumerate(((w_query, q_out), (w_key, k_out))):
        raw = contract(low, weight[...], 1, 0)
        out[...] = raw
        sums_out[side : side + 1, :] = row_of(jnp.sum(raw * raw, axis=-1, keepdims=True))
    v_out[...] = contract(low, w_value[...], 1, 0).astype(jnp.bfloat16)


def project_in(tokens, gain, w_query, w_key, w_value):
    length, width = tokens.shape
    columns = w_query.shape[1]
    block = min(256, length)
    wide = pl.BlockSpec((block, columns), lambda i: (i, 0))
    return pl.pallas_call(
        project_in_body,
        grid=(length // block,),
        in_specs=[pl.BlockSpec((block, width), lambda i: (i, 0)), fixed((1, width))]
        + [fixed(w_query.shape)] * 3,
        out_specs=[
            pl.BlockSpec((block, width), lambda i: (i, 0)),
            wide,
            wide,
            wide,
            pl.BlockSpec((2, block), lambda i: (0, i)),
        ],
        out_shape=[
            jax.ShapeDtypeStruct((length, width), jnp.bfloat16),
            jax.ShapeDtypeStruct((length, columns), jnp.float32),
            jax.ShapeDtypeStruct((length, columns), jnp.float32),
            jax.ShapeDtypeStruct((length, columns), jnp.bfloat16),
            jax.ShapeDtypeStruct((2, length), jnp.float32),
        ],
        compiler_params=kernel_params(),
        cost_estimate=cost(6 * length * width * columns, 8 * length * width),
        name="project_in",
    )(tokens, gain, w_query, w_key, w_value)


def turned(values, cosine, sine):
    return values * cosine + pltpu.roll(values, values.shape[1] // 2, 1) * sine


def head_blocks(length):
    block = min(256, length)
    return [(start, start + block) for start in range(0, length, block)]


def block_probs(queries, keys, start, end):
    scores = contract(queries, keys, 1, 1)
    down = lax.broadcasted_iota(jnp.int32, scores.shape, 0) + start
    across = lax.broadcasted_iota(jnp.int32, scores.shape, 1)
    scores = jnp.where(down >= across, scores, -1e30)
    exponent = jnp.exp(scores - jnp.max(scores, axis=-1, keepdims=True))
    return exponent * (1.0 / jnp.sum(exponent, axis=-1, keepdims=True))


def pair_split(rows, core, own_rows):
    low = jnp.concatenate(
        [rows[at : at + own_rows] for at in range(0, rows.shape[0], 2 * own_rows)], axis=0
    )
    high = jnp.concatenate(
        [rows[at : at + own_rows] for at in range(own_rows, rows.shape[0], 2 * own_rows)], axis=0
    )
    return jnp.where(core == 0, low, high), jnp.where(core == 0, high, low)


def attend_body(
    own_rows,
    full_cols,
    scalars,
    query_raw,
    key_raw,
    values,
    sums,
    cosine,
    sine,
    gains,
    q_out,
    k_out,
    near_out,
    far_out,
):
    length, columns = query_raw.shape
    core = scalars[0] & 1
    query_inv = inverse_norm(sums, 0, full_cols)
    key_inv = inverse_norm(sums, 1, full_cols)
    for head in range(columns // HEAD_DIM):
        here = pl.ds(head * HEAD_DIM, HEAD_DIM)
        query_normed = query_raw[:, here] * query_inv * gains[0:1, here]
        key_normed = key_raw[:, here] * key_inv * gains[1:2, here]
        q_out[:, here] = (
            turned(query_normed, cosine[...], sine[...]) * HEAD_DIM ** (-0.5)
        ).astype(jnp.bfloat16)
        k_out[:, here] = turned(key_normed, cosine[...], sine[...]).astype(jnp.bfloat16)
        for start, end in head_blocks(length):
            rows = pl.ds(start, end - start)
            probs = block_probs(q_out[rows, here], k_out[pl.ds(0, end), here], start, end)
            near, far = pair_split(
                contract(probs.astype(jnp.bfloat16), values[pl.ds(0, end), here], 1, 0),
                core,
                own_rows,
            )
            half = pl.ds(start // 2, (end - start) // 2)
            near_out[half, here] = near.astype(jnp.bfloat16)
            far_out[half, here] = far.astype(jnp.bfloat16)


def attend(here, own_rows, full_cols, *args):
    length, columns = args[0].shape
    shapes = [(length, columns)] * 2 + [(length // 2, columns)] * 2
    return pl.pallas_call(
        lambda *refs: attend_body(own_rows, full_cols, *refs),
        grid_spec=pltpu.PrefetchScalarGridSpec(
            num_scalar_prefetch=1,
            grid=(1,),
            in_specs=[fixed(arg.shape) for arg in args],
            out_specs=[fixed(shape, False) for shape in shapes],
        ),
        out_shape=[jax.ShapeDtypeStruct(shape, jnp.bfloat16) for shape in shapes],
        compiler_params=kernel_params(),
        cost_estimate=cost(4 * length * length * columns, 16 * length * columns),
        name="attend",
    )(here, *args)


def attend_back_body(
    own_rows,
    full_cols,
    scalars,
    near,
    far,
    queries,
    keys,
    values,
    query_raw,
    key_raw,
    sums,
    cosine,
    sine,
    gains,
    *refs,
):
    query_scaled, key_scaled, value_low, inner_out, gain_out = refs[:5]
    grads, grad_key, grad_value = refs[5:]
    length, columns = queries.shape
    core = scalars[0] & 1
    inners = [None, None]
    for at in range(length // (2 * own_rows)):
        mine, other = near[pl.ds(at * own_rows, own_rows), :], far[pl.ds(at * own_rows, own_rows), :]
        first = pl.ds(2 * at * own_rows, own_rows)
        second = pl.ds((2 * at + 1) * own_rows, own_rows)
        grads[first, :] = jnp.where(core == 0, mine, other)
        grads[second, :] = jnp.where(core == 0, other, mine)
    for head in range(columns // HEAD_DIM):
        here = pl.ds(head * HEAD_DIM, HEAD_DIM)
        grad_key[...] = jnp.zeros_like(grad_key)
        grad_value[...] = jnp.zeros_like(grad_value)
        for start, end in head_blocks(length):
            rows, past = pl.ds(start, end - start), pl.ds(0, end)
            probs = block_probs(queries[rows, here], keys[past, here], start, end)
            grad_probs = contract(grads[rows, here], values[past, here], 1, 1)
            grad_scores = (
                probs * (grad_probs - jnp.sum(probs * grad_probs, axis=-1, keepdims=True))
            ).astype(jnp.bfloat16)
            grad_value[past, :] += contract(probs.astype(jnp.bfloat16), grads[rows, here], 0, 0)
            grad_key[past, :] += contract(grad_scores, queries[rows, here], 0, 0)
            query_scaled[rows, here] = contract(grad_scores, keys[past, here], 1, 0)
        value_low[:, here] = grad_value[...].astype(jnp.bfloat16)
        sides = (
            (query_scaled[:, here] * HEAD_DIM ** (-0.5), query_raw, query_scaled),
            (grad_key[...], key_raw, key_scaled),
        )
        for side, (grad, raw, scaled_out) in enumerate(sides):
            normed = turned(grad, cosine[...], -sine[...])
            normal = raw[:, here] * inverse_norm(sums, side, full_cols)
            gain_out[side : side + 1, here] = jnp.sum(normed * normal, axis=0, keepdims=True)
            scaled = normed * gains[side : side + 1, here]
            scaled_out[:, here] = scaled
            inner = jnp.sum(scaled * normal, axis=-1, keepdims=True)
            inners[side] = inner if inners[side] is None else inners[side] + inner
    block = min(256, length)
    for side in range(2):
        for at in range(0, length, block):
            inner_out[side : side + 1, at : at + block] = row_of(inners[side][at : at + block])


def attend_back(here, own_rows, full_cols, *args):
    length, columns = args[2].shape
    wide = jax.ShapeDtypeStruct((length, columns), jnp.float32)
    outs = [
        wide,
        wide,
        jax.ShapeDtypeStruct((length, columns), jnp.bfloat16),
        jax.ShapeDtypeStruct((2, length), jnp.float32),
        jax.ShapeDtypeStruct((2, columns), jnp.float32),
    ]
    return pl.pallas_call(
        lambda *refs: attend_back_body(own_rows, full_cols, *refs),
        grid_spec=pltpu.PrefetchScalarGridSpec(
            num_scalar_prefetch=1,
            grid=(1,),
            in_specs=[fixed(arg.shape) for arg in args],
            out_specs=[fixed(out.shape, False) for out in outs],
            scratch_shapes=[pltpu.VMEM((length, columns), jnp.bfloat16)]
            + [pltpu.VMEM((length, HEAD_DIM), jnp.float32)] * 2,
        ),
        out_shape=outs,
        compiler_params=kernel_params(),
        cost_estimate=cost(8 * length * length * columns, 40 * length * columns),
        name="attend_back",
    )(here, *args)


def near_scatter(pieces):
    size = lax.axis_size("tensor")
    groups = [list(range(core, size, 2)) for core in range(2)]
    return lax.all_to_all(
        pieces, "tensor", split_axis=0, concat_axis=0, axis_index_groups=groups, tiled=True
    )


def line_sum(part, after):
    index = lax.axis_index("expert")
    bits = axis_bits("expert")[::-1]
    after = list(after) + [None] * (2 * len(bits))
    for bit in bits:
        half = part.shape[0] // 2
        high = (index // bit) % 2
        kept = lax.dynamic_slice_in_dim(part, high * half, half, 0)
        sent = lax.dynamic_slice_in_dim(part, (1 - high) * half, half, 0)
        wait = after.pop(0)
        if wait is not None:
            sent = tie(sent, wait)
        part = (
            kept.astype(jnp.float32) + swap(sent, "expert", bit).astype(jnp.float32)
        ).astype(jnp.bfloat16)
    for bit in bits[::-1]:
        high = (index // bit) % 2 == 1
        wait = after.pop(0)
        if wait is not None:
            part = tie(part, wait)
        other = swap(part, "expert", bit)
        part = jnp.concatenate([jnp.where(high, other, part), jnp.where(high, part, other)], axis=0)
    return part.astype(jnp.float32)


def send_body(indices, places, scalars, act, *refs):
    gates, (down_own, down_other), outs = refs[:places], refs[places : places + 2], refs[-places:]
    units = down_own.shape[1]
    value = contract(act[:, :units], down_own[0], 1, 0) + contract(
        act[:, units:], down_other[0], 1, 0
    )
    own_rows = outs[0].shape[1]
    for place in range(places):

        @pl.when(pl.program_id(1) == place)
        def _():
            sent = (gates[place][...] * value).astype(jnp.bfloat16)
            for at, i in enumerate(indices):
                outs[place][(scalars[0] ^ i) // 2] = sent[at * own_rows : (at + 1) * own_rows]


def expert_send(here, indices, act_all, gates, downs):
    rows = gates[0].shape[0]
    count = len(indices)
    places = len(gates)
    _, units, width = downs.shape
    block = min(1024, width // 2)
    return pl.pallas_call(
        lambda *refs: send_body(indices, places, *refs),
        grid_spec=pltpu.PrefetchScalarGridSpec(
            num_scalar_prefetch=1,
            grid=(width // block, places),
            in_specs=[pl.BlockSpec((rows, 2 * units), lambda j, k, *_: (k, 0))]
            + [fixed((rows, 1))] * places
            + [
                pl.BlockSpec((1, units, block), lambda j, k, at: (at[0] & 1, 0, j)),
                pl.BlockSpec((1, units, block), lambda j, k, at: (1 - (at[0] & 1), 0, j)),
            ],
            out_specs=[pl.BlockSpec((count, rows // count, block), lambda j, k, *_: (0, 0, j))]
            * places,
        ),
        out_shape=[jax.ShapeDtypeStruct((count, rows // count, width), jnp.bfloat16)] * places,
        compiler_params=kernel_params(),
        cost_estimate=cost(
            4 * places * rows * width * units, places * 4 * rows * width + 4 * width * units
        ),
        name="expert_send",
    )(here, act_all, *gates, downs, downs)


def on_device(
    tokens,
    positions,
    routes,
    slot_ids,
    attn_gain,
    w_query,
    w_key,
    w_value,
    query_gain,
    key_gain,
    w_out,
    ffn_gain,
    router,
    w_gate,
    w_up,
    w_down,
    grad_out,
):
    tensor_size = lax.axis_size("tensor")
    expert_size = lax.axis_size("expert")
    local_count = tensor_size // 2
    tensor_index = lax.axis_index("tensor")
    expert_index = lax.axis_index("expert")
    own_local = tensor_index // 2
    own_expert = expert_index * local_count + own_local
    length, model_width = tokens.shape
    heads_here = w_query.shape[1] // HEAD_DIM
    full_cols = w_query.shape[1] * tensor_size
    expert_count = router.shape[1]
    capacity = 3 * length * TOP // (2 * expert_count)
    own_rows = length // tensor_size
    chunks = list(range(expert_size))
    bits = axis_bits("tensor")
    near_bits = bits[:-1]
    last = len(near_bits)

    def own_slice(rows):
        return lax.dynamic_slice_in_dim(rows, tensor_index * own_rows, own_rows, 0)

    pairs = [[2 * i, 2 * i + 1] for i in range(tensor_size // 2)]

    def pair_gather(values):
        return lax.all_gather(values, "tensor", axis_index_groups=pairs)

    grad_own = own_slice(grad_out)
    grad_near, _ = plane_rows(grad_out, 0, own_rows, sorted_order=True)
    grad_rows_of = {0: grad_out}
    grad_sent = {}
    for chunk in range(1, expert_size):
        if chunk == 1 or chunk % 4 == 1:
            groups = [[i, i ^ chunk] for i in range(expert_size) if i < i ^ chunk]
            grad_rows_of[chunk] = lax.all_gather(grad_near, "expert", axis_index_groups=groups)
        else:
            grad_sent[chunk] = swap(grad_own, "expert", chunk)
    out_pair = jnp.where(
        jnp.arange(2)[:, None, None] == tensor_index % 2,
        w_out[None],
        swap(w_out, "tensor", 1)[None],
    )
    expert_iota = jnp.arange(expert_count, dtype=jnp.int32)
    kept_table = jnp.sum(
        (
            (routes.T[:, None, :] == expert_iota[None, :, None]) & (slot_ids.T < capacity)[:, None, :]
        ).astype(jnp.float32),
        axis=0,
    )
    targets = jnp.arange(expert_size, dtype=jnp.int32) * local_count + own_local
    kept_rows = lax.all_to_all(
        jnp.take(kept_table, targets, axis=0).reshape(expert_size, tensor_size, own_rows),
        "expert",
        split_axis=0,
        concat_axis=0,
        tiled=True,
    )

    def here(chunk):
        from_plane = expert_index ^ chunk
        paired = chunk % 4 == 1
        side = jnp.where(from_plane > expert_index, 1, 0) if paired else 0 * from_plane
        return jnp.stack([tensor_index, from_plane, side]).astype(jnp.int32)

    score_scale = HEAD_DIM ** (-0.5)
    half_dim = HEAD_DIM // 2
    frequency = THETA ** (-2.0 * jnp.arange(half_dim, dtype=jnp.float32) / HEAD_DIM)
    angles = positions.astype(jnp.float32)[:, None] * frequency[None, :]
    cosine_table = jnp.concatenate([jnp.cos(angles)] * 2, axis=-1)
    sine_half = jnp.sin(angles)
    sine_table = jnp.concatenate([-sine_half, sine_half], axis=-1)
    attn_in, query_raw, key_raw, value_rows, square_sums = project_in(
        tokens, attn_gain[None, :], w_query, w_key, w_value
    )
    w_all = jnp.concatenate([w_query, w_key, w_value], axis=1)
    gains = jnp.stack([query_gain, key_gain])
    for at, bit in enumerate(bits[::-1]):
        square_sums = square_sums + swap(square_sums, "tensor", bit)
        if at == len(bits) - 2:
            early_sums = square_sums
    indices = sorted(direct_combos(near_bits))
    ready = here(0)
    if 2 in grad_sent:
        pieces = direct_gather(grad_sent[2], near_bits, (early_sums,))
        grad_rows_of[2] = jnp.concatenate([pieces[i] for i in indices], axis=0)[None]
        ready = tie(ready, *[pieces[i] for i in indices if i])
    gates, ups, downs, w_pair = [
        pair_gather(tie(weights, attn_in)) for weights in (w_gate[0], w_up[0], w_down[0], w_all)
    ]
    query_rows, key_rows, mixed_near, mixed_far = attend(
        ready,
        own_rows,
        full_cols,
        query_raw,
        key_raw,
        value_rows,
        square_sums,
        cosine_table,
        sine_table,
        gains,
    )
    mixed_other = swap(mixed_far, "tensor", 1)
    attn_parts = near_product(
        here(0), indices, mixed_near, mixed_other, w_out, out_pair, False
    )
    attn_moved = [swap(attn_parts[i], "tensor", i) for i in indices if i]
    hidden, ffn_in = residual(
        tie(own_slice(tokens), grad_rows_of[1], *[grad_sent[c] for c in grad_sent if c > 2]),
        ffn_gain[None, :],
        [attn_parts[0]] + attn_moved,
    )
    chosen = (expert_iota == own_expert).astype(jnp.float32)[None, :]
    received = [ffn_in]
    gathered = [direct_gather(ffn_in, near_bits)]
    for chunk in chunks[1:]:
        sent = tie(ffn_in, gathered[0][near_bits[0]]) if chunk > 2 else ffn_in
        received.append(swap(sent, "expert", chunk))
    chain = None
    sums = []
    gate_columns = []
    late_pieces = {}
    for at, chunk in enumerate(chunks):
        scalars = here(chunk)
        if at:
            after = [gathered[at - 1][i] for i in gathered[at - 1] if i]
            if at >= 2:
                after.append(gate_columns[at - 2])
            gathered.append(direct_gather(received[at], near_bits, after))
        if at >= 3:
            scalars = tie(scalars, sums[at - 3])
        here_now = [gathered[at][i] for i in indices if i]
        if at and chunk + 2 in grad_sent:
            late_pieces[chunk + 2] = gather_stage(
                {0: grad_sent[chunk + 2]}, 0, 0, near_bits, here_now
            )
        if chunk + 1 in late_pieces:
            pieces = late_pieces[chunk + 1]
            for stage in range(1, last):
                pieces = gather_stage(pieces, 0, stage, near_bits, here_now)
            grad_rows_of[chunk + 1] = jnp.concatenate([pieces[i] for i in indices], axis=0)[None]
        pieces, gate_column, chain = expert_chunk(
            at,
            expert_size,
            gathered[at],
            grad_rows_of[chunk],
            scalars,
            kept_rows,
            chosen,
            router,
            gates,
            ups,
            downs,
            chain,
        )
        gate_columns.append(gate_column)
        sums.append(near_scatter(pieces))

    def plane_total(near):
        return jnp.sum(near.astype(jnp.float32), axis=0).astype(jnp.bfloat16)

    dl_all, x_all, dy_all, act_all, own_dp, other_dp, gated_own, gated_other = chain
    row_totals = [plane_total(near) for near in sums[1:-1]]
    sent_pieces = expert_send(tie(here(0), *row_totals), indices, act_all, gate_columns, downs)
    row_totals.append(plane_total(tie(sums[-1], sent_pieces[0])))
    grad_parts = [sums[0]] + [
        swap(total, "expert", chunk) for total, chunk in zip(row_totals, chunks[1:])
    ]
    sent_near = {1: near_scatter(tie(sent_pieces[1], row_totals[-1]))}
    grad_parts[0] = tie(grad_parts[0], sent_near[1])
    grad_hidden, hidden_low, grad_ffn_gain = norm_back(
        hidden, grad_own, ffn_gain[None, :], grad_parts[0], grad_parts[1:]
    )
    hidden_near, back_own, back_other = mixed_back(
        tie(here(0), w_pair), direct_gather(hidden_low, near_bits), w_out, out_pair
    )
    back_far = swap(back_other, "tensor", 1)
    sent_moved = [swap(plane_total(sent_near[1]), "expert", 1)]
    sent_near[0] = near_scatter(tie(sent_pieces[0], sent_near[1]))
    for chunk in chunks[2:]:
        sent_near[chunk] = near_scatter(
            tie(sent_pieces[chunk], hidden_near if chunk == 2 else back_far)
        )
        sent_moved.append(swap(plane_total(sent_near[chunk]), "expert", chunk))

    units = own_dp.shape[1] // 2
    other_wide = swap(contract(x_all, other_dp, 0, 0).astype(jnp.bfloat16), "tensor", 1)
    other_down = swap(contract(gated_other, dy_all, 0, 0).astype(jnp.bfloat16), "tensor", 1)
    grad_gate_w = contract(x_all, own_dp[:, :units], 0, 0) + other_wide[:, :units].astype(jnp.float32)
    grad_up_w = contract(x_all, own_dp[:, units:], 0, 0) + other_wide[:, units:].astype(jnp.float32)
    grad_down = contract(gated_own, dy_all, 0, 0) + other_down.astype(jnp.float32)
    grad_router_part = contract(dl_all, x_all, 0, 0)

    grad_w_out = contract(mixed_near, hidden_near, 0, 0)
    grad_w_out_other = contract(mixed_other, hidden_near, 0, 0).astype(jnp.bfloat16)
    grad_w_out_low = (
        grad_w_out + swap(grad_w_out_other, "tensor", 1).astype(jnp.float32)
    ).astype(jnp.bfloat16)
    query_scaled, key_scaled, value_low, inner_sums, gain_parts = attend_back(
        here(0),
        own_rows,
        full_cols,
        back_own,
        back_far,
        query_rows,
        key_rows,
        value_rows,
        query_raw,
        key_raw,
        square_sums,
        cosine_table,
        sine_table,
        gains,
    )
    grad_w_value = contract(attn_in, value_low, 0, 0).astype(jnp.bfloat16)
    inner_sums = spread_sum(inner_sums, "tensor")
    inner_sums = tie(inner_sums, grad_w_out_low, grad_w_value)
    low_all, low_near, low_far = finish(
        here(0),
        own_rows,
        full_cols,
        query_scaled,
        key_scaled,
        value_low,
        query_raw,
        key_raw,
        square_sums,
        inner_sums,
    )
    grad_attn = near_product(
        here(0), indices, low_near, swap(low_far, "tensor", 1), w_all, w_pair, True
    )
    columns_here = w_query.shape[1]
    grad_w_both = contract(attn_in, low_all[:, : 2 * columns_here], 0, 0).astype(jnp.bfloat16)
    grad_attn_moved = [swap(grad_attn[i], "tensor", i) for i in indices if i]
    _, token_low, grad_attn_gain = norm_back(
        own_slice(tokens), grad_hidden, attn_gain[None, :], grad_attn[0], grad_attn_moved
    )

    def gather_rows(piece):
        pieces = direct_gather(piece, near_bits)
        return {**pieces, **{i ^ 1: swap(near, "tensor", 1) for i, near in pieces.items()}}

    token_pieces = gather_rows(token_low)
    grad_tokens = place_rows(here(0), token_pieces)
    late = [token_pieces[i] for i in indices if i]
    moe_sum = hidden + jnp.sum(tie(sent_near[0], *late).astype(jnp.float32), axis=0)
    for moved in sent_moved:
        moe_sum = moe_sum + moved.astype(jnp.float32)
    output = place_rows(here(0), gather_rows(moe_sum.astype(jnp.bfloat16)))
    sum_both = line_sum(grad_w_both, [None, late[-1], None])
    sum_query, sum_key = sum_both[:, :columns_here], sum_both[:, columns_here:]
    sum_value, sum_out = [
        part.astype(jnp.float32)
        for part in lax.psum(
            (grad_w_value, grad_w_out_low), "expert"
        )
    ]
    plane_sums = spread_sum(
        tie(jnp.concatenate([grad_router_part, grad_ffn_gain, grad_attn_gain], axis=0), *late),
        "tensor",
    )
    scales = gain_parts.reshape(-1)
    scales = jnp.pad(scales, (0, model_width - scales.shape[0]))
    all_sums = spread_sum(jnp.concatenate([plane_sums, scales[None, :]], axis=0), "expert")
    return (
        output,
        grad_tokens,
        all_sums[expert_count + 1],
        sum_query,
        sum_key,
        sum_value,
        all_sums[expert_count + 2, :columns_here],
        all_sums[expert_count + 2, columns_here : 2 * columns_here],
        sum_out,
        all_sums[expert_count],
        all_sums[:expert_count].T,
        grad_gate_w[None],
        grad_up_w[None],
        grad_down[None],
    )


def solution(mesh):
    placed = (
        P("expert", None),
        P("expert"),
        P("expert", None),
        P("expert", None),
        P(),
        P(None, "tensor"),
        P(None, "tensor"),
        P(None, "tensor"),
        P("tensor"),
        P("tensor"),
        P("tensor", None),
        P(),
        P(),
        P(("expert", "tensor"), None, None),
        P(("expert", "tensor"), None, None),
        P(("expert", "tensor"), None, None),
        P("expert", None),
    )
    return jax.shard_map(
        on_device,
        mesh=mesh,
        in_specs=placed,
        out_specs=(
            P("expert", None),
            P("expert", None),
            P(),
            P(None, "tensor"),
            P(None, "tensor"),
            P(None, "tensor"),
            P("tensor"),
            P("tensor"),
            P("tensor", None),
            P(),
            P(),
            P(("expert", "tensor"), None, None),
            P(("expert", "tensor"), None, None),
            P(("expert", "tensor"), None, None),
        ),
        check_vma=False,
    )
```

```python
import jax
import jax.numpy as jnp
from jax import lax
from jax.experimental import pallas as pl
from jax.experimental.pallas import tpu as pltpu
from jax.sharding import PartitionSpec as P

HEAD_DIM = 128
TOP = 8


EPS = 1e-05
THETA = 10000.0


def rms_forward(values):
    inverse = lax.rsqrt(jnp.mean(values * values, axis=-1, keepdims=True) + EPS)
    return (values * inverse, inverse)


def rms_backward(grad_normed, normal_rows, inverse, gain_row):
    gain_grad = jnp.sum(grad_normed * normal_rows, axis=0)
    scaled = grad_normed * gain_row
    grad_rows = inverse * (
        scaled - normal_rows * jnp.mean(scaled * normal_rows, axis=-1, keepdims=True)
    )
    return (grad_rows, gain_grad)


def swap(values, axis, bit):
    return lax.ppermute(values, axis, [(i, i ^ bit) for i in range(lax.axis_size(axis))])


def axis_bits(axis):
    size = lax.axis_size(axis)
    return [size >> (k + 1) for k in range(size.bit_length() - 1)]


def spread_sum(values, axis):
    for bit in axis_bits(axis)[::-1]:
        values = values + swap(values, axis, bit)
    return values


def plane_order(turn):
    bits = axis_bits("tensor")[:-1]
    if turn % 2:
        bits = bits[::-1]
    order = [0]
    for bit in bits:
        order = order + [bit ^ i for i in order]
    return bits, order


def plane_gather(piece, turn):
    bits, _ = plane_order(turn)
    pieces = [piece]
    for bit in bits:
        pieces = pieces + [swap(p, "tensor", bit) for p in pieces]
    near = jnp.concatenate(pieces, axis=0)
    return near, swap(near, "tensor", 1)


def plane_scatter(near, far, turn):
    bits, _ = plane_order(turn)
    total = near.astype(jnp.float32) + swap(far, "tensor", 1).astype(jnp.float32)
    for bit in bits[::-1]:
        half = total.shape[0] // 2
        sent = total[half:].astype(jnp.bfloat16)
        total = total[:half].astype(jnp.bfloat16).astype(jnp.float32) + swap(
            sent, "tensor", bit
        ).astype(jnp.float32)
    return total


def plane_rows(values, turn, own_rows, sorted_order=False):
    _, order = plane_order(turn)
    if sorted_order:
        order = sorted(order)
    index = lax.axis_index("tensor")

    def block(i):
        return lax.dynamic_slice_in_dim(values, (index ^ i) * own_rows, own_rows, 0)

    near = jnp.concatenate([block(i) for i in order], axis=0)
    far = jnp.concatenate([block(i ^ 1) for i in order], axis=0)
    return near, far


def natural_rows(near, far, turn, own_rows):
    _, order = plane_order(turn)
    index = lax.axis_index("tensor")
    both = jnp.concatenate([near, far], axis=0)
    place = {}
    for at, i in enumerate(order):
        place[i] = at
        place[i ^ 1] = at + len(order)
    table = jnp.array([place[i] for i in range(2 * len(order))], jnp.int32)
    return jnp.concatenate(
        [
            lax.dynamic_slice_in_dim(both, table[index ^ i] * own_rows, own_rows, 0)
            for i in range(2 * len(order))
        ],
        axis=0,
    )


def contract(left, right, left_dim, right_dim):
    return lax.dot_general(
        left, right, (((left_dim,), (right_dim,)), ((), ())), preferred_element_type=jnp.float32
    )


def tie(values, *after):
    return lax.optimization_barrier((values, *after))[0]


def stages(turn, bits):
    if turn % 2:
        bits = bits[::-1]
    found = [[] for _ in bits]
    order = [(0, ())]
    for bit in bits:
        order = order + [(bit ^ i, used + (bit,)) for i, used in order]
    for i, used in order[1:]:
        found[len(used) - 1].append((i, i ^ used[-1], used[-1]))
    return found


def gather_stage(pieces, turn, stage, bits, after=()):
    pieces = dict(pieces)
    for i, source, bit in stages(turn, bits)[stage]:
        sent = pieces[source]
        if after:
            sent = tie(sent, *after)
        pieces[i] = swap(sent, "tensor", bit)
    return pieces


def direct_combos(bits):
    combos = [0]
    for bit in bits:
        combos = combos + [bit ^ i for i in combos]
    return combos


def direct_gather(piece, bits, after=()):
    pieces = {0: piece}
    for i in direct_combos(bits)[1:]:
        pieces[i] = swap(tie(piece, *after) if after else piece, "tensor", i)
    return pieces


def gather_all(piece, turn, bits):
    pieces = {0: piece}
    for stage in range(len(bits)):
        pieces = gather_stage(pieces, turn, stage, bits)
    return pieces


def scatter_stage(sums, turn, stage, bits, after=()):
    sums = dict(sums)
    for i, target, bit in stages(turn, bits)[len(bits) - 1 - stage]:
        sent = sums.pop(i).astype(jnp.bfloat16)
        if after:
            sent = tie(sent, *after)
        sums[target] = sums[target].astype(jnp.float32) + swap(sent, "tensor", bit).astype(
            jnp.float32
        )
    return sums


MEGABYTE = 1024 * 1024


def kernel_params():
    return pltpu.CompilerParams(vmem_limit_bytes=58 * MEGABYTE)


def cost(flops, moved):
    return pl.CostEstimate(flops=flops, bytes_accessed=moved, transcendentals=0)


def column_of(row):
    n = row.shape[1]
    down = lax.broadcasted_iota(jnp.int32, (n, n), 0)
    across = lax.broadcasted_iota(jnp.int32, (n, n), 1)
    return jnp.sum(jnp.where(down == across, row, 0.0), axis=1, keepdims=True)


def fixed(shape, single=True):
    if single:
        return pl.BlockSpec(
            shape, lambda *_: (0,) * len(shape), pipeline_mode=pl.Buffered(1)
        )
    return pl.BlockSpec(shape, lambda *_: (0,) * len(shape))


def expert_body(indices, local, place, scalars, *refs):
    count = len(indices)
    x_parts, refs = refs[:count], refs[count:]
    dy_source, kept, chosen, router, gates, ups, downs = refs[:7]
    core = scalars[0] & 1
    gate_own, gate_other = gates.at[core], gates.at[1 - core]
    up_own, up_other = ups.at[core], ups.at[1 - core]
    down_own, down_other = downs.at[core], downs.at[1 - core]
    scratch = refs[-13:]
    pieces, gate_out, dl_all, x_all, dy_all, act_all, own_dp, other_dp, gated_own, gated_other = refs[
        -23:-13
    ]
    rows, grads, wide, tall, raw, inner, act, slopes, gated, done, probs_ref, dots, sems = scratch
    rows_here, width = rows.shape
    units = gate_own.shape[1]
    own_rows = rows_here // count
    used = []
    dy_parts = []
    for i in indices:
        if local:
            at = pl.multiple_of((scalars[0] ^ i) * own_rows, own_rows)
            dy_parts.append(dy_source.at[pl.ds(at, own_rows)])
        else:
            dy_parts.append(dy_source.at[(scalars[0] ^ i) // 2])

    def start(source, target):
        copy = pltpu.make_async_copy(source, target, sems.at[len(used)])
        used.append(copy)
        copy.start()
        return copy

    def spread(parts, target):
        size = rows_here // len(parts)
        return [start(part, target.at[pl.ds(at * size, size)]) for at, part in enumerate(parts)]

    x_copies = spread(x_parts, rows)
    order = [gate_own, up_own, gate_other, up_other]
    wide_copies = [
        start(weight, wide.at[:, pl.ds(at * units, units)]) for at, weight in enumerate(order[:2])
    ]
    dy_copies = spread(dy_parts, grads)
    tall_copies = [start(down_own, tall.at[pl.ds(0, units)])]
    wide_copies += [
        start(weight, wide.at[:, pl.ds((at + 2) * units, units)])
        for at, weight in enumerate(order[2:])
    ]
    tall_copies.append(start(down_other, tall.at[pl.ds(units, units)]))

    here_rows = pl.ds(place * rows_here, rows_here)
    for copy in x_copies:
        copy.wait()
    outgoing = [start(rows, x_all.at[here_rows])]
    logits = contract(rows[...], router[...], 1, 0)
    exponent = jnp.exp(logits - jnp.max(logits, axis=-1, keepdims=True))
    probs = exponent / jnp.sum(exponent, axis=-1, keepdims=True)
    kept_column = jnp.concatenate(
        [column_of(kept[scalars[1], pl.ds(scalars[0] ^ i, 1), :]) for i in indices], axis=0
    )
    probs_ref[...] = probs
    gate_out[...] = jnp.sum(probs * chosen[...], axis=-1, keepdims=True) * kept_column
    dots[...] = jnp.zeros_like(dots)

    block = min(64, rows_here)
    for half in range(2):
        columns = pl.ds(half * units, units)
        for part in range(2):
            at = 2 * half + part
            wide_copies[at].wait()
            raw[:, pl.ds(part * units, units)] = contract(
                rows[...], wide[:, pl.ds(at * units, units)], 1, 0
            )
        if half == 0:
            for copy in dy_copies:
                copy.wait()
            outgoing.append(start(grads, dy_all.at[here_rows]))
        tall_copies[half].wait()
        inner[...] = contract(grads[...], tall[columns, :], 1, 1)

        @pl.loop(0, rows_here // block)
        def _(at):
            here = pl.ds(at * block, block)
            pre_gate = raw[here, pl.ds(0, units)]
            pre_up = raw[here, pl.ds(units, units)]
            inward = inner[here, :]
            gate = gate_out[here, :]
            sigmoid_gate = 1.0 / (1.0 + jnp.exp(-pre_gate))
            silu_gate = pre_gate * sigmoid_gate
            active = (silu_gate * pre_up).astype(jnp.bfloat16)
            act[here, columns] = active
            active = active.astype(jnp.float32)
            gated[here, columns] = (gate * active).astype(jnp.bfloat16)
            dots[here, :] += jnp.sum(inward * active, axis=-1, keepdims=True)
            grad_active = gate * inward
            slopes[here, pl.ds(2 * half * units, units)] = (
                grad_active * pre_up * sigmoid_gate * (1.0 + pre_gate * (1.0 - sigmoid_gate))
            ).astype(jnp.bfloat16)
            slopes[here, pl.ds((2 * half + 1) * units, units)] = (grad_active * silu_gate).astype(
                jnp.bfloat16
            )

    outgoing += [
        start(act, act_all.at[here_rows]),
        start(slopes.at[:, pl.ds(0, 2 * units)], own_dp.at[here_rows]),
        start(slopes.at[:, pl.ds(2 * units, 2 * units)], other_dp.at[here_rows]),
        start(gated.at[:, pl.ds(0, units)], gated_own.at[here_rows]),
        start(gated.at[:, pl.ds(units, units)], gated_other.at[here_rows]),
    ]
    grad_logits = (dots[...] * gate_out[...] * (chosen[...] - probs_ref[...])).astype(jnp.bfloat16)
    dl_all[...] = grad_logits
    step = min(512, width)
    for at in range(width // step):
        columns = pl.ds(at * step, step)
        done[:, columns] = (
            contract(slopes[...], wide[columns, :], 1, 1)
            + contract(grad_logits, router[columns, :], 1, 1)
        ).astype(jnp.bfloat16)
    for at, i in enumerate(indices):
        to = (scalars[0] ^ i) // 2
        outgoing.append(start(done.at[pl.ds(at * own_rows, own_rows)], pieces.at[to]))
    for copy in outgoing:
        copy.wait()


def expert_chunk(
    place, places, x_pieces, dy_source, here, kept, chosen, router, gates, ups, downs, chain
):
    indices = sorted(x_pieces)
    count = len(indices)
    own_rows, width = x_pieces[0].shape
    rows = own_rows * count
    units = gates.shape[2]
    experts = router.shape[1]
    extra = () if chain is None else tuple(chain)
    hbm = pl.BlockSpec(memory_space=pl.ANY)
    first = count + 8
    kept_shapes = [
        (rows * places, experts),
        (rows * places, width),
        (rows * places, width),
        (rows * places, 2 * units),
        (rows * places, 2 * units),
        (rows * places, 2 * units),
        (rows * places, units),
        (rows * places, units),
    ]
    results = pl.pallas_call(
        lambda *refs: expert_body(indices, dy_source.ndim == 2, place, *refs),
        grid_spec=pltpu.PrefetchScalarGridSpec(
            num_scalar_prefetch=1,
            grid=(1,),
            in_specs=[hbm] * (count + 1)
            + [fixed(kept.shape), fixed((1, experts)), fixed((width, experts))]
            + [hbm] * (3 + len(extra)),
            out_specs=[hbm]
            + [
                fixed((rows, 1), False),
                pl.BlockSpec((rows, experts), lambda j, *_: (place, 0)),
            ]
            + [hbm] * 7,
            scratch_shapes=[
                pltpu.VMEM((rows, width), jnp.bfloat16),
                pltpu.VMEM((rows, width), jnp.bfloat16),
                pltpu.VMEM((width, 4 * units), jnp.bfloat16),
                pltpu.VMEM((2 * units, width), jnp.bfloat16),
                pltpu.VMEM((rows, 2 * units), jnp.float32),
                pltpu.VMEM((rows, units), jnp.float32),
                pltpu.VMEM((rows, 2 * units), jnp.bfloat16),
                pltpu.VMEM((rows, 4 * units), jnp.bfloat16),
                pltpu.VMEM((rows, 2 * units), jnp.bfloat16),
                pltpu.VMEM((rows, width), jnp.bfloat16),
                pltpu.VMEM((rows, experts), jnp.float32),
                pltpu.VMEM((rows, 1), jnp.float32),
                pltpu.SemaphoreType.DMA((3 * count + 13,)),
            ],
        ),
        out_shape=[jax.ShapeDtypeStruct((count, own_rows, width), jnp.bfloat16)]
        + [jax.ShapeDtypeStruct((rows, 1), jnp.float32)]
        + [jax.ShapeDtypeStruct(shape, jnp.bfloat16) for shape in kept_shapes],
        input_output_aliases={first + i: 2 + i for i in range(len(extra))},
        compiler_params=kernel_params(),
        cost_estimate=cost(80 * rows * width * units, 10 * rows * width + 12 * width * units),
        name="expert_chunk",
    )(
        here,
        *[x_pieces[i] for i in indices],
        dy_source,
        kept,
        chosen,
        router,
        gates,
        ups,
        downs,
        *extra,
    )
    return results[0], results[1], results[2:]


def finish_body(own_rows, full_cols, scalars, *refs):
    (query_scaled, key_scaled, value_low, query_raw, key_raw) = refs[:5]
    sums, inner_sums, low_out, near_out, far_out = refs[5:]
    columns = value_low.shape[1]
    core = scalars[0] & 1
    for side, (scaled, raw) in enumerate(((query_scaled, query_raw), (key_scaled, key_raw))):
        inverse = inverse_norm(sums, side, full_cols)
        normal = raw[...] * inverse
        low_out[:, side * columns : (side + 1) * columns] = (
            inverse * (scaled[...] - normal * (tall_column(inner_sums[...], side) / full_cols))
        ).astype(jnp.bfloat16)
    low_out[:, 2 * columns :] = value_low[...]
    for at in range(low_out.shape[0] // (2 * own_rows)):
        first = low_out[pl.ds(2 * at * own_rows, own_rows), :]
        second = low_out[pl.ds((2 * at + 1) * own_rows, own_rows), :]
        near_out[pl.ds(at * own_rows, own_rows), :] = jnp.where(core == 0, first, second)
        far_out[pl.ds(at * own_rows, own_rows), :] = jnp.where(core == 0, second, first)


def finish(here, own_rows, full_cols, *args):
    rows, columns = args[0].shape
    shapes = [(rows, 3 * columns)] + [(rows // 2, 3 * columns)] * 2
    return pl.pallas_call(
        lambda *refs: finish_body(own_rows, full_cols, *refs),
        grid_spec=pltpu.PrefetchScalarGridSpec(
            num_scalar_prefetch=1,
            grid=(1,),
            in_specs=[fixed(arg.shape) for arg in args],
            out_specs=[fixed(shape, False) for shape in shapes],
        ),
        out_shape=[jax.ShapeDtypeStruct(shape, jnp.bfloat16) for shape in shapes],
        compiler_params=kernel_params(),
        cost_estimate=cost(20 * rows * columns, 24 * rows * columns),
        name="finish",
    )(here, *args)


def near_product_body(indices, transposed, scalars, own, other, own_weight, other_weight, *refs):
    pieces, value = refs[:-1], refs[-1]
    side = 1 if transposed else 0
    value[...] = contract(own[...], own_weight[...], 1, side) + contract(
        other[...], other_weight[0], 1, side
    )
    own_rows = pieces[0].shape[0]
    for at, i in enumerate(indices):
        here = pl.ds(pl.multiple_of((scalars[0] ^ i) // 2 * own_rows, own_rows), own_rows)
        pieces[at][...] = value[here, :].astype(jnp.bfloat16)


def near_product(here, indices, own, other, own_weight, pair_weight, transposed):
    rows, depth = own.shape
    width = own_weight.shape[0 if transposed else 1]
    block = min(512, width // 2)
    count = len(indices)
    if transposed:
        mine = pl.BlockSpec((block, depth), lambda j, at: (j, 0))
        theirs = pl.BlockSpec((1, block, depth), lambda j, at: (1 - (at[0] & 1), j, 0))
    else:
        mine = pl.BlockSpec((depth, block), lambda j, at: (0, j))
        theirs = pl.BlockSpec((1, depth, block), lambda j, at: (1 - (at[0] & 1), 0, j))
    results = pl.pallas_call(
        lambda *refs: near_product_body(indices, transposed, *refs),
        grid_spec=pltpu.PrefetchScalarGridSpec(
            num_scalar_prefetch=1,
            grid=(width // block,),
            in_specs=[fixed(own.shape), fixed(other.shape), mine, theirs],
            out_specs=[pl.BlockSpec((rows // count, block), lambda j, at: (0, j))] * count,
            scratch_shapes=[pltpu.VMEM((rows, block), jnp.float32)],
        ),
        out_shape=[jax.ShapeDtypeStruct((rows // count, width), jnp.bfloat16)] * count,
        compiler_params=kernel_params(),
        cost_estimate=cost(4 * rows * depth * width, 2 * rows * width + 4 * depth * width),
        name="near_product",
    )(here, own, other, own_weight, pair_weight)
    return dict(zip(indices, results))


def total_of(parts):
    total = parts[0][...].astype(jnp.float32)
    for part in parts[1:]:
        total = total + part[...].astype(jnp.float32)
    return jnp.sum(total, axis=0) if total.ndim == 3 else total


def residual_body(tokens, gain, *refs):
    hidden_out, low_out = refs[-2:]
    hidden = tokens[...].astype(jnp.float32) + total_of(refs[:-2])
    normal, _ = rms_forward(hidden)
    hidden_out[...] = hidden
    low_out[...] = (normal * gain[...]).astype(jnp.bfloat16)


def residual(tokens, gain, parts):
    rows, width = tokens.shape
    return pl.pallas_call(
        residual_body,
        grid=(1,),
        in_specs=[fixed(tokens.shape), fixed((1, width))] + [fixed(part.shape) for part in parts],
        out_specs=[fixed((rows, width), False)] * 2,
        out_shape=[
            jax.ShapeDtypeStruct((rows, width), jnp.float32),
            jax.ShapeDtypeStruct((rows, width), jnp.bfloat16),
        ],
        compiler_params=kernel_params(),
        cost_estimate=cost(10 * rows * width, 20 * rows * width),
        name="residual",
    )(tokens, gain, *parts)


def norm_back_body(values, passed, gain, near, *refs):
    grad_out, low_out, gain_out = refs[-3:]
    grad = total_of([near]) + total_of(refs[:-3]) if len(refs) > 3 else total_of([near])
    normal, inverse = rms_forward(values[...].astype(jnp.float32))
    gain_out[...] = jnp.sum(grad * normal, axis=0, keepdims=True)
    scaled = grad * gain[...]
    result = passed[...].astype(jnp.float32) + inverse * (
        scaled - normal * jnp.mean(scaled * normal, axis=-1, keepdims=True)
    )
    grad_out[...] = result
    low_out[...] = result.astype(jnp.bfloat16)


def norm_back(values, passed, gain, near, parts):
    rows, width = values.shape
    args = (values, passed, gain, near, *parts)
    return pl.pallas_call(
        norm_back_body,
        grid=(1,),
        in_specs=[fixed(arg.shape) for arg in args],
        out_specs=[fixed((rows, width), False)] * 2 + [fixed((1, width), False)],
        out_shape=[
            jax.ShapeDtypeStruct((rows, width), jnp.float32),
            jax.ShapeDtypeStruct((rows, width), jnp.bfloat16),
            jax.ShapeDtypeStruct((1, width), jnp.float32),
        ],
        compiler_params=kernel_params(),
        cost_estimate=cost(20 * rows * width, 20 * rows * width),
        name="norm_back",
    )(*args)


def mixed_back_body(indices, scalars, own_weight, other_weight, *refs):
    count = len(indices)
    pieces = refs[:count]
    rows_out, own_out, other_out, lows = refs[count:]
    own_rows = pieces[0].shape[0]
    for at, i in enumerate(indices):
        here = pl.ds(pl.multiple_of((scalars[0] ^ i) // 2 * own_rows, own_rows), own_rows)
        lows[here, :] = pieces[at][...]
    rows_out[...] = lows[...]
    own_out[...] = contract(lows[...], own_weight[...], 1, 1).astype(jnp.bfloat16)
    other_out[...] = contract(lows[...], other_weight[0], 1, 1).astype(jnp.bfloat16)


def mixed_back(here, pieces, own_weight, pair_weight):
    indices = sorted(pieces)
    own_rows, width = pieces[0].shape
    rows = own_rows * len(indices)
    depth = own_weight.shape[0]
    shapes = [(rows, width), (rows, depth), (rows, depth)]
    return pl.pallas_call(
        lambda *refs: mixed_back_body(indices, *refs),
        grid_spec=pltpu.PrefetchScalarGridSpec(
            num_scalar_prefetch=1,
            grid=(1,),
            in_specs=[
                fixed(own_weight.shape),
                pl.BlockSpec((1, depth, width), lambda j, at: (1 - (at[0] & 1), 0, 0)),
            ]
            + [fixed((own_rows, width))] * len(indices),
            out_specs=[fixed(shape, False) for shape in shapes],
            scratch_shapes=[pltpu.VMEM((rows, width), jnp.bfloat16)],
        ),
        out_shape=[jax.ShapeDtypeStruct(shape, jnp.bfloat16) for shape in shapes],
        compiler_params=kernel_params(),
        cost_estimate=cost(4 * rows * depth * width, 4 * rows * width + 4 * depth * width),
        name="mixed_back",
    )(here, own_weight, pair_weight, *[pieces[i] for i in indices])


def place_body(indices, own_rows, scalars, *refs):
    pieces, out, sems = refs[: len(indices)], refs[-2], refs[-1]
    copies = []
    for at, i in enumerate(indices):
        here = pl.ds(pl.multiple_of((scalars[0] ^ i) * own_rows, own_rows), own_rows)
        copies.append(pltpu.make_async_copy(pieces[at], out.at[here], sems.at[at]))
        copies[-1].start()
    for copy in copies:
        copy.wait()


def place_rows(here, pieces):
    indices = sorted(pieces)
    own_rows, width = pieces[0].shape
    return pl.pallas_call(
        lambda *refs: place_body(indices, own_rows, *refs),
        grid_spec=pltpu.PrefetchScalarGridSpec(
            num_scalar_prefetch=1,
            grid=(1,),
            in_specs=[fixed((own_rows, width))] * len(indices),
            out_specs=pl.BlockSpec(memory_space=pl.ANY),
            scratch_shapes=[pltpu.SemaphoreType.DMA((len(indices),))],
        ),
        out_shape=jax.ShapeDtypeStruct((own_rows * len(indices), width), pieces[0].dtype),
        compiler_params=kernel_params(),
        cost_estimate=cost(0, 4 * own_rows * len(indices) * width),
        name="place_rows",
    )(here, *[pieces[i] for i in indices])


def row_of(column):
    n = column.shape[0]
    down = lax.broadcasted_iota(jnp.int32, (n, n), 0)
    across = lax.broadcasted_iota(jnp.int32, (n, n), 1)
    return jnp.sum(jnp.where(down == across, column, 0.0), axis=0, keepdims=True)


def tall_column(rows, side):
    block = min(256, rows.shape[1])
    return jnp.concatenate(
        [
            column_of(rows[side : side + 1, at : at + block])
            for at in range(0, rows.shape[1], block)
        ],
        axis=0,
    )


def inverse_norm(sums, side, full_cols):
    return lax.rsqrt(tall_column(sums[...], side) / full_cols + EPS)


def project_in_body(tokens, gain, w_query, w_key, w_value, low_out, q_out, k_out, v_out, sums_out):
    normal, _ = rms_forward(tokens[...].astype(jnp.float32))
    low = (normal * gain[...]).astype(jnp.bfloat16)
    low_out[...] = low
    for side, (weight, out) in enumerate(((w_query, q_out), (w_key, k_out))):
        raw = contract(low, weight[...], 1, 0)
        out[...] = raw
        sums_out[side : side + 1, :] = row_of(jnp.sum(raw * raw, axis=-1, keepdims=True))
    v_out[...] = contract(low, w_value[...], 1, 0).astype(jnp.bfloat16)


def project_in(tokens, gain, w_query, w_key, w_value):
    length, width = tokens.shape
    columns = w_query.shape[1]
    block = min(256, length)
    wide = pl.BlockSpec((block, columns), lambda i: (i, 0))
    return pl.pallas_call(
        project_in_body,
        grid=(length // block,),
        in_specs=[pl.BlockSpec((block, width), lambda i: (i, 0)), fixed((1, width))]
        + [fixed(w_query.shape)] * 3,
        out_specs=[
            pl.BlockSpec((block, width), lambda i: (i, 0)),
            wide,
            wide,
            wide,
            pl.BlockSpec((2, block), lambda i: (0, i)),
        ],
        out_shape=[
            jax.ShapeDtypeStruct((length, width), jnp.bfloat16),
            jax.ShapeDtypeStruct((length, columns), jnp.float32),
            jax.ShapeDtypeStruct((length, columns), jnp.float32),
            jax.ShapeDtypeStruct((length, columns), jnp.bfloat16),
            jax.ShapeDtypeStruct((2, length), jnp.float32),
        ],
        compiler_params=kernel_params(),
        cost_estimate=cost(6 * length * width * columns, 8 * length * width),
        name="project_in",
    )(tokens, gain, w_query, w_key, w_value)


def turned(values, cosine, sine):
    return values * cosine + pltpu.roll(values, values.shape[1] // 2, 1) * sine


def head_blocks(length):
    block = min(256, length)
    return [(start, start + block) for start in range(0, length, block)]


def block_probs(queries, keys, start, end):
    scores = contract(queries, keys, 1, 1)
    down = lax.broadcasted_iota(jnp.int32, scores.shape, 0) + start
    across = lax.broadcasted_iota(jnp.int32, scores.shape, 1)
    scores = jnp.where(down >= across, scores, -1e30)
    exponent = jnp.exp(scores - jnp.max(scores, axis=-1, keepdims=True))
    return exponent * (1.0 / jnp.sum(exponent, axis=-1, keepdims=True))


def pair_split(rows, core, own_rows):
    low = jnp.concatenate(
        [rows[at : at + own_rows] for at in range(0, rows.shape[0], 2 * own_rows)], axis=0
    )
    high = jnp.concatenate(
        [rows[at : at + own_rows] for at in range(own_rows, rows.shape[0], 2 * own_rows)], axis=0
    )
    return jnp.where(core == 0, low, high), jnp.where(core == 0, high, low)


def attend_body(
    own_rows,
    full_cols,
    scalars,
    query_raw,
    key_raw,
    values,
    sums,
    cosine,
    sine,
    gains,
    q_out,
    k_out,
    near_out,
    far_out,
):
    length, columns = query_raw.shape
    core = scalars[0] & 1
    query_inv = inverse_norm(sums, 0, full_cols)
    key_inv = inverse_norm(sums, 1, full_cols)
    for head in range(columns // HEAD_DIM):
        here = pl.ds(head * HEAD_DIM, HEAD_DIM)
        query_normed = query_raw[:, here] * query_inv * gains[0:1, here]
        key_normed = key_raw[:, here] * key_inv * gains[1:2, here]
        q_out[:, here] = (
            turned(query_normed, cosine[...], sine[...]) * HEAD_DIM ** (-0.5)
        ).astype(jnp.bfloat16)
        k_out[:, here] = turned(key_normed, cosine[...], sine[...]).astype(jnp.bfloat16)
        for start, end in head_blocks(length):
            rows = pl.ds(start, end - start)
            probs = block_probs(q_out[rows, here], k_out[pl.ds(0, end), here], start, end)
            near, far = pair_split(
                contract(probs.astype(jnp.bfloat16), values[pl.ds(0, end), here], 1, 0),
                core,
                own_rows,
            )
            half = pl.ds(start // 2, (end - start) // 2)
            near_out[half, here] = near.astype(jnp.bfloat16)
            far_out[half, here] = far.astype(jnp.bfloat16)


def attend(here, own_rows, full_cols, *args):
    length, columns = args[0].shape
    shapes = [(length, columns)] * 2 + [(length // 2, columns)] * 2
    return pl.pallas_call(
        lambda *refs: attend_body(own_rows, full_cols, *refs),
        grid_spec=pltpu.PrefetchScalarGridSpec(
            num_scalar_prefetch=1,
            grid=(1,),
            in_specs=[fixed(arg.shape) for arg in args],
            out_specs=[fixed(shape, False) for shape in shapes],
        ),
        out_shape=[jax.ShapeDtypeStruct(shape, jnp.bfloat16) for shape in shapes],
        compiler_params=kernel_params(),
        cost_estimate=cost(4 * length * length * columns, 16 * length * columns),
        name="attend",
    )(here, *args)


def attend_back_body(
    own_rows,
    full_cols,
    scalars,
    near,
    far,
    queries,
    keys,
    values,
    query_raw,
    key_raw,
    sums,
    cosine,
    sine,
    gains,
    *refs,
):
    query_scaled, key_scaled, value_low, inner_out, gain_out = refs[:5]
    grads, grad_key, grad_value = refs[5:]
    length, columns = queries.shape
    core = scalars[0] & 1
    inners = [None, None]
    for at in range(length // (2 * own_rows)):
        mine, other = near[pl.ds(at * own_rows, own_rows), :], far[pl.ds(at * own_rows, own_rows), :]
        first = pl.ds(2 * at * own_rows, own_rows)
        second = pl.ds((2 * at + 1) * own_rows, own_rows)
        grads[first, :] = jnp.where(core == 0, mine, other)
        grads[second, :] = jnp.where(core == 0, other, mine)
    for head in range(columns // HEAD_DIM):
        here = pl.ds(head * HEAD_DIM, HEAD_DIM)
        grad_key[...] = jnp.zeros_like(grad_key)
        grad_value[...] = jnp.zeros_like(grad_value)
        for start, end in head_blocks(length):
            rows, past = pl.ds(start, end - start), pl.ds(0, end)
            probs = block_probs(queries[rows, here], keys[past, here], start, end)
            grad_probs = contract(grads[rows, here], values[past, here], 1, 1)
            grad_scores = (
                probs * (grad_probs - jnp.sum(probs * grad_probs, axis=-1, keepdims=True))
            ).astype(jnp.bfloat16)
            grad_value[past, :] += contract(probs.astype(jnp.bfloat16), grads[rows, here], 0, 0)
            grad_key[past, :] += contract(grad_scores, queries[rows, here], 0, 0)
            query_scaled[rows, here] = contract(grad_scores, keys[past, here], 1, 0)
        value_low[:, here] = grad_value[...].astype(jnp.bfloat16)
        sides = (
            (query_scaled[:, here] * HEAD_DIM ** (-0.5), query_raw, query_scaled),
            (grad_key[...], key_raw, key_scaled),
        )
        for side, (grad, raw, scaled_out) in enumerate(sides):
            normed = turned(grad, cosine[...], -sine[...])
            normal = raw[:, here] * inverse_norm(sums, side, full_cols)
            gain_out[side : side + 1, here] = jnp.sum(normed * normal, axis=0, keepdims=True)
            scaled = normed * gains[side : side + 1, here]
            scaled_out[:, here] = scaled
            inner = jnp.sum(scaled * normal, axis=-1, keepdims=True)
            inners[side] = inner if inners[side] is None else inners[side] + inner
    block = min(256, length)
    for side in range(2):
        for at in range(0, length, block):
            inner_out[side : side + 1, at : at + block] = row_of(inners[side][at : at + block])


def attend_back(here, own_rows, full_cols, *args):
    length, columns = args[2].shape
    wide = jax.ShapeDtypeStruct((length, columns), jnp.float32)
    outs = [
        wide,
        wide,
        jax.ShapeDtypeStruct((length, columns), jnp.bfloat16),
        jax.ShapeDtypeStruct((2, length), jnp.float32),
        jax.ShapeDtypeStruct((2, columns), jnp.float32),
    ]
    return pl.pallas_call(
        lambda *refs: attend_back_body(own_rows, full_cols, *refs),
        grid_spec=pltpu.PrefetchScalarGridSpec(
            num_scalar_prefetch=1,
            grid=(1,),
            in_specs=[fixed(arg.shape) for arg in args],
            out_specs=[fixed(out.shape, False) for out in outs],
            scratch_shapes=[pltpu.VMEM((length, columns), jnp.bfloat16)]
            + [pltpu.VMEM((length, HEAD_DIM), jnp.float32)] * 2,
        ),
        out_shape=outs,
        compiler_params=kernel_params(),
        cost_estimate=cost(8 * length * length * columns, 40 * length * columns),
        name="attend_back",
    )(here, *args)


def near_scatter(pieces):
    size = lax.axis_size("tensor")
    groups = [list(range(core, size, 2)) for core in range(2)]
    return lax.all_to_all(
        pieces, "tensor", split_axis=0, concat_axis=0, axis_index_groups=groups, tiled=True
    )


def line_step(part, step):
    bits = axis_bits("expert")[::-1]
    index = lax.axis_index("expert")
    if step < len(bits):
        bit = bits[step]
        half = part.shape[0] // 2
        high = (index // bit) % 2
        kept = lax.dynamic_slice_in_dim(part, high * half, half, 0)
        sent = lax.dynamic_slice_in_dim(part, (1 - high) * half, half, 0)
        return (
            kept.astype(jnp.float32) + swap(sent, "expert", bit).astype(jnp.float32)
        ).astype(jnp.bfloat16)
    bit = bits[2 * len(bits) - 1 - step]
    high = (index // bit) % 2 == 1
    other = swap(part, "expert", bit)
    return jnp.concatenate([jnp.where(high, other, part), jnp.where(high, part, other)], axis=0)


def send_body(indices, places, scalars, act, *refs):
    gates, (down_own, down_other), outs = refs[:places], refs[places : places + 2], refs[-places:]
    units = down_own.shape[1]
    value = contract(act[:, :units], down_own[0], 1, 0) + contract(
        act[:, units:], down_other[0], 1, 0
    )
    own_rows = outs[0].shape[1]
    for place in range(places):

        @pl.when(pl.program_id(1) == place)
        def _():
            sent = (gates[place][...] * value).astype(jnp.bfloat16)
            for at, i in enumerate(indices):
                outs[place][(scalars[0] ^ i) // 2] = sent[at * own_rows : (at + 1) * own_rows]


def expert_send(here, indices, act_all, gates, downs):
    rows = gates[0].shape[0]
    count = len(indices)
    places = len(gates)
    _, units, width = downs.shape
    block = min(1024, width // 2)
    return pl.pallas_call(
        lambda *refs: send_body(indices, places, *refs),
        grid_spec=pltpu.PrefetchScalarGridSpec(
            num_scalar_prefetch=1,
            grid=(width // block, places),
            in_specs=[pl.BlockSpec((rows, 2 * units), lambda j, k, *_: (k, 0))]
            + [fixed((rows, 1))] * places
            + [
                pl.BlockSpec((1, units, block), lambda j, k, at: (at[0] & 1, 0, j)),
                pl.BlockSpec((1, units, block), lambda j, k, at: (1 - (at[0] & 1), 0, j)),
            ],
            out_specs=[pl.BlockSpec((count, rows // count, block), lambda j, k, *_: (0, 0, j))]
            * places,
        ),
        out_shape=[jax.ShapeDtypeStruct((count, rows // count, width), jnp.bfloat16)] * places,
        compiler_params=kernel_params(),
        cost_estimate=cost(
            4 * places * rows * width * units, places * 4 * rows * width + 4 * width * units
        ),
        name="expert_send",
    )(here, act_all, *gates, downs, downs)


def on_device(
    tokens,
    positions,
    routes,
    slot_ids,
    attn_gain,
    w_query,
    w_key,
    w_value,
    query_gain,
    key_gain,
    w_out,
    ffn_gain,
    router,
    w_gate,
    w_up,
    w_down,
    grad_out,
):
    tensor_size = lax.axis_size("tensor")
    expert_size = lax.axis_size("expert")
    local_count = tensor_size // 2
    tensor_index = lax.axis_index("tensor")
    expert_index = lax.axis_index("expert")
    own_local = tensor_index // 2
    own_expert = expert_index * local_count + own_local
    length, model_width = tokens.shape
    heads_here = w_query.shape[1] // HEAD_DIM
    full_cols = w_query.shape[1] * tensor_size
    expert_count = router.shape[1]
    capacity = 3 * length * TOP // (2 * expert_count)
    own_rows = length // tensor_size
    chunks = list(range(expert_size))
    bits = axis_bits("tensor")
    near_bits = bits[:-1]
    last = len(near_bits)

    def own_slice(rows):
        return lax.dynamic_slice_in_dim(rows, tensor_index * own_rows, own_rows, 0)

    pairs = [[2 * i, 2 * i + 1] for i in range(tensor_size // 2)]

    def pair_gather(values):
        return lax.all_gather(values, "tensor", axis_index_groups=pairs)

    grad_own = own_slice(grad_out)
    near_groups = [list(range(core, tensor_size, 2)) for core in range(2)]
    grad_sent = {chunk: swap(grad_own, "expert", chunk) for chunk in chunks[1:]}
    grad_rows_of = {0: grad_out}
    out_pair = jnp.where(
        jnp.arange(2)[:, None, None] == tensor_index % 2,
        w_out[None],
        swap(w_out, "tensor", 1)[None],
    )
    expert_iota = jnp.arange(expert_count, dtype=jnp.int32)
    kept_table = jnp.sum(
        (
            (routes.T[:, None, :] == expert_iota[None, :, None]) & (slot_ids.T < capacity)[:, None, :]
        ).astype(jnp.float32),
        axis=0,
    )
    targets = jnp.arange(expert_size, dtype=jnp.int32) * local_count + own_local
    kept_rows = lax.all_to_all(
        jnp.take(kept_table, targets, axis=0).reshape(expert_size, tensor_size, own_rows),
        "expert",
        split_axis=0,
        concat_axis=0,
        tiled=True,
    )

    def here(chunk):
        return jnp.stack([tensor_index, expert_index ^ chunk]).astype(jnp.int32)

    score_scale = HEAD_DIM ** (-0.5)
    half_dim = HEAD_DIM // 2
    frequency = THETA ** (-2.0 * jnp.arange(half_dim, dtype=jnp.float32) / HEAD_DIM)
    angles = positions.astype(jnp.float32)[:, None] * frequency[None, :]
    cosine_table = jnp.concatenate([jnp.cos(angles)] * 2, axis=-1)
    sine_half = jnp.sin(angles)
    sine_table = jnp.concatenate([-sine_half, sine_half], axis=-1)
    attn_in, query_raw, key_raw, value_rows, square_sums = project_in(
        tokens, attn_gain[None, :], w_query, w_key, w_value
    )
    w_all = jnp.concatenate([w_query, w_key, w_value], axis=1)
    gains = jnp.stack([query_gain, key_gain])
    square_sums = spread_sum(square_sums, "tensor")
    indices = sorted(direct_combos(near_bits))
    gates, ups, downs = [pair_gather(weights[0]) for weights in (w_gate, w_up, w_down)]
    query_rows, key_rows, mixed_near, mixed_far = attend(
        here(0),
        own_rows,
        full_cols,
        query_raw,
        key_raw,
        value_rows,
        square_sums,
        cosine_table,
        sine_table,
        gains,
    )
    mixed_other = swap(mixed_far, "tensor", 1)
    w_pair = pair_gather(w_all)
    attn_parts = near_product(
        here(0), indices, mixed_near, mixed_other, w_out, out_pair, False
    )
    attn_moved = [swap(attn_parts[i], "tensor", i) for i in indices if i]
    hidden, ffn_in = residual(
        own_slice(tokens),
        ffn_gain[None, :],
        [attn_parts[0]] + attn_moved,
    )
    chosen = (expert_iota == own_expert).astype(jnp.float32)[None, :]
    received = [ffn_in]
    gathered = [direct_gather(ffn_in, near_bits)]
    for chunk in chunks[1:]:
        sent = tie(ffn_in, gathered[0][near_bits[0]]) if chunk > 2 else ffn_in
        received.append(swap(sent, "expert", chunk))
    waited = {1: [square_sums], 2: attn_moved}
    for chunk, piece in grad_sent.items():
        piece = tie(piece, *waited.get(chunk, [gathered[0][i] for i in indices if i] + received[1:2]))
        grad_rows_of[chunk] = lax.all_gather(piece, "tensor", axis_index_groups=near_groups)
    chain = None
    sums = []
    gate_columns = []
    for at, chunk in enumerate(chunks):
        scalars = here(chunk)
        if at:
            after = [gathered[at - 1][i] for i in gathered[at - 1] if i]
            if at >= 2:
                after.append(gate_columns[at - 2])
            gathered.append(direct_gather(received[at], near_bits, after))
        if at >= 3:
            scalars = tie(scalars, sums[at - 3])
        pieces, gate_column, chain = expert_chunk(
            at,
            expert_size,
            gathered[at],
            grad_rows_of[chunk],
            scalars,
            kept_rows,
            chosen,
            router,
            gates,
            ups,
            downs,
            chain,
        )
        gate_columns.append(gate_column)
        sums.append(near_scatter(pieces))

    def plane_total(near):
        return jnp.sum(near.astype(jnp.float32), axis=0).astype(jnp.bfloat16)

    dl_all, x_all, dy_all, act_all, own_dp, other_dp, gated_own, gated_other = chain
    row_totals = [plane_total(near) for near in sums[1:-1]]
    sent_pieces = expert_send(tie(here(0), *row_totals), indices, act_all, gate_columns, downs)
    row_totals.append(plane_total(tie(sums[-1], sent_pieces[0])))
    grad_parts = [sums[0]] + [
        swap(total, "expert", chunk) for total, chunk in zip(row_totals, chunks[1:])
    ]
    sent_near = {1: near_scatter(tie(sent_pieces[1], row_totals[-1]))}
    sent_near[2] = near_scatter(tie(sent_pieces[2], sent_near[1]))
    grad_parts[0] = tie(grad_parts[0], sent_near[1], sent_near[2])
    grad_hidden, hidden_low, grad_ffn_gain = norm_back(
        hidden, grad_own, ffn_gain[None, :], grad_parts[0], grad_parts[1:]
    )
    hidden_near, back_own, back_other = mixed_back(
        here(0), direct_gather(hidden_low, near_bits), w_out, out_pair
    )
    back_far = swap(back_other, "tensor", 1)
    sent_moved = [swap(plane_total(sent_near[chunk]), "expert", chunk) for chunk in (1, 2)]
    for chunk in chunks[3:]:
        sent_near[chunk] = near_scatter(tie(sent_pieces[chunk], hidden_near))
        sent_moved.append(swap(plane_total(sent_near[chunk]), "expert", chunk))

    units = own_dp.shape[1] // 2
    other_wide = swap(contract(x_all, other_dp, 0, 0).astype(jnp.bfloat16), "tensor", 1)
    other_down = swap(contract(gated_other, dy_all, 0, 0).astype(jnp.bfloat16), "tensor", 1)
    grad_gate_w = contract(x_all, own_dp[:, :units], 0, 0) + other_wide[:, :units].astype(jnp.float32)
    grad_up_w = contract(x_all, own_dp[:, units:], 0, 0) + other_wide[:, units:].astype(jnp.float32)
    grad_down = contract(gated_own, dy_all, 0, 0) + other_down.astype(jnp.float32)
    grad_router_part = contract(dl_all, x_all, 0, 0)

    grad_w_out = contract(mixed_near, hidden_near, 0, 0)
    grad_w_out_other = contract(mixed_other, hidden_near, 0, 0).astype(jnp.bfloat16)
    grad_w_out_low = (
        grad_w_out + swap(grad_w_out_other, "tensor", 1).astype(jnp.float32)
    ).astype(jnp.bfloat16)
    query_scaled, key_scaled, value_low, inner_sums, gain_parts = attend_back(
        tie(here(0), sent_moved[0], grad_w_out_other),
        own_rows,
        full_cols,
        back_own,
        back_far,
        query_rows,
        key_rows,
        value_rows,
        query_raw,
        key_raw,
        square_sums,
        cosine_table,
        sine_table,
        gains,
    )
    grad_w_value = contract(attn_in, value_low, 0, 0).astype(jnp.bfloat16)
    inner_sums = spread_sum(tie(inner_sums, *[sent_near[chunk] for chunk in chunks[3:]]), "tensor")
    sent_near[0] = near_scatter(tie(sent_pieces[0], inner_sums))
    inner_sums = tie(inner_sums, grad_w_out_low, grad_w_value, sent_moved[1])
    line_steps = 2 * len(axis_bits("expert"))
    early_lines = [line_step(part, 0) for part in (grad_w_out_low, grad_w_value)]
    low_all, low_near, low_far = finish(
        here(0),
        own_rows,
        full_cols,
        query_scaled,
        key_scaled,
        value_low,
        query_raw,
        key_raw,
        square_sums,
        inner_sums,
    )
    grad_attn = near_product(
        tie(here(0), *early_lines, *sent_moved[2:]), indices, low_near, swap(low_far, "tensor", 1), w_all, w_pair, True
    )
    columns_here = w_query.shape[1]
    grad_w_both = contract(attn_in, low_all[:, : 2 * columns_here], 0, 0).astype(jnp.bfloat16)
    grad_attn_moved = [swap(grad_attn[i], "tensor", i) for i in indices if i]
    early_lines = [line_step(part, 1) for part in early_lines]
    _, token_low, grad_attn_gain = norm_back(
        tie(own_slice(tokens), *early_lines, sent_near[0]), grad_hidden, attn_gain[None, :], grad_attn[0], grad_attn_moved
    )

    def gather_rows(piece):
        pieces = direct_gather(piece, near_bits)
        return {**pieces, **{i ^ 1: swap(near, "tensor", 1) for i, near in pieces.items()}}

    token_pieces = gather_rows(token_low)
    grad_tokens = place_rows(here(0), token_pieces)
    late = [token_pieces[i] for i in indices if i]
    both_lines = line_step(grad_w_both, 0)
    early_lines = [line_step(part, 2) for part in early_lines]
    moe_sum = hidden + jnp.sum(sent_near[0].astype(jnp.float32), axis=0)
    for moved in sent_moved:
        moe_sum = moe_sum + moved.astype(jnp.float32)
    out_pieces = gather_rows(tie(moe_sum.astype(jnp.bfloat16), *late))
    output = place_rows(here(0), out_pieces)
    both_lines = line_step(tie(both_lines, *late), 1)
    for step in range(3, line_steps):
        early_lines = [line_step(part, step) for part in early_lines]
    for step in range(2, line_steps):
        both_lines = line_step(both_lines, step)
    sum_out, sum_value = [part.astype(jnp.float32) for part in early_lines]
    sum_both = both_lines.astype(jnp.float32)
    sum_query, sum_key = sum_both[:, :columns_here], sum_both[:, columns_here:]
    plane_sums = spread_sum(
        tie(jnp.concatenate([grad_router_part, grad_ffn_gain, grad_attn_gain], axis=0), *late),
        "tensor",
    )
    scales = gain_parts.reshape(-1)
    scales = jnp.pad(scales, (0, model_width - scales.shape[0]))
    all_sums = spread_sum(jnp.concatenate([plane_sums, scales[None, :]], axis=0), "expert")
    return (
        output,
        grad_tokens,
        all_sums[expert_count + 1],
        sum_query,
        sum_key,
        sum_value,
        all_sums[expert_count + 2, :columns_here],
        all_sums[expert_count + 2, columns_here : 2 * columns_here],
        sum_out,
        all_sums[expert_count],
        all_sums[:expert_count].T,
        grad_gate_w[None],
        grad_up_w[None],
        grad_down[None],
    )


def solution(mesh):
    placed = (
        P("expert", None),
        P("expert"),
        P("expert", None),
        P("expert", None),
        P(),
        P(None, "tensor"),
        P(None, "tensor"),
        P(None, "tensor"),
        P("tensor"),
        P("tensor"),
        P("tensor", None),
        P(),
        P(),
        P(("expert", "tensor"), None, None),
        P(("expert", "tensor"), None, None),
        P(("expert", "tensor"), None, None),
        P("expert", None),
    )
    return jax.shard_map(
        on_device,
        mesh=mesh,
        in_specs=placed,
        out_specs=(
            P("expert", None),
            P("expert", None),
            P(),
            P(None, "tensor"),
            P(None, "tensor"),
            P(None, "tensor"),
            P("tensor"),
            P("tensor"),
            P("tensor", None),
            P(),
            P(),
            P(("expert", "tensor"), None, None),
            P(("expert", "tensor"), None, None),
            P(("expert", "tensor"), None, None),
        ),
        check_vma=False,
    )
```

```python
import jax
import jax.numpy as jnp
from jax import lax
from jax.experimental import pallas as pl
from jax.experimental.pallas import tpu as pltpu
from jax.sharding import PartitionSpec as P

HEAD_DIM = 128
TOP = 8


EPS = 1e-05
THETA = 10000.0


def rms_forward(values):
    inverse = lax.rsqrt(jnp.mean(values * values, axis=-1, keepdims=True) + EPS)
    return (values * inverse, inverse)


def rms_backward(grad_normed, normal_rows, inverse, gain_row):
    gain_grad = jnp.sum(grad_normed * normal_rows, axis=0)
    scaled = grad_normed * gain_row
    grad_rows = inverse * (
        scaled - normal_rows * jnp.mean(scaled * normal_rows, axis=-1, keepdims=True)
    )
    return (grad_rows, gain_grad)


def swap(values, axis, bit):
    return lax.ppermute(values, axis, [(i, i ^ bit) for i in range(lax.axis_size(axis))])


def axis_bits(axis):
    size = lax.axis_size(axis)
    return [size >> (k + 1) for k in range(size.bit_length() - 1)]


def spread_sum(values, axis):
    for bit in axis_bits(axis)[::-1]:
        values = values + swap(values, axis, bit)
    return values


def plane_order(turn):
    bits = axis_bits("tensor")[:-1]
    if turn % 2:
        bits = bits[::-1]
    order = [0]
    for bit in bits:
        order = order + [bit ^ i for i in order]
    return bits, order


def plane_gather(piece, turn):
    bits, _ = plane_order(turn)
    pieces = [piece]
    for bit in bits:
        pieces = pieces + [swap(p, "tensor", bit) for p in pieces]
    near = jnp.concatenate(pieces, axis=0)
    return near, swap(near, "tensor", 1)


def plane_scatter(near, far, turn):
    bits, _ = plane_order(turn)
    total = near.astype(jnp.float32) + swap(far, "tensor", 1).astype(jnp.float32)
    for bit in bits[::-1]:
        half = total.shape[0] // 2
        sent = total[half:].astype(jnp.bfloat16)
        total = total[:half].astype(jnp.bfloat16).astype(jnp.float32) + swap(
            sent, "tensor", bit
        ).astype(jnp.float32)
    return total


def plane_rows(values, turn, own_rows, sorted_order=False):
    _, order = plane_order(turn)
    if sorted_order:
        order = sorted(order)
    index = lax.axis_index("tensor")

    def block(i):
        return lax.dynamic_slice_in_dim(values, (index ^ i) * own_rows, own_rows, 0)

    near = jnp.concatenate([block(i) for i in order], axis=0)
    far = jnp.concatenate([block(i ^ 1) for i in order], axis=0)
    return near, far


def natural_rows(near, far, turn, own_rows):
    _, order = plane_order(turn)
    index = lax.axis_index("tensor")
    both = jnp.concatenate([near, far], axis=0)
    place = {}
    for at, i in enumerate(order):
        place[i] = at
        place[i ^ 1] = at + len(order)
    table = jnp.array([place[i] for i in range(2 * len(order))], jnp.int32)
    return jnp.concatenate(
        [
            lax.dynamic_slice_in_dim(both, table[index ^ i] * own_rows, own_rows, 0)
            for i in range(2 * len(order))
        ],
        axis=0,
    )


def contract(left, right, left_dim, right_dim):
    return lax.dot_general(
        left, right, (((left_dim,), (right_dim,)), ((), ())), preferred_element_type=jnp.float32
    )


def tie(values, *after):
    return lax.optimization_barrier((values, *after))[0]


def stages(turn, bits):
    if turn % 2:
        bits = bits[::-1]
    found = [[] for _ in bits]
    order = [(0, ())]
    for bit in bits:
        order = order + [(bit ^ i, used + (bit,)) for i, used in order]
    for i, used in order[1:]:
        found[len(used) - 1].append((i, i ^ used[-1], used[-1]))
    return found


def gather_stage(pieces, turn, stage, bits, after=()):
    pieces = dict(pieces)
    for i, source, bit in stages(turn, bits)[stage]:
        sent = pieces[source]
        if after:
            sent = tie(sent, *after)
        pieces[i] = swap(sent, "tensor", bit)
    return pieces


def direct_combos(bits):
    combos = [0]
    for bit in bits:
        combos = combos + [bit ^ i for i in combos]
    return combos


def direct_gather(piece, bits, after=()):
    pieces = {0: piece}
    for i in direct_combos(bits)[1:]:
        pieces[i] = swap(tie(piece, *after) if after else piece, "tensor", i)
    return pieces


def gather_all(piece, turn, bits):
    pieces = {0: piece}
    for stage in range(len(bits)):
        pieces = gather_stage(pieces, turn, stage, bits)
    return pieces


def scatter_stage(sums, turn, stage, bits, after=()):
    sums = dict(sums)
    for i, target, bit in stages(turn, bits)[len(bits) - 1 - stage]:
        sent = sums.pop(i).astype(jnp.bfloat16)
        if after:
            sent = tie(sent, *after)
        sums[target] = sums[target].astype(jnp.float32) + swap(sent, "tensor", bit).astype(
            jnp.float32
        )
    return sums


MEGABYTE = 1024 * 1024


def kernel_params():
    return pltpu.CompilerParams(vmem_limit_bytes=58 * MEGABYTE)


def cost(flops, moved):
    return pl.CostEstimate(flops=flops, bytes_accessed=moved, transcendentals=0)


def column_of(row):
    n = row.shape[1]
    down = lax.broadcasted_iota(jnp.int32, (n, n), 0)
    across = lax.broadcasted_iota(jnp.int32, (n, n), 1)
    return jnp.sum(jnp.where(down == across, row, 0.0), axis=1, keepdims=True)


def fixed(shape, single=True):
    if single:
        return pl.BlockSpec(
            shape, lambda *_: (0,) * len(shape), pipeline_mode=pl.Buffered(1)
        )
    return pl.BlockSpec(shape, lambda *_: (0,) * len(shape))


def expert_body(indices, local, place, scalars, *refs):
    count = len(indices)
    x_parts, refs = refs[:count], refs[count:]
    dy_source, kept, chosen, router, gates, ups, downs = refs[:7]
    core = scalars[0] & 1
    gate_own, gate_other = gates.at[core], gates.at[1 - core]
    up_own, up_other = ups.at[core], ups.at[1 - core]
    down_own, down_other = downs.at[core], downs.at[1 - core]
    scratch = refs[-13:]
    pieces, gate_out, dl_all, x_all, dy_all, act_all, own_dp, other_dp, gated_own, gated_other = refs[
        -23:-13
    ]
    rows, grads, wide, tall, raw, inner, act, slopes, gated, done, probs_ref, dots, sems = scratch
    rows_here, width = rows.shape
    units = gate_own.shape[1]
    own_rows = rows_here // count
    used = []
    dy_parts = []
    for i in indices:
        if local:
            at = pl.multiple_of((scalars[0] ^ i) * own_rows, own_rows)
            dy_parts.append(dy_source.at[pl.ds(at, own_rows)])
        else:
            dy_parts.append(dy_source.at[(scalars[0] ^ i) // 2])

    def start(source, target):
        copy = pltpu.make_async_copy(source, target, sems.at[len(used)])
        used.append(copy)
        copy.start()
        return copy

    def spread(parts, target):
        size = rows_here // len(parts)
        return [start(part, target.at[pl.ds(at * size, size)]) for at, part in enumerate(parts)]

    x_copies = spread(x_parts, rows)
    order = [gate_own, up_own, gate_other, up_other]
    wide_copies = [
        start(weight, wide.at[:, pl.ds(at * units, units)]) for at, weight in enumerate(order[:2])
    ]
    dy_copies = spread(dy_parts, grads)
    tall_copies = [start(down_own, tall.at[pl.ds(0, units)])]
    wide_copies += [
        start(weight, wide.at[:, pl.ds((at + 2) * units, units)])
        for at, weight in enumerate(order[2:])
    ]
    tall_copies.append(start(down_other, tall.at[pl.ds(units, units)]))

    here_rows = pl.ds(place * rows_here, rows_here)
    for copy in x_copies:
        copy.wait()
    outgoing = [start(rows, x_all.at[here_rows])]
    logits = contract(rows[...], router[...], 1, 0)
    exponent = jnp.exp(logits - jnp.max(logits, axis=-1, keepdims=True))
    probs = exponent / jnp.sum(exponent, axis=-1, keepdims=True)
    kept_column = jnp.concatenate(
        [column_of(kept[scalars[1], pl.ds(scalars[0] ^ i, 1), :]) for i in indices], axis=0
    )
    probs_ref[...] = probs
    gate_out[...] = jnp.sum(probs * chosen[...], axis=-1, keepdims=True) * kept_column
    dots[...] = jnp.zeros_like(dots)

    block = min(64, rows_here)
    for half in range(2):
        columns = pl.ds(half * units, units)
        for part in range(2):
            at = 2 * half + part
            wide_copies[at].wait()
            raw[:, pl.ds(part * units, units)] = contract(
                rows[...], wide[:, pl.ds(at * units, units)], 1, 0
            )
        if half == 0:
            for copy in dy_copies:
                copy.wait()
            outgoing.append(start(grads, dy_all.at[here_rows]))
        tall_copies[half].wait()
        inner[...] = contract(grads[...], tall[columns, :], 1, 1)

        @pl.loop(0, rows_here // block)
        def _(at):
            here = pl.ds(at * block, block)
            pre_gate = raw[here, pl.ds(0, units)]
            pre_up = raw[here, pl.ds(units, units)]
            inward = inner[here, :]
            gate = gate_out[here, :]
            sigmoid_gate = 1.0 / (1.0 + jnp.exp(-pre_gate))
            silu_gate = pre_gate * sigmoid_gate
            active = (silu_gate * pre_up).astype(jnp.bfloat16)
            act[here, columns] = active
            active = active.astype(jnp.float32)
            gated[here, columns] = (gate * active).astype(jnp.bfloat16)
            dots[here, :] += jnp.sum(inward * active, axis=-1, keepdims=True)
            grad_active = gate * inward
            slopes[here, pl.ds(2 * half * units, units)] = (
                grad_active * pre_up * sigmoid_gate * (1.0 + pre_gate * (1.0 - sigmoid_gate))
            ).astype(jnp.bfloat16)
            slopes[here, pl.ds((2 * half + 1) * units, units)] = (grad_active * silu_gate).astype(
                jnp.bfloat16
            )

    outgoing += [
        start(act, act_all.at[here_rows]),
        start(slopes.at[:, pl.ds(0, 2 * units)], own_dp.at[here_rows]),
        start(slopes.at[:, pl.ds(2 * units, 2 * units)], other_dp.at[here_rows]),
        start(gated.at[:, pl.ds(0, units)], gated_own.at[here_rows]),
        start(gated.at[:, pl.ds(units, units)], gated_other.at[here_rows]),
    ]
    grad_logits = (dots[...] * gate_out[...] * (chosen[...] - probs_ref[...])).astype(jnp.bfloat16)
    dl_all[...] = grad_logits
    step = min(512, width)
    for at in range(width // step):
        columns = pl.ds(at * step, step)
        done[:, columns] = (
            contract(slopes[...], wide[columns, :], 1, 1)
            + contract(grad_logits, router[columns, :], 1, 1)
        ).astype(jnp.bfloat16)
    for at, i in enumerate(indices):
        to = (scalars[0] ^ i) // 2
        outgoing.append(start(done.at[pl.ds(at * own_rows, own_rows)], pieces.at[to]))
    for copy in outgoing:
        copy.wait()


def expert_chunk(
    place, places, x_pieces, dy_source, here, kept, chosen, router, gates, ups, downs, chain
):
    indices = sorted(x_pieces)
    count = len(indices)
    own_rows, width = x_pieces[0].shape
    rows = own_rows * count
    units = gates.shape[2]
    experts = router.shape[1]
    extra = () if chain is None else tuple(chain)
    hbm = pl.BlockSpec(memory_space=pl.ANY)
    first = count + 8
    kept_shapes = [
        (rows * places, experts),
        (rows * places, width),
        (rows * places, width),
        (rows * places, 2 * units),
        (rows * places, 2 * units),
        (rows * places, 2 * units),
        (rows * places, units),
        (rows * places, units),
    ]
    results = pl.pallas_call(
        lambda *refs: expert_body(indices, dy_source.ndim == 2, place, *refs),
        grid_spec=pltpu.PrefetchScalarGridSpec(
            num_scalar_prefetch=1,
            grid=(1,),
            in_specs=[hbm] * (count + 1)
            + [fixed(kept.shape), fixed((1, experts)), fixed((width, experts))]
            + [hbm] * (3 + len(extra)),
            out_specs=[hbm]
            + [
                fixed((rows, 1), False),
                pl.BlockSpec((rows, experts), lambda j, *_: (place, 0)),
            ]
            + [hbm] * 7,
            scratch_shapes=[
                pltpu.VMEM((rows, width), jnp.bfloat16),
                pltpu.VMEM((rows, width), jnp.bfloat16),
                pltpu.VMEM((width, 4 * units), jnp.bfloat16),
                pltpu.VMEM((2 * units, width), jnp.bfloat16),
                pltpu.VMEM((rows, 2 * units), jnp.float32),
                pltpu.VMEM((rows, units), jnp.float32),
                pltpu.VMEM((rows, 2 * units), jnp.bfloat16),
                pltpu.VMEM((rows, 4 * units), jnp.bfloat16),
                pltpu.VMEM((rows, 2 * units), jnp.bfloat16),
                pltpu.VMEM((rows, width), jnp.bfloat16),
                pltpu.VMEM((rows, experts), jnp.float32),
                pltpu.VMEM((rows, 1), jnp.float32),
                pltpu.SemaphoreType.DMA((3 * count + 13,)),
            ],
        ),
        out_shape=[jax.ShapeDtypeStruct((count, own_rows, width), jnp.bfloat16)]
        + [jax.ShapeDtypeStruct((rows, 1), jnp.float32)]
        + [jax.ShapeDtypeStruct(shape, jnp.bfloat16) for shape in kept_shapes],
        input_output_aliases={first + i: 2 + i for i in range(len(extra))},
        compiler_params=kernel_params(),
        cost_estimate=cost(80 * rows * width * units, 10 * rows * width + 12 * width * units),
        name="expert_chunk",
    )(
        here,
        *[x_pieces[i] for i in indices],
        dy_source,
        kept,
        chosen,
        router,
        gates,
        ups,
        downs,
        *extra,
    )
    return results[0], results[1], results[2:]


def finish_body(own_rows, full_cols, scalars, *refs):
    (query_scaled, key_scaled, value_low, query_raw, key_raw) = refs[:5]
    sums, inner_sums, low_out, near_out, far_out = refs[5:]
    columns = value_low.shape[1]
    core = scalars[0] & 1
    for side, (scaled, raw) in enumerate(((query_scaled, query_raw), (key_scaled, key_raw))):
        inverse = inverse_norm(sums, side, full_cols)
        normal = raw[...] * inverse
        low_out[:, side * columns : (side + 1) * columns] = (
            inverse * (scaled[...] - normal * (tall_column(inner_sums[...], side) / full_cols))
        ).astype(jnp.bfloat16)
    low_out[:, 2 * columns :] = value_low[...]
    for at in range(low_out.shape[0] // (2 * own_rows)):
        first = low_out[pl.ds(2 * at * own_rows, own_rows), :]
        second = low_out[pl.ds((2 * at + 1) * own_rows, own_rows), :]
        near_out[pl.ds(at * own_rows, own_rows), :] = jnp.where(core == 0, first, second)
        far_out[pl.ds(at * own_rows, own_rows), :] = jnp.where(core == 0, second, first)


def finish(here, own_rows, full_cols, *args):
    rows, columns = args[0].shape
    shapes = [(rows, 3 * columns)] + [(rows // 2, 3 * columns)] * 2
    return pl.pallas_call(
        lambda *refs: finish_body(own_rows, full_cols, *refs),
        grid_spec=pltpu.PrefetchScalarGridSpec(
            num_scalar_prefetch=1,
            grid=(1,),
            in_specs=[fixed(arg.shape) for arg in args],
            out_specs=[fixed(shape, False) for shape in shapes],
        ),
        out_shape=[jax.ShapeDtypeStruct(shape, jnp.bfloat16) for shape in shapes],
        compiler_params=kernel_params(),
        cost_estimate=cost(20 * rows * columns, 24 * rows * columns),
        name="finish",
    )(here, *args)


def near_product_body(indices, transposed, scalars, own, other, own_weight, other_weight, *refs):
    pieces, value = refs[:-1], refs[-1]
    side = 1 if transposed else 0
    value[...] = contract(own[...], own_weight[...], 1, side) + contract(
        other[...], other_weight[0], 1, side
    )
    own_rows = pieces[0].shape[0]
    for at, i in enumerate(indices):
        here = pl.ds(pl.multiple_of((scalars[0] ^ i) // 2 * own_rows, own_rows), own_rows)
        pieces[at][...] = value[here, :].astype(jnp.bfloat16)


def near_product(here, indices, own, other, own_weight, pair_weight, transposed):
    rows, depth = own.shape
    width = own_weight.shape[0 if transposed else 1]
    block = min(512, width // 2)
    count = len(indices)
    if transposed:
        mine = pl.BlockSpec((block, depth), lambda j, at: (j, 0))
        theirs = pl.BlockSpec((1, block, depth), lambda j, at: (1 - (at[0] & 1), j, 0))
    else:
        mine = pl.BlockSpec((depth, block), lambda j, at: (0, j))
        theirs = pl.BlockSpec((1, depth, block), lambda j, at: (1 - (at[0] & 1), 0, j))
    results = pl.pallas_call(
        lambda *refs: near_product_body(indices, transposed, *refs),
        grid_spec=pltpu.PrefetchScalarGridSpec(
            num_scalar_prefetch=1,
            grid=(width // block,),
            in_specs=[fixed(own.shape), fixed(other.shape), mine, theirs],
            out_specs=[pl.BlockSpec((rows // count, block), lambda j, at: (0, j))] * count,
            scratch_shapes=[pltpu.VMEM((rows, block), jnp.float32)],
        ),
        out_shape=[jax.ShapeDtypeStruct((rows // count, width), jnp.bfloat16)] * count,
        compiler_params=kernel_params(),
        cost_estimate=cost(4 * rows * depth * width, 2 * rows * width + 4 * depth * width),
        name="near_product",
    )(here, own, other, own_weight, pair_weight)
    return dict(zip(indices, results))


def total_of(parts):
    total = parts[0][...].astype(jnp.float32)
    for part in parts[1:]:
        total = total + part[...].astype(jnp.float32)
    return jnp.sum(total, axis=0) if total.ndim == 3 else total


def residual_body(tokens, gain, *refs):
    hidden_out, low_out = refs[-2:]
    hidden = tokens[...].astype(jnp.float32) + total_of(refs[:-2])
    normal, _ = rms_forward(hidden)
    hidden_out[...] = hidden
    low_out[...] = (normal * gain[...]).astype(jnp.bfloat16)


def residual(tokens, gain, parts):
    rows, width = tokens.shape
    return pl.pallas_call(
        residual_body,
        grid=(1,),
        in_specs=[fixed(tokens.shape), fixed((1, width))] + [fixed(part.shape) for part in parts],
        out_specs=[fixed((rows, width), False)] * 2,
        out_shape=[
            jax.ShapeDtypeStruct((rows, width), jnp.float32),
            jax.ShapeDtypeStruct((rows, width), jnp.bfloat16),
        ],
        compiler_params=kernel_params(),
        cost_estimate=cost(10 * rows * width, 20 * rows * width),
        name="residual",
    )(tokens, gain, *parts)


def norm_back_body(values, passed, gain, near, *refs):
    grad_out, low_out, gain_out = refs[-3:]
    grad = total_of([near]) + total_of(refs[:-3]) if len(refs) > 3 else total_of([near])
    normal, inverse = rms_forward(values[...].astype(jnp.float32))
    gain_out[...] = jnp.sum(grad * normal, axis=0, keepdims=True)
    scaled = grad * gain[...]
    result = passed[...].astype(jnp.float32) + inverse * (
        scaled - normal * jnp.mean(scaled * normal, axis=-1, keepdims=True)
    )
    grad_out[...] = result
    low_out[...] = result.astype(jnp.bfloat16)


def norm_back(values, passed, gain, near, parts):
    rows, width = values.shape
    args = (values, passed, gain, near, *parts)
    return pl.pallas_call(
        norm_back_body,
        grid=(1,),
        in_specs=[fixed(arg.shape) for arg in args],
        out_specs=[fixed((rows, width), False)] * 2 + [fixed((1, width), False)],
        out_shape=[
            jax.ShapeDtypeStruct((rows, width), jnp.float32),
            jax.ShapeDtypeStruct((rows, width), jnp.bfloat16),
            jax.ShapeDtypeStruct((1, width), jnp.float32),
        ],
        compiler_params=kernel_params(),
        cost_estimate=cost(20 * rows * width, 20 * rows * width),
        name="norm_back",
    )(*args)


def mixed_back_body(indices, scalars, own_weight, other_weight, *refs):
    count = len(indices)
    pieces = refs[:count]
    rows_out, own_out, other_out, lows = refs[count:]
    own_rows = pieces[0].shape[0]
    for at, i in enumerate(indices):
        here = pl.ds(pl.multiple_of((scalars[0] ^ i) // 2 * own_rows, own_rows), own_rows)
        lows[here, :] = pieces[at][...]
    rows_out[...] = lows[...]
    own_out[...] = contract(lows[...], own_weight[...], 1, 1).astype(jnp.bfloat16)
    other_out[...] = contract(lows[...], other_weight[0], 1, 1).astype(jnp.bfloat16)


def mixed_back(here, pieces, own_weight, pair_weight):
    indices = sorted(pieces)
    own_rows, width = pieces[0].shape
    rows = own_rows * len(indices)
    depth = own_weight.shape[0]
    shapes = [(rows, width), (rows, depth), (rows, depth)]
    return pl.pallas_call(
        lambda *refs: mixed_back_body(indices, *refs),
        grid_spec=pltpu.PrefetchScalarGridSpec(
            num_scalar_prefetch=1,
            grid=(1,),
            in_specs=[
                fixed(own_weight.shape),
                pl.BlockSpec((1, depth, width), lambda j, at: (1 - (at[0] & 1), 0, 0)),
            ]
            + [fixed((own_rows, width))] * len(indices),
            out_specs=[fixed(shape, False) for shape in shapes],
            scratch_shapes=[pltpu.VMEM((rows, width), jnp.bfloat16)],
        ),
        out_shape=[jax.ShapeDtypeStruct(shape, jnp.bfloat16) for shape in shapes],
        compiler_params=kernel_params(),
        cost_estimate=cost(4 * rows * depth * width, 4 * rows * width + 4 * depth * width),
        name="mixed_back",
    )(here, own_weight, pair_weight, *[pieces[i] for i in indices])


def place_body(indices, own_rows, scalars, *refs):
    pieces, out, sems = refs[: len(indices)], refs[-2], refs[-1]
    copies = []
    for at, i in enumerate(indices):
        here = pl.ds(pl.multiple_of((scalars[0] ^ i) * own_rows, own_rows), own_rows)
        copies.append(pltpu.make_async_copy(pieces[at], out.at[here], sems.at[at]))
        copies[-1].start()
    for copy in copies:
        copy.wait()


def place_rows(here, pieces):
    indices = sorted(pieces)
    own_rows, width = pieces[0].shape
    return pl.pallas_call(
        lambda *refs: place_body(indices, own_rows, *refs),
        grid_spec=pltpu.PrefetchScalarGridSpec(
            num_scalar_prefetch=1,
            grid=(1,),
            in_specs=[fixed((own_rows, width))] * len(indices),
            out_specs=pl.BlockSpec(memory_space=pl.ANY),
            scratch_shapes=[pltpu.SemaphoreType.DMA((len(indices),))],
        ),
        out_shape=jax.ShapeDtypeStruct((own_rows * len(indices), width), pieces[0].dtype),
        compiler_params=kernel_params(),
        cost_estimate=cost(0, 4 * own_rows * len(indices) * width),
        name="place_rows",
    )(here, *[pieces[i] for i in indices])


def row_of(column):
    n = column.shape[0]
    down = lax.broadcasted_iota(jnp.int32, (n, n), 0)
    across = lax.broadcasted_iota(jnp.int32, (n, n), 1)
    return jnp.sum(jnp.where(down == across, column, 0.0), axis=0, keepdims=True)


def tall_column(rows, side):
    block = min(256, rows.shape[1])
    return jnp.concatenate(
        [
            column_of(rows[side : side + 1, at : at + block])
            for at in range(0, rows.shape[1], block)
        ],
        axis=0,
    )


def inverse_norm(sums, side, full_cols):
    return lax.rsqrt(tall_column(sums[...], side) / full_cols + EPS)


def project_in_body(tokens, gain, w_query, w_key, w_value, low_out, q_out, k_out, v_out, sums_out):
    normal, _ = rms_forward(tokens[...].astype(jnp.float32))
    low = (normal * gain[...]).astype(jnp.bfloat16)
    low_out[...] = low
    for side, (weight, out) in enumerate(((w_query, q_out), (w_key, k_out))):
        raw = contract(low, weight[...], 1, 0)
        out[...] = raw
        sums_out[side : side + 1, :] = row_of(jnp.sum(raw * raw, axis=-1, keepdims=True))
    v_out[...] = contract(low, w_value[...], 1, 0).astype(jnp.bfloat16)


def project_in(tokens, gain, w_query, w_key, w_value):
    length, width = tokens.shape
    columns = w_query.shape[1]
    block = min(256, length)
    wide = pl.BlockSpec((block, columns), lambda i: (i, 0))
    return pl.pallas_call(
        project_in_body,
        grid=(length // block,),
        in_specs=[pl.BlockSpec((block, width), lambda i: (i, 0)), fixed((1, width))]
        + [fixed(w_query.shape)] * 3,
        out_specs=[
            pl.BlockSpec((block, width), lambda i: (i, 0)),
            wide,
            wide,
            wide,
            pl.BlockSpec((2, block), lambda i: (0, i)),
        ],
        out_shape=[
            jax.ShapeDtypeStruct((length, width), jnp.bfloat16),
            jax.ShapeDtypeStruct((length, columns), jnp.float32),
            jax.ShapeDtypeStruct((length, columns), jnp.float32),
            jax.ShapeDtypeStruct((length, columns), jnp.bfloat16),
            jax.ShapeDtypeStruct((2, length), jnp.float32),
        ],
        compiler_params=kernel_params(),
        cost_estimate=cost(6 * length * width * columns, 8 * length * width),
        name="project_in",
    )(tokens, gain, w_query, w_key, w_value)


def turned(values, cosine, sine):
    return values * cosine + pltpu.roll(values, values.shape[1] // 2, 1) * sine


def head_blocks(length):
    block = min(256, length)
    return [(start, start + block) for start in range(0, length, block)]


def block_probs(queries, keys, start, end):
    scores = contract(queries, keys, 1, 1)
    down = lax.broadcasted_iota(jnp.int32, scores.shape, 0) + start
    across = lax.broadcasted_iota(jnp.int32, scores.shape, 1)
    scores = jnp.where(down >= across, scores, -1e30)
    exponent = jnp.exp(scores - jnp.max(scores, axis=-1, keepdims=True))
    return exponent * (1.0 / jnp.sum(exponent, axis=-1, keepdims=True))


def pair_split(rows, core, own_rows):
    low = jnp.concatenate(
        [rows[at : at + own_rows] for at in range(0, rows.shape[0], 2 * own_rows)], axis=0
    )
    high = jnp.concatenate(
        [rows[at : at + own_rows] for at in range(own_rows, rows.shape[0], 2 * own_rows)], axis=0
    )
    return jnp.where(core == 0, low, high), jnp.where(core == 0, high, low)


def attend_body(
    own_rows,
    full_cols,
    scalars,
    query_raw,
    key_raw,
    values,
    sums,
    cosine,
    sine,
    gains,
    q_out,
    k_out,
    near_out,
    far_out,
):
    length, columns = query_raw.shape
    core = scalars[0] & 1
    query_inv = inverse_norm(sums, 0, full_cols)
    key_inv = inverse_norm(sums, 1, full_cols)
    for head in range(columns // HEAD_DIM):
        here = pl.ds(head * HEAD_DIM, HEAD_DIM)
        query_normed = query_raw[:, here] * query_inv * gains[0:1, here]
        key_normed = key_raw[:, here] * key_inv * gains[1:2, here]
        q_out[:, here] = (
            turned(query_normed, cosine[...], sine[...]) * HEAD_DIM ** (-0.5)
        ).astype(jnp.bfloat16)
        k_out[:, here] = turned(key_normed, cosine[...], sine[...]).astype(jnp.bfloat16)
        for start, end in head_blocks(length):
            rows = pl.ds(start, end - start)
            probs = block_probs(q_out[rows, here], k_out[pl.ds(0, end), here], start, end)
            near, far = pair_split(
                contract(probs.astype(jnp.bfloat16), values[pl.ds(0, end), here], 1, 0),
                core,
                own_rows,
            )
            half = pl.ds(start // 2, (end - start) // 2)
            near_out[half, here] = near.astype(jnp.bfloat16)
            far_out[half, here] = far.astype(jnp.bfloat16)


def attend(here, own_rows, full_cols, *args):
    length, columns = args[0].shape
    shapes = [(length, columns)] * 2 + [(length // 2, columns)] * 2
    return pl.pallas_call(
        lambda *refs: attend_body(own_rows, full_cols, *refs),
        grid_spec=pltpu.PrefetchScalarGridSpec(
            num_scalar_prefetch=1,
            grid=(1,),
            in_specs=[fixed(arg.shape) for arg in args],
            out_specs=[fixed(shape, False) for shape in shapes],
        ),
        out_shape=[jax.ShapeDtypeStruct(shape, jnp.bfloat16) for shape in shapes],
        compiler_params=kernel_params(),
        cost_estimate=cost(4 * length * length * columns, 16 * length * columns),
        name="attend",
    )(here, *args)


def attend_back_body(
    own_rows,
    full_cols,
    scalars,
    near,
    far,
    queries,
    keys,
    values,
    query_raw,
    key_raw,
    sums,
    cosine,
    sine,
    gains,
    *refs,
):
    query_scaled, key_scaled, value_low, inner_out, gain_out = refs[:5]
    grads, grad_key, grad_value = refs[5:]
    length, columns = queries.shape
    core = scalars[0] & 1
    inners = [None, None]
    for at in range(length // (2 * own_rows)):
        mine, other = near[pl.ds(at * own_rows, own_rows), :], far[pl.ds(at * own_rows, own_rows), :]
        first = pl.ds(2 * at * own_rows, own_rows)
        second = pl.ds((2 * at + 1) * own_rows, own_rows)
        grads[first, :] = jnp.where(core == 0, mine, other)
        grads[second, :] = jnp.where(core == 0, other, mine)
    for head in range(columns // HEAD_DIM):
        here = pl.ds(head * HEAD_DIM, HEAD_DIM)
        grad_key[...] = jnp.zeros_like(grad_key)
        grad_value[...] = jnp.zeros_like(grad_value)
        for start, end in head_blocks(length):
            rows, past = pl.ds(start, end - start), pl.ds(0, end)
            probs = block_probs(queries[rows, here], keys[past, here], start, end)
            grad_probs = contract(grads[rows, here], values[past, here], 1, 1)
            grad_scores = (
                probs * (grad_probs - jnp.sum(probs * grad_probs, axis=-1, keepdims=True))
            ).astype(jnp.bfloat16)
            grad_value[past, :] += contract(probs.astype(jnp.bfloat16), grads[rows, here], 0, 0)
            grad_key[past, :] += contract(grad_scores, queries[rows, here], 0, 0)
            query_scaled[rows, here] = contract(grad_scores, keys[past, here], 1, 0)
        value_low[:, here] = grad_value[...].astype(jnp.bfloat16)
        sides = (
            (query_scaled[:, here] * HEAD_DIM ** (-0.5), query_raw, query_scaled),
            (grad_key[...], key_raw, key_scaled),
        )
        for side, (grad, raw, scaled_out) in enumerate(sides):
            normed = turned(grad, cosine[...], -sine[...])
            normal = raw[:, here] * inverse_norm(sums, side, full_cols)
            gain_out[side : side + 1, here] = jnp.sum(normed * normal, axis=0, keepdims=True)
            scaled = normed * gains[side : side + 1, here]
            scaled_out[:, here] = scaled
            inner = jnp.sum(scaled * normal, axis=-1, keepdims=True)
            inners[side] = inner if inners[side] is None else inners[side] + inner
    block = min(256, length)
    for side in range(2):
        for at in range(0, length, block):
            inner_out[side : side + 1, at : at + block] = row_of(inners[side][at : at + block])


def attend_back(here, own_rows, full_cols, *args):
    length, columns = args[2].shape
    wide = jax.ShapeDtypeStruct((length, columns), jnp.float32)
    outs = [
        wide,
        wide,
        jax.ShapeDtypeStruct((length, columns), jnp.bfloat16),
        jax.ShapeDtypeStruct((2, length), jnp.float32),
        jax.ShapeDtypeStruct((2, columns), jnp.float32),
    ]
    return pl.pallas_call(
        lambda *refs: attend_back_body(own_rows, full_cols, *refs),
        grid_spec=pltpu.PrefetchScalarGridSpec(
            num_scalar_prefetch=1,
            grid=(1,),
            in_specs=[fixed(arg.shape) for arg in args],
            out_specs=[fixed(out.shape, False) for out in outs],
            scratch_shapes=[pltpu.VMEM((length, columns), jnp.bfloat16)]
            + [pltpu.VMEM((length, HEAD_DIM), jnp.float32)] * 2,
        ),
        out_shape=outs,
        compiler_params=kernel_params(),
        cost_estimate=cost(8 * length * length * columns, 40 * length * columns),
        name="attend_back",
    )(here, *args)


def near_scatter(pieces):
    size = lax.axis_size("tensor")
    groups = [list(range(core, size, 2)) for core in range(2)]
    return lax.all_to_all(
        pieces, "tensor", split_axis=0, concat_axis=0, axis_index_groups=groups, tiled=True
    )


def line_step(part, step):
    bits = axis_bits("expert")[::-1]
    index = lax.axis_index("expert")
    if step < len(bits):
        bit = bits[step]
        half = part.shape[0] // 2
        high = (index // bit) % 2
        kept = lax.dynamic_slice_in_dim(part, high * half, half, 0)
        sent = lax.dynamic_slice_in_dim(part, (1 - high) * half, half, 0)
        return (
            kept.astype(jnp.float32) + swap(sent, "expert", bit).astype(jnp.float32)
        ).astype(jnp.bfloat16)
    bit = bits[2 * len(bits) - 1 - step]
    high = (index // bit) % 2 == 1
    other = swap(part, "expert", bit)
    return jnp.concatenate([jnp.where(high, other, part), jnp.where(high, part, other)], axis=0)


def send_body(indices, places, scalars, act, *refs):
    gates, (down_own, down_other), outs = refs[:places], refs[places : places + 2], refs[-places:]
    units = down_own.shape[1]
    value = contract(act[:, :units], down_own[0], 1, 0) + contract(
        act[:, units:], down_other[0], 1, 0
    )
    own_rows = outs[0].shape[1]
    for place in range(places):

        @pl.when(pl.program_id(1) == place)
        def _():
            sent = (gates[place][...] * value).astype(jnp.bfloat16)
            for at, i in enumerate(indices):
                outs[place][(scalars[0] ^ i) // 2] = sent[at * own_rows : (at + 1) * own_rows]


def expert_send(here, indices, act_all, gates, downs):
    rows = gates[0].shape[0]
    count = len(indices)
    places = len(gates)
    _, units, width = downs.shape
    block = min(1024, width // 2)
    return pl.pallas_call(
        lambda *refs: send_body(indices, places, *refs),
        grid_spec=pltpu.PrefetchScalarGridSpec(
            num_scalar_prefetch=1,
            grid=(width // block, places),
            in_specs=[pl.BlockSpec((rows, 2 * units), lambda j, k, *_: (k, 0))]
            + [fixed((rows, 1))] * places
            + [
                pl.BlockSpec((1, units, block), lambda j, k, at: (at[0] & 1, 0, j)),
                pl.BlockSpec((1, units, block), lambda j, k, at: (1 - (at[0] & 1), 0, j)),
            ],
            out_specs=[pl.BlockSpec((count, rows // count, block), lambda j, k, *_: (0, 0, j))]
            * places,
        ),
        out_shape=[jax.ShapeDtypeStruct((count, rows // count, width), jnp.bfloat16)] * places,
        compiler_params=kernel_params(),
        cost_estimate=cost(
            4 * places * rows * width * units, places * 4 * rows * width + 4 * width * units
        ),
        name="expert_send",
    )(here, act_all, *gates, downs, downs)


def on_device(
    tokens,
    positions,
    routes,
    slot_ids,
    attn_gain,
    w_query,
    w_key,
    w_value,
    query_gain,
    key_gain,
    w_out,
    ffn_gain,
    router,
    w_gate,
    w_up,
    w_down,
    grad_out,
):
    tensor_size = lax.axis_size("tensor")
    expert_size = lax.axis_size("expert")
    local_count = tensor_size // 2
    tensor_index = lax.axis_index("tensor")
    expert_index = lax.axis_index("expert")
    own_local = tensor_index // 2
    own_expert = expert_index * local_count + own_local
    length, model_width = tokens.shape
    heads_here = w_query.shape[1] // HEAD_DIM
    full_cols = w_query.shape[1] * tensor_size
    expert_count = router.shape[1]
    capacity = 3 * length * TOP // (2 * expert_count)
    own_rows = length // tensor_size
    chunks = list(range(expert_size))
    bits = axis_bits("tensor")
    near_bits = bits[:-1]
    last = len(near_bits)

    def own_slice(rows):
        return lax.dynamic_slice_in_dim(rows, tensor_index * own_rows, own_rows, 0)

    pairs = [[2 * i, 2 * i + 1] for i in range(tensor_size // 2)]

    def pair_gather(values):
        return lax.all_gather(values, "tensor", axis_index_groups=pairs)

    grad_own = own_slice(grad_out)
    near_groups = [list(range(core, tensor_size, 2)) for core in range(2)]
    grad_sent = {chunk: swap(grad_own, "expert", chunk) for chunk in chunks[1:]}
    grad_rows_of = {0: grad_out}
    out_pair = jnp.where(
        jnp.arange(2)[:, None, None] == tensor_index % 2,
        w_out[None],
        swap(w_out, "tensor", 1)[None],
    )
    expert_iota = jnp.arange(expert_count, dtype=jnp.int32)
    kept_table = jnp.sum(
        (
            (routes.T[:, None, :] == expert_iota[None, :, None]) & (slot_ids.T < capacity)[:, None, :]
        ).astype(jnp.float32),
        axis=0,
    )
    targets = jnp.arange(expert_size, dtype=jnp.int32) * local_count + own_local
    kept_rows = lax.all_to_all(
        jnp.take(kept_table, targets, axis=0).reshape(expert_size, tensor_size, own_rows),
        "expert",
        split_axis=0,
        concat_axis=0,
        tiled=True,
    )

    def here(chunk):
        return jnp.stack([tensor_index, expert_index ^ chunk]).astype(jnp.int32)

    score_scale = HEAD_DIM ** (-0.5)
    half_dim = HEAD_DIM // 2
    frequency = THETA ** (-2.0 * jnp.arange(half_dim, dtype=jnp.float32) / HEAD_DIM)
    angles = positions.astype(jnp.float32)[:, None] * frequency[None, :]
    cosine_table = jnp.concatenate([jnp.cos(angles)] * 2, axis=-1)
    sine_half = jnp.sin(angles)
    sine_table = jnp.concatenate([-sine_half, sine_half], axis=-1)
    attn_in, query_raw, key_raw, value_rows, square_sums = project_in(
        tokens, attn_gain[None, :], w_query, w_key, w_value
    )
    w_all = jnp.concatenate([w_query, w_key, w_value], axis=1)
    gains = jnp.stack([query_gain, key_gain])
    square_sums = spread_sum(square_sums, "tensor")
    indices = sorted(direct_combos(near_bits))
    gates, ups, downs = [pair_gather(weights[0]) for weights in (w_gate, w_up, w_down)]
    query_rows, key_rows, mixed_near, mixed_far = attend(
        here(0),
        own_rows,
        full_cols,
        query_raw,
        key_raw,
        value_rows,
        square_sums,
        cosine_table,
        sine_table,
        gains,
    )
    mixed_other = swap(mixed_far, "tensor", 1)
    w_pair = pair_gather(w_all)
    attn_parts = near_product(
        here(0), indices, mixed_near, mixed_other, w_out, out_pair, False
    )
    attn_moved = [swap(attn_parts[i], "tensor", i) for i in indices if i]
    hidden, ffn_in = residual(
        own_slice(tokens),
        ffn_gain[None, :],
        [attn_parts[0]] + attn_moved,
    )
    chosen = (expert_iota == own_expert).astype(jnp.float32)[None, :]
    received = [ffn_in]
    gathered = [direct_gather(ffn_in, near_bits)]
    for chunk in chunks[1:]:
        sent = tie(ffn_in, gathered[0][near_bits[0]]) if chunk > 2 else ffn_in
        received.append(swap(sent, "expert", chunk))
    waited = {1: [square_sums], 2: attn_moved}
    for chunk, piece in grad_sent.items():
        piece = tie(piece, *waited.get(chunk, [gathered[0][i] for i in indices if i] + received[1:2]))
        grad_rows_of[chunk] = lax.all_gather(piece, "tensor", axis_index_groups=near_groups)
    chain = None
    sums = []
    gate_columns = []
    for at, chunk in enumerate(chunks):
        scalars = here(chunk)
        if at:
            after = [gathered[at - 1][i] for i in gathered[at - 1] if i]
            if at >= 2:
                after.append(gate_columns[at - 2])
            gathered.append(direct_gather(received[at], near_bits, after))
        if at >= 3:
            scalars = tie(scalars, sums[at - 3])
        if at + 1 == expert_size:
            scalars = tie(scalars, w_pair)
        pieces, gate_column, chain = expert_chunk(
            at,
            expert_size,
            gathered[at],
            grad_rows_of[chunk],
            scalars,
            kept_rows,
            chosen,
            router,
            gates,
            ups,
            downs,
            chain,
        )
        gate_columns.append(gate_column)
        sums.append(near_scatter(pieces))

    def plane_total(near):
        return jnp.sum(near.astype(jnp.float32), axis=0).astype(jnp.bfloat16)

    dl_all, x_all, dy_all, act_all, own_dp, other_dp, gated_own, gated_other = chain
    row_totals = [plane_total(near) for near in sums[1:-1]]
    sent_pieces = expert_send(tie(here(0), *row_totals), indices, act_all, gate_columns, downs)
    grad_parts = [sums[0]] + [
        swap(total, "expert", chunk) for total, chunk in zip(row_totals, chunks[1:])
    ]
    row_totals.append(plane_total(tie(sums[-1], sent_pieces[0], *grad_parts[1:])))
    grad_parts.append(swap(row_totals[-1], "expert", chunks[-1]))
    sent_near = {1: near_scatter(tie(sent_pieces[1], row_totals[-1]))}
    grad_parts[0] = tie(grad_parts[0], sent_near[1])
    grad_hidden, hidden_low, grad_ffn_gain = norm_back(
        hidden, grad_own, ffn_gain[None, :], grad_parts[0], grad_parts[1:]
    )
    hidden_near, back_own, back_other = mixed_back(
        here(0), direct_gather(hidden_low, near_bits), w_out, out_pair
    )
    back_far = swap(back_other, "tensor", 1)
    for chunk in chunks[2:-1]:
        sent_near[chunk] = near_scatter(tie(sent_pieces[chunk], hidden_near))

    units = own_dp.shape[1] // 2
    other_wide = swap(contract(x_all, tie(other_dp, hidden_low), 0, 0).astype(jnp.bfloat16), "tensor", 1)
    other_down = swap(contract(gated_other, dy_all, 0, 0).astype(jnp.bfloat16), "tensor", 1)
    grad_router_part = contract(dl_all, x_all, 0, 0)

    grad_w_out = contract(mixed_near, hidden_near, 0, 0)
    grad_w_out_other = contract(mixed_other, hidden_near, 0, 0).astype(jnp.bfloat16)
    grad_w_out_low = (
        grad_w_out + swap(grad_w_out_other, "tensor", 1).astype(jnp.float32)
    ).astype(jnp.bfloat16)
    query_scaled, key_scaled, value_low, inner_sums, gain_parts = attend_back(
        tie(here(0), grad_w_out_other),
        own_rows,
        full_cols,
        back_own,
        back_far,
        query_rows,
        key_rows,
        value_rows,
        query_raw,
        key_raw,
        square_sums,
        cosine_table,
        sine_table,
        gains,
    )
    grad_w_value = contract(attn_in, value_low, 0, 0).astype(jnp.bfloat16)
    inner_sums = spread_sum(
        tie(inner_sums, *[sent_near[chunk] for chunk in chunks[2:-1]]), "tensor"
    )
    sent_near[chunks[-1]] = near_scatter(tie(sent_pieces[chunks[-1]], inner_sums))
    inner_sums = tie(inner_sums, grad_w_out_low, grad_w_value)
    line_steps = 2 * len(axis_bits("expert"))
    low_all, low_near, low_far = finish(
        here(0),
        own_rows,
        full_cols,
        query_scaled,
        key_scaled,
        value_low,
        query_raw,
        key_raw,
        square_sums,
        inner_sums,
    )
    grad_attn = near_product(
        here(0), indices, low_near, swap(low_far, "tensor", 1), w_all, w_pair, True
    )
    columns_here = w_query.shape[1]
    grad_w_both = contract(attn_in, low_all[:, : 2 * columns_here], 0, 0).astype(jnp.bfloat16)
    grad_attn_moved = [swap(grad_attn[i], "tensor", i) for i in indices if i]
    own_dp, gated_own = lax.optimization_barrier((own_dp, gated_own, grad_attn[0]))[:2]
    grad_gate_w = contract(x_all, own_dp[:, :units], 0, 0) + other_wide[:, :units].astype(jnp.float32)
    grad_up_w = contract(x_all, own_dp[:, units:], 0, 0) + other_wide[:, units:].astype(jnp.float32)
    grad_down = contract(gated_own, dy_all, 0, 0) + other_down.astype(jnp.float32)
    sent_moved = [
        swap(plane_total(tie(sent_near[chunk], grad_attn[0])), "expert", chunk)
        for chunk in chunks[1:]
    ]
    _, token_low, grad_attn_gain = norm_back(
        tie(own_slice(tokens), sent_near[chunks[-1]]), grad_hidden, attn_gain[None, :], grad_attn[0], grad_attn_moved
    )

    def gather_rows(piece):
        pieces = direct_gather(piece, near_bits)
        return {**pieces, **{i ^ 1: swap(near, "tensor", 1) for i, near in pieces.items()}}

    token_pieces = gather_rows(token_low)
    grad_tokens = place_rows(here(0), token_pieces)
    late = [token_pieces[i] for i in indices if i]
    both_lines = line_step(grad_w_both, 0)
    sent_near[0] = near_scatter(tie(sent_pieces[0], *late))
    moe_sum = hidden + jnp.sum(sent_near[0].astype(jnp.float32), axis=0)
    for moved in sent_moved:
        moe_sum = moe_sum + moved.astype(jnp.float32)
    out_pieces = gather_rows(tie(moe_sum.astype(jnp.bfloat16), *late))
    output = place_rows(here(0), out_pieces)
    both_lines = line_step(tie(both_lines, *late), 1)
    for step in range(2, line_steps):
        both_lines = line_step(both_lines, step)
    sum_out, sum_value = [
        part.astype(jnp.float32) for part in lax.psum((grad_w_out_low, grad_w_value), "expert")
    ]
    sum_both = both_lines.astype(jnp.float32)
    sum_query, sum_key = sum_both[:, :columns_here], sum_both[:, columns_here:]
    plane_sums = spread_sum(
        tie(jnp.concatenate([grad_router_part, grad_ffn_gain, grad_attn_gain], axis=0), *late),
        "tensor",
    )
    scales = gain_parts.reshape(-1)
    scales = jnp.pad(scales, (0, model_width - scales.shape[0]))
    all_sums = spread_sum(jnp.concatenate([plane_sums, scales[None, :]], axis=0), "expert")
    return (
        output,
        grad_tokens,
        all_sums[expert_count + 1],
        sum_query,
        sum_key,
        sum_value,
        all_sums[expert_count + 2, :columns_here],
        all_sums[expert_count + 2, columns_here : 2 * columns_here],
        sum_out,
        all_sums[expert_count],
        all_sums[:expert_count].T,
        grad_gate_w[None],
        grad_up_w[None],
        grad_down[None],
    )


def solution(mesh):
    placed = (
        P("expert", None),
        P("expert"),
        P("expert", None),
        P("expert", None),
        P(),
        P(None, "tensor"),
        P(None, "tensor"),
        P(None, "tensor"),
        P("tensor"),
        P("tensor"),
        P("tensor", None),
        P(),
        P(),
        P(("expert", "tensor"), None, None),
        P(("expert", "tensor"), None, None),
        P(("expert", "tensor"), None, None),
        P("expert", None),
    )
    return jax.shard_map(
        on_device,
        mesh=mesh,
        in_specs=placed,
        out_specs=(
            P("expert", None),
            P("expert", None),
            P(),
            P(None, "tensor"),
            P(None, "tensor"),
            P(None, "tensor"),
            P("tensor"),
            P("tensor"),
            P("tensor", None),
            P(),
            P(),
            P(("expert", "tensor"), None, None),
            P(("expert", "tensor"), None, None),
            P(("expert", "tensor"), None, None),
        ),
        check_vma=False,
    )
```

```python
import jax
import jax.numpy as jnp
from jax import lax
from jax.experimental import pallas as pl
from jax.experimental.pallas import tpu as pltpu
from jax.sharding import PartitionSpec as P

HEAD_DIM = 128
TOP = 8


EPS = 1e-05
THETA = 10000.0


def rms_forward(values):
    inverse = lax.rsqrt(jnp.mean(values * values, axis=-1, keepdims=True) + EPS)
    return (values * inverse, inverse)


def rms_backward(grad_normed, normal_rows, inverse, gain_row):
    gain_grad = jnp.sum(grad_normed * normal_rows, axis=0)
    scaled = grad_normed * gain_row
    grad_rows = inverse * (
        scaled - normal_rows * jnp.mean(scaled * normal_rows, axis=-1, keepdims=True)
    )
    return (grad_rows, gain_grad)


def swap(values, axis, bit):
    return lax.ppermute(values, axis, [(i, i ^ bit) for i in range(lax.axis_size(axis))])


def axis_bits(axis):
    size = lax.axis_size(axis)
    return [size >> (k + 1) for k in range(size.bit_length() - 1)]


def spread_sum(values, axis):
    for bit in axis_bits(axis)[::-1]:
        values = values + swap(values, axis, bit)
    return values


def plane_order(turn):
    bits = axis_bits("tensor")[:-1]
    if turn % 2:
        bits = bits[::-1]
    order = [0]
    for bit in bits:
        order = order + [bit ^ i for i in order]
    return bits, order


def plane_gather(piece, turn):
    bits, _ = plane_order(turn)
    pieces = [piece]
    for bit in bits:
        pieces = pieces + [swap(p, "tensor", bit) for p in pieces]
    near = jnp.concatenate(pieces, axis=0)
    return near, swap(near, "tensor", 1)


def plane_scatter(near, far, turn):
    bits, _ = plane_order(turn)
    total = near.astype(jnp.float32) + swap(far, "tensor", 1).astype(jnp.float32)
    for bit in bits[::-1]:
        half = total.shape[0] // 2
        sent = total[half:].astype(jnp.bfloat16)
        total = total[:half].astype(jnp.bfloat16).astype(jnp.float32) + swap(
            sent, "tensor", bit
        ).astype(jnp.float32)
    return total


def plane_rows(values, turn, own_rows, sorted_order=False):
    _, order = plane_order(turn)
    if sorted_order:
        order = sorted(order)
    index = lax.axis_index("tensor")

    def block(i):
        return lax.dynamic_slice_in_dim(values, (index ^ i) * own_rows, own_rows, 0)

    near = jnp.concatenate([block(i) for i in order], axis=0)
    far = jnp.concatenate([block(i ^ 1) for i in order], axis=0)
    return near, far


def natural_rows(near, far, turn, own_rows):
    _, order = plane_order(turn)
    index = lax.axis_index("tensor")
    both = jnp.concatenate([near, far], axis=0)
    place = {}
    for at, i in enumerate(order):
        place[i] = at
        place[i ^ 1] = at + len(order)
    table = jnp.array([place[i] for i in range(2 * len(order))], jnp.int32)
    return jnp.concatenate(
        [
            lax.dynamic_slice_in_dim(both, table[index ^ i] * own_rows, own_rows, 0)
            for i in range(2 * len(order))
        ],
        axis=0,
    )


def contract(left, right, left_dim, right_dim):
    return lax.dot_general(
        left, right, (((left_dim,), (right_dim,)), ((), ())), preferred_element_type=jnp.float32
    )


def tie(values, *after):
    return lax.optimization_barrier((values, *after))[0]


def stages(turn, bits):
    if turn % 2:
        bits = bits[::-1]
    found = [[] for _ in bits]
    order = [(0, ())]
    for bit in bits:
        order = order + [(bit ^ i, used + (bit,)) for i, used in order]
    for i, used in order[1:]:
        found[len(used) - 1].append((i, i ^ used[-1], used[-1]))
    return found


def gather_stage(pieces, turn, stage, bits, after=()):
    pieces = dict(pieces)
    for i, source, bit in stages(turn, bits)[stage]:
        sent = pieces[source]
        if after:
            sent = tie(sent, *after)
        pieces[i] = swap(sent, "tensor", bit)
    return pieces


def direct_combos(bits):
    combos = [0]
    for bit in bits:
        combos = combos + [bit ^ i for i in combos]
    return combos


def direct_gather(piece, bits, after=()):
    pieces = {0: piece}
    for i in direct_combos(bits)[1:]:
        pieces[i] = swap(tie(piece, *after) if after else piece, "tensor", i)
    return pieces


def gather_all(piece, turn, bits):
    pieces = {0: piece}
    for stage in range(len(bits)):
        pieces = gather_stage(pieces, turn, stage, bits)
    return pieces


def scatter_stage(sums, turn, stage, bits, after=()):
    sums = dict(sums)
    for i, target, bit in stages(turn, bits)[len(bits) - 1 - stage]:
        sent = sums.pop(i).astype(jnp.bfloat16)
        if after:
            sent = tie(sent, *after)
        sums[target] = sums[target].astype(jnp.float32) + swap(sent, "tensor", bit).astype(
            jnp.float32
        )
    return sums


MEGABYTE = 1024 * 1024


def kernel_params():
    return pltpu.CompilerParams(vmem_limit_bytes=58 * MEGABYTE)


def cost(flops, moved):
    return pl.CostEstimate(flops=flops, bytes_accessed=moved, transcendentals=0)


def column_of(row):
    n = row.shape[1]
    down = lax.broadcasted_iota(jnp.int32, (n, n), 0)
    across = lax.broadcasted_iota(jnp.int32, (n, n), 1)
    return jnp.sum(jnp.where(down == across, row, 0.0), axis=1, keepdims=True)


def fixed(shape, single=True):
    if single:
        return pl.BlockSpec(
            shape, lambda *_: (0,) * len(shape), pipeline_mode=pl.Buffered(1)
        )
    return pl.BlockSpec(shape, lambda *_: (0,) * len(shape))


def expert_body(indices, local, place, scalars, *refs):
    count = len(indices)
    x_parts, refs = refs[:count], refs[count:]
    dy_source, kept, chosen, router, gates, ups, downs = refs[:7]
    core = scalars[0] & 1
    gate_own, gate_other = gates.at[core], gates.at[1 - core]
    up_own, up_other = ups.at[core], ups.at[1 - core]
    down_own, down_other = downs.at[core], downs.at[1 - core]
    scratch = refs[-13:]
    pieces, gate_out, dl_all, x_all, dy_all, act_all, own_dp, other_dp, gated_own, gated_other = refs[
        -23:-13
    ]
    rows, grads, wide, tall, raw, inner, act, slopes, gated, done, probs_ref, dots, sems = scratch
    rows_here, width = rows.shape
    units = gate_own.shape[1]
    own_rows = rows_here // count
    used = []
    dy_parts = []
    for i in indices:
        if local:
            at = pl.multiple_of((scalars[0] ^ i) * own_rows, own_rows)
            dy_parts.append(dy_source.at[pl.ds(at, own_rows)])
        else:
            dy_parts.append(dy_source.at[(scalars[0] ^ i) // 2])

    def start(source, target):
        copy = pltpu.make_async_copy(source, target, sems.at[len(used)])
        used.append(copy)
        copy.start()
        return copy

    def spread(parts, target):
        size = rows_here // len(parts)
        return [start(part, target.at[pl.ds(at * size, size)]) for at, part in enumerate(parts)]

    x_copies = spread(x_parts, rows)
    order = [gate_own, up_own, gate_other, up_other]
    wide_copies = [
        start(weight, wide.at[:, pl.ds(at * units, units)]) for at, weight in enumerate(order[:2])
    ]
    dy_copies = spread(dy_parts, grads)
    tall_copies = [start(down_own, tall.at[pl.ds(0, units)])]
    wide_copies += [
        start(weight, wide.at[:, pl.ds((at + 2) * units, units)])
        for at, weight in enumerate(order[2:])
    ]
    tall_copies.append(start(down_other, tall.at[pl.ds(units, units)]))

    here_rows = pl.ds(place * rows_here, rows_here)
    for copy in x_copies:
        copy.wait()
    outgoing = [start(rows, x_all.at[here_rows])]
    logits = contract(rows[...], router[...], 1, 0)
    exponent = jnp.exp(logits - jnp.max(logits, axis=-1, keepdims=True))
    probs = exponent / jnp.sum(exponent, axis=-1, keepdims=True)
    kept_column = jnp.concatenate(
        [column_of(kept[scalars[1], pl.ds(scalars[0] ^ i, 1), :]) for i in indices], axis=0
    )
    probs_ref[...] = probs
    gate_out[...] = jnp.sum(probs * chosen[...], axis=-1, keepdims=True) * kept_column
    dots[...] = jnp.zeros_like(dots)

    block = min(64, rows_here)
    for half in range(2):
        columns = pl.ds(half * units, units)
        for part in range(2):
            at = 2 * half + part
            wide_copies[at].wait()
            raw[:, pl.ds(part * units, units)] = contract(
                rows[...], wide[:, pl.ds(at * units, units)], 1, 0
            )
        if half == 0:
            for copy in dy_copies:
                copy.wait()
            outgoing.append(start(grads, dy_all.at[here_rows]))
        tall_copies[half].wait()
        inner[...] = contract(grads[...], tall[columns, :], 1, 1)

        @pl.loop(0, rows_here // block)
        def _(at):
            here = pl.ds(at * block, block)
            pre_gate = raw[here, pl.ds(0, units)]
            pre_up = raw[here, pl.ds(units, units)]
            inward = inner[here, :]
            gate = gate_out[here, :]
            sigmoid_gate = 1.0 / (1.0 + jnp.exp(-pre_gate))
            silu_gate = pre_gate * sigmoid_gate
            active = (silu_gate * pre_up).astype(jnp.bfloat16)
            act[here, columns] = active
            active = active.astype(jnp.float32)
            gated[here, columns] = (gate * active).astype(jnp.bfloat16)
            dots[here, :] += jnp.sum(inward * active, axis=-1, keepdims=True)
            grad_active = gate * inward
            slopes[here, pl.ds(2 * half * units, units)] = (
                grad_active * pre_up * sigmoid_gate * (1.0 + pre_gate * (1.0 - sigmoid_gate))
            ).astype(jnp.bfloat16)
            slopes[here, pl.ds((2 * half + 1) * units, units)] = (grad_active * silu_gate).astype(
                jnp.bfloat16
            )

    outgoing += [
        start(act, act_all.at[here_rows]),
        start(slopes.at[:, pl.ds(0, 2 * units)], own_dp.at[here_rows]),
        start(slopes.at[:, pl.ds(2 * units, 2 * units)], other_dp.at[here_rows]),
        start(gated.at[:, pl.ds(0, units)], gated_own.at[here_rows]),
        start(gated.at[:, pl.ds(units, units)], gated_other.at[here_rows]),
    ]
    grad_logits = (dots[...] * gate_out[...] * (chosen[...] - probs_ref[...])).astype(jnp.bfloat16)
    dl_all[...] = grad_logits
    step = min(512, width)
    for at in range(width // step):
        columns = pl.ds(at * step, step)
        done[:, columns] = (
            contract(slopes[...], wide[columns, :], 1, 1)
            + contract(grad_logits, router[columns, :], 1, 1)
        ).astype(jnp.bfloat16)
    for at, i in enumerate(indices):
        to = (scalars[0] ^ i) // 2
        outgoing.append(start(done.at[pl.ds(at * own_rows, own_rows)], pieces.at[to]))
    for copy in outgoing:
        copy.wait()


def expert_chunk(
    place, places, x_pieces, dy_source, here, kept, chosen, router, gates, ups, downs, chain
):
    indices = sorted(x_pieces)
    count = len(indices)
    own_rows, width = x_pieces[0].shape
    rows = own_rows * count
    units = gates.shape[2]
    experts = router.shape[1]
    extra = () if chain is None else tuple(chain)
    hbm = pl.BlockSpec(memory_space=pl.ANY)
    first = count + 8
    kept_shapes = [
        (rows * places, experts),
        (rows * places, width),
        (rows * places, width),
        (rows * places, 2 * units),
        (rows * places, 2 * units),
        (rows * places, 2 * units),
        (rows * places, units),
        (rows * places, units),
    ]
    results = pl.pallas_call(
        lambda *refs: expert_body(indices, dy_source.ndim == 2, place, *refs),
        grid_spec=pltpu.PrefetchScalarGridSpec(
            num_scalar_prefetch=1,
            grid=(1,),
            in_specs=[hbm] * (count + 1)
            + [fixed(kept.shape), fixed((1, experts)), fixed((width, experts))]
            + [hbm] * (3 + len(extra)),
            out_specs=[hbm]
            + [
                fixed((rows, 1), False),
                pl.BlockSpec((rows, experts), lambda j, *_: (place, 0)),
            ]
            + [hbm] * 7,
            scratch_shapes=[
                pltpu.VMEM((rows, width), jnp.bfloat16),
                pltpu.VMEM((rows, width), jnp.bfloat16),
                pltpu.VMEM((width, 4 * units), jnp.bfloat16),
                pltpu.VMEM((2 * units, width), jnp.bfloat16),
                pltpu.VMEM((rows, 2 * units), jnp.float32),
                pltpu.VMEM((rows, units), jnp.float32),
                pltpu.VMEM((rows, 2 * units), jnp.bfloat16),
                pltpu.VMEM((rows, 4 * units), jnp.bfloat16),
                pltpu.VMEM((rows, 2 * units), jnp.bfloat16),
                pltpu.VMEM((rows, width), jnp.bfloat16),
                pltpu.VMEM((rows, experts), jnp.float32),
                pltpu.VMEM((rows, 1), jnp.float32),
                pltpu.SemaphoreType.DMA((3 * count + 13,)),
            ],
        ),
        out_shape=[jax.ShapeDtypeStruct((count, own_rows, width), jnp.bfloat16)]
        + [jax.ShapeDtypeStruct((rows, 1), jnp.float32)]
        + [jax.ShapeDtypeStruct(shape, jnp.bfloat16) for shape in kept_shapes],
        input_output_aliases={first + i: 2 + i for i in range(len(extra))},
        compiler_params=kernel_params(),
        cost_estimate=cost(80 * rows * width * units, 10 * rows * width + 12 * width * units),
        name="expert_chunk",
    )(
        here,
        *[x_pieces[i] for i in indices],
        dy_source,
        kept,
        chosen,
        router,
        gates,
        ups,
        downs,
        *extra,
    )
    return results[0], results[1], results[2:]


def finish_body(own_rows, full_cols, scalars, *refs):
    (query_scaled, key_scaled, value_low, query_raw, key_raw) = refs[:5]
    sums, inner_sums, low_out, near_out, far_out = refs[5:]
    columns = value_low.shape[1]
    core = scalars[0] & 1
    for side, (scaled, raw) in enumerate(((query_scaled, query_raw), (key_scaled, key_raw))):
        inverse = inverse_norm(sums, side, full_cols)
        normal = raw[...] * inverse
        low_out[:, side * columns : (side + 1) * columns] = (
            inverse * (scaled[...] - normal * (tall_column(inner_sums[...], side) / full_cols))
        ).astype(jnp.bfloat16)
    low_out[:, 2 * columns :] = value_low[...]
    for at in range(low_out.shape[0] // (2 * own_rows)):
        first = low_out[pl.ds(2 * at * own_rows, own_rows), :]
        second = low_out[pl.ds((2 * at + 1) * own_rows, own_rows), :]
        near_out[pl.ds(at * own_rows, own_rows), :] = jnp.where(core == 0, first, second)
        far_out[pl.ds(at * own_rows, own_rows), :] = jnp.where(core == 0, second, first)


def finish(here, own_rows, full_cols, *args):
    rows, columns = args[0].shape
    shapes = [(rows, 3 * columns)] + [(rows // 2, 3 * columns)] * 2
    return pl.pallas_call(
        lambda *refs: finish_body(own_rows, full_cols, *refs),
        grid_spec=pltpu.PrefetchScalarGridSpec(
            num_scalar_prefetch=1,
            grid=(1,),
            in_specs=[fixed(arg.shape) for arg in args],
            out_specs=[fixed(shape, False) for shape in shapes],
        ),
        out_shape=[jax.ShapeDtypeStruct(shape, jnp.bfloat16) for shape in shapes],
        compiler_params=kernel_params(),
        cost_estimate=cost(20 * rows * columns, 24 * rows * columns),
        name="finish",
    )(here, *args)


def near_product_body(indices, transposed, scalars, own, other, own_weight, other_weight, *refs):
    pieces, value = refs[:-1], refs[-1]
    side = 1 if transposed else 0
    value[...] = contract(own[...], own_weight[...], 1, side) + contract(
        other[...], other_weight[0], 1, side
    )
    own_rows = pieces[0].shape[0]
    for at, i in enumerate(indices):
        here = pl.ds(pl.multiple_of((scalars[0] ^ i) // 2 * own_rows, own_rows), own_rows)
        pieces[at][...] = value[here, :].astype(jnp.bfloat16)


def near_product(here, indices, own, other, own_weight, pair_weight, transposed):
    rows, depth = own.shape
    width = own_weight.shape[0 if transposed else 1]
    block = min(512, width // 2)
    count = len(indices)
    if transposed:
        mine = pl.BlockSpec((block, depth), lambda j, at: (j, 0))
        theirs = pl.BlockSpec((1, block, depth), lambda j, at: (1 - (at[0] & 1), j, 0))
    else:
        mine = pl.BlockSpec((depth, block), lambda j, at: (0, j))
        theirs = pl.BlockSpec((1, depth, block), lambda j, at: (1 - (at[0] & 1), 0, j))
    results = pl.pallas_call(
        lambda *refs: near_product_body(indices, transposed, *refs),
        grid_spec=pltpu.PrefetchScalarGridSpec(
            num_scalar_prefetch=1,
            grid=(width // block,),
            in_specs=[fixed(own.shape), fixed(other.shape), mine, theirs],
            out_specs=[pl.BlockSpec((rows // count, block), lambda j, at: (0, j))] * count,
            scratch_shapes=[pltpu.VMEM((rows, block), jnp.float32)],
        ),
        out_shape=[jax.ShapeDtypeStruct((rows // count, width), jnp.bfloat16)] * count,
        compiler_params=kernel_params(),
        cost_estimate=cost(4 * rows * depth * width, 2 * rows * width + 4 * depth * width),
        name="near_product",
    )(here, own, other, own_weight, pair_weight)
    return dict(zip(indices, results))


def total_of(parts):
    total = parts[0][...].astype(jnp.float32)
    for part in parts[1:]:
        total = total + part[...].astype(jnp.float32)
    return jnp.sum(total, axis=0) if total.ndim == 3 else total


def residual_body(tokens, gain, *refs):
    hidden_out, low_out = refs[-2:]
    hidden = tokens[...].astype(jnp.float32) + total_of(refs[:-2])
    normal, _ = rms_forward(hidden)
    hidden_out[...] = hidden
    low_out[...] = (normal * gain[...]).astype(jnp.bfloat16)


def residual(tokens, gain, parts):
    rows, width = tokens.shape
    return pl.pallas_call(
        residual_body,
        grid=(1,),
        in_specs=[fixed(tokens.shape), fixed((1, width))] + [fixed(part.shape) for part in parts],
        out_specs=[fixed((rows, width), False)] * 2,
        out_shape=[
            jax.ShapeDtypeStruct((rows, width), jnp.float32),
            jax.ShapeDtypeStruct((rows, width), jnp.bfloat16),
        ],
        compiler_params=kernel_params(),
        cost_estimate=cost(10 * rows * width, 20 * rows * width),
        name="residual",
    )(tokens, gain, *parts)


def norm_back_body(values, passed, gain, near, *refs):
    grad_out, low_out, gain_out = refs[-3:]
    grad = total_of([near]) + total_of(refs[:-3]) if len(refs) > 3 else total_of([near])
    normal, inverse = rms_forward(values[...].astype(jnp.float32))
    gain_out[...] = jnp.sum(grad * normal, axis=0, keepdims=True)
    scaled = grad * gain[...]
    result = passed[...].astype(jnp.float32) + inverse * (
        scaled - normal * jnp.mean(scaled * normal, axis=-1, keepdims=True)
    )
    grad_out[...] = result
    low_out[...] = result.astype(jnp.bfloat16)


def norm_back(values, passed, gain, near, parts):
    rows, width = values.shape
    args = (values, passed, gain, near, *parts)
    return pl.pallas_call(
        norm_back_body,
        grid=(1,),
        in_specs=[fixed(arg.shape) for arg in args],
        out_specs=[fixed((rows, width), False)] * 2 + [fixed((1, width), False)],
        out_shape=[
            jax.ShapeDtypeStruct((rows, width), jnp.float32),
            jax.ShapeDtypeStruct((rows, width), jnp.bfloat16),
            jax.ShapeDtypeStruct((1, width), jnp.float32),
        ],
        compiler_params=kernel_params(),
        cost_estimate=cost(20 * rows * width, 20 * rows * width),
        name="norm_back",
    )(*args)


def mixed_back_body(indices, scalars, own_weight, other_weight, *refs):
    count = len(indices)
    pieces = refs[:count]
    rows_out, own_out, other_out, lows = refs[count:]
    own_rows = pieces[0].shape[0]
    for at, i in enumerate(indices):
        here = pl.ds(pl.multiple_of((scalars[0] ^ i) // 2 * own_rows, own_rows), own_rows)
        lows[here, :] = pieces[at][...]
    rows_out[...] = lows[...]
    own_out[...] = contract(lows[...], own_weight[...], 1, 1).astype(jnp.bfloat16)
    other_out[...] = contract(lows[...], other_weight[0], 1, 1).astype(jnp.bfloat16)


def mixed_back(here, pieces, own_weight, pair_weight):
    indices = sorted(pieces)
    own_rows, width = pieces[0].shape
    rows = own_rows * len(indices)
    depth = own_weight.shape[0]
    shapes = [(rows, width), (rows, depth), (rows, depth)]
    return pl.pallas_call(
        lambda *refs: mixed_back_body(indices, *refs),
        grid_spec=pltpu.PrefetchScalarGridSpec(
            num_scalar_prefetch=1,
            grid=(1,),
            in_specs=[
                fixed(own_weight.shape),
                pl.BlockSpec((1, depth, width), lambda j, at: (1 - (at[0] & 1), 0, 0)),
            ]
            + [fixed((own_rows, width))] * len(indices),
            out_specs=[fixed(shape, False) for shape in shapes],
            scratch_shapes=[pltpu.VMEM((rows, width), jnp.bfloat16)],
        ),
        out_shape=[jax.ShapeDtypeStruct(shape, jnp.bfloat16) for shape in shapes],
        compiler_params=kernel_params(),
        cost_estimate=cost(4 * rows * depth * width, 4 * rows * width + 4 * depth * width),
        name="mixed_back",
    )(here, own_weight, pair_weight, *[pieces[i] for i in indices])


def place_body(indices, own_rows, scalars, *refs):
    pieces, out, sems = refs[: len(indices)], refs[-2], refs[-1]
    copies = []
    for at, i in enumerate(indices):
        here = pl.ds(pl.multiple_of((scalars[0] ^ i) * own_rows, own_rows), own_rows)
        copies.append(pltpu.make_async_copy(pieces[at], out.at[here], sems.at[at]))
        copies[-1].start()
    for copy in copies:
        copy.wait()


def place_rows(here, pieces):
    indices = sorted(pieces)
    own_rows, width = pieces[0].shape
    return pl.pallas_call(
        lambda *refs: place_body(indices, own_rows, *refs),
        grid_spec=pltpu.PrefetchScalarGridSpec(
            num_scalar_prefetch=1,
            grid=(1,),
            in_specs=[fixed((own_rows, width))] * len(indices),
            out_specs=pl.BlockSpec(memory_space=pl.ANY),
            scratch_shapes=[pltpu.SemaphoreType.DMA((len(indices),))],
        ),
        out_shape=jax.ShapeDtypeStruct((own_rows * len(indices), width), pieces[0].dtype),
        compiler_params=kernel_params(),
        cost_estimate=cost(0, 4 * own_rows * len(indices) * width),
        name="place_rows",
    )(here, *[pieces[i] for i in indices])


def row_of(column):
    n = column.shape[0]
    down = lax.broadcasted_iota(jnp.int32, (n, n), 0)
    across = lax.broadcasted_iota(jnp.int32, (n, n), 1)
    return jnp.sum(jnp.where(down == across, column, 0.0), axis=0, keepdims=True)


def tall_column(rows, side):
    block = min(256, rows.shape[1])
    return jnp.concatenate(
        [
            column_of(rows[side : side + 1, at : at + block])
            for at in range(0, rows.shape[1], block)
        ],
        axis=0,
    )


def inverse_norm(sums, side, full_cols):
    return lax.rsqrt(tall_column(sums[...], side) / full_cols + EPS)


def project_in_body(tokens, gain, w_query, w_key, w_value, low_out, q_out, k_out, v_out, sums_out):
    normal, _ = rms_forward(tokens[...].astype(jnp.float32))
    low = (normal * gain[...]).astype(jnp.bfloat16)
    low_out[...] = low
    for side, (weight, out) in enumerate(((w_query, q_out), (w_key, k_out))):
        raw = contract(low, weight[...], 1, 0)
        out[...] = raw
        sums_out[side : side + 1, :] = row_of(jnp.sum(raw * raw, axis=-1, keepdims=True))
    v_out[...] = contract(low, w_value[...], 1, 0).astype(jnp.bfloat16)


def project_in(tokens, gain, w_query, w_key, w_value):
    length, width = tokens.shape
    columns = w_query.shape[1]
    block = min(256, length)
    wide = pl.BlockSpec((block, columns), lambda i: (i, 0))
    return pl.pallas_call(
        project_in_body,
        grid=(length // block,),
        in_specs=[pl.BlockSpec((block, width), lambda i: (i, 0)), fixed((1, width))]
        + [fixed(w_query.shape)] * 3,
        out_specs=[
            pl.BlockSpec((block, width), lambda i: (i, 0)),
            wide,
            wide,
            wide,
            pl.BlockSpec((2, block), lambda i: (0, i)),
        ],
        out_shape=[
            jax.ShapeDtypeStruct((length, width), jnp.bfloat16),
            jax.ShapeDtypeStruct((length, columns), jnp.float32),
            jax.ShapeDtypeStruct((length, columns), jnp.float32),
            jax.ShapeDtypeStruct((length, columns), jnp.bfloat16),
            jax.ShapeDtypeStruct((2, length), jnp.float32),
        ],
        compiler_params=kernel_params(),
        cost_estimate=cost(6 * length * width * columns, 8 * length * width),
        name="project_in",
    )(tokens, gain, w_query, w_key, w_value)


def turned(values, cosine, sine):
    return values * cosine + pltpu.roll(values, values.shape[1] // 2, 1) * sine


def head_blocks(length):
    block = min(256, length)
    return [(start, start + block) for start in range(0, length, block)]


def block_probs(queries, keys, start, end):
    scores = contract(queries, keys, 1, 1)
    down = lax.broadcasted_iota(jnp.int32, scores.shape, 0) + start
    across = lax.broadcasted_iota(jnp.int32, scores.shape, 1)
    scores = jnp.where(down >= across, scores, -1e30)
    exponent = jnp.exp(scores - jnp.max(scores, axis=-1, keepdims=True))
    return exponent * (1.0 / jnp.sum(exponent, axis=-1, keepdims=True))


def pair_split(rows, core, own_rows):
    low = jnp.concatenate(
        [rows[at : at + own_rows] for at in range(0, rows.shape[0], 2 * own_rows)], axis=0
    )
    high = jnp.concatenate(
        [rows[at : at + own_rows] for at in range(own_rows, rows.shape[0], 2 * own_rows)], axis=0
    )
    return jnp.where(core == 0, low, high), jnp.where(core == 0, high, low)


def attend_body(
    own_rows,
    full_cols,
    scalars,
    query_raw,
    key_raw,
    values,
    sums,
    cosine,
    sine,
    gains,
    q_out,
    k_out,
    near_out,
    far_out,
):
    length, columns = query_raw.shape
    core = scalars[0] & 1
    query_inv = inverse_norm(sums, 0, full_cols)
    key_inv = inverse_norm(sums, 1, full_cols)
    for head in range(columns // HEAD_DIM):
        here = pl.ds(head * HEAD_DIM, HEAD_DIM)
        query_normed = query_raw[:, here] * query_inv * gains[0:1, here]
        key_normed = key_raw[:, here] * key_inv * gains[1:2, here]
        q_out[:, here] = (
            turned(query_normed, cosine[...], sine[...]) * HEAD_DIM ** (-0.5)
        ).astype(jnp.bfloat16)
        k_out[:, here] = turned(key_normed, cosine[...], sine[...]).astype(jnp.bfloat16)
        for start, end in head_blocks(length):
            rows = pl.ds(start, end - start)
            probs = block_probs(q_out[rows, here], k_out[pl.ds(0, end), here], start, end)
            near, far = pair_split(
                contract(probs.astype(jnp.bfloat16), values[pl.ds(0, end), here], 1, 0),
                core,
                own_rows,
            )
            half = pl.ds(start // 2, (end - start) // 2)
            near_out[half, here] = near.astype(jnp.bfloat16)
            far_out[half, here] = far.astype(jnp.bfloat16)


def attend(here, own_rows, full_cols, *args):
    length, columns = args[0].shape
    shapes = [(length, columns)] * 2 + [(length // 2, columns)] * 2
    return pl.pallas_call(
        lambda *refs: attend_body(own_rows, full_cols, *refs),
        grid_spec=pltpu.PrefetchScalarGridSpec(
            num_scalar_prefetch=1,
            grid=(1,),
            in_specs=[fixed(arg.shape) for arg in args],
            out_specs=[fixed(shape, False) for shape in shapes],
        ),
        out_shape=[jax.ShapeDtypeStruct(shape, jnp.bfloat16) for shape in shapes],
        compiler_params=kernel_params(),
        cost_estimate=cost(4 * length * length * columns, 16 * length * columns),
        name="attend",
    )(here, *args)


def attend_back_body(
    own_rows,
    full_cols,
    scalars,
    near,
    far,
    queries,
    keys,
    values,
    query_raw,
    key_raw,
    sums,
    cosine,
    sine,
    gains,
    *refs,
):
    query_scaled, key_scaled, value_low, inner_out, gain_out = refs[:5]
    grads, grad_key, grad_value = refs[5:]
    length, columns = queries.shape
    core = scalars[0] & 1
    inners = [None, None]
    for at in range(length // (2 * own_rows)):
        mine, other = near[pl.ds(at * own_rows, own_rows), :], far[pl.ds(at * own_rows, own_rows), :]
        first = pl.ds(2 * at * own_rows, own_rows)
        second = pl.ds((2 * at + 1) * own_rows, own_rows)
        grads[first, :] = jnp.where(core == 0, mine, other)
        grads[second, :] = jnp.where(core == 0, other, mine)
    for head in range(columns // HEAD_DIM):
        here = pl.ds(head * HEAD_DIM, HEAD_DIM)
        grad_key[...] = jnp.zeros_like(grad_key)
        grad_value[...] = jnp.zeros_like(grad_value)
        for start, end in head_blocks(length):
            rows, past = pl.ds(start, end - start), pl.ds(0, end)
            probs = block_probs(queries[rows, here], keys[past, here], start, end)
            grad_probs = contract(grads[rows, here], values[past, here], 1, 1)
            grad_scores = (
                probs * (grad_probs - jnp.sum(probs * grad_probs, axis=-1, keepdims=True))
            ).astype(jnp.bfloat16)
            grad_value[past, :] += contract(probs.astype(jnp.bfloat16), grads[rows, here], 0, 0)
            grad_key[past, :] += contract(grad_scores, queries[rows, here], 0, 0)
            query_scaled[rows, here] = contract(grad_scores, keys[past, here], 1, 0)
        value_low[:, here] = grad_value[...].astype(jnp.bfloat16)
        sides = (
            (query_scaled[:, here] * HEAD_DIM ** (-0.5), query_raw, query_scaled),
            (grad_key[...], key_raw, key_scaled),
        )
        for side, (grad, raw, scaled_out) in enumerate(sides):
            normed = turned(grad, cosine[...], -sine[...])
            normal = raw[:, here] * inverse_norm(sums, side, full_cols)
            gain_out[side : side + 1, here] = jnp.sum(normed * normal, axis=0, keepdims=True)
            scaled = normed * gains[side : side + 1, here]
            scaled_out[:, here] = scaled
            inner = jnp.sum(scaled * normal, axis=-1, keepdims=True)
            inners[side] = inner if inners[side] is None else inners[side] + inner
    block = min(256, length)
    for side in range(2):
        for at in range(0, length, block):
            inner_out[side : side + 1, at : at + block] = row_of(inners[side][at : at + block])


def attend_back(here, own_rows, full_cols, *args):
    length, columns = args[2].shape
    wide = jax.ShapeDtypeStruct((length, columns), jnp.float32)
    outs = [
        wide,
        wide,
        jax.ShapeDtypeStruct((length, columns), jnp.bfloat16),
        jax.ShapeDtypeStruct((2, length), jnp.float32),
        jax.ShapeDtypeStruct((2, columns), jnp.float32),
    ]
    return pl.pallas_call(
        lambda *refs: attend_back_body(own_rows, full_cols, *refs),
        grid_spec=pltpu.PrefetchScalarGridSpec(
            num_scalar_prefetch=1,
            grid=(1,),
            in_specs=[fixed(arg.shape) for arg in args],
            out_specs=[fixed(out.shape, False) for out in outs],
            scratch_shapes=[pltpu.VMEM((length, columns), jnp.bfloat16)]
            + [pltpu.VMEM((length, HEAD_DIM), jnp.float32)] * 2,
        ),
        out_shape=outs,
        compiler_params=kernel_params(),
        cost_estimate=cost(8 * length * length * columns, 40 * length * columns),
        name="attend_back",
    )(here, *args)


def near_scatter(pieces):
    size = lax.axis_size("tensor")
    groups = [list(range(core, size, 2)) for core in range(2)]
    return lax.all_to_all(
        pieces, "tensor", split_axis=0, concat_axis=0, axis_index_groups=groups, tiled=True
    )


def line_step(part, step):
    bits = axis_bits("expert")[::-1]
    index = lax.axis_index("expert")
    if step < len(bits):
        bit = bits[step]
        half = part.shape[0] // 2
        high = (index // bit) % 2
        kept = lax.dynamic_slice_in_dim(part, high * half, half, 0)
        sent = lax.dynamic_slice_in_dim(part, (1 - high) * half, half, 0)
        return (
            kept.astype(jnp.float32) + swap(sent, "expert", bit).astype(jnp.float32)
        ).astype(jnp.bfloat16)
    bit = bits[2 * len(bits) - 1 - step]
    high = (index // bit) % 2 == 1
    other = swap(part, "expert", bit)
    return jnp.concatenate([jnp.where(high, other, part), jnp.where(high, part, other)], axis=0)


def send_body(indices, places, scalars, act, *refs):
    gates, (down_own, down_other), outs = refs[:places], refs[places : places + 2], refs[-places:]
    units = down_own.shape[1]
    value = contract(act[:, :units], down_own[0], 1, 0) + contract(
        act[:, units:], down_other[0], 1, 0
    )
    own_rows = outs[0].shape[1]
    for place in range(places):

        @pl.when(pl.program_id(1) == place)
        def _():
            sent = (gates[place][...] * value).astype(jnp.bfloat16)
            for at, i in enumerate(indices):
                outs[place][(scalars[0] ^ i) // 2] = sent[at * own_rows : (at + 1) * own_rows]


def expert_send(here, indices, act_all, gates, downs):
    rows = gates[0].shape[0]
    count = len(indices)
    places = len(gates)
    _, units, width = downs.shape
    block = min(1024, width // 2)
    return pl.pallas_call(
        lambda *refs: send_body(indices, places, *refs),
        grid_spec=pltpu.PrefetchScalarGridSpec(
            num_scalar_prefetch=1,
            grid=(width // block, places),
            in_specs=[pl.BlockSpec((rows, 2 * units), lambda j, k, *_: (k, 0))]
            + [fixed((rows, 1))] * places
            + [
                pl.BlockSpec((1, units, block), lambda j, k, at: (at[0] & 1, 0, j)),
                pl.BlockSpec((1, units, block), lambda j, k, at: (1 - (at[0] & 1), 0, j)),
            ],
            out_specs=[pl.BlockSpec((count, rows // count, block), lambda j, k, *_: (0, 0, j))]
            * places,
        ),
        out_shape=[jax.ShapeDtypeStruct((count, rows // count, width), jnp.bfloat16)] * places,
        compiler_params=kernel_params(),
        cost_estimate=cost(
            4 * places * rows * width * units, places * 4 * rows * width + 4 * width * units
        ),
        name="expert_send",
    )(here, act_all, *gates, downs, downs)


def on_device(
    tokens,
    positions,
    routes,
    slot_ids,
    attn_gain,
    w_query,
    w_key,
    w_value,
    query_gain,
    key_gain,
    w_out,
    ffn_gain,
    router,
    w_gate,
    w_up,
    w_down,
    grad_out,
):
    tensor_size = lax.axis_size("tensor")
    expert_size = lax.axis_size("expert")
    local_count = tensor_size // 2
    tensor_index = lax.axis_index("tensor")
    expert_index = lax.axis_index("expert")
    own_local = tensor_index // 2
    own_expert = expert_index * local_count + own_local
    length, model_width = tokens.shape
    heads_here = w_query.shape[1] // HEAD_DIM
    full_cols = w_query.shape[1] * tensor_size
    expert_count = router.shape[1]
    capacity = 3 * length * TOP // (2 * expert_count)
    own_rows = length // tensor_size
    chunks = list(range(expert_size))
    bits = axis_bits("tensor")
    near_bits = bits[:-1]
    last = len(near_bits)

    def own_slice(rows):
        return lax.dynamic_slice_in_dim(rows, tensor_index * own_rows, own_rows, 0)

    pairs = [[2 * i, 2 * i + 1] for i in range(tensor_size // 2)]

    def pair_gather(values):
        return lax.all_gather(values, "tensor", axis_index_groups=pairs)

    grad_own = own_slice(grad_out)
    near_groups = [list(range(core, tensor_size, 2)) for core in range(2)]
    grad_sent = {chunk: swap(grad_own, "expert", chunk) for chunk in chunks[1:]}
    grad_rows_of = {0: grad_out}
    out_pair = jnp.where(
        jnp.arange(2)[:, None, None] == tensor_index % 2,
        w_out[None],
        swap(w_out, "tensor", 1)[None],
    )
    expert_iota = jnp.arange(expert_count, dtype=jnp.int32)
    kept_table = jnp.sum(
        (
            (routes.T[:, None, :] == expert_iota[None, :, None]) & (slot_ids.T < capacity)[:, None, :]
        ).astype(jnp.float32),
        axis=0,
    )
    targets = jnp.arange(expert_size, dtype=jnp.int32) * local_count + own_local
    kept_rows = lax.all_to_all(
        jnp.take(kept_table, targets, axis=0).reshape(expert_size, tensor_size, own_rows),
        "expert",
        split_axis=0,
        concat_axis=0,
        tiled=True,
    )

    def here(chunk):
        return jnp.stack([tensor_index, expert_index ^ chunk]).astype(jnp.int32)

    score_scale = HEAD_DIM ** (-0.5)
    half_dim = HEAD_DIM // 2
    frequency = THETA ** (-2.0 * jnp.arange(half_dim, dtype=jnp.float32) / HEAD_DIM)
    angles = positions.astype(jnp.float32)[:, None] * frequency[None, :]
    cosine_table = jnp.concatenate([jnp.cos(angles)] * 2, axis=-1)
    sine_half = jnp.sin(angles)
    sine_table = jnp.concatenate([-sine_half, sine_half], axis=-1)
    attn_in, query_raw, key_raw, value_rows, square_sums = project_in(
        tokens, attn_gain[None, :], w_query, w_key, w_value
    )
    w_all = jnp.concatenate([w_query, w_key, w_value], axis=1)
    gains = jnp.stack([query_gain, key_gain])
    square_sums = spread_sum(square_sums, "tensor")
    indices = sorted(direct_combos(near_bits))
    gates, ups, downs = [pair_gather(weights[0]) for weights in (w_gate, w_up, w_down)]
    query_rows, key_rows, mixed_near, mixed_far = attend(
        here(0),
        own_rows,
        full_cols,
        query_raw,
        key_raw,
        value_rows,
        square_sums,
        cosine_table,
        sine_table,
        gains,
    )
    mixed_other = swap(mixed_far, "tensor", 1)
    w_pair = pair_gather(w_all)
    attn_parts = near_product(
        here(0), indices, mixed_near, mixed_other, w_out, out_pair, False
    )
    attn_moved = [swap(attn_parts[i], "tensor", i) for i in indices if i]
    hidden, ffn_in = residual(
        own_slice(tokens),
        ffn_gain[None, :],
        [attn_parts[0]] + attn_moved,
    )
    chosen = (expert_iota == own_expert).astype(jnp.float32)[None, :]
    received = [ffn_in]
    gathered = [direct_gather(ffn_in, near_bits)]
    for chunk in chunks[1:]:
        sent = tie(ffn_in, gathered[0][near_bits[0]]) if chunk > 2 else ffn_in
        received.append(swap(sent, "expert", chunk))
    waited = {1: [square_sums], 2: attn_moved}
    for chunk, piece in grad_sent.items():
        piece = tie(piece, *waited.get(chunk, [gathered[0][i] for i in indices if i] + received[1:2]))
        grad_rows_of[chunk] = lax.all_gather(piece, "tensor", axis_index_groups=near_groups)
    chain = None
    sums = []
    gate_columns = []
    for at, chunk in enumerate(chunks):
        scalars = here(chunk)
        if at:
            after = [gathered[at - 1][i] for i in gathered[at - 1] if i]
            if at >= 2:
                after.append(gate_columns[at - 2])
            gathered.append(direct_gather(received[at], near_bits, after))
        if at >= 3:
            scalars = tie(scalars, sums[at - 3])
        if at + 1 == expert_size:
            scalars = tie(scalars, w_pair)
        pieces, gate_column, chain = expert_chunk(
            at,
            expert_size,
            gathered[at],
            grad_rows_of[chunk],
            scalars,
            kept_rows,
            chosen,
            router,
            gates,
            ups,
            downs,
            chain,
        )
        gate_columns.append(gate_column)
        sums.append(near_scatter(pieces))

    def plane_total(near):
        return jnp.sum(near.astype(jnp.float32), axis=0).astype(jnp.bfloat16)

    dl_all, x_all, dy_all, act_all, own_dp, other_dp, gated_own, gated_other = chain
    row_totals = [plane_total(near) for near in sums[1:-1]]
    sent_pieces = expert_send(tie(here(0), *row_totals), indices, act_all, gate_columns, downs)
    grad_parts = [sums[0]] + [
        swap(total, "expert", chunk) for total, chunk in zip(row_totals, chunks[1:])
    ]
    row_totals.append(plane_total(tie(sums[-1], sent_pieces[0], *grad_parts[1:])))
    grad_parts.append(swap(row_totals[-1], "expert", chunks[-1]))
    sent_near = {1: near_scatter(tie(sent_pieces[1], row_totals[-1]))}
    grad_parts[0] = tie(grad_parts[0], sent_near[1])
    grad_hidden, hidden_low, grad_ffn_gain = norm_back(
        hidden, grad_own, ffn_gain[None, :], grad_parts[0], grad_parts[1:]
    )
    hidden_near, back_own, back_other = mixed_back(
        here(0), direct_gather(hidden_low, near_bits), w_out, out_pair
    )
    back_far = swap(back_other, "tensor", 1)
    for chunk in chunks[2:-1]:
        sent_near[chunk] = near_scatter(tie(sent_pieces[chunk], hidden_near))

    units = own_dp.shape[1] // 2
    other_wide = swap(contract(x_all, tie(other_dp, hidden_low), 0, 0).astype(jnp.bfloat16), "tensor", 1)
    other_down = swap(contract(gated_other, dy_all, 0, 0).astype(jnp.bfloat16), "tensor", 1)
    grad_router_part = contract(dl_all, x_all, 0, 0)

    grad_w_out = contract(mixed_near, hidden_near, 0, 0)
    grad_w_out_other = contract(mixed_other, hidden_near, 0, 0).astype(jnp.bfloat16)
    grad_w_out_low = (
        grad_w_out + swap(grad_w_out_other, "tensor", 1).astype(jnp.float32)
    ).astype(jnp.bfloat16)
    query_scaled, key_scaled, value_low, inner_sums, gain_parts = attend_back(
        tie(here(0), grad_w_out_other),
        own_rows,
        full_cols,
        back_own,
        back_far,
        query_rows,
        key_rows,
        value_rows,
        query_raw,
        key_raw,
        square_sums,
        cosine_table,
        sine_table,
        gains,
    )
    grad_w_value = contract(attn_in, value_low, 0, 0).astype(jnp.bfloat16)
    inner_sums = spread_sum(
        tie(inner_sums, *[sent_near[chunk] for chunk in chunks[2:-1]]), "tensor"
    )
    sent_near[chunks[-1]] = near_scatter(tie(sent_pieces[chunks[-1]], inner_sums))
    sent_moved = [
        swap(plane_total(sent_near[chunk]), "expert", chunk) for chunk in chunks[1:-1]
    ]
    inner_sums = tie(inner_sums, grad_w_out_low, grad_w_value, *sent_moved)
    line_steps = 2 * len(axis_bits("expert"))
    low_all, low_near, low_far = finish(
        here(0),
        own_rows,
        full_cols,
        query_scaled,
        key_scaled,
        value_low,
        query_raw,
        key_raw,
        square_sums,
        inner_sums,
    )
    grad_attn = near_product(
        here(0), indices, low_near, swap(low_far, "tensor", 1), w_all, w_pair, True
    )
    columns_here = w_query.shape[1]
    grad_w_both = contract(attn_in, low_all[:, : 2 * columns_here], 0, 0).astype(jnp.bfloat16)
    grad_attn_moved = [swap(grad_attn[i], "tensor", i) for i in indices if i]
    own_dp, gated_own = lax.optimization_barrier((own_dp, gated_own, grad_attn[0]))[:2]
    grad_gate_w = contract(x_all, own_dp[:, :units], 0, 0) + other_wide[:, :units].astype(jnp.float32)
    grad_up_w = contract(x_all, own_dp[:, units:], 0, 0) + other_wide[:, units:].astype(jnp.float32)
    grad_down = contract(gated_own, dy_all, 0, 0) + other_down.astype(jnp.float32)
    sent_moved.append(
        swap(plane_total(tie(sent_near[chunks[-1]], grad_attn[0])), "expert", chunks[-1])
    )
    _, token_low, grad_attn_gain = norm_back(
        tie(own_slice(tokens), sent_near[chunks[-1]]), grad_hidden, attn_gain[None, :], grad_attn[0], grad_attn_moved
    )

    def gather_rows(piece):
        pieces = direct_gather(piece, near_bits)
        return {**pieces, **{i ^ 1: swap(near, "tensor", 1) for i, near in pieces.items()}}

    token_pieces = gather_rows(token_low)
    grad_tokens = place_rows(here(0), token_pieces)
    late = [token_pieces[i] for i in indices if i]
    both_lines = line_step(grad_w_both, 0)
    sent_near[0] = near_scatter(tie(sent_pieces[0], token_low))
    moe_sum = hidden + jnp.sum(sent_near[0].astype(jnp.float32), axis=0)
    for moved in sent_moved:
        moe_sum = moe_sum + moved.astype(jnp.float32)
    out_pieces = gather_rows(tie(moe_sum.astype(jnp.bfloat16), *late))
    output = place_rows(here(0), out_pieces)
    both_lines = line_step(tie(both_lines, *late, *[out_pieces[i] for i in indices if i]), 1)
    for step in range(2, line_steps):
        both_lines = line_step(both_lines, step)
    sum_out, sum_value = [
        part.astype(jnp.float32) for part in lax.psum((grad_w_out_low, grad_w_value), "expert")
    ]
    sum_both = both_lines.astype(jnp.float32)
    sum_query, sum_key = sum_both[:, :columns_here], sum_both[:, columns_here:]
    plane_sums = spread_sum(
        tie(jnp.concatenate([grad_router_part, grad_ffn_gain, grad_attn_gain], axis=0), *late, sent_near[0], sent_moved[-1]),
        "tensor",
    )
    scales = gain_parts.reshape(-1)
    scales = jnp.pad(scales, (0, model_width - scales.shape[0]))
    all_sums = spread_sum(jnp.concatenate([plane_sums, scales[None, :]], axis=0), "expert")
    return (
        output,
        grad_tokens,
        all_sums[expert_count + 1],
        sum_query,
        sum_key,
        sum_value,
        all_sums[expert_count + 2, :columns_here],
        all_sums[expert_count + 2, columns_here : 2 * columns_here],
        sum_out,
        all_sums[expert_count],
        all_sums[:expert_count].T,
        grad_gate_w[None],
        grad_up_w[None],
        grad_down[None],
    )


def solution(mesh):
    placed = (
        P("expert", None),
        P("expert"),
        P("expert", None),
        P("expert", None),
        P(),
        P(None, "tensor"),
        P(None, "tensor"),
        P(None, "tensor"),
        P("tensor"),
        P("tensor"),
        P("tensor", None),
        P(),
        P(),
        P(("expert", "tensor"), None, None),
        P(("expert", "tensor"), None, None),
        P(("expert", "tensor"), None, None),
        P("expert", None),
    )
    return jax.shard_map(
        on_device,
        mesh=mesh,
        in_specs=placed,
        out_specs=(
            P("expert", None),
            P("expert", None),
            P(),
            P(None, "tensor"),
            P(None, "tensor"),
            P(None, "tensor"),
            P("tensor"),
            P("tensor"),
            P("tensor", None),
            P(),
            P(),
            P(("expert", "tensor"), None, None),
            P(("expert", "tensor"), None, None),
            P(("expert", "tensor"), None, None),
        ),
        check_vma=False,
    )
```
